32 devices in a mesh: dom: 32 (over z, y, x, core).
Axes of the slice: x: 2, y: 2, z: 4, core: 2. Of those that a mesh axis runs over, the one named last changes fastest.
Arguments:
- a_blocks: bfloat16 [768, 64, 448], P('dom'), may hold values from -0.25 to 0.25
- p_blocks: bfloat16 [768, 64, 1728], P('dom'), may hold values from -0.59765625 to 0.59765625
- cols_a: int32 [768, 7], P('dom'), may hold values from 0 to 767, as said below
- cols_p: int32 [768, 27], P('dom'), may hold values from 0 to 95, as said below
Outputs:
- coarse_op: float32 [96, 64, 4032], P('dom')
The draws below stay inside these ranges and needn't reach their ends.
Inputs may be any that keep to these rules, and one draw needn't show every extreme that they name: `cols_a`: row e lists e itself first, then 7 - 1 other distinct rows, all in the aggregates agg(e) - 1, agg(e) and agg(e) + 1, counted cyclically. `cols_p`: the 27 entries of a row are distinct aggregates within 15 of the row's own aggregate, counted cyclically.
All inputs are finite; a program needn't handle non-finite values.
Results may differ from the reference program's by a relative error of at most 0.0041.
Values may be sent and summed in bfloat16 or wider, within the bound.
No kernel may reach another device: no remote copies, remote signals or barrier semaphores. Data moves between devices by JAX's collectives and lax.ppermute only.
A program may use at most 192 MiB of HBM per device.

```python
import jax
import jax.numpy as jnp
from jax import lax

BS = 64
KA = 7
KP = 27
AGG = 8
H = 15
NC = 3
NB = 24
NF = 768
NCT = 96
WIN = 31
WSLOT = 33
BAND = 63
N_DOM = 32


def pick_rows(row_key):
    return jax.random.permutation(row_key, 3 * AGG - 1)[:KA - 1]


def pick_aggs(row_key):
    return jax.random.permutation(row_key, WIN)[:KP]


def draw_cols_a(key, part):
    row_ids = jnp.arange(NF, dtype=jnp.int32)
    row_keys = jax.random.split(jax.random.fold_in(key, 11), NF)
    picks = jax.vmap(pick_rows)(row_keys).astype(jnp.int32)
    own_pos = AGG + row_ids % AGG
    picks = picks + (picks >= own_pos[:, None]).astype(jnp.int32)
    base_row = (row_ids // AGG - 1) * AGG
    others = (base_row[:, None] + picks) % NF
    return jnp.concatenate([row_ids[:, None], others], axis=1).astype(jnp.int32)


def draw_cols_p(key, part):
    row_ids = jnp.arange(NF, dtype=jnp.int32)
    row_keys = jax.random.split(jax.random.fold_in(key, 23), NF)
    picks = jax.vmap(pick_aggs)(row_keys).astype(jnp.int32)
    own_agg = row_ids // AGG
    return ((own_agg[:, None] - H + picks) % NCT).astype(jnp.int32)


def block_scale(rng, extent, shards, least, top_value):
    loudness = 1.0
    for dim, shards_of in shards:
        steps = jax.random.uniform(jax.random.fold_in(jax.random.fold_in(rng, 6), dim), (shards_of,), jnp.float32, least / len(shards), top_value / len(shards))
        loudness = loudness * jnp.repeat(jnp.exp(steps), extent[dim] // shards_of).reshape((-1,) + (1,) * (len(extent) - 1 - dim))
    return loudness


def gaussian(own_key, extent, deviation, reach, shards=(), kind=jnp.bfloat16):
    array = deviation * jax.random.normal(own_key, extent, jnp.float32)
    if shards:
        array = array * block_scale(own_key, extent, shards, -0.22, 0.18)
    return jnp.clip(array, -reach, reach).astype(kind)


def setup_inputs(seed: int = 0) -> dict:
    seeds = jax.random.split(jax.random.key(seed), 5)
    return {
        "a_blocks": gaussian(seeds[0], (NF, BS, KA * BS), (KA * BS) ** -0.5, 0.25, ((0, 32),)),
        "p_blocks": gaussian(seeds[1], (NF, BS, KP * BS), 0.1, 0.59765625, ((0, 32),)),
        "cols_a": draw_cols_a(jax.random.fold_in(seeds[4], 71), 0),
        "cols_p": draw_cols_p(jax.random.fold_in(seeds[4], 71), 0),
    }


def band_form(p_rows, cols_rows, first_agg, count_agg):
    row_count = p_rows.shape[0]
    own_agg = (first_agg + jnp.arange(row_count, dtype=jnp.int32) // AGG) % count_agg
    offset = (cols_rows - own_agg[:, None] + H) % count_agg
    picker = (offset[:, :, None] == jnp.arange(WIN, dtype=jnp.int32)[None, None, :]).astype(jnp.float32)
    shaped = p_rows.reshape(row_count, BS, KP, BS).astype(jnp.float32)
    banded = jnp.einsum("riqc,rqs->risc", shaped, picker)
    return banded.astype(jnp.bfloat16).reshape(row_count, BS, WIN * BS)


def reference(a_blocks, p_blocks, cols_a, cols_p):
    count_agg = NC * N_DOM
    count_rows = NB * N_DOM

    def device_step(coarse, device):
        first_agg = device * NC
        first_row = device * NB
        ext_index = (first_row - AGG + jnp.arange(NB + 2 * AGG, dtype=jnp.int32)) % count_rows
        ext_band = band_form(p_blocks[ext_index], cols_p[ext_index], first_agg - 1, count_agg)
        own_band = ext_band[AGG:AGG + NB]
        padded = jnp.pad(ext_band, ((0, 0), (0, 0), (2 * BS, 2 * BS)))
        own_cols = lax.dynamic_slice_in_dim(cols_a, first_row, NB, 0)
        row_ids = first_row + jnp.arange(NB, dtype=jnp.int32)
        local_cols = (own_cols - first_row + AGG) % count_rows
        agg_shift = (own_cols // AGG - (row_ids // AGG)[:, None] + 1) % count_agg
        start_slot = (2 - agg_shift) * BS

        def frame_one(row_index, slot_index):
            zero_index = jnp.zeros((), jnp.int32)
            return lax.dynamic_slice(padded, (row_index.astype(jnp.int32), zero_index, slot_index.astype(jnp.int32)), (1, BS, WSLOT * BS))[0]

        frames = jax.vmap(jax.vmap(frame_one))(local_cols, start_slot)
        own_a = lax.dynamic_slice_in_dim(a_blocks, first_row, NB, 0).reshape(NB, BS, KA, BS)
        widened = jnp.einsum("eikj,ekjw->eiw", own_a.astype(jnp.float32), frames.astype(jnp.float32)).astype(jnp.bfloat16)
        p_group = own_band.reshape(NC, AGG * BS, WIN * BS).astype(jnp.float32)
        w_group = widened.reshape(NC, AGG * BS, WSLOT * BS).astype(jnp.float32)
        products = jnp.einsum("akx,aky->axy", p_group, w_group)
        partial_value = jnp.zeros(((NC + 2 * H) * BS, (NC + 2 * H + 2) * BS), jnp.float32)
        for local_agg in range(NC):
            offset = local_agg * BS
            partial_value = partial_value.at[offset:offset + WIN * BS, offset:offset + WSLOT * BS].add(products[local_agg])
        rounded = lax.optimization_barrier(partial_value.astype(jnp.bfloat16)).astype(jnp.float32)
        rows_band = rounded.reshape(NC + 2 * H, BS, (NC + 2 * H + 2) * BS)
        wide_cols = jnp.pad(rows_band, ((0, 0), (0, 0), (2 * H * BS, BAND * BS)))

        def skew_row(row_block, position):
            return lax.dynamic_slice_in_dim(row_block, position * BS, BAND * BS, 1)

        skewed = jax.vmap(skew_row)(wide_cols, jnp.arange(NC + 2 * H, dtype=jnp.int32))
        coarse_rows = (first_agg - H + jnp.arange(NC + 2 * H, dtype=jnp.int32)) % count_agg
        return coarse.at[coarse_rows].add(skewed), None

    start = jnp.zeros((count_agg, BS, BAND * BS), jnp.float32)
    coarse, unused = lax.scan(device_step, start, jnp.arange(N_DOM, dtype=jnp.int32))
    return coarse
```

```python
import functools

import jax
import jax.numpy as jnp
from jax import lax
from jax.experimental import pallas as pl
from jax.experimental.pallas import tpu as pltpu
from jax.sharding import PartitionSpec as P

BS = 64
KA = 7
KP = 27
AGG = 8
H = 15
NC = 3
NB = 24
WIN = 31
WSLOT = 33
BAND = 63

QUAD = 4
LANES = QUAD * BS
EXT = NB + 2 * AGG
COLS = NC + 2 * H + 2
PAD = 4
WCOLS = 44
WINDOW = 40
FAR = 36
TILES = WINDOW // QUAD
GROUPS = 5
K = NB * BS
AW = AGG * BS
FRAME = 70
NT = (((1,), (1,)), ((), ()))
ROW_ORDER = [(j, i) for j in (0, 2, 1) for i in range(GROUPS)]


def eye(n):
    rows = lax.broadcasted_iota(jnp.int32, (n, n), 0)
    lanes = lax.broadcasted_iota(jnp.int32, (n, n), 1)
    return jnp.where(rows == lanes, 1.0, 0.0).astype(jnp.bfloat16)


def low_half():
    return lax.broadcasted_iota(jnp.int32, (BS, 2 * BS), 1) < BS


def transpose_quad(block, turned, width):
    for start in range(0, width, LANES):
        size = min(LANES, width - start)
        part = lax.dot_general(
            eye(size), block[:, start : start + size], NT, preferred_element_type=jnp.float32
        )
        turned[start // BS : (start + size) // BS] = part.astype(jnp.bfloat16).reshape(
            size // BS, BS, LANES
        )


def spread_quad(turned, index, first, store, count):
    half = low_half()

    def place(slot, carry):
        for pair in range(2):
            lanes = slice(pair * 2 * BS, (pair + 1) * 2 * BS)
            left = turned[index[first + 2 * pair, slot], :, lanes]
            right = turned[index[first + 2 * pair + 1, slot], :, lanes]
            store(slot, pair, jnp.where(half, left, right))
        return carry

    lax.fori_loop(0, count, place, 0)


def build_kernel(
    core, inv_p, inv_a, p_own, p_lo, p_hi, a_own, send, far, pt_rows, wt, ext, at, turned_p, turned_a, lhs
):
    s = core[0]
    turned_p[KP] = jnp.zeros((BS, LANES), jnp.bfloat16)
    turned_a[KA] = jnp.zeros((BS, LANES), jnp.bfloat16)

    def band_quad(source, source_row, quad):
        block = source[pl.ds(source_row, QUAD)].reshape(LANES, KP * BS)
        transpose_quad(block, turned_p, KP * BS)

        def store(slot, pair, value):
            lane = pl.multiple_of(quad * LANES + pair * 2 * BS, 2 * BS)
            ext[slot, :, pl.ds(lane, 2 * BS)] = value

        spread_quad(turned_p, inv_p, quad * QUAD, store, COLS)

    halo_quads = AGG // QUAD

    @pl.loop(0, halo_quads)
    def _(quad):
        band_quad(p_lo, quad * QUAD, quad)

    @pl.loop(0, NB // QUAD)
    def _(quad):
        band_quad(p_own, quad * QUAD, quad + halo_quads)

    @pl.loop(0, halo_quads)
    def _(quad):
        band_quad(p_hi, quad * QUAD, quad + halo_quads + NB // QUAD)

    @pl.loop(0, NB // QUAD)
    def _(quad):
        block = a_own[pl.ds(quad * QUAD, QUAD)].reshape(LANES, KA * BS)
        transpose_quad(block, turned_a, KA * BS)
        agg = quad // halo_quads

        def store(slot, pair, value):
            lane = pl.multiple_of((quad % halo_quads) * LANES + pair * 2 * BS, 2 * BS)
            at[agg, slot, :, pl.ds(lane, 2 * BS)] = value

        spread_quad(turned_a, inv_a, quad * QUAD, store, 3 * AGG)

    wt[0 : PAD + NC - 1] = jnp.zeros((PAD + NC - 1, BS, K), jnp.bfloat16)
    wt[PAD + WSLOT :] = jnp.zeros((WCOLS - PAD - WSLOT, BS, K), jnp.bfloat16)
    chunk = WSLOT // 3

    @pl.loop(0, NC)
    def _(agg):
        lane = pl.multiple_of(agg * AW, AW)

        @pl.loop(0, 3)
        def _(part):
            first = agg + part * chunk
            left = ext[pl.ds(first, chunk), :, pl.ds(lane, 3 * AW)].reshape(chunk * BS, 3 * AW)
            right = at[agg].reshape(3 * AW, AW)
            value = jnp.dot(left, right, preferred_element_type=jnp.float32)
            wt[pl.ds(PAD + first, chunk), :, pl.ds(lane, AW)] = value.astype(jnp.bfloat16).reshape(
                chunk, BS, AW
            )

    own_lanes = slice(AW, AW + K)
    for position, (j, i) in enumerate(ROW_ORDER):
        pt_rows[position] = ext[6 * i + 3 + j + 1, :, own_lanes]
    far_first = 30 * s
    for place, j in enumerate((0, 2, 1)):
        for i in range(GROUPS):
            lhs[place * 6 + i] = ext[6 * i + 6 * (1 - s) + j + 1, :, own_lanes]
        lhs[place * 6 + GROUPS] = ext[far_first + j + 1, :, own_lanes]

    def emit(place, count, first_col, tile):
        right = wt[pl.ds(first_col + QUAD * tile, QUAD)].reshape(LANES, K)
        left = lhs[6 * place : 6 * (place + count)].reshape(count * 6 * BS, K)
        value = lax.dot_general(left, right, NT, preferred_element_type=jnp.float32)
        value = value.astype(jnp.bfloat16).reshape(count * 6, BS, LANES)
        lane = pl.multiple_of(tile * LANES, LANES)
        for k in range(count):
            send[pl.ds((place + k) * GROUPS, GROUPS), :, pl.ds(lane, LANES)] = value[
                6 * k : 6 * k + GROUPS
            ]
        far_tile = tile - s

        @pl.when((far_tile >= 0) & (far_tile < FAR // QUAD))
        def _():
            far_lane = pl.multiple_of(far_tile * LANES, LANES)
            for k in range(count):
                far[(0, 2, 1)[place + k], :, pl.ds(far_lane, LANES)] = value[6 * k + GROUPS]

    @pl.loop(0, TILES)
    def _(tile):
        emit(0, 2, PAD - 4 * s, tile)
        emit(2, 1, PAD - 1 - 2 * s, tile)


def sum_kernel(core, pt_rows, wt, arrived, *outs):
    s = core[0]

    def emit(place, count, first_col, tile):
        right = wt[pl.ds(first_col + QUAD * tile, QUAD)].reshape(LANES, K)
        rows = pl.ds(place * GROUPS, count * GROUPS)
        left = pt_rows[rows].reshape(count * GROUPS * BS, K)
        value = lax.dot_general(left, right, NT, preferred_element_type=jnp.float32)
        lane = pl.multiple_of(tile * LANES, LANES)
        value = value.reshape(count * GROUPS, BS, LANES)
        value = value + arrived[rows, :, pl.ds(lane, LANES)].astype(jnp.float32)
        for k in range(count):
            for i in range(GROUPS):
                target = outs[i]
                target[(0, 2, 1)[place + k], :, pl.ds(lane, LANES)] = value[
                    k * GROUPS + i
                ].astype(target.dtype)

    @pl.loop(0, TILES)
    def _(tile):
        emit(0, 2, PAD - 1 - 2 * s, tile)
        emit(2, 1, PAD - 4 * s, tile)


def total_kernel(core, own, m0, m1, m3, m4, far, out, frame):
    s = core[0]
    j = pl.program_id(0)
    frame[...] = jnp.zeros_like(frame)

    def add(message, start, blocks):
        lane = pl.multiple_of((start + 2) * BS, 2 * BS)
        frame[:, pl.ds(lane, blocks * BS)] += message[0].astype(jnp.float32)

    top = 2 * ((27 - 3 * s - j) // 2)
    for i, message in enumerate((m0, m1, own, m3, m4)):
        add(message, top - 6 * i, WINDOW)
    far_start = jnp.where(s == 1, jnp.where(j == 0, 30, 28), jnp.where(j == 2, -2, 0))
    add(far, far_start, FAR)
    out[0] = frame[:, 2 * BS : (2 + BAND) * BS]


def permuted(block, pairs):
    return lax.ppermute(block, "dom", pairs)


def inverse_index(offset, slots, empty):
    order = jnp.arange(offset.shape[1], dtype=jnp.int32)[None, :, None]
    hit = offset[:, :, None] == jnp.arange(slots, dtype=jnp.int32)[None, None, :]
    return empty + jnp.sum(jnp.where(hit, order - empty, 0), axis=1)


def body(a_blocks, p_blocks, cols_a, cols_p):
    devices = lax.axis_size("dom")
    device = lax.axis_index("dom")
    count_agg = NC * devices
    count_rows = NB * devices
    first_agg = device * NC
    first_row = device * NB
    core = (device % 2).astype(jnp.int32).reshape(1)

    def shifted(distance):
        return [(i, (i + distance) % devices) for i in range(devices)]

    p_lo = permuted(p_blocks[NB - AGG :], shifted(1))
    p_hi = permuted(p_blocks[:AGG], shifted(-1))
    cols_lo = permuted(cols_p[NB - AGG :], shifted(1))
    cols_hi = permuted(cols_p[:AGG], shifted(-1))
    ext_cols = jnp.concatenate([cols_lo, cols_p, cols_hi])
    ext_agg = jnp.arange(EXT, dtype=jnp.int32)[:, None] // AGG
    slot = (ext_cols - first_agg - (ext_agg - 1) + H) % count_agg
    inv_p = inverse_index(slot + ext_agg, COLS, KP)
    own_agg = jnp.arange(NB, dtype=jnp.int32)[:, None] // AGG
    inv_a = inverse_index((cols_a - first_row - (own_agg - 1) * AGG) % count_rows, 3 * AGG, KA)

    smem = pl.BlockSpec(memory_space=pltpu.SMEM)
    vmem = pl.BlockSpec(memory_space=pltpu.VMEM)
    bf16 = jnp.bfloat16
    params = pltpu.CompilerParams(vmem_limit_bytes=60 * 1024 * 1024)
    send, far, pt_rows, wt = pl.pallas_call(
        build_kernel,
        out_shape=[
            jax.ShapeDtypeStruct((3 * GROUPS, BS, WINDOW * BS), bf16),
            jax.ShapeDtypeStruct((NC, BS, FAR * BS), bf16),
            jax.ShapeDtypeStruct((3 * GROUPS, BS, K), bf16),
            jax.ShapeDtypeStruct((WCOLS, BS, K), bf16),
        ],
        in_specs=[smem] * 3 + [vmem] * 4,
        out_specs=[vmem] * 4,
        scratch_shapes=[
            pltpu.VMEM((COLS, BS, EXT * BS), bf16),
            pltpu.VMEM((NC, 3 * AGG, BS, AW), bf16),
            pltpu.VMEM((KP + 1, BS, LANES), bf16),
            pltpu.VMEM((KA + 1, BS, LANES), bf16),
            pltpu.VMEM((18, BS, K), bf16),
        ],
        compiler_params=params,
        cost_estimate=pl.CostEstimate(flops=24 * 10**9, bytes_accessed=30 * 10**6, transcendentals=0),
        name="build",
    )(core, inv_p, inv_a, p_blocks, p_lo, p_hi, a_blocks)

    arrived = permuted(send, [(i, i ^ 1) for i in range(devices)])
    far = permuted(far, [(i, (i + (5 if i % 2 else -5)) % devices) for i in range(devices)])
    message = jax.ShapeDtypeStruct((NC, BS, WINDOW * BS), bf16)
    m0, m1, own, m3, m4 = pl.pallas_call(
        sum_kernel,
        out_shape=[message, message, jax.ShapeDtypeStruct(message.shape, jnp.float32), message, message],
        in_specs=[smem] + [vmem] * 3,
        out_specs=[vmem] * 5,
        compiler_params=params,
        cost_estimate=pl.CostEstimate(flops=8 * 10**9, bytes_accessed=25 * 10**6, transcendentals=0),
        name="add_core",
    )(core, pt_rows, wt, arrived)
    m0 = permuted(m0, shifted(-4))
    m4 = permuted(m4, shifted(4))
    m1 = permuted(m1, shifted(-2))
    m3 = permuted(m3, shifted(2))

    def row_block(blocks):
        return pl.BlockSpec((1, BS, blocks * BS), lambda j: (j, 0, 0))

    return pl.pallas_call(
        total_kernel,
        grid=(NC,),
        out_shape=jax.ShapeDtypeStruct((NC, BS, BAND * BS), jnp.float32),
        in_specs=[smem] + [row_block(WINDOW)] * 5 + [row_block(FAR)],
        out_specs=row_block(BAND),
        scratch_shapes=[pltpu.VMEM((BS, FRAME * BS), jnp.float32)],
        compiler_params=params,
        cost_estimate=pl.CostEstimate(flops=10**7, bytes_accessed=10**7, transcendentals=0),
        name="total",
    )(core, own, m0, m1, m3, m4, far)


def solution(mesh):
    in_specs = (P("dom", None, None), P("dom", None, None), P("dom", None), P("dom", None))
    out_specs = P("dom", None, None)
    return jax.shard_map(body, mesh=mesh, in_specs=in_specs, out_specs=out_specs, check_vma=False)
```

```python
import functools

import jax
import jax.numpy as jnp
from jax import lax
from jax.experimental import pallas as pl
from jax.experimental.pallas import tpu as pltpu
from jax.sharding import PartitionSpec as P

BS = 64
KA = 7
KP = 27
AGG = 8
H = 15
NC = 3
NB = 24
WIN = 31
WSLOT = 33
BAND = 63

QUAD = 4
LANES = QUAD * BS
EXT = NB + 2 * AGG
COLS = NC + 2 * H + 2
PAD = 4
WCOLS = 44
WINDOW = 38
TILES = 10
GROUPS = 5
K = NB * BS
AW = AGG * BS
FRAME = 76
NT = (((1,), (1,)), ((), ()))
ROWS = NC * GROUPS


def eye(n):
    rows = lax.broadcasted_iota(jnp.int32, (n, n), 0)
    lanes = lax.broadcasted_iota(jnp.int32, (n, n), 1)
    return jnp.where(rows == lanes, 1.0, 0.0).astype(jnp.bfloat16)


def low_half():
    return lax.broadcasted_iota(jnp.int32, (BS, 2 * BS), 1) < BS


def transpose_quad(block, turned, width):
    for start in range(0, width, LANES):
        size = min(LANES, width - start)
        part = lax.dot_general(
            eye(size), block[:, start : start + size], NT, preferred_element_type=jnp.float32
        )
        turned[start // BS : (start + size) // BS] = part.astype(jnp.bfloat16).reshape(
            size // BS, BS, LANES
        )


def spread_quad(turned, index, first, store, count, unroll):
    half = low_half()

    def place(slot, carry):
        for pair in range(2):
            lanes = slice(pair * 2 * BS, (pair + 1) * 2 * BS)
            left = turned[index[first + 2 * pair, slot], :, lanes]
            right = turned[index[first + 2 * pair + 1, slot], :, lanes]
            store(slot, pair, jnp.where(half, left, right))
        return carry

    lax.fori_loop(0, count, place, 0, unroll=unroll)


def build_kernel(
    core, inv_p, inv_a, p_own, p_lo, p_hi, a_own, send, far, pt_rows, wt, ext, at, turned_p, turned_a, lhs
):
    s = core[0]
    turned_p[KP] = jnp.zeros((BS, LANES), jnp.bfloat16)
    turned_a[KA] = jnp.zeros((BS, LANES), jnp.bfloat16)

    def band_quad(source, source_row, quad):
        block = source[pl.ds(source_row, QUAD)].reshape(LANES, KP * BS)
        transpose_quad(block, turned_p, KP * BS)

        def store(slot, pair, value):
            lane = pl.multiple_of(quad * LANES + pair * 2 * BS, 2 * BS)
            ext[slot, :, pl.ds(lane, 2 * BS)] = value

        spread_quad(turned_p, inv_p, quad * QUAD, store, COLS, 7)

    halo_quads = AGG // QUAD

    @pl.loop(0, halo_quads)
    def _(quad):
        band_quad(p_lo, quad * QUAD, quad)

    @pl.loop(0, NB // QUAD)
    def _(quad):
        band_quad(p_own, quad * QUAD, quad + halo_quads)

    @pl.loop(0, halo_quads)
    def _(quad):
        band_quad(p_hi, quad * QUAD, quad + halo_quads + NB // QUAD)

    @pl.loop(0, NB // QUAD)
    def _(quad):
        block = a_own[pl.ds(quad * QUAD, QUAD)].reshape(LANES, KA * BS)
        transpose_quad(block, turned_a, KA * BS)
        agg = quad // halo_quads

        def store(slot, pair, value):
            lane = pl.multiple_of((quad % halo_quads) * LANES + pair * 2 * BS, 2 * BS)
            at[agg, slot, :, pl.ds(lane, 2 * BS)] = value

        spread_quad(turned_a, inv_a, quad * QUAD, store, 3 * AGG, 8)

    wt[0 : PAD + NC - 1] = jnp.zeros((PAD + NC - 1, BS, K), jnp.bfloat16)
    wt[PAD + WSLOT :] = jnp.zeros((WCOLS - PAD - WSLOT, BS, K), jnp.bfloat16)
    chunk = WSLOT // 3

    @pl.loop(0, NC)
    def _(agg):
        lane = pl.multiple_of(agg * AW, AW)

        @pl.loop(0, 3)
        def _(part):
            first = agg + part * chunk
            left = ext[pl.ds(first, chunk), :, pl.ds(lane, 3 * AW)].reshape(chunk * BS, 3 * AW)
            right = at[agg].reshape(3 * AW, AW)
            value = jnp.dot(left, right, preferred_element_type=jnp.float32)
            wt[pl.ds(PAD + first, chunk), :, pl.ds(lane, AW)] = value.astype(jnp.bfloat16).reshape(
                chunk, BS, AW
            )

    own_lanes = slice(AW, AW + K)
    for i in range(GROUPS):
        for j in range(NC):
            pt_rows[NC * i + j] = ext[6 * i + 3 + j + 1, :, own_lanes]
            lhs[NC * i + j] = ext[6 * i + 6 * (1 - s) + j + 1, :, own_lanes]
    for j in range(NC):
        lhs[ROWS + j] = ext[30 * s + j + 1, :, own_lanes]

    def emit(tile, width):
        right = wt[pl.ds(PAD - 3 * s + QUAD * tile, width // BS)].reshape(width, K)
        left = lhs[...].reshape((ROWS + NC) * BS, K)
        value = lax.dot_general(left, right, NT, preferred_element_type=jnp.float32)
        value = value.astype(jnp.bfloat16).reshape(ROWS + NC, BS, width)
        lane = pl.multiple_of(tile * LANES, LANES)
        send[:, :, pl.ds(lane, width)] = value[:ROWS]
        far[:, :, pl.ds(lane, width)] = value[ROWS:]

    @pl.loop(0, TILES - 1)
    def _(tile):
        emit(tile, LANES)

    emit(TILES - 1, LANES // 2)


def sum_kernel(core, pt_rows, wt, arrived, *outs):
    s = core[0]

    def emit(tile, width):
        right = wt[pl.ds(PAD - 3 * s + QUAD * tile, width // BS)].reshape(width, K)
        left = pt_rows[...].reshape(ROWS * BS, K)
        value = lax.dot_general(left, right, NT, preferred_element_type=jnp.float32)
        lane = pl.multiple_of(tile * LANES, LANES)
        value = value.reshape(ROWS, BS, width)
        value = value + arrived[:, :, pl.ds(lane, width)].astype(jnp.float32)
        for i in range(GROUPS):
            part = value[NC * i : NC * (i + 1)]
            outs[i][:, :, pl.ds(lane, width)] = part.astype(outs[i].dtype)

    @pl.loop(0, TILES - 1)
    def _(tile):
        emit(tile, LANES)

    emit(TILES - 1, LANES // 2)


def total_kernel(core, own, m0, m1, m3, m4, far, out, frame):
    s = core[0]
    j = pl.program_id(0)
    frame[...] = jnp.zeros_like(frame)

    def add(message, start):
        odd = start & 1
        lane = pl.multiple_of((start - odd + 6) * BS, 2 * BS)
        frame[odd, :, pl.ds(lane, WINDOW * BS)] += message[0].astype(jnp.float32)

    for i, message in enumerate((m0, m1, own, m3, m4)):
        add(message, 27 - 3 * s - j - 6 * i)
    add(far, jnp.where(s == 1, 30 - j, -3 - j))
    first, last = 6 * BS, (6 + BAND) * BS
    out[0] = frame[0, :, first:last] + frame[1, :, first - BS : last - BS]


def permuted(block, pairs):
    return lax.ppermute(block, "dom", pairs)


def inverse_index(offset, slots, empty):
    order = jnp.arange(offset.shape[1], dtype=jnp.int32)[None, :, None]
    hit = offset[:, :, None] == jnp.arange(slots, dtype=jnp.int32)[None, None, :]
    return empty + jnp.sum(jnp.where(hit, order - empty, 0), axis=1)


def body(a_blocks, p_blocks, cols_a, cols_p):
    devices = lax.axis_size("dom")
    device = lax.axis_index("dom")
    count_agg = NC * devices
    count_rows = NB * devices
    first_agg = device * NC
    first_row = device * NB
    core = (device % 2).astype(jnp.int32).reshape(1)

    def shifted(distance):
        return [(i, (i + distance) % devices) for i in range(devices)]

    p_lo = permuted(p_blocks[NB - AGG :], shifted(1))
    p_hi = permuted(p_blocks[:AGG], shifted(-1))
    cols_lo = permuted(cols_p[NB - AGG :], shifted(1))
    cols_hi = permuted(cols_p[:AGG], shifted(-1))
    ext_cols = jnp.concatenate([cols_lo, cols_p, cols_hi])
    ext_agg = jnp.arange(EXT, dtype=jnp.int32)[:, None] // AGG
    slot = (ext_cols - first_agg - (ext_agg - 1) + H) % count_agg
    inv_p = inverse_index(slot + ext_agg, COLS, KP)
    own_agg = jnp.arange(NB, dtype=jnp.int32)[:, None] // AGG
    inv_a = inverse_index((cols_a - first_row - (own_agg - 1) * AGG) % count_rows, 3 * AGG, KA)

    smem = pl.BlockSpec(memory_space=pltpu.SMEM)
    vmem = pl.BlockSpec(memory_space=pltpu.VMEM)
    bf16 = jnp.bfloat16
    params = pltpu.CompilerParams(vmem_limit_bytes=60 * 1024 * 1024)
    send, far, pt_rows, wt = pl.pallas_call(
        build_kernel,
        out_shape=[
            jax.ShapeDtypeStruct((ROWS, BS, WINDOW * BS), bf16),
            jax.ShapeDtypeStruct((NC, BS, WINDOW * BS), bf16),
            jax.ShapeDtypeStruct((ROWS, BS, K), bf16),
            jax.ShapeDtypeStruct((WCOLS, BS, K), bf16),
        ],
        in_specs=[smem] * 3 + [vmem] * 4,
        out_specs=[vmem] * 4,
        scratch_shapes=[
            pltpu.VMEM((COLS, BS, EXT * BS), bf16),
            pltpu.VMEM((NC, 3 * AGG, BS, AW), bf16),
            pltpu.VMEM((KP + 1, BS, LANES), bf16),
            pltpu.VMEM((KA + 1, BS, LANES), bf16),
            pltpu.VMEM((ROWS + NC, BS, K), bf16),
        ],
        compiler_params=params,
        cost_estimate=pl.CostEstimate(flops=24 * 10**9, bytes_accessed=30 * 10**6, transcendentals=0),
        name="build",
    )(core, inv_p, inv_a, p_blocks, p_lo, p_hi, a_blocks)

    arrived = permuted(send, [(i, i ^ 1) for i in range(devices)])
    far = permuted(far, [(i, (i + (5 if i % 2 else -5)) % devices) for i in range(devices)])
    message = jax.ShapeDtypeStruct((NC, BS, WINDOW * BS), bf16)
    m0, m1, own, m3, m4 = pl.pallas_call(
        sum_kernel,
        out_shape=[message, message, jax.ShapeDtypeStruct(message.shape, jnp.float32), message, message],
        in_specs=[smem] + [vmem] * 3,
        out_specs=[vmem] * 5,
        compiler_params=params,
        cost_estimate=pl.CostEstimate(flops=8 * 10**9, bytes_accessed=25 * 10**6, transcendentals=0),
        name="add_core",
    )(core, pt_rows, wt, arrived)
    m0 = permuted(m0, shifted(-4))
    m4 = permuted(m4, shifted(4))
    m1 = permuted(m1, shifted(-2))
    m3 = permuted(m3, shifted(2))

    def row_block(blocks):
        return pl.BlockSpec((1, BS, blocks * BS), lambda j: (j, 0, 0))

    return pl.pallas_call(
        total_kernel,
        grid=(NC,),
        out_shape=jax.ShapeDtypeStruct((NC, BS, BAND * BS), jnp.float32),
        in_specs=[smem] + [row_block(WINDOW)] * 6,
        out_specs=row_block(BAND),
        scratch_shapes=[pltpu.VMEM((2, BS, FRAME * BS), jnp.float32)],
        compiler_params=params,
        cost_estimate=pl.CostEstimate(flops=10**7, bytes_accessed=10**7, transcendentals=0),
        name="total",
    )(core, own, m0, m1, m3, m4, far)


def solution(mesh):
    in_specs = (P("dom", None, None), P("dom", None, None), P("dom", None), P("dom", None))
    out_specs = P("dom", None, None)
    return jax.shard_map(body, mesh=mesh, in_specs=in_specs, out_specs=out_specs, check_vma=False)
```

```python
import jax
import jax.numpy as jnp
from jax import lax
from jax.experimental import pallas as pl
from jax.experimental.pallas import tpu as pltpu
from jax.sharding import PartitionSpec as P

BS = 64
KA = 7
KP = 27
AGG = 8
H = 15
NC = 3
NB = 24
WIN = 31
WSLOT = 33
BAND = 63

QUAD = 4
LANES = QUAD * BS
EXT = NB + 2 * AGG
COLS = NC + 2 * H + 2
WCOLS = 40
WINDOW = 38
TILES = 10
GROUPS = 5
K = NB * BS
AW = AGG * BS
FRAME = 76
NT = (((1,), (1,)), ((), ()))
ROWS = NC * GROUPS


def eye(n):
    rows = lax.broadcasted_iota(jnp.int32, (n, n), 0)
    lanes = lax.broadcasted_iota(jnp.int32, (n, n), 1)
    return jnp.where(rows == lanes, 1.0, 0.0).astype(jnp.bfloat16)


def low_half():
    return lax.broadcasted_iota(jnp.int32, (BS, 2 * BS), 1) < BS


def transpose_quad(block, turned, width):
    for start in range(0, width, LANES):
        size = min(LANES, width - start)
        part = lax.dot_general(
            eye(size), block[:, start : start + size], NT, preferred_element_type=jnp.float32
        )
        turned[start // BS : (start + size) // BS] = part.astype(jnp.bfloat16).reshape(
            size // BS, BS, LANES
        )


def spread_quad(turned, index, first, store, count, unroll):
    half = low_half()

    def place(slot, carry):
        for pair in range(2):
            lanes = slice(pair * 2 * BS, (pair + 1) * 2 * BS)
            left = turned[index[first + 2 * pair, slot], :, lanes]
            right = turned[index[first + 2 * pair + 1, slot], :, lanes]
            store(slot, pair, jnp.where(half, left, right))
        return carry

    lax.fori_loop(0, count, place, 0, unroll=unroll)


def fast_kernel(
    core,
    inv_own,
    inv_fast,
    inv_a,
    p_own,
    p_fast,
    a_own,
    send,
    far,
    pt_fast,
    pt_slow,
    pt_other,
    wt,
    rest,
    at_halo,
    p_buf,
    ext,
    at,
    turned_p,
    turned_a,
    lhs,
    send_buf,
    far_buf,
    fast_buf,
    slow_buf,
    other_buf,
    wt_buf,
    rest_buf,
    in_sems,
    out_sems,
):
    s = core[0]
    own_quads = NB // QUAD
    halo_quads = AGG // QUAD

    def load(quad):
        if quad < own_quads:
            source = p_own.at[quad * QUAD : (quad + 1) * QUAD]
        else:
            source = p_fast.at[(quad - own_quads) * QUAD : (quad - own_quads + 1) * QUAD]
        target = p_buf.at[quad * QUAD : (quad + 1) * QUAD]
        return pltpu.make_async_copy(source, target, in_sems.at[quad])

    for quad in range(own_quads + halo_quads):
        load(quad).start()

    turned_p[KP] = jnp.zeros((BS, LANES), jnp.bfloat16)
    turned_a[KA] = jnp.zeros((BS, LANES), jnp.bfloat16)

    @pl.loop(0, own_quads)
    def _(quad):
        block = a_own[pl.ds(quad * QUAD, QUAD)].reshape(LANES, KA * BS)
        transpose_quad(block, turned_a, KA * BS)
        agg = quad // halo_quads

        def store(slot, pair, value):
            lane = pl.multiple_of((quad % halo_quads) * LANES + pair * 2 * BS, 2 * BS)
            at[agg, slot, :, pl.ds(lane, 2 * BS)] = value

        spread_quad(turned_a, inv_a, quad * QUAD, store, 3 * AGG, 8)

    slow_agg = 2 * s
    halo_copy = pltpu.make_async_copy(at.at[slow_agg, pl.ds(16 * s, AGG)], at_halo, out_sems.at[0])
    halo_copy.start()

    def band_quad(source_row, index, index_row, first_lane):
        block = p_buf[pl.ds(source_row, QUAD)].reshape(LANES, KP * BS)
        transpose_quad(block, turned_p, KP * BS)

        def store(slot, pair, value):
            lane = pl.multiple_of(first_lane + pair * 2 * BS, 2 * BS)
            ext[slot, :, pl.ds(lane, 2 * BS)] = value

        spread_quad(turned_p, index, index_row, store, COLS, 7)

    for quad in range(own_quads + halo_quads):
        load(quad).wait()

    @pl.loop(0, own_quads)
    def _(quad):
        band_quad(quad * QUAD, inv_own, quad * QUAD, AW + quad * LANES)

    @pl.loop(0, halo_quads)
    def _(quad):
        first_lane = (AW + K) * (1 - s) + quad * LANES
        band_quad((own_quads + quad) * QUAD, inv_fast, quad * QUAD, first_lane)

    fast_lanes = pl.ds(pl.multiple_of(AW + (1 - s) * AW, AW), 2 * AW)
    slow_lanes = pl.ds(pl.multiple_of(AW + 2 * s * AW, AW), AW)
    for i in range(GROUPS):
        for j in range(NC):
            row = NC * i + j
            mine, other = 6 * i + 3 + j + 1, 6 * i + 6 * (1 - s) + j + 1
            fast_buf[row] = ext[mine, :, fast_lanes]
            slow_buf[row] = ext[mine, :, slow_lanes]
            other_buf[row] = ext[other, :, slow_lanes]
            lhs[row] = ext[other, :, fast_lanes]
    for j in range(NC):
        lhs[ROWS + j] = ext[30 * s + j + 1, :, fast_lanes]
        slow_buf[ROWS + j] = ext[30 * s + j + 1, :, slow_lanes]
    copies = [halo_copy]

    def write(source, target):
        copy = pltpu.make_async_copy(source, target, out_sems.at[len(copies)])
        copy.start()
        copies.append(copy)

    write(other_buf, pt_other)
    write(fast_buf, pt_fast)
    write(slow_buf, pt_slow)

    wt_buf[0:7] = jnp.zeros((7, BS, 2 * AW), jnp.bfloat16)
    wt_buf[33:] = jnp.zeros((WCOLS - 33, BS, 2 * AW), jnp.bfloat16)
    chunk = WSLOT // 3

    @pl.loop(0, 2)
    def _(place):
        agg = place + 1 - s
        lane = pl.multiple_of(agg * AW, AW)
        target = pl.multiple_of(place * AW, AW)

        @pl.loop(0, 3)
        def _(part):
            first = agg + part * chunk
            left = ext[pl.ds(first, chunk), :, pl.ds(lane, 3 * AW)].reshape(chunk * BS, 3 * AW)
            value = jnp.dot(
                left, at[agg].reshape(3 * AW, AW), preferred_element_type=jnp.float32
            )
            wt_buf[pl.ds(3 * s + first, chunk), :, pl.ds(target, AW)] = value.astype(
                jnp.bfloat16
            ).reshape(chunk, BS, AW)

    write(wt_buf, wt)

    @pl.loop(0, 3)
    def _(part):
        lane = pl.multiple_of(AW + s * AW, AW)
        left = ext[pl.ds(slow_agg + part * chunk, chunk), :, pl.ds(lane, 2 * AW)]
        right = at[slow_agg, pl.ds(AGG - AGG * s, 2 * AGG)].reshape(2 * AW, AW)
        value = jnp.dot(
            left.reshape(chunk * BS, 2 * AW), right, preferred_element_type=jnp.float32
        )
        rest_buf[pl.ds(part * chunk, chunk)] = value.reshape(chunk, BS, AW)

    write(rest_buf, rest)

    def emit(tile, width):
        right = wt_buf[pl.ds(QUAD * tile, width // BS)].reshape(width, 2 * AW)
        left = lhs[...].reshape((ROWS + NC) * BS, 2 * AW)
        value = lax.dot_general(left, right, NT, preferred_element_type=jnp.float32)
        value = value.astype(jnp.bfloat16).reshape(ROWS + NC, BS, width)
        lanes = pl.ds(pl.multiple_of(tile * LANES, LANES), width)
        send_buf[:, :, lanes] = value[:ROWS]
        far_buf[:, :, lanes] = value[ROWS:]

    half = TILES // 2

    @pl.loop(0, half)
    def _(tile):
        emit(tile, LANES)

    write(send_buf.at[:, :, : half * LANES], send.at[:, :, : half * LANES])

    @pl.loop(half, TILES - 1)
    def _(tile):
        emit(tile, LANES)

    emit(TILES - 1, LANES // 2)
    write(send_buf.at[:, :, half * LANES :], send.at[:, :, half * LANES :])
    write(far_buf, far)
    for copy in copies:
        copy.wait()


def mine_kernel(pt_fast, wt, out):
    right = wt[...].reshape(LANES, 2 * AW)
    left = pt_fast[...].reshape(ROWS * BS, 2 * AW)
    value = lax.dot_general(left, right, NT, preferred_element_type=jnp.float32)
    out[...] = value.astype(out.dtype).reshape(ROWS, BS, LANES)


def slow_kernel(core, inv_slow, p_slow, at_halo, rest, wt, turned_p, ext):
    s = core[0]
    turned_p[KP] = jnp.zeros((BS, LANES), jnp.bfloat16)

    @pl.loop(0, AGG // QUAD)
    def _(quad):
        block = p_slow[pl.ds(quad * QUAD, QUAD)].reshape(LANES, KP * BS)
        transpose_quad(block, turned_p, KP * BS)

        def store(slot, pair, value):
            lane = pl.multiple_of(quad * LANES + pair * 2 * BS, 2 * BS)
            ext[slot, :, pl.ds(lane, 2 * BS)] = value

        spread_quad(turned_p, inv_slow, quad * QUAD, store, WSLOT, 11)

    wt[0:5] = jnp.zeros((5, BS, AW), jnp.bfloat16)
    wt[WSLOT:] = jnp.zeros((WCOLS - WSLOT, BS, AW), jnp.bfloat16)
    chunk = WSLOT // 3

    @pl.loop(0, 3)
    def _(part):
        rows = pl.ds(part * chunk, chunk)
        value = jnp.dot(
            ext[rows].reshape(chunk * BS, AW),
            at_halo[...].reshape(AW, AW),
            preferred_element_type=jnp.float32,
        )
        value = value.reshape(chunk, BS, AW) + rest[rows]
        wt[pl.ds(5 * s + part * chunk, chunk)] = value.astype(jnp.bfloat16)


def join_kernel(pt_slow, pt_other, wt_slow, wt_other, mine, arrived, far_fast, *outs):
    right = wt_slow[...].reshape(LANES, AW)
    left = pt_slow[...].reshape((ROWS + NC) * BS, AW)
    value = lax.dot_general(left, right, NT, preferred_element_type=jnp.float32)
    value = value.reshape(ROWS + NC, BS, LANES)
    right = wt_other[...].reshape(LANES, AW)
    left = pt_other[...].reshape(ROWS * BS, AW)
    other = lax.dot_general(left, right, NT, preferred_element_type=jnp.float32)
    other = other.reshape(ROWS, BS, LANES) + mine[...].astype(jnp.float32)
    near = value[:ROWS] + (other + arrived[...].astype(jnp.float32))
    for i in range(GROUPS):
        outs[i][...] = near[NC * i : NC * (i + 1)].astype(outs[i].dtype)
    outs[GROUPS][...] = (value[ROWS:] + far_fast[...].astype(jnp.float32)).astype(jnp.bfloat16)


def total_kernel(core, own, m0, m1, m3, m4, far, out, frame):
    s = core[0]
    j = pl.program_id(0)
    frame[...] = jnp.zeros_like(frame)

    def add(message, start):
        odd = start & 1
        lane = pl.multiple_of((start - odd + 6) * BS, 2 * BS)
        frame[odd, :, pl.ds(lane, WINDOW * BS)] += message[0].astype(jnp.float32)

    for i, message in enumerate((m0, m1, own, m3, m4)):
        add(message, 27 - 3 * s - j - 6 * i)
    add(far, jnp.where(s == 1, 30 - j, -3 - j))
    first, last = 6 * BS, (6 + BAND) * BS
    out[0] = frame[0, :, first:last] + frame[1, :, first - BS : last - BS]


def permuted(block, pairs):
    return lax.ppermute(block, "dom", pairs)


def inverse_index(offset, slots, empty):
    order = jnp.arange(offset.shape[1], dtype=jnp.int32)[None, :, None]
    hit = offset[:, :, None] == jnp.arange(slots, dtype=jnp.int32)[None, None, :]
    return empty + jnp.sum(jnp.where(hit, order - empty, 0), axis=1)


def body(a_blocks, p_blocks, cols_a, cols_p):
    devices = lax.axis_size("dom")
    device = lax.axis_index("dom")
    count_agg = NC * devices
    count_rows = NB * devices
    first_agg = device * NC
    first_row = device * NB
    core = (device % 2).astype(jnp.int32).reshape(1)

    def shifted(distance):
        return [(i, (i + distance) % devices) for i in range(devices)]

    high = NB - AGG
    parity = device % 2

    def halo(array, first, pairs):
        return permuted(lax.dynamic_slice_in_dim(array, first, AGG), pairs)

    outward = [(i, (i + (1 if i % 2 else -1)) % devices) for i in range(devices)]
    inward = [(i, i ^ 1) for i in range(devices)]
    cols_slow = halo(cols_p, high * parity, outward)
    p_slow = halo(p_blocks, high * parity, outward)
    cols_fast = halo(cols_p, high * (1 - parity), inward)
    p_fast = halo(p_blocks, high * (1 - parity), inward)

    def slots(cols, agg):
        return (cols - agg + H) % count_agg

    own_agg = jnp.arange(NB, dtype=jnp.int32)[:, None] // AGG
    inv_own = inverse_index(slots(cols_p, first_agg + own_agg) + own_agg + 1, COLS, KP)
    fast_place = NC * (1 - parity) - parity
    inv_fast = inverse_index(slots(cols_fast, first_agg + fast_place) + fast_place + 1, COLS, KP)
    slow_place = NC * parity - (1 - parity)
    inv_slow = inverse_index(slots(cols_slow, first_agg + slow_place) + 2 * parity, WSLOT, KP)
    inv_a = inverse_index((cols_a - first_row - (own_agg - 1) * AGG) % count_rows, 3 * AGG, KA)

    smem = pl.BlockSpec(memory_space=pltpu.SMEM)
    vmem = pl.BlockSpec(memory_space=pltpu.VMEM)
    hbm = pl.BlockSpec(memory_space=pl.ANY)
    bf16 = jnp.bfloat16

    def params(mebibytes):
        return pltpu.CompilerParams(vmem_limit_bytes=mebibytes * 1024 * 1024)

    def cost(flops, size):
        return pl.CostEstimate(flops=flops, bytes_accessed=size, transcendentals=0)

    shapes = [
        (ROWS, BS, WINDOW * BS),
        (NC, BS, WINDOW * BS),
        (ROWS, BS, 2 * AW),
        (ROWS + NC, BS, AW),
        (ROWS, BS, AW),
        (WCOLS, BS, 2 * AW),
        (WSLOT, BS, AW),
        (AGG, BS, AW),
    ]
    kinds = [bf16] * 6 + [jnp.float32, bf16]
    send, far, pt_fast, pt_slow, pt_other, wt_fast, rest, at_halo = pl.pallas_call(
        fast_kernel,
        out_shape=[jax.ShapeDtypeStruct(shape, kind) for shape, kind in zip(shapes, kinds)],
        in_specs=[smem] * 4 + [hbm, hbm, vmem],
        out_specs=[hbm] * 8,
        scratch_shapes=[
            pltpu.VMEM((NB + AGG, BS, KP * BS), bf16),
            pltpu.VMEM((COLS, BS, EXT * BS), bf16),
            pltpu.VMEM((NC, 3 * AGG, BS, AW), bf16),
            pltpu.VMEM((KP + 1, BS, LANES), bf16),
            pltpu.VMEM((KA + 1, BS, LANES), bf16),
            pltpu.VMEM((ROWS + NC, BS, 2 * AW), bf16),
        ]
        + [pltpu.VMEM(shape, kind) for shape, kind in zip(shapes[:7], kinds[:7])]
        + [pltpu.SemaphoreType.DMA(((NB + AGG) // QUAD,)), pltpu.SemaphoreType.DMA((9,))],
        compiler_params=params(56),
        cost_estimate=cost(20 * 10**9, 30 * 10**6),
        name="fast",
    )(core, inv_own, inv_fast, inv_a, p_blocks, p_fast, a_blocks)

    arrived = permuted(send, inward)
    pt_other = permuted(pt_other, inward)

    def lane_tile(rows):
        return pl.BlockSpec((rows, BS, LANES), lambda n: (0, 0, n))

    def col_tile(width):
        return pl.BlockSpec((QUAD, BS, width), lambda n: (n, 0, 0))

    def whole(rows, width):
        return pl.BlockSpec((rows, BS, width), lambda n: (0, 0, 0))

    mine = pl.pallas_call(
        mine_kernel,
        grid=(TILES,),
        out_shape=jax.ShapeDtypeStruct((ROWS, BS, WINDOW * BS), bf16),
        in_specs=[whole(ROWS, 2 * AW), col_tile(2 * AW)],
        out_specs=lane_tile(ROWS),
        compiler_params=params(16),
        cost_estimate=cost(60 * 10**9, 120 * 10**6),
        name="mine",
    )(pt_fast, wt_fast)

    wt_slow = pl.pallas_call(
        slow_kernel,
        out_shape=jax.ShapeDtypeStruct((WCOLS, BS, AW), bf16),
        in_specs=[smem] * 2 + [vmem] * 3,
        out_specs=vmem,
        scratch_shapes=[
            pltpu.VMEM((KP + 1, BS, LANES), bf16),
            pltpu.VMEM((WSLOT, BS, AW), bf16),
        ],
        compiler_params=params(24),
        cost_estimate=cost(20 * 10**9, 120 * 10**6),
        name="slow",
    )(core, inv_slow, p_slow, at_halo, rest)
    wt_other = permuted(wt_slow, inward)

    message = jax.ShapeDtypeStruct((NC, BS, WINDOW * BS), bf16)
    m0, m1, own, m3, m4, far = pl.pallas_call(
        join_kernel,
        grid=(TILES,),
        out_shape=[message] * 2
        + [jax.ShapeDtypeStruct(message.shape, jnp.float32)]
        + [message] * 3,
        in_specs=[whole(ROWS + NC, AW), whole(ROWS, AW)]
        + [col_tile(AW)] * 2
        + [lane_tile(ROWS)] * 2
        + [lane_tile(NC)],
        out_specs=[lane_tile(NC)] * 6,
        compiler_params=params(24),
        cost_estimate=cost(5 * 10**9, 22 * 10**6),
        name="join",
    )(pt_slow, pt_other, wt_slow, wt_other, mine, arrived, far)
    far = permuted(far, [(i, (i + (5 if i % 2 else -5)) % devices) for i in range(devices)])
    m0 = permuted(m0, shifted(-4))
    m4 = permuted(m4, shifted(4))
    m1 = permuted(m1, shifted(-2))
    m3 = permuted(m3, shifted(2))

    def row_block(blocks):
        return pl.BlockSpec((1, BS, blocks * BS), lambda j: (j, 0, 0))

    return pl.pallas_call(
        total_kernel,
        grid=(NC,),
        out_shape=jax.ShapeDtypeStruct((NC, BS, BAND * BS), jnp.float32),
        in_specs=[smem] + [row_block(WINDOW)] * 6,
        out_specs=row_block(BAND),
        scratch_shapes=[pltpu.VMEM((2, BS, FRAME * BS), jnp.float32)],
        compiler_params=params(20),
        cost_estimate=pl.CostEstimate(flops=10**7, bytes_accessed=10**7, transcendentals=0),
        name="total",
    )(core, own, m0, m1, m3, m4, far)


def solution(mesh):
    in_specs = (P("dom", None, None), P("dom", None, None), P("dom", None), P("dom", None))
    out_specs = P("dom", None, None)
    return jax.shard_map(body, mesh=mesh, in_specs=in_specs, out_specs=out_specs, check_vma=False)
```

```python
import functools

import jax
import jax.numpy as jnp
from jax import lax
from jax.experimental import pallas as pl
from jax.experimental.pallas import tpu as pltpu
from jax.sharding import PartitionSpec as P

BS = 64
KA = 7
KP = 27
AGG = 8
H = 15
NC = 3
NB = 24
WIN = 31
WSLOT = 33
BAND = 63

QUAD = 4
LANES = QUAD * BS
EXT = NB + 2 * AGG
COLS = NC + 2 * H + 2
WCOLS = 40
WINDOW = 38
TILES = 10
GROUPS = 5
K = NB * BS
AW = AGG * BS
FRAME = 76
NT = (((1,), (1,)), ((), ()))
ROWS = NC * GROUPS
FIRST = 2 * NC
REST = ROWS - FIRST
ORDER = (0, 4, 1, 3, 2)


def eye(n):
    rows = lax.broadcasted_iota(jnp.int32, (n, n), 0)
    lanes = lax.broadcasted_iota(jnp.int32, (n, n), 1)
    return jnp.where(rows == lanes, 1.0, 0.0).astype(jnp.bfloat16)


def low_half():
    return lax.broadcasted_iota(jnp.int32, (BS, 2 * BS), 1) < BS


def transpose_quad(block, turned, width):
    for start in range(0, width, LANES):
        size = min(LANES, width - start)
        part = lax.dot_general(
            eye(size), block[:, start : start + size], NT, preferred_element_type=jnp.float32
        )
        turned[start // BS : (start + size) // BS] = part.astype(jnp.bfloat16).reshape(
            size // BS, BS, LANES
        )


def spread_quad(turned, index, first, store, count, unroll):
    half = low_half()

    def place(slot, carry):
        for pair in range(2):
            lanes = slice(pair * 2 * BS, (pair + 1) * 2 * BS)
            left = turned[index[first + 2 * pair, slot], :, lanes]
            right = turned[index[first + 2 * pair + 1, slot], :, lanes]
            store(slot, pair, jnp.where(half, left, right))
        return carry

    lax.fori_loop(0, count, place, 0, unroll=unroll)


def fast_kernel(
    core,
    inv_own,
    inv_fast,
    inv_a,
    p_own,
    p_fast,
    a_own,
    send_low,
    send_high,
    send_rest,
    far,
    fast_first,
    fast_rest,
    slow_first,
    slow_rest,
    other_first,
    other_rest,
    wt,
    rest,
    at_halo,
    p_buf,
    ext,
    at,
    turned_p,
    turned_a,
    lhs,
    send_buf,
    far_buf,
    fast_buf,
    slow_buf,
    other_buf,
    wt_buf,
    rest_buf,
    in_sems,
    out_sems,
):
    s = core[0]
    own_quads = NB // QUAD
    halo_quads = AGG // QUAD

    def load(quad):
        if quad < own_quads:
            source = p_own.at[quad * QUAD : (quad + 1) * QUAD]
        else:
            source = p_fast.at[(quad - own_quads) * QUAD : (quad - own_quads + 1) * QUAD]
        target = p_buf.at[quad * QUAD : (quad + 1) * QUAD]
        return pltpu.make_async_copy(source, target, in_sems.at[quad])

    for quad in range(own_quads + halo_quads):
        load(quad).start()

    turned_p[KP] = jnp.zeros((BS, LANES), jnp.bfloat16)
    turned_a[KA] = jnp.zeros((BS, LANES), jnp.bfloat16)

    @pl.loop(0, own_quads)
    def _(quad):
        block = a_own[pl.ds(quad * QUAD, QUAD)].reshape(LANES, KA * BS)
        transpose_quad(block, turned_a, KA * BS)
        agg = quad // halo_quads

        def store(slot, pair, value):
            lane = pl.multiple_of((quad % halo_quads) * LANES + pair * 2 * BS, 2 * BS)
            at[agg, slot, :, pl.ds(lane, 2 * BS)] = value

        spread_quad(turned_a, inv_a, quad * QUAD, store, 3 * AGG, 8)

    slow_agg = 2 * s
    halo_copy = pltpu.make_async_copy(at.at[slow_agg, pl.ds(16 * s, AGG)], at_halo, out_sems.at[0])
    halo_copy.start()

    def band_quad(source_row, index, index_row, first_lane):
        block = p_buf[pl.ds(source_row, QUAD)].reshape(LANES, KP * BS)
        transpose_quad(block, turned_p, KP * BS)

        def store(slot, pair, value):
            lane = pl.multiple_of(first_lane + pair * 2 * BS, 2 * BS)
            ext[slot, :, pl.ds(lane, 2 * BS)] = value

        spread_quad(turned_p, index, index_row, store, COLS, 7)

    for quad in range(own_quads + halo_quads):
        load(quad).wait()

    @pl.loop(0, own_quads)
    def _(quad):
        band_quad(quad * QUAD, inv_own, quad * QUAD, AW + quad * LANES)

    @pl.loop(0, halo_quads)
    def _(quad):
        first_lane = (AW + K) * (1 - s) + quad * LANES
        band_quad((own_quads + quad) * QUAD, inv_fast, quad * QUAD, first_lane)

    fast_lanes = pl.ds(pl.multiple_of(AW + (1 - s) * AW, AW), 2 * AW)
    slow_lanes = pl.ds(pl.multiple_of(AW + 2 * s * AW, AW), AW)
    for place, i in enumerate(ORDER):
        for j in range(NC):
            row = NC * place + j
            mine, other = 6 * i + 3 + j + 1, 6 * i + 6 * (1 - s) + j + 1
            fast_buf[row] = ext[mine, :, fast_lanes]
            slow_buf[row if place < 2 else row + NC] = ext[mine, :, slow_lanes]
            other_buf[row] = ext[other, :, slow_lanes]
            lhs[row] = ext[other, :, fast_lanes]
    for j in range(NC):
        lhs[ROWS + j] = ext[30 * s + j + 1, :, fast_lanes]
        slow_buf[FIRST + j] = ext[30 * s + j + 1, :, slow_lanes]
    copies = [halo_copy]

    def write(source, target):
        copy = pltpu.make_async_copy(source, target, out_sems.at[len(copies)])
        copy.start()
        copies.append(copy)

    write(other_buf.at[:FIRST], other_first)
    write(other_buf.at[FIRST:], other_rest)
    write(fast_buf.at[:FIRST], fast_first)
    write(fast_buf.at[FIRST:], fast_rest)
    write(slow_buf.at[: FIRST + NC], slow_first)
    write(slow_buf.at[FIRST + NC :], slow_rest)

    wt_buf[0:7] = jnp.zeros((7, BS, 2 * AW), jnp.bfloat16)
    wt_buf[33:] = jnp.zeros((WCOLS - 33, BS, 2 * AW), jnp.bfloat16)
    chunk = WSLOT // 3

    @pl.loop(0, 2)
    def _(place):
        agg = place + 1 - s
        lane = pl.multiple_of(agg * AW, AW)
        target = pl.multiple_of(place * AW, AW)

        @pl.loop(0, 3)
        def _(part):
            first = agg + part * chunk
            left = ext[pl.ds(first, chunk), :, pl.ds(lane, 3 * AW)].reshape(chunk * BS, 3 * AW)
            value = jnp.dot(
                left, at[agg].reshape(3 * AW, AW), preferred_element_type=jnp.float32
            )
            wt_buf[pl.ds(3 * s + first, chunk), :, pl.ds(target, AW)] = value.astype(
                jnp.bfloat16
            ).reshape(chunk, BS, AW)

    write(wt_buf, wt)

    @pl.loop(0, 3)
    def _(part):
        lane = pl.multiple_of(AW + s * AW, AW)
        left = ext[pl.ds(slow_agg + part * chunk, chunk), :, pl.ds(lane, 2 * AW)]
        right = at[slow_agg, pl.ds(AGG - AGG * s, 2 * AGG)].reshape(2 * AW, AW)
        value = jnp.dot(
            left.reshape(chunk * BS, 2 * AW), right, preferred_element_type=jnp.float32
        )
        rest_buf[pl.ds(part * chunk, chunk)] = value.reshape(chunk, BS, AW)

    write(rest_buf, rest)

    def emit(tile, width):
        right = wt_buf[pl.ds(QUAD * tile, width // BS)].reshape(width, 2 * AW)
        left = lhs[...].reshape((ROWS + NC) * BS, 2 * AW)
        value = lax.dot_general(left, right, NT, preferred_element_type=jnp.float32)
        value = value.astype(jnp.bfloat16).reshape(ROWS + NC, BS, width)
        lanes = pl.ds(pl.multiple_of(tile * LANES, LANES), width)
        send_buf[:, :, lanes] = value[:ROWS]
        far_buf[:, :, lanes] = value[ROWS:]

    @pl.loop(0, TILES - 1)
    def _(tile):
        emit(tile, LANES)

    emit(TILES - 1, LANES // 2)
    write(send_buf.at[:NC], send_low)
    write(send_buf.at[NC:FIRST], send_high)
    write(send_buf.at[FIRST:], send_rest)
    write(far_buf, far)
    for copy in copies:
        copy.wait()


def tile_dot(rows, cols):
    left = rows[...].reshape(rows.shape[0] * BS, rows.shape[2])
    right = cols[...].reshape(LANES, cols.shape[2])
    value = lax.dot_general(left, right, NT, preferred_element_type=jnp.float32)
    return value.reshape(rows.shape[0], BS, LANES)


def mine_kernel(pt_fast, wt_fast, low, high, out):
    value = tile_dot(pt_fast, wt_fast)
    out[:NC] = value[:NC] + low[...].astype(jnp.float32)
    out[NC:] = value[NC:] + high[...].astype(jnp.float32)


def slow_kernel(core, inv_slow, p_slow, at_halo, rest, wt, turned_p, ext, at_buf, rest_buf, sems):
    s = core[0]
    copies = [
        pltpu.make_async_copy(at_halo, at_buf, sems.at[0]),
        pltpu.make_async_copy(rest, rest_buf, sems.at[1]),
    ]
    for copy in copies:
        copy.start()
    turned_p[KP] = jnp.zeros((BS, LANES), jnp.bfloat16)

    @pl.loop(0, AGG // QUAD)
    def _(quad):
        block = p_slow[pl.ds(quad * QUAD, QUAD)].reshape(LANES, KP * BS)
        transpose_quad(block, turned_p, KP * BS)

        def store(slot, pair, value):
            lane = pl.multiple_of(quad * LANES + pair * 2 * BS, 2 * BS)
            ext[slot, :, pl.ds(lane, 2 * BS)] = value

        spread_quad(turned_p, inv_slow, quad * QUAD, store, WSLOT, 11)

    wt[0:5] = jnp.zeros((5, BS, AW), jnp.bfloat16)
    wt[WSLOT:] = jnp.zeros((WCOLS - WSLOT, BS, AW), jnp.bfloat16)
    chunk = WSLOT // 3
    for copy in copies:
        copy.wait()

    @pl.loop(0, 3)
    def _(part):
        rows = pl.ds(part * chunk, chunk)
        value = jnp.dot(
            ext[rows].reshape(chunk * BS, AW),
            at_buf[...].reshape(AW, AW),
            preferred_element_type=jnp.float32,
        )
        value = value.reshape(chunk, BS, AW) + rest_buf[rows]
        wt[pl.ds(5 * s + part * chunk, chunk)] = value.astype(jnp.bfloat16)


def join_first_kernel(slow, other, wt_slow, wt_other, mine, far_fast, m0, m4, far):
    value = tile_dot(slow, wt_slow)
    near = value[:FIRST] + (tile_dot(other, wt_other) + mine[...])
    m0[...] = near[:NC].astype(jnp.bfloat16)
    m4[...] = near[NC:].astype(jnp.bfloat16)
    far[...] = (value[FIRST:] + far_fast[...].astype(jnp.float32)).astype(jnp.bfloat16)


def join_rest_kernel(fast, slow, other, wt_fast, wt_slow, wt_other, arrived, m1, m3, own):
    value = tile_dot(fast, wt_fast) + tile_dot(slow, wt_slow) + tile_dot(other, wt_other)
    value = value + arrived[...].astype(jnp.float32)
    m1[...] = value[:NC].astype(jnp.bfloat16)
    m3[...] = value[NC : 2 * NC].astype(jnp.bfloat16)
    own[...] = value[2 * NC :]


def frame_add(frame, message, start):
    odd = start & 1
    lane = pl.multiple_of((start - odd + 6) * BS, 2 * BS)
    frame[odd, :, pl.ds(lane, WINDOW * BS)] += message[0].astype(jnp.float32)


def frame_sum(frame):
    first, last = 6 * BS, (6 + BAND) * BS
    return frame[0, :, first:last] + frame[1, :, first - BS : last - BS]


def early_kernel(core, own, m0, m4, far, out, frame):
    s = core[0]
    j = pl.program_id(0)
    frame[...] = jnp.zeros_like(frame)
    top = 27 - 3 * s - j
    frame_add(frame, m0, top)
    frame_add(frame, own, top - 12)
    frame_add(frame, m4, top - 24)
    frame_add(frame, far, jnp.where(s == 1, 30 - j, -3 - j))
    out[0] = frame_sum(frame)


def total_kernel(core, early, m1, m3, out, frame):
    s = core[0]
    j = pl.program_id(0)
    frame[...] = jnp.zeros_like(frame)
    top = 27 - 3 * s - j
    frame_add(frame, m1, top - 6)
    frame_add(frame, m3, top - 18)
    out[0] = early[0] + frame_sum(frame)


def pick_kernel(core, source, out, sems, *, outer):
    s = core[0]
    first = (NB - AGG) * (s if outer else 1 - s)
    step = AGG // 4
    copies = [
        pltpu.make_async_copy(
            source.at[pl.ds(first + k * step, step)],
            out.at[k * step : (k + 1) * step],
            sems.at[k],
        )
        for k in range(4)
    ]
    for copy in copies:
        copy.start()
    for copy in copies:
        copy.wait()


def permuted(block, pairs):
    return lax.ppermute(block, "dom", pairs)


def inverse_index(offset, slots, empty):
    order = jnp.arange(offset.shape[1], dtype=jnp.int32)[None, :, None]
    hit = offset[:, :, None] == jnp.arange(slots, dtype=jnp.int32)[None, None, :]
    return empty + jnp.sum(jnp.where(hit, order - empty, 0), axis=1)


def body(a_blocks, p_blocks, cols_a, cols_p):
    devices = lax.axis_size("dom")
    device = lax.axis_index("dom")
    count_agg = NC * devices
    count_rows = NB * devices
    first_agg = device * NC
    first_row = device * NB
    core = (device % 2).astype(jnp.int32).reshape(1)

    def shifted(distance):
        return [(i, (i + distance) % devices) for i in range(devices)]

    parity = device % 2
    smem = pl.BlockSpec(memory_space=pltpu.SMEM)
    vmem = pl.BlockSpec(memory_space=pltpu.VMEM)
    hbm = pl.BlockSpec(memory_space=pltpu.HBM)
    bf16 = jnp.bfloat16

    def params(mebibytes):
        return pltpu.CompilerParams(vmem_limit_bytes=mebibytes * 1024 * 1024)

    def cost(flops, size):
        return pl.CostEstimate(flops=flops, bytes_accessed=size, transcendentals=0)

    def picked(outer):
        return pl.pallas_call(
            functools.partial(pick_kernel, outer=outer),
            out_shape=jax.ShapeDtypeStruct((AGG,) + p_blocks.shape[1:], bf16),
            in_specs=[smem, hbm],
            out_specs=hbm,
            scratch_shapes=[pltpu.SemaphoreType.DMA((4,))],
            compiler_params=params(60),
            name="pick_outer" if outer else "pick_inner",
        )(core, p_blocks)

    outward = [(i, (i + (1 if i % 2 else -1)) % devices) for i in range(devices)]
    inward = [(i, i ^ 1) for i in range(devices)]
    p_slow = permuted(picked(True), outward)
    p_fast = permuted(picked(False), inward)
    edge_cols = jnp.stack([cols_p[:AGG], cols_p[NB - AGG :]])
    cols_slow = permuted(edge_cols[parity], outward)
    cols_fast = permuted(edge_cols[1 - parity], inward)

    def slots(cols, agg):
        return (cols - agg + H) % count_agg

    own_agg = jnp.arange(NB, dtype=jnp.int32)[:, None] // AGG
    inv_own = inverse_index(slots(cols_p, first_agg + own_agg) + own_agg + 1, COLS, KP)
    fast_place = NC * (1 - parity) - parity
    inv_fast = inverse_index(slots(cols_fast, first_agg + fast_place) + fast_place + 1, COLS, KP)
    slow_place = NC * parity - (1 - parity)
    inv_slow = inverse_index(slots(cols_slow, first_agg + slow_place) + 2 * parity, WSLOT, KP)
    inv_a = inverse_index((cols_a - first_row - (own_agg - 1) * AGG) % count_rows, 3 * AGG, KA)

    def block(rows, width, kind=bf16):
        return jax.ShapeDtypeStruct((rows, BS, width), kind)

    span = WINDOW * BS
    outs = [
        block(NC, span),
        block(NC, span),
        block(REST, span),
        block(NC, span),
        block(FIRST, 2 * AW),
        block(REST, 2 * AW),
        block(FIRST + NC, AW),
        block(REST, AW),
        block(FIRST, AW),
        block(REST, AW),
        block(WCOLS, 2 * AW),
        block(WSLOT, AW, jnp.float32),
        block(AGG, AW),
    ]
    (
        send_low,
        send_high,
        send_rest,
        far,
        fast_first,
        fast_rest,
        slow_first,
        slow_rest,
        other_first,
        other_rest,
        wt_fast,
        rest,
        at_halo,
    ) = pl.pallas_call(
        fast_kernel,
        out_shape=outs,
        in_specs=[smem] * 4 + [hbm, hbm, vmem],
        out_specs=[hbm] * len(outs),
        scratch_shapes=[
            pltpu.VMEM((NB + AGG, BS, KP * BS), bf16),
            pltpu.VMEM((COLS, BS, EXT * BS), bf16),
            pltpu.VMEM((NC, 3 * AGG, BS, AW), bf16),
            pltpu.VMEM((KP + 1, BS, LANES), bf16),
            pltpu.VMEM((KA + 1, BS, LANES), bf16),
            pltpu.VMEM((ROWS + NC, BS, 2 * AW), bf16),
            pltpu.VMEM((ROWS, BS, span), bf16),
            pltpu.VMEM((NC, BS, span), bf16),
            pltpu.VMEM((ROWS, BS, 2 * AW), bf16),
            pltpu.VMEM((ROWS + NC, BS, AW), bf16),
            pltpu.VMEM((ROWS, BS, AW), bf16),
            pltpu.VMEM((WCOLS, BS, 2 * AW), bf16),
            pltpu.VMEM((WSLOT, BS, AW), jnp.float32),
            pltpu.SemaphoreType.DMA(((NB + AGG) // QUAD,)),
            pltpu.SemaphoreType.DMA((len(outs),)),
        ],
        compiler_params=params(56),
        cost_estimate=cost(20 * 10**9, 30 * 10**6),
        name="fast",
    )(core, inv_own, inv_fast, inv_a, p_blocks, p_fast, a_blocks)

    low = permuted(send_low, inward)
    high = permuted(send_high, inward)
    other_first = permuted(other_first, inward)
    p_slow, low, high, other_first = lax.optimization_barrier((p_slow, low, high, other_first))

    def lane_tile(rows):
        return pl.BlockSpec((rows, BS, LANES), lambda n: (0, 0, n))

    def col_tile(width):
        return pl.BlockSpec((QUAD, BS, width), lambda n: (n, 0, 0))

    def whole(rows, width):
        return pl.BlockSpec((rows, BS, width), lambda n: (0, 0, 0))

    wt_slow = pl.pallas_call(
        slow_kernel,
        out_shape=block(WCOLS, AW),
        in_specs=[smem] * 2 + [vmem, hbm, hbm],
        out_specs=vmem,
        scratch_shapes=[
            pltpu.VMEM((KP + 1, BS, LANES), bf16),
            pltpu.VMEM((WSLOT, BS, AW), bf16),
            pltpu.VMEM((AGG, BS, AW), bf16),
            pltpu.VMEM((WSLOT, BS, AW), jnp.float32),
            pltpu.SemaphoreType.DMA((2,)),
        ],
        compiler_params=params(60),
        cost_estimate=cost(20 * 10**9, 200 * 10**6),
        name="slow",
    )(core, inv_slow, p_slow, at_halo, rest)
    wt_other = permuted(wt_slow, inward)

    wt_slow, low, high = lax.optimization_barrier((wt_slow, low, high))
    mine = pl.pallas_call(
        mine_kernel,
        grid=(TILES,),
        out_shape=block(FIRST, span, jnp.float32),
        in_specs=[whole(FIRST, 2 * AW), col_tile(2 * AW), lane_tile(NC), lane_tile(NC)],
        out_specs=lane_tile(FIRST),
        compiler_params=params(60),
        cost_estimate=cost(10**10, 100 * 10**6),
        name="mine",
    )(fast_first, wt_fast, low, high)
    mine, wt_other, send_rest, other_rest = lax.optimization_barrier(
        (mine, wt_other, send_rest, other_rest)
    )
    arrived_rest = permuted(send_rest, inward)
    other_rest = permuted(other_rest, inward)
    m0, m4, far = pl.pallas_call(
        join_first_kernel,
        grid=(TILES,),
        out_shape=[block(NC, span)] * 3,
        in_specs=[whole(FIRST + NC, AW), whole(FIRST, AW)]
        + [col_tile(AW)] * 2
        + [lane_tile(FIRST), lane_tile(NC)],
        out_specs=[lane_tile(NC)] * 3,
        compiler_params=params(16),
        cost_estimate=cost(3 * 10**9, 10**7),
        name="join_first",
    )(slow_first, other_first, wt_slow, wt_other, mine, far)
    m0 = permuted(m0, shifted(-4))
    m4 = permuted(m4, shifted(4))
    far = permuted(far, [(i, (i + (5 if i % 2 else -5)) % devices) for i in range(devices)])
    m1, m3, own = pl.pallas_call(
        join_rest_kernel,
        grid=(TILES,),
        out_shape=[block(NC, span)] * 2 + [block(NC, span, jnp.float32)],
        in_specs=[whole(REST, 2 * AW), whole(REST, AW), whole(REST, AW)]
        + [col_tile(2 * AW), col_tile(AW), col_tile(AW), lane_tile(REST)],
        out_specs=[lane_tile(NC)] * 3,
        compiler_params=params(24),
        cost_estimate=cost(40 * 10**9, 200 * 10**6),
        name="join_rest",
    )(fast_rest, slow_rest, other_rest, wt_fast, wt_slow, wt_other, arrived_rest)
    m1 = permuted(m1, shifted(-2))
    m3 = permuted(m3, shifted(2))

    def row_block(blocks):
        return pl.BlockSpec((1, BS, blocks * BS), lambda j: (j, 0, 0))

    def summed(kernel, name, *terms):
        return pl.pallas_call(
            kernel,
            grid=(NC,),
            out_shape=block(NC, BAND * BS, jnp.float32),
            in_specs=[smem] + [row_block(term.shape[2] // BS) for term in terms],
            out_specs=row_block(BAND),
            scratch_shapes=[pltpu.VMEM((2, BS, FRAME * BS), jnp.float32)],
            compiler_params=params(20),
            cost_estimate=cost(10**7, 10**7),
            name=name,
        )(core, *terms)

    early = summed(early_kernel, "early", own, m0, m4, far)
    return summed(total_kernel, "total", early, m1, m3)


def solution(mesh):
    in_specs = (P("dom", None, None), P("dom", None, None), P("dom", None), P("dom", None))
    out_specs = P("dom", None, None)
    return jax.shard_map(body, mesh=mesh, in_specs=in_specs, out_specs=out_specs, check_vma=False)
```

```python
import functools

import jax
import jax.numpy as jnp
from jax import lax
from jax.experimental import pallas as pl
from jax.experimental.pallas import tpu as pltpu
from jax.sharding import PartitionSpec as P

BS = 64
KA = 7
KP = 27
AGG = 8
H = 15
NC = 3
NB = 24
WIN = 31
WSLOT = 33
BAND = 63

QUAD = 4
LANES = QUAD * BS
EXT = NB + 2 * AGG
COLS = NC + 2 * H + 2
WCOLS = 40
WINDOW = 38
TILES = 10
GROUPS = 5
K = NB * BS
AW = AGG * BS
FRAME = 76
NT = (((1,), (1,)), ((), ()))
ROWS = NC * GROUPS
FIRST = 2 * NC
REST = ROWS - FIRST
ORDER = (0, 4, 1, 3, 2)


def eye(n):
    rows = lax.broadcasted_iota(jnp.int32, (n, n), 0)
    lanes = lax.broadcasted_iota(jnp.int32, (n, n), 1)
    return jnp.where(rows == lanes, 1.0, 0.0).astype(jnp.bfloat16)


def low_half():
    return lax.broadcasted_iota(jnp.int32, (BS, 2 * BS), 1) < BS


def transpose_quad(block, turned, width):
    for start in range(0, width, LANES):
        size = min(LANES, width - start)
        part = lax.dot_general(
            eye(size), block[:, start : start + size], NT, preferred_element_type=jnp.float32
        )
        turned[start // BS : (start + size) // BS] = part.astype(jnp.bfloat16).reshape(
            size // BS, BS, LANES
        )


def spread_quad(turned, index, first, store, count, unroll):
    half = low_half()

    def place(slot, carry):
        for pair in range(2):
            lanes = slice(pair * 2 * BS, (pair + 1) * 2 * BS)
            left = turned[index[first + 2 * pair, slot], :, lanes]
            right = turned[index[first + 2 * pair + 1, slot], :, lanes]
            store(slot, pair, jnp.where(half, left, right))
        return carry

    lax.fori_loop(0, count, place, 0, unroll=unroll)


def fast_kernel(
    core,
    inv_own,
    inv_fast,
    inv_a,
    p_own,
    p_fast,
    a_own,
    send_low,
    send_high,
    send_rest,
    far,
    fast_first,
    fast_rest,
    slow_first,
    slow_rest,
    other_first,
    other_rest,
    wt,
    rest,
    at_halo,
    p_buf,
    ext,
    at,
    turned_p,
    turned_a,
    lhs,
    send_buf,
    far_buf,
    fast_buf,
    slow_buf,
    other_buf,
    wt_buf,
    rest_buf,
    in_sems,
    out_sems,
):
    s = core[0]
    own_quads = NB // QUAD
    halo_quads = AGG // QUAD

    def load(quad):
        if quad < own_quads:
            source = p_own.at[quad * QUAD : (quad + 1) * QUAD]
        else:
            source = p_fast.at[(quad - own_quads) * QUAD : (quad - own_quads + 1) * QUAD]
        target = p_buf.at[quad * QUAD : (quad + 1) * QUAD]
        return pltpu.make_async_copy(source, target, in_sems.at[quad])

    for quad in range(own_quads + halo_quads):
        load(quad).start()

    turned_p[KP] = jnp.zeros((BS, LANES), jnp.bfloat16)
    turned_a[KA] = jnp.zeros((BS, LANES), jnp.bfloat16)

    @pl.loop(0, own_quads)
    def _(quad):
        block = a_own[pl.ds(quad * QUAD, QUAD)].reshape(LANES, KA * BS)
        transpose_quad(block, turned_a, KA * BS)
        agg = quad // halo_quads

        def store(slot, pair, value):
            lane = pl.multiple_of((quad % halo_quads) * LANES + pair * 2 * BS, 2 * BS)
            at[agg, slot, :, pl.ds(lane, 2 * BS)] = value

        spread_quad(turned_a, inv_a, quad * QUAD, store, 3 * AGG, 8)

    slow_agg = 2 * s
    halo_copy = pltpu.make_async_copy(at.at[slow_agg, pl.ds(16 * s, AGG)], at_halo, out_sems.at[0])
    halo_copy.start()

    def band_quad(source_row, index, index_row, first_lane):
        block = p_buf[pl.ds(source_row, QUAD)].reshape(LANES, KP * BS)
        transpose_quad(block, turned_p, KP * BS)

        def store(slot, pair, value):
            lane = pl.multiple_of(first_lane + pair * 2 * BS, 2 * BS)
            ext[slot, :, pl.ds(lane, 2 * BS)] = value

        spread_quad(turned_p, index, index_row, store, COLS, 7)

    for quad in range(own_quads + halo_quads):
        load(quad).wait()

    @pl.loop(0, own_quads)
    def _(quad):
        band_quad(quad * QUAD, inv_own, quad * QUAD, AW + quad * LANES)

    @pl.loop(0, halo_quads)
    def _(quad):
        first_lane = (AW + K) * (1 - s) + quad * LANES
        band_quad((own_quads + quad) * QUAD, inv_fast, quad * QUAD, first_lane)

    fast_lanes = pl.ds(pl.multiple_of(AW + (1 - s) * AW, AW), 2 * AW)
    slow_lanes = pl.ds(pl.multiple_of(AW + 2 * s * AW, AW), AW)
    for place, i in enumerate(ORDER):
        for j in range(NC):
            row = NC * place + j
            mine, other = 6 * i + 3 + j + 1, 6 * i + 6 * (1 - s) + j + 1
            fast_buf[row] = ext[mine, :, fast_lanes]
            slow_buf[row if place < 2 else row + NC] = ext[mine, :, slow_lanes]
            other_buf[row] = ext[other, :, slow_lanes]
            lhs[row] = ext[other, :, fast_lanes]
    for j in range(NC):
        lhs[ROWS + j] = ext[30 * s + j + 1, :, fast_lanes]
        slow_buf[FIRST + j] = ext[30 * s + j + 1, :, slow_lanes]
    copies = [halo_copy]

    def write(source, target):
        copy = pltpu.make_async_copy(source, target, out_sems.at[len(copies)])
        copy.start()
        copies.append(copy)

    write(other_buf.at[:FIRST], other_first)
    write(other_buf.at[FIRST:], other_rest)
    write(fast_buf.at[:FIRST], fast_first)
    write(fast_buf.at[FIRST:], fast_rest)
    write(slow_buf.at[: FIRST + NC], slow_first)
    write(slow_buf.at[FIRST + NC :], slow_rest)

    wt_buf[0:7] = jnp.zeros((7, BS, 2 * AW), jnp.bfloat16)
    wt_buf[33:] = jnp.zeros((WCOLS - 33, BS, 2 * AW), jnp.bfloat16)
    chunk = WSLOT // 3

    @pl.loop(0, 2)
    def _(place):
        agg = place + 1 - s
        lane = pl.multiple_of(agg * AW, AW)
        target = pl.multiple_of(place * AW, AW)

        @pl.loop(0, 3)
        def _(part):
            first = agg + part * chunk
            left = ext[pl.ds(first, chunk), :, pl.ds(lane, 3 * AW)].reshape(chunk * BS, 3 * AW)
            value = jnp.dot(
                left, at[agg].reshape(3 * AW, AW), preferred_element_type=jnp.float32
            )
            wt_buf[pl.ds(3 * s + first, chunk), :, pl.ds(target, AW)] = value.astype(
                jnp.bfloat16
            ).reshape(chunk, BS, AW)

    write(wt_buf, wt)

    @pl.loop(0, 3)
    def _(part):
        lane = pl.multiple_of(AW + s * AW, AW)
        left = ext[pl.ds(slow_agg + part * chunk, chunk), :, pl.ds(lane, 2 * AW)]
        right = at[slow_agg, pl.ds(AGG - AGG * s, 2 * AGG)].reshape(2 * AW, AW)
        value = jnp.dot(
            left.reshape(chunk * BS, 2 * AW), right, preferred_element_type=jnp.float32
        )
        rest_buf[pl.ds(part * chunk, chunk)] = value.reshape(chunk, BS, AW)

    write(rest_buf, rest)

    def emit(tile, width):
        right = wt_buf[pl.ds(QUAD * tile, width // BS)].reshape(width, 2 * AW)
        left = lhs[...].reshape((ROWS + NC) * BS, 2 * AW)
        value = lax.dot_general(left, right, NT, preferred_element_type=jnp.float32)
        value = value.astype(jnp.bfloat16).reshape(ROWS + NC, BS, width)
        lanes = pl.ds(pl.multiple_of(tile * LANES, LANES), width)
        send_buf[:, :, lanes] = value[:ROWS]
        far_buf[:, :, lanes] = value[ROWS:]

    each_tile(emit)
    write(send_buf.at[:NC], send_low)
    write(send_buf.at[NC:FIRST], send_high)
    write(send_buf.at[FIRST:], send_rest)
    write(far_buf, far)
    for copy in copies:
        copy.wait()


def each_tile(step):
    @pl.loop(0, TILES - 1)
    def _(tile):
        step(tile, LANES)

    step(TILES - 1, LANES // 2)


def tile_dot(rows, cols, tile, width):
    left = rows[...].reshape(rows.shape[0] * BS, rows.shape[2])
    right = cols[pl.ds(QUAD * tile, width // BS)].reshape(width, cols.shape[2])
    value = lax.dot_general(left, right, NT, preferred_element_type=jnp.float32)
    return value.reshape(rows.shape[0], BS, width)


def tile_lanes(tile, width):
    return pl.ds(pl.multiple_of(tile * LANES, LANES), width)


def mine_kernel(fast, slow, wt_fast, wt_slow, low, high, far_fast, out, far):
    def step(tile, width):
        lanes = tile_lanes(tile, width)
        inner = tile_dot(fast, wt_fast, tile, width)
        outer = tile_dot(slow, wt_slow, tile, width)
        near = inner + outer[:FIRST]
        out[:NC, :, lanes] = near[:NC] + low[:, :, lanes].astype(jnp.float32)
        out[NC:, :, lanes] = near[NC:] + high[:, :, lanes].astype(jnp.float32)
        tail = outer[FIRST:] + far_fast[:, :, lanes].astype(jnp.float32)
        far[:, :, lanes] = tail.astype(jnp.bfloat16)

    each_tile(step)


def slow_kernel(core, inv_slow, p_slow, at_halo, rest, wt, turned_p, ext):
    s = core[0]
    turned_p[KP] = jnp.zeros((BS, LANES), jnp.bfloat16)

    @pl.loop(0, AGG // QUAD)
    def _(quad):
        block = p_slow[pl.ds(quad * QUAD, QUAD)].reshape(LANES, KP * BS)
        transpose_quad(block, turned_p, KP * BS)

        def store(slot, pair, value):
            lane = pl.multiple_of(quad * LANES + pair * 2 * BS, 2 * BS)
            ext[slot, :, pl.ds(lane, 2 * BS)] = value

        spread_quad(turned_p, inv_slow, quad * QUAD, store, WSLOT, 11)

    wt[0:5] = jnp.zeros((5, BS, AW), jnp.bfloat16)
    wt[WSLOT:] = jnp.zeros((WCOLS - WSLOT, BS, AW), jnp.bfloat16)
    chunk = WSLOT // 3

    @pl.loop(0, 3)
    def _(part):
        rows = pl.ds(part * chunk, chunk)
        value = jnp.dot(
            ext[rows].reshape(chunk * BS, AW),
            at_halo[...].reshape(AW, AW),
            preferred_element_type=jnp.float32,
        )
        value = value.reshape(chunk, BS, AW) + rest[rows]
        wt[pl.ds(5 * s + part * chunk, chunk)] = value.astype(jnp.bfloat16)


def join_first_kernel(other, wt_other, mine, m0, m4):
    def step(tile, width):
        lanes = tile_lanes(tile, width)
        value = tile_dot(other, wt_other, tile, width) + mine[:, :, lanes]
        m0[:, :, lanes] = value[:NC].astype(jnp.bfloat16)
        m4[:, :, lanes] = value[NC:].astype(jnp.bfloat16)

    each_tile(step)


def join_rest_kernel(fast, slow, other, wt_fast, wt_slow, wt_other, arrived, m1, m3, own):
    def step(tile, width):
        lanes = tile_lanes(tile, width)
        value = tile_dot(fast, wt_fast, tile, width) + tile_dot(slow, wt_slow, tile, width)
        value = value + tile_dot(other, wt_other, tile, width)
        value = value + arrived[:, :, lanes].astype(jnp.float32)
        m1[:, :, lanes] = value[:NC].astype(jnp.bfloat16)
        m3[:, :, lanes] = value[NC : 2 * NC].astype(jnp.bfloat16)
        own[:, :, lanes] = value[2 * NC :]

    each_tile(step)


def frame_add(frame, message, start):
    odd = start & 1
    lane = pl.multiple_of((start - odd + 6) * BS, 2 * BS)
    frame[odd, :, pl.ds(lane, WINDOW * BS)] += message[0].astype(jnp.float32)


def frame_sum(frame):
    first, last = 6 * BS, (6 + BAND) * BS
    return frame[0, :, first:last] + frame[1, :, first - BS : last - BS]


def early_kernel(core, own, m0, m4, far, out, frame):
    s = core[0]
    j = pl.program_id(0)
    frame[...] = jnp.zeros_like(frame)
    top = 27 - 3 * s - j
    frame_add(frame, m0, top)
    frame_add(frame, own, top - 12)
    frame_add(frame, m4, top - 24)
    frame_add(frame, far, jnp.where(s == 1, 30 - j, -3 - j))
    out[0] = frame_sum(frame)


def total_kernel(core, early, m1, m3, out, frame):
    s = core[0]
    j = pl.program_id(0)
    frame[...] = jnp.zeros_like(frame)
    top = 27 - 3 * s - j
    frame_add(frame, m1, top - 6)
    frame_add(frame, m3, top - 18)
    out[0] = early[0] + frame_sum(frame)


def pick_kernel(core, source, out, sems, *, outer):
    s = core[0]
    first = (NB - AGG) * (s if outer else 1 - s)
    step = AGG // 4
    copies = [
        pltpu.make_async_copy(
            source.at[pl.ds(first + k * step, step)],
            out.at[k * step : (k + 1) * step],
            sems.at[k],
        )
        for k in range(4)
    ]
    for copy in copies:
        copy.start()
    for copy in copies:
        copy.wait()


def permuted(block, pairs):
    return lax.ppermute(block, "dom", pairs)


def inverse_index(offset, slots, empty):
    order = jnp.arange(offset.shape[1], dtype=jnp.int32)[None, :, None]
    hit = offset[:, :, None] == jnp.arange(slots, dtype=jnp.int32)[None, None, :]
    return empty + jnp.sum(jnp.where(hit, order - empty, 0), axis=1)


def body(a_blocks, p_blocks, cols_a, cols_p):
    devices = lax.axis_size("dom")
    device = lax.axis_index("dom")
    count_agg = NC * devices
    count_rows = NB * devices
    first_agg = device * NC
    first_row = device * NB
    core = (device % 2).astype(jnp.int32).reshape(1)

    def shifted(distance):
        return [(i, (i + distance) % devices) for i in range(devices)]

    parity = device % 2
    smem = pl.BlockSpec(memory_space=pltpu.SMEM)
    vmem = pl.BlockSpec(memory_space=pltpu.VMEM)
    hbm = pl.BlockSpec(memory_space=pltpu.HBM)
    bf16 = jnp.bfloat16

    def params(mebibytes):
        return pltpu.CompilerParams(vmem_limit_bytes=mebibytes * 1024 * 1024)

    def cost(flops, size):
        return pl.CostEstimate(flops=flops, bytes_accessed=size, transcendentals=0)

    def picked(outer):
        return pl.pallas_call(
            functools.partial(pick_kernel, outer=outer),
            out_shape=jax.ShapeDtypeStruct((AGG,) + p_blocks.shape[1:], bf16),
            in_specs=[smem, hbm],
            out_specs=vmem,
            scratch_shapes=[pltpu.SemaphoreType.DMA((4,))],
            compiler_params=params(60),
            name="pick_outer" if outer else "pick_inner",
        )(core, p_blocks)

    outward = [(i, (i + (1 if i % 2 else -1)) % devices) for i in range(devices)]
    inward = [(i, i ^ 1) for i in range(devices)]
    p_slow = permuted(picked(True), outward)
    p_fast = permuted(picked(False), inward)
    edge_cols = jnp.stack([cols_p[:AGG], cols_p[NB - AGG :]])
    cols_slow = permuted(edge_cols[parity], outward)
    cols_fast = permuted(edge_cols[1 - parity], inward)

    def slots(cols, agg):
        return (cols - agg + H) % count_agg

    own_agg = jnp.arange(NB, dtype=jnp.int32)[:, None] // AGG
    inv_own = inverse_index(slots(cols_p, first_agg + own_agg) + own_agg + 1, COLS, KP)
    fast_place = NC * (1 - parity) - parity
    inv_fast = inverse_index(slots(cols_fast, first_agg + fast_place) + fast_place + 1, COLS, KP)
    slow_place = NC * parity - (1 - parity)
    inv_slow = inverse_index(slots(cols_slow, first_agg + slow_place) + 2 * parity, WSLOT, KP)
    inv_a = inverse_index((cols_a - first_row - (own_agg - 1) * AGG) % count_rows, 3 * AGG, KA)

    def block(rows, width, kind=bf16):
        return jax.ShapeDtypeStruct((rows, BS, width), kind)

    span = WINDOW * BS
    outs = [
        block(NC, span),
        block(NC, span),
        block(REST, span),
        block(NC, span),
        block(FIRST, 2 * AW),
        block(REST, 2 * AW),
        block(FIRST + NC, AW),
        block(REST, AW),
        block(FIRST, AW),
        block(REST, AW),
        block(WCOLS, 2 * AW),
        block(WSLOT, AW, jnp.float32),
        block(AGG, AW),
    ]
    (
        send_low,
        send_high,
        send_rest,
        far,
        fast_first,
        fast_rest,
        slow_first,
        slow_rest,
        other_first,
        other_rest,
        wt_fast,
        rest,
        at_halo,
    ) = pl.pallas_call(
        fast_kernel,
        out_shape=outs,
        in_specs=[smem] * 4 + [hbm, hbm, vmem],
        out_specs=[hbm] * len(outs),
        scratch_shapes=[
            pltpu.VMEM((NB + AGG, BS, KP * BS), bf16),
            pltpu.VMEM((COLS, BS, EXT * BS), bf16),
            pltpu.VMEM((NC, 3 * AGG, BS, AW), bf16),
            pltpu.VMEM((KP + 1, BS, LANES), bf16),
            pltpu.VMEM((KA + 1, BS, LANES), bf16),
            pltpu.VMEM((ROWS + NC, BS, 2 * AW), bf16),
            pltpu.VMEM((ROWS, BS, span), bf16),
            pltpu.VMEM((NC, BS, span), bf16),
            pltpu.VMEM((ROWS, BS, 2 * AW), bf16),
            pltpu.VMEM((ROWS + NC, BS, AW), bf16),
            pltpu.VMEM((ROWS, BS, AW), bf16),
            pltpu.VMEM((WCOLS, BS, 2 * AW), bf16),
            pltpu.VMEM((WSLOT, BS, AW), jnp.float32),
            pltpu.SemaphoreType.DMA(((NB + AGG) // QUAD,)),
            pltpu.SemaphoreType.DMA((len(outs),)),
        ],
        compiler_params=params(56),
        cost_estimate=cost(20 * 10**9, 30 * 10**6),
        name="fast",
    )(core, inv_own, inv_fast, inv_a, p_blocks, p_fast, a_blocks)

    low = permuted(send_low, inward)
    high = permuted(send_high, inward)
    other_first = permuted(other_first, inward)
    p_slow, low, high, other_first = lax.optimization_barrier((p_slow, low, high, other_first))

    wt_slow = pl.pallas_call(
        slow_kernel,
        out_shape=block(WCOLS, AW),
        in_specs=[smem] * 2 + [vmem] * 3,
        out_specs=vmem,
        scratch_shapes=[
            pltpu.VMEM((KP + 1, BS, LANES), bf16),
            pltpu.VMEM((WSLOT, BS, AW), bf16),
        ],
        compiler_params=params(24),
        cost_estimate=cost(20 * 10**9, 200 * 10**6),
        name="slow",
    )(core, inv_slow, p_slow, at_halo, rest)
    wt_other = permuted(wt_slow, inward)

    wt_slow, low, high = lax.optimization_barrier((wt_slow, low, high))
    mine, far = pl.pallas_call(
        mine_kernel,
        out_shape=[block(FIRST, span, jnp.float32), block(NC, span)],
        in_specs=[vmem] * 7,
        out_specs=[vmem] * 2,
        compiler_params=params(24),
        cost_estimate=cost(10**10, 100 * 10**6),
        name="mine",
    )(fast_first, slow_first, wt_fast, wt_slow, low, high, far)
    far = permuted(far, [(i, (i + (5 if i % 2 else -5)) % devices) for i in range(devices)])
    mine, wt_other, send_rest, other_rest = lax.optimization_barrier(
        (mine, wt_other, send_rest, other_rest)
    )
    arrived_rest = permuted(send_rest, inward)
    other_rest = permuted(other_rest, inward)
    m0, m4 = pl.pallas_call(
        join_first_kernel,
        out_shape=[block(NC, span)] * 2,
        in_specs=[vmem] * 3,
        out_specs=[vmem] * 2,
        compiler_params=params(16),
        cost_estimate=cost(3 * 10**9, 10**7),
        name="join_first",
    )(other_first, wt_other, mine)
    m0 = permuted(m0, shifted(-4))
    m4 = permuted(m4, shifted(4))
    m1, m3, own = pl.pallas_call(
        join_rest_kernel,
        out_shape=[block(NC, span)] * 2 + [block(NC, span, jnp.float32)],
        in_specs=[vmem] * 7,
        out_specs=[vmem] * 3,
        compiler_params=params(30),
        cost_estimate=cost(40 * 10**9, 200 * 10**6),
        name="join_rest",
    )(fast_rest, slow_rest, other_rest, wt_fast, wt_slow, wt_other, arrived_rest)
    m1 = permuted(m1, shifted(-2))
    m3 = permuted(m3, shifted(2))

    def row_block(blocks):
        return pl.BlockSpec((1, BS, blocks * BS), lambda j: (j, 0, 0))

    def summed(kernel, name, *terms):
        return pl.pallas_call(
            kernel,
            grid=(NC,),
            out_shape=block(NC, BAND * BS, jnp.float32),
            in_specs=[smem] + [row_block(term.shape[2] // BS) for term in terms],
            out_specs=row_block(BAND),
            scratch_shapes=[pltpu.VMEM((2, BS, FRAME * BS), jnp.float32)],
            compiler_params=params(20),
            cost_estimate=cost(10**7, 10**7),
            name=name,
        )(core, *terms)

    early = summed(early_kernel, "early", own, m0, m4, far)
    return summed(total_kernel, "total", early, m1, m3)


def solution(mesh):
    in_specs = (P("dom", None, None), P("dom", None, None), P("dom", None), P("dom", None))
    out_specs = P("dom", None, None)
    return jax.shard_map(body, mesh=mesh, in_specs=in_specs, out_specs=out_specs, check_vma=False)
```

```python
import functools

import jax
import jax.numpy as jnp
from jax import lax
from jax.experimental import pallas as pl
from jax.experimental.pallas import tpu as pltpu
from jax.sharding import PartitionSpec as P

BS = 64
KA = 7
KP = 27
AGG = 8
H = 15
NC = 3
NB = 24
WIN = 31
WSLOT = 33
BAND = 63

QUAD = 4
LANES = QUAD * BS
EXT = NB + 2 * AGG
COLS = NC + 2 * H + 2
WCOLS = 40
WINDOW = 38
TILES = 10
GROUPS = 5
K = NB * BS
AW = AGG * BS
FRAME = 76
NT = (((1,), (1,)), ((), ()))
ROWS = NC * GROUPS
FIRST = 2 * NC
REST = ROWS - FIRST
MERGED = WINDOW + 6


def eye(n):
    rows = lax.broadcasted_iota(jnp.int32, (n, n), 0)
    lanes = lax.broadcasted_iota(jnp.int32, (n, n), 1)
    return jnp.where(rows == lanes, 1.0, 0.0).astype(jnp.bfloat16)


def low_half():
    return lax.broadcasted_iota(jnp.int32, (BS, 2 * BS), 1) < BS


def transpose_quad(block, turned, width):
    for start in range(0, width, LANES):
        size = min(LANES, width - start)
        part = lax.dot_general(
            eye(size), block[:, start : start + size], NT, preferred_element_type=jnp.float32
        )
        turned[start // BS : (start + size) // BS] = part.astype(jnp.bfloat16).reshape(
            size // BS, BS, LANES
        )


def spread_quad(turned, index, first, store, count, unroll):
    half = low_half()

    def place(slot, carry):
        for pair in range(2):
            lanes = slice(pair * 2 * BS, (pair + 1) * 2 * BS)
            left = turned[index[first + 2 * pair, slot], :, lanes]
            right = turned[index[first + 2 * pair + 1, slot], :, lanes]
            store(slot, pair, jnp.where(half, left, right))
        return carry

    lax.fori_loop(0, count, place, 0, unroll=unroll)


def fast_kernel(
    core,
    inv_own,
    inv_fast,
    inv_a,
    p_own,
    p_fast,
    a_own,
    send_low,
    send_high,
    send_rest,
    far,
    inner,
    fast_rest,
    slow_first,
    slow_rest,
    other_first,
    other_rest,
    wt,
    rest,
    at_halo,
    p_buf,
    ext,
    at,
    turned_p,
    turned_a,
    lhs,
    send_buf,
    far_buf,
    inner_buf,
    fast_buf,
    slow_buf,
    other_buf,
    wt_buf,
    rest_buf,
    in_sems,
    out_sems,
):
    s = core[0]
    own_quads = NB // QUAD
    halo_quads = AGG // QUAD

    def load(quad):
        if quad < own_quads:
            source = p_own.at[quad * QUAD : (quad + 1) * QUAD]
        else:
            source = p_fast.at[(quad - own_quads) * QUAD : (quad - own_quads + 1) * QUAD]
        target = p_buf.at[quad * QUAD : (quad + 1) * QUAD]
        return pltpu.make_async_copy(source, target, in_sems.at[quad])

    for quad in range(own_quads + halo_quads):
        load(quad).start()

    turned_p[KP] = jnp.zeros((BS, LANES), jnp.bfloat16)
    turned_a[KA] = jnp.zeros((BS, LANES), jnp.bfloat16)

    @pl.loop(0, own_quads)
    def _(quad):
        block = a_own[pl.ds(quad * QUAD, QUAD)].reshape(LANES, KA * BS)
        transpose_quad(block, turned_a, KA * BS)
        agg = quad // halo_quads

        def store(slot, pair, value):
            lane = pl.multiple_of((quad % halo_quads) * LANES + pair * 2 * BS, 2 * BS)
            at[agg, slot, :, pl.ds(lane, 2 * BS)] = value

        spread_quad(turned_a, inv_a, quad * QUAD, store, 3 * AGG, 8)

    slow_agg = 2 * s
    halo_copy = pltpu.make_async_copy(at.at[slow_agg, pl.ds(16 * s, AGG)], at_halo, out_sems.at[0])
    halo_copy.start()

    def band_quad(source_row, index, index_row, first_lane):
        block = p_buf[pl.ds(source_row, QUAD)].reshape(LANES, KP * BS)
        transpose_quad(block, turned_p, KP * BS)

        def store(slot, pair, value):
            lane = pl.multiple_of(first_lane + pair * 2 * BS, 2 * BS)
            ext[slot, :, pl.ds(lane, 2 * BS)] = value

        spread_quad(turned_p, index, index_row, store, COLS, 7)

    for quad in range(own_quads + halo_quads):
        load(quad).wait()

    @pl.loop(0, own_quads)
    def _(quad):
        band_quad(quad * QUAD, inv_own, quad * QUAD, AW + quad * LANES)

    @pl.loop(0, halo_quads)
    def _(quad):
        first_lane = (AW + K) * (1 - s) + quad * LANES
        band_quad((own_quads + quad) * QUAD, inv_fast, quad * QUAD, first_lane)

    fast_lanes = pl.ds(pl.multiple_of(AW + (1 - s) * AW, AW), 2 * AW)
    slow_lanes = pl.ds(pl.multiple_of(AW + 2 * s * AW, AW), AW)
    x = core[1]
    for place, i in enumerate((1 + 2 * x, 4 * x, 4 - 4 * x, 3 - 2 * x, 2)):
        for j in range(NC):
            row = NC * place + j
            mine, other = 6 * i + 3 + j + 1, 6 * i + 6 * (1 - s) + j + 1
            if place < 2:
                lhs[ROWS + NC + row] = ext[mine, :, fast_lanes]
            else:
                fast_buf[row - FIRST] = ext[mine, :, fast_lanes]
            slow_buf[row if place < 2 else row + NC] = ext[mine, :, slow_lanes]
            other_buf[row] = ext[other, :, slow_lanes]
            lhs[row] = ext[other, :, fast_lanes]
    for j in range(NC):
        lhs[ROWS + j] = ext[30 * s + j + 1, :, fast_lanes]
        slow_buf[FIRST + j] = ext[30 * s + j + 1, :, slow_lanes]
    copies = [halo_copy]

    def write(source, target):
        copy = pltpu.make_async_copy(source, target, out_sems.at[len(copies)])
        copy.start()
        copies.append(copy)

    write(other_buf.at[:FIRST], other_first)
    write(other_buf.at[FIRST:], other_rest)
    write(fast_buf, fast_rest)
    write(slow_buf.at[: FIRST + NC], slow_first)
    write(slow_buf.at[FIRST + NC :], slow_rest)

    wt_buf[0:7] = jnp.zeros((7, BS, 2 * AW), jnp.bfloat16)
    wt_buf[33:] = jnp.zeros((WCOLS - 33, BS, 2 * AW), jnp.bfloat16)
    chunk = WSLOT // 3

    @pl.loop(0, 2)
    def _(place):
        agg = place + 1 - s
        lane = pl.multiple_of(agg * AW, AW)
        target = pl.multiple_of(place * AW, AW)

        @pl.loop(0, 3)
        def _(part):
            first = agg + part * chunk
            left = ext[pl.ds(first, chunk), :, pl.ds(lane, 3 * AW)].reshape(chunk * BS, 3 * AW)
            value = jnp.dot(
                left, at[agg].reshape(3 * AW, AW), preferred_element_type=jnp.float32
            )
            wt_buf[pl.ds(3 * s + first, chunk), :, pl.ds(target, AW)] = value.astype(
                jnp.bfloat16
            ).reshape(chunk, BS, AW)

    write(wt_buf, wt)

    @pl.loop(0, 3)
    def _(part):
        lane = pl.multiple_of(AW + s * AW, AW)
        left = ext[pl.ds(slow_agg + part * chunk, chunk), :, pl.ds(lane, 2 * AW)]
        right = at[slow_agg, pl.ds(AGG - AGG * s, 2 * AGG)].reshape(2 * AW, AW)
        value = jnp.dot(
            left.reshape(chunk * BS, 2 * AW), right, preferred_element_type=jnp.float32
        )
        rest_buf[pl.ds(part * chunk, chunk)] = value.reshape(chunk, BS, AW)

    write(rest_buf, rest)

    def emit(tile, width):
        right = wt_buf[pl.ds(QUAD * tile, width // BS)].reshape(width, 2 * AW)
        left = lhs[...].reshape((ROWS + NC + FIRST) * BS, 2 * AW)
        value = lax.dot_general(left, right, NT, preferred_element_type=jnp.float32)
        value = value.astype(jnp.bfloat16).reshape(ROWS + NC + FIRST, BS, width)
        lanes = pl.ds(pl.multiple_of(tile * LANES, LANES), width)
        send_buf[:, :, lanes] = value[:ROWS]
        far_buf[:, :, lanes] = value[ROWS : ROWS + NC]
        inner_buf[:, :, lanes] = value[ROWS + NC :]

    each_tile(emit)
    write(send_buf.at[:NC], send_low)
    write(send_buf.at[NC:FIRST], send_high)
    write(send_buf.at[FIRST:], send_rest)
    write(far_buf, far)
    write(inner_buf, inner)
    for copy in copies:
        copy.wait()


def each_tile(step):
    @pl.loop(0, TILES - 1)
    def _(tile):
        step(tile, LANES)

    step(TILES - 1, LANES // 2)


def tile_dot(rows, cols, tile, width):
    left = rows[...].reshape(rows.shape[0] * BS, rows.shape[2])
    right = cols[pl.ds(QUAD * tile, width // BS)].reshape(width, cols.shape[2])
    value = lax.dot_general(left, right, NT, preferred_element_type=jnp.float32)
    return value.reshape(rows.shape[0], BS, width)


def tile_lanes(tile, width):
    return pl.ds(pl.multiple_of(tile * LANES, LANES), width)


def mine_kernel(slow, wt_slow, inner, low, high, far_fast, out, far):
    def step(tile, width):
        lanes = tile_lanes(tile, width)
        outer = tile_dot(slow, wt_slow, tile, width)
        near = outer[:FIRST] + inner[:, :, lanes].astype(jnp.float32)
        out[:NC, :, lanes] = near[:NC] + low[:, :, lanes].astype(jnp.float32)
        out[NC:, :, lanes] = near[NC:] + high[:, :, lanes].astype(jnp.float32)
        tail = outer[FIRST:] + far_fast[:, :, lanes].astype(jnp.float32)
        far[:, :, lanes] = tail.astype(jnp.bfloat16)

    each_tile(step)


def slow_kernel(core, inv_slow, p_slow, at_halo, rest, wt, turned_p, ext):
    s = core[0]
    turned_p[KP] = jnp.zeros((BS, LANES), jnp.bfloat16)

    @pl.loop(0, AGG // QUAD)
    def _(quad):
        block = p_slow[pl.ds(quad * QUAD, QUAD)].reshape(LANES, KP * BS)
        transpose_quad(block, turned_p, KP * BS)

        def store(slot, pair, value):
            lane = pl.multiple_of(quad * LANES + pair * 2 * BS, 2 * BS)
            ext[slot, :, pl.ds(lane, 2 * BS)] = value

        spread_quad(turned_p, inv_slow, quad * QUAD, store, WSLOT, 11)

    wt[0:5] = jnp.zeros((5, BS, AW), jnp.bfloat16)
    wt[WSLOT:] = jnp.zeros((WCOLS - WSLOT, BS, AW), jnp.bfloat16)
    chunk = WSLOT // 3

    @pl.loop(0, 3)
    def _(part):
        rows = pl.ds(part * chunk, chunk)
        value = jnp.dot(
            ext[rows].reshape(chunk * BS, AW),
            at_halo[...].reshape(AW, AW),
            preferred_element_type=jnp.float32,
        )
        value = value.reshape(chunk, BS, AW) + rest[rows]
        wt[pl.ds(5 * s + part * chunk, chunk)] = value.astype(jnp.bfloat16)


def join_first_kernel(other, wt_other, mine, relay, direct):
    def step(tile, width):
        lanes = tile_lanes(tile, width)
        value = tile_dot(other, wt_other, tile, width) + mine[:, :, lanes]
        relay[:, :, lanes] = value[:NC].astype(jnp.bfloat16)
        direct[:, :, lanes] = value[NC:].astype(jnp.bfloat16)

    each_tile(step)


def join_rest_kernel(fast, slow, other, wt_fast, wt_slow, wt_other, arrived, merge, pair, own):
    def step(tile, width):
        lanes = tile_lanes(tile, width)
        value = tile_dot(fast, wt_fast, tile, width) + tile_dot(slow, wt_slow, tile, width)
        value = value + tile_dot(other, wt_other, tile, width)
        value = value + arrived[:, :, lanes].astype(jnp.float32)
        merge[:, :, lanes] = value[:NC]
        pair[:, :, lanes] = value[NC : 2 * NC].astype(jnp.bfloat16)
        own[:, :, lanes] = value[2 * NC :]

    each_tile(step)


def merge_kernel(core, rows, relay, out, frame):
    x = core[1]
    step = 6 * BS
    for j in range(NC):
        frame[...] = jnp.zeros_like(frame)
        frame[:, pl.ds(pl.multiple_of(step * x, step), WINDOW * BS)] = rows[j]
        lanes = pl.ds(pl.multiple_of(step * (1 - x), step), WINDOW * BS)
        frame[:, lanes] += relay[j].astype(jnp.float32)
        out[j] = frame[...].astype(jnp.bfloat16)


def in_frame(s, j, frame, messages, store):
    odd = (j + 1 - s) % 2
    frame[...] = jnp.zeros_like(frame)
    for message, start in messages:
        lane = pl.multiple_of((start - odd + 6) * BS, 2 * BS)
        frame[:, pl.ds(lane, message.shape[2])] += message[j].astype(jnp.float32)
    first, last = 6 * BS, (6 + BAND) * BS

    @pl.when(odd == 0)
    def _():
        store(frame[:, first:last])

    @pl.when(odd == 1)
    def _():
        store(frame[:, first - BS : last - BS])


def early_kernel(core, own, direct, out, frame):
    s, x = core[0], core[1]
    for j in range(NC):
        top = 27 - 3 * s - j

        def store(value, j=j):
            out[j] = value

        in_frame(s, j, frame, [(own, top - 12), (direct, top - 24 * x)], store)


def total_kernel(core, early, pair, merged, far, out, frame, buf, sems):
    s, x = core[0], core[1]
    copies = []
    for j in range(NC):
        top = 27 - 3 * s - j
        far_start = jnp.where(s == 1, 30 - j, -3 - j)

        def store(value, j=j):
            buf[j] = value + early[j]

        messages = [(pair, top - 6 - 12 * x), (merged, top - 24 + 18 * x), (far, far_start)]
        in_frame(s, j, frame, messages, store)
        copy = pltpu.make_async_copy(buf.at[j], out.at[j], sems.at[j])
        copy.start()
        copies.append(copy)
    for copy in copies:
        copy.wait()


def pick_kernel(core, source, out, sems, *, outer):
    s = core[0]
    first = (NB - AGG) * (s if outer else 1 - s)
    step = AGG // 4
    copies = [
        pltpu.make_async_copy(
            source.at[pl.ds(first + k * step, step)],
            out.at[k * step : (k + 1) * step],
            sems.at[k],
        )
        for k in range(4)
    ]
    for copy in copies:
        copy.start()
    for copy in copies:
        copy.wait()


def permuted(block, pairs):
    return lax.ppermute(block, "dom", pairs)


def inverse_index(offset, slots, empty):
    order = jnp.arange(offset.shape[1], dtype=jnp.int32)[None, :, None]
    hit = offset[:, :, None] == jnp.arange(slots, dtype=jnp.int32)[None, None, :]
    return empty + jnp.sum(jnp.where(hit, order - empty, 0), axis=1)


def body(a_blocks, p_blocks, cols_a, cols_p):
    devices = lax.axis_size("dom")
    device = lax.axis_index("dom")
    count_agg = NC * devices
    count_rows = NB * devices
    first_agg = device * NC
    first_row = device * NB
    core = jnp.stack([device % 2, device // 2 % 2]).astype(jnp.int32)

    def shifted(distance):
        return [(i, (i + distance) % devices) for i in range(devices)]

    parity = device % 2
    smem = pl.BlockSpec(memory_space=pltpu.SMEM)
    vmem = pl.BlockSpec(memory_space=pltpu.VMEM)
    hbm = pl.BlockSpec(memory_space=pltpu.HBM)
    bf16 = jnp.bfloat16

    def params(mebibytes):
        return pltpu.CompilerParams(vmem_limit_bytes=mebibytes * 1024 * 1024)

    def cost(flops, size):
        return pl.CostEstimate(flops=flops, bytes_accessed=size, transcendentals=0)

    def picked(outer):
        return pl.pallas_call(
            functools.partial(pick_kernel, outer=outer),
            out_shape=jax.ShapeDtypeStruct((AGG,) + p_blocks.shape[1:], bf16),
            in_specs=[smem, hbm],
            out_specs=vmem,
            scratch_shapes=[pltpu.SemaphoreType.DMA((4,))],
            compiler_params=params(60),
            name="pick_outer" if outer else "pick_inner",
        )(core, p_blocks)

    outward = [(i, (i + (1 if i % 2 else -1)) % devices) for i in range(devices)]
    inward = [(i, i ^ 1) for i in range(devices)]
    p_slow = permuted(picked(True), outward)
    p_fast = permuted(picked(False), inward)
    edge_cols = jnp.stack([cols_p[:AGG], cols_p[NB - AGG :]])
    cols_slow = permuted(edge_cols[parity], outward)
    cols_fast = permuted(edge_cols[1 - parity], inward)

    def slots(cols, agg):
        return (cols - agg + H) % count_agg

    own_agg = jnp.arange(NB, dtype=jnp.int32)[:, None] // AGG
    inv_own = inverse_index(slots(cols_p, first_agg + own_agg) + own_agg + 1, COLS, KP)
    fast_place = NC * (1 - parity) - parity
    inv_fast = inverse_index(slots(cols_fast, first_agg + fast_place) + fast_place + 1, COLS, KP)
    slow_place = NC * parity - (1 - parity)
    inv_slow = inverse_index(slots(cols_slow, first_agg + slow_place) + 2 * parity, WSLOT, KP)
    inv_a = inverse_index((cols_a - first_row - (own_agg - 1) * AGG) % count_rows, 3 * AGG, KA)

    def block(rows, width, kind=bf16):
        return jax.ShapeDtypeStruct((rows, BS, width), kind)

    span = WINDOW * BS
    outs = [
        block(NC, span),
        block(NC, span),
        block(REST, span),
        block(NC, span),
        block(FIRST, span),
        block(REST, 2 * AW),
        block(FIRST + NC, AW),
        block(REST, AW),
        block(FIRST, AW),
        block(REST, AW),
        block(WCOLS, 2 * AW),
        block(WSLOT, AW, jnp.float32),
        block(AGG, AW),
    ]
    (
        send_low,
        send_high,
        send_rest,
        far,
        inner,
        fast_rest,
        slow_first,
        slow_rest,
        other_first,
        other_rest,
        wt_fast,
        rest,
        at_halo,
    ) = pl.pallas_call(
        fast_kernel,
        out_shape=outs,
        in_specs=[smem] * 4 + [hbm, hbm, vmem],
        out_specs=[hbm] * len(outs),
        scratch_shapes=[
            pltpu.VMEM((NB + AGG, BS, KP * BS), bf16),
            pltpu.VMEM((COLS, BS, EXT * BS), bf16),
            pltpu.VMEM((NC, 3 * AGG, BS, AW), bf16),
            pltpu.VMEM((KP + 1, BS, LANES), bf16),
            pltpu.VMEM((KA + 1, BS, LANES), bf16),
            pltpu.VMEM((ROWS + NC + FIRST, BS, 2 * AW), bf16),
            pltpu.VMEM((ROWS, BS, span), bf16),
            pltpu.VMEM((NC, BS, span), bf16),
            pltpu.VMEM((FIRST, BS, span), bf16),
            pltpu.VMEM((REST, BS, 2 * AW), bf16),
            pltpu.VMEM((ROWS + NC, BS, AW), bf16),
            pltpu.VMEM((ROWS, BS, AW), bf16),
            pltpu.VMEM((WCOLS, BS, 2 * AW), bf16),
            pltpu.VMEM((WSLOT, BS, AW), jnp.float32),
            pltpu.SemaphoreType.DMA(((NB + AGG) // QUAD,)),
            pltpu.SemaphoreType.DMA((len(outs),)),
        ],
        compiler_params=params(56),
        cost_estimate=cost(20 * 10**9, 30 * 10**6),
        name="fast",
    )(core, inv_own, inv_fast, inv_a, p_blocks, p_fast, a_blocks)

    low = permuted(send_low, inward)
    high = permuted(send_high, inward)
    other_first = permuted(other_first, inward)
    p_slow, low, high, other_first = lax.optimization_barrier((p_slow, low, high, other_first))

    wt_slow = pl.pallas_call(
        slow_kernel,
        out_shape=block(WCOLS, AW),
        in_specs=[smem] * 2 + [vmem] * 3,
        out_specs=vmem,
        scratch_shapes=[
            pltpu.VMEM((KP + 1, BS, LANES), bf16),
            pltpu.VMEM((WSLOT, BS, AW), bf16),
        ],
        compiler_params=params(24),
        cost_estimate=cost(20 * 10**9, 200 * 10**6),
        name="slow",
    )(core, inv_slow, p_slow, at_halo, rest)
    wt_other = permuted(wt_slow, inward)

    wt_slow, low, high = lax.optimization_barrier((wt_slow, low, high))
    mine, far = pl.pallas_call(
        mine_kernel,
        out_shape=[block(FIRST, span, jnp.float32), block(NC, span)],
        in_specs=[vmem] * 6,
        out_specs=[vmem] * 2,
        compiler_params=params(24),
        cost_estimate=cost(10**10, 100 * 10**6),
        name="mine",
    )(slow_first, wt_slow, inner, low, high, far)
    mine, wt_other, send_rest, other_rest = lax.optimization_barrier(
        (mine, wt_other, send_rest, other_rest)
    )
    arrived_rest = permuted(send_rest, inward)
    other_rest = permuted(other_rest, inward)
    relay, direct = pl.pallas_call(
        join_first_kernel,
        out_shape=[block(NC, span)] * 2,
        in_specs=[vmem] * 3,
        out_specs=[vmem] * 2,
        compiler_params=params(16),
        cost_estimate=cost(3 * 10**9, 10**7),
        name="join_first",
    )(other_first, wt_other, mine)
    along_x = [(i, i ^ 2) for i in range(devices)]
    x_sign = [1 if i // 2 % 2 else -1 for i in range(devices)]
    relay = permuted(relay, along_x)
    direct = permuted(direct, [(i, (i + 4 * x_sign[i]) % devices) for i in range(devices)])
    merge, pair, own = pl.pallas_call(
        join_rest_kernel,
        out_shape=[block(NC, span, jnp.float32), block(NC, span), block(NC, span, jnp.float32)],
        in_specs=[vmem] * 7,
        out_specs=[vmem] * 3,
        compiler_params=params(30),
        cost_estimate=cost(40 * 10**9, 200 * 10**6),
        name="join_rest",
    )(fast_rest, slow_rest, other_rest, wt_fast, wt_slow, wt_other, arrived_rest)
    relay, direct, pair, far = lax.optimization_barrier((relay, direct, pair, far))
    merged = pl.pallas_call(
        merge_kernel,
        out_shape=block(NC, MERGED * BS),
        in_specs=[smem, vmem, vmem],
        out_specs=vmem,
        scratch_shapes=[pltpu.VMEM((BS, MERGED * BS), jnp.float32)],
        compiler_params=params(16),
        cost_estimate=cost(10**7, 10**7),
        name="merge",
    )(core, merge, relay)
    merged = permuted(merged, [(i, (i - 4 * x_sign[i]) % devices) for i in range(devices)])
    pair = permuted(pair, along_x)
    far = permuted(far, [(i, (i + (5 if i % 2 else -5)) % devices) for i in range(devices)])

    total = block(NC, BAND * BS, jnp.float32)
    frame = pltpu.VMEM((BS, FRAME * BS), jnp.float32)
    early = pl.pallas_call(
        early_kernel,
        out_shape=total,
        in_specs=[smem, vmem, vmem],
        out_specs=vmem,
        scratch_shapes=[frame],
        compiler_params=params(16),
        cost_estimate=cost(10**7, 10**7),
        name="early",
    )(core, own, direct)
    return pl.pallas_call(
        total_kernel,
        out_shape=total,
        in_specs=[smem] + [vmem] * 4,
        out_specs=hbm,
        scratch_shapes=[
            frame,
            pltpu.VMEM(total.shape, jnp.float32),
            pltpu.SemaphoreType.DMA((NC,)),
        ],
        compiler_params=params(20),
        cost_estimate=cost(10**7, 10**7),
        name="total",
    )(core, early, pair, merged, far)


def solution(mesh):
    in_specs = (P("dom", None, None), P("dom", None, None), P("dom", None), P("dom", None))
    out_specs = P("dom", None, None)
    return jax.shard_map(body, mesh=mesh, in_specs=in_specs, out_specs=out_specs, check_vma=False)
```

```python
import functools

import jax
import jax.numpy as jnp
from jax import lax
from jax.experimental import pallas as pl
from jax.experimental.pallas import tpu as pltpu
from jax.sharding import PartitionSpec as P

BS = 64
KA = 7
KP = 27
AGG = 8
H = 15
NC = 3
NB = 24
WIN = 31
WSLOT = 33
BAND = 63

QUAD = 4
LANES = QUAD * BS
EXT = NB + 2 * AGG
COLS = NC + 2 * H + 2
WCOLS = 40
WINDOW = 38
TILES = 10
GROUPS = 5
K = NB * BS
AW = AGG * BS
FRAME = 76
NT = (((1,), (1,)), ((), ()))
ROWS = NC * GROUPS
FIRST = 2 * NC
REST = ROWS - FIRST
MERGED = WINDOW + 6


def eye(n):
    rows = lax.broadcasted_iota(jnp.int32, (n, n), 0)
    lanes = lax.broadcasted_iota(jnp.int32, (n, n), 1)
    return jnp.where(rows == lanes, 1.0, 0.0).astype(jnp.bfloat16)


def low_half():
    return lax.broadcasted_iota(jnp.int32, (BS, 2 * BS), 1) < BS


def transpose_quad(unit, block, turned, width):
    for start in range(0, width, LANES):
        size = min(LANES, width - start)
        part = lax.dot_general(
            unit[:size, :size],
            block[:, start : start + size],
            NT,
            preferred_element_type=jnp.float32,
        )
        turned[start // BS : (start + size) // BS] = part.astype(jnp.bfloat16).reshape(
            size // BS, BS, LANES
        )


def spread_quad(turned, index, first, store, count, unroll):
    half = low_half()

    def place(slot, carry):
        for pair in range(2):
            lanes = slice(pair * 2 * BS, (pair + 1) * 2 * BS)
            left = turned[index[first + 2 * pair, slot], :, lanes]
            right = turned[index[first + 2 * pair + 1, slot], :, lanes]
            store(slot, pair, jnp.where(half, left, right))
        return carry

    lax.fori_loop(0, count, place, 0, unroll=unroll)


def fast_kernel(
    core,
    inv_own,
    inv_fast,
    inv_a,
    p_own,
    p_fast,
    a_own,
    send_low,
    send_high,
    far,
    inner,
    send_rest,
    fast_rest,
    slow_first,
    slow_rest,
    other_first,
    other_rest,
    wt,
    rest,
    at_halo,
    p_buf,
    ext,
    at,
    unit,
    turned_p,
    turned_a,
    lhs,
    rows_buf,
    fast_buf,
    slow_buf,
    other_buf,
    wt_buf,
    rest_buf,
    in_sems,
    out_sems,
):
    s = core[0]
    own_quads = NB // QUAD
    halo_quads = AGG // QUAD

    def load(quad):
        if quad < own_quads:
            source = p_own.at[quad * QUAD : (quad + 1) * QUAD]
        else:
            source = p_fast.at[(quad - own_quads) * QUAD : (quad - own_quads + 1) * QUAD]
        target = p_buf.at[quad * QUAD : (quad + 1) * QUAD]
        return pltpu.make_async_copy(source, target, in_sems.at[quad])

    for quad in range(own_quads + halo_quads):
        load(quad).start()

    unit[...] = eye(LANES)
    turned_p[KP] = jnp.zeros((BS, LANES), jnp.bfloat16)
    turned_a[KA] = jnp.zeros((BS, LANES), jnp.bfloat16)

    @pl.loop(0, own_quads)
    def _(quad):
        block = a_own[pl.ds(quad * QUAD, QUAD)].reshape(LANES, KA * BS)
        transpose_quad(unit, block, turned_a, KA * BS)
        agg = quad // halo_quads

        def store(slot, pair, value):
            lane = pl.multiple_of((quad % halo_quads) * LANES + pair * 2 * BS, 2 * BS)
            at[agg, slot, :, pl.ds(lane, 2 * BS)] = value

        spread_quad(turned_a, inv_a, quad * QUAD, store, 3 * AGG, 8)

    slow_agg = 2 * s
    halo_copy = pltpu.make_async_copy(at.at[slow_agg, pl.ds(16 * s, AGG)], at_halo, out_sems.at[0])
    halo_copy.start()

    def band_quad(source_row, index, index_row, first_lane):
        block = p_buf[pl.ds(source_row, QUAD)].reshape(LANES, KP * BS)
        transpose_quad(unit, block, turned_p, KP * BS)

        def store(slot, pair, value):
            lane = pl.multiple_of(first_lane + pair * 2 * BS, 2 * BS)
            ext[slot, :, pl.ds(lane, 2 * BS)] = value

        spread_quad(turned_p, index, index_row, store, COLS, 7)

    for quad in range(own_quads + halo_quads):
        load(quad).wait()

    @pl.loop(0, own_quads)
    def _(quad):
        band_quad(quad * QUAD, inv_own, quad * QUAD, AW + quad * LANES)

    @pl.loop(0, halo_quads)
    def _(quad):
        first_lane = (AW + K) * (1 - s) + quad * LANES
        band_quad((own_quads + quad) * QUAD, inv_fast, quad * QUAD, first_lane)

    fast_lanes = pl.ds(pl.multiple_of(AW + (1 - s) * AW, AW), 2 * AW)
    slow_lanes = pl.ds(pl.multiple_of(AW + 2 * s * AW, AW), AW)
    x = core[1]
    for place, i in enumerate((1 + 2 * x, 4 * x, 4 - 4 * x, 3 - 2 * x, 2)):
        for j in range(NC):
            row = NC * place + j
            mine, other = 6 * i + 3 + j + 1, 6 * i + 6 * (1 - s) + j + 1
            if place < 2:
                lhs[row] = ext[other, :, fast_lanes]
                lhs[FIRST + NC + row] = ext[mine, :, fast_lanes]
            else:
                lhs[ROWS + row - FIRST] = ext[other, :, fast_lanes]
                fast_buf[row - FIRST] = ext[mine, :, fast_lanes]
            slow_buf[row if place < 2 else row + NC] = ext[mine, :, slow_lanes]
            other_buf[row] = ext[other, :, slow_lanes]
    for j in range(NC):
        lhs[FIRST + j] = ext[30 * s + j + 1, :, fast_lanes]
        slow_buf[FIRST + j] = ext[30 * s + j + 1, :, slow_lanes]
    copies = [halo_copy]

    def write(source, target):
        copy = pltpu.make_async_copy(source, target, out_sems.at[len(copies)])
        copy.start()
        copies.append(copy)

    write(other_buf.at[:FIRST], other_first)
    write(other_buf.at[FIRST:], other_rest)
    write(fast_buf, fast_rest)
    write(slow_buf.at[: FIRST + NC], slow_first)
    write(slow_buf.at[FIRST + NC :], slow_rest)

    wt_buf[0:7] = jnp.zeros((7, BS, 2 * AW), jnp.bfloat16)
    wt_buf[33:] = jnp.zeros((WCOLS - 33, BS, 2 * AW), jnp.bfloat16)
    chunk = WSLOT // 3

    @pl.loop(0, 2)
    def _(place):
        agg = place + 1 - s
        lane = pl.multiple_of(agg * AW, AW)
        target = pl.multiple_of(place * AW, AW)

        @pl.loop(0, 3)
        def _(part):
            first = agg + part * chunk
            left = ext[pl.ds(first, chunk), :, pl.ds(lane, 3 * AW)].reshape(chunk * BS, 3 * AW)
            value = jnp.dot(
                left, at[agg].reshape(3 * AW, AW), preferred_element_type=jnp.float32
            )
            wt_buf[pl.ds(3 * s + first, chunk), :, pl.ds(target, AW)] = value.astype(
                jnp.bfloat16
            ).reshape(chunk, BS, AW)

    write(wt_buf, wt)

    @pl.loop(0, 3)
    def _(part):
        lane = pl.multiple_of(AW + s * AW, AW)
        left = ext[pl.ds(slow_agg + part * chunk, chunk), :, pl.ds(lane, 2 * AW)]
        right = at[slow_agg, pl.ds(AGG - AGG * s, 2 * AGG)].reshape(2 * AW, AW)
        value = jnp.dot(
            left.reshape(chunk * BS, 2 * AW), right, preferred_element_type=jnp.float32
        )
        rest_buf[pl.ds(part * chunk, chunk)] = value.reshape(chunk, BS, AW)

    write(rest_buf, rest)

    def emit(tile, width):
        right = wt_buf[pl.ds(QUAD * tile, width // BS)].reshape(width, 2 * AW)
        left = lhs[...].reshape((ROWS + REST) * BS, 2 * AW)
        value = lax.dot_general(left, right, NT, preferred_element_type=jnp.float32)
        rows_buf[:, :, tile_lanes(tile, width)] = value.astype(jnp.bfloat16).reshape(
            ROWS + REST, BS, width
        )

    parts = (
        (send_low, 0),
        (send_high, NC),
        (far, FIRST),
        (inner, FIRST + NC),
        (send_rest, ROWS),
    )
    bounds = (0, 4, 8, TILES)
    for first, last in zip(bounds[:-1], bounds[1:]):

        @pl.loop(first, min(last, TILES - 1))
        def _(tile):
            emit(tile, LANES)

        if last == TILES:
            emit(TILES - 1, LANES // 2)
        lanes = slice(first * LANES, min(last * LANES, WINDOW * BS))
        for target, row in parts:
            rows = slice(row, row + target.shape[0])
            write(rows_buf.at[rows, :, lanes], target.at[:, :, lanes])
    for copy in copies:
        copy.wait()


def each_tile(step):
    @pl.loop(0, TILES - 1)
    def _(tile):
        step(tile, LANES)

    step(TILES - 1, LANES // 2)


def tile_dot(rows, cols, tile, width):
    left = rows[...].reshape(rows.shape[0] * BS, rows.shape[2])
    right = cols[pl.ds(QUAD * tile, width // BS)].reshape(width, cols.shape[2])
    value = lax.dot_general(left, right, NT, preferred_element_type=jnp.float32)
    return value.reshape(rows.shape[0], BS, width)


def tile_lanes(tile, width):
    return pl.ds(pl.multiple_of(tile * LANES, LANES), width)


def mine_kernel(slow, wt_slow, inner, low, high, far_fast, out, far):
    def step(tile, width):
        lanes = tile_lanes(tile, width)
        outer = tile_dot(slow, wt_slow, tile, width)
        near = outer[:FIRST] + inner[:, :, lanes].astype(jnp.float32)
        out[:NC, :, lanes] = near[:NC] + low[:, :, lanes].astype(jnp.float32)
        out[NC:, :, lanes] = near[NC:] + high[:, :, lanes].astype(jnp.float32)
        tail = outer[FIRST:] + far_fast[:, :, lanes].astype(jnp.float32)
        far[:, :, lanes] = tail.astype(jnp.bfloat16)

    each_tile(step)


def slow_kernel(core, inv_slow, p_slow, at_halo, rest, wt, unit, turned_p, ext):
    s = core[0]
    unit[...] = eye(LANES)
    turned_p[KP] = jnp.zeros((BS, LANES), jnp.bfloat16)

    @pl.loop(0, AGG // QUAD)
    def _(quad):
        block = p_slow[pl.ds(quad * QUAD, QUAD)].reshape(LANES, KP * BS)
        transpose_quad(unit, block, turned_p, KP * BS)

        def store(slot, pair, value):
            lane = pl.multiple_of(quad * LANES + pair * 2 * BS, 2 * BS)
            ext[slot, :, pl.ds(lane, 2 * BS)] = value

        spread_quad(turned_p, inv_slow, quad * QUAD, store, WSLOT, 11)

    wt[0:5] = jnp.zeros((5, BS, AW), jnp.bfloat16)
    wt[WSLOT:] = jnp.zeros((WCOLS - WSLOT, BS, AW), jnp.bfloat16)
    chunk = WSLOT // 3

    @pl.loop(0, 3)
    def _(part):
        rows = pl.ds(part * chunk, chunk)
        value = jnp.dot(
            ext[rows].reshape(chunk * BS, AW),
            at_halo[...].reshape(AW, AW),
            preferred_element_type=jnp.float32,
        )
        value = value.reshape(chunk, BS, AW) + rest[rows]
        wt[pl.ds(5 * s + part * chunk, chunk)] = value.astype(jnp.bfloat16)


def join_first_kernel(other, wt_other, mine, relay, direct):
    def step(tile, width):
        lanes = tile_lanes(tile, width)
        value = tile_dot(other, wt_other, tile, width) + mine[:, :, lanes]
        relay[:, :, lanes] = value[:NC].astype(jnp.bfloat16)
        direct[:, :, lanes] = value[NC:].astype(jnp.bfloat16)

    each_tile(step)


def join_rest_kernel(fast, slow, other, wt_fast, wt_slow, wt_other, arrived, merge, pair, own):
    def step(tile, width):
        lanes = tile_lanes(tile, width)
        value = tile_dot(fast, wt_fast, tile, width) + tile_dot(slow, wt_slow, tile, width)
        value = value + tile_dot(other, wt_other, tile, width)
        value = value + arrived[:, :, lanes].astype(jnp.float32)
        merge[:, :, lanes] = value[:NC]
        pair[:, :, lanes] = value[NC : 2 * NC].astype(jnp.bfloat16)
        own[:, :, lanes] = value[2 * NC :]

    each_tile(step)


def stage_kernel(at_halo, rest, at_out, rest_out, sems):
    copies = [
        pltpu.make_async_copy(at_halo, at_out, sems.at[0]),
        pltpu.make_async_copy(rest, rest_out, sems.at[1]),
    ]
    for copy in copies:
        copy.start()
    for copy in copies:
        copy.wait()


def merge_kernel(core, rows, relay, out, frame):
    x = core[1]
    step = 6 * BS
    for j in range(NC):
        frame[...] = jnp.zeros_like(frame)
        frame[:, pl.ds(pl.multiple_of(step * x, step), WINDOW * BS)] = rows[j]
        lanes = pl.ds(pl.multiple_of(step * (1 - x), step), WINDOW * BS)
        frame[:, lanes] += relay[j].astype(jnp.float32)
        out[j] = frame[...].astype(jnp.bfloat16)


def in_frame(s, j, frame, messages, store):
    odd = (j + 1 - s) % 2
    frame[...] = jnp.zeros_like(frame)
    for message, start in messages:
        lane = pl.multiple_of((start - odd + 6) * BS, 2 * BS)
        frame[:, pl.ds(lane, message.shape[2])] += message[j].astype(jnp.float32)
    first, last = 6 * BS, (6 + BAND) * BS

    @pl.when(odd == 0)
    def _():
        store(frame[:, first:last])

    @pl.when(odd == 1)
    def _():
        store(frame[:, first - BS : last - BS])


def early_kernel(core, own, direct, pair, far, out, frame):
    s, x = core[0], core[1]
    for j in range(NC):
        top = 27 - 3 * s - j
        far_start = jnp.where(s == 1, 30 - j, -3 - j)
        messages = [(own, top - 12), (direct, top - 24 * x), (pair, top - 6 - 12 * x)]
        messages.append((far, far_start))

        def store(value, j=j):
            out[j] = value

        in_frame(s, j, frame, messages, store)


def total_kernel(core, early, merged, out, frame, buf, sems):
    s, x = core[0], core[1]
    copies = []
    for j in range(NC):

        def store(value, j=j):
            buf[j] = value + early[j]

        in_frame(s, j, frame, [(merged, 3 - 3 * s - j + 18 * x)], store)
        copy = pltpu.make_async_copy(buf.at[j], out.at[j], sems.at[j])
        copy.start()
        copies.append(copy)
    for copy in copies:
        copy.wait()


def pick_kernel(core, source, outer, inner, sems):
    s = core[0]
    step = AGG // 4
    copies = []
    for target, side in ((outer, s), (inner, 1 - s)):
        for k in range(4):
            rows = pl.ds((NB - AGG) * side + k * step, step)
            into = target.at[k * step : (k + 1) * step]
            copies.append(pltpu.make_async_copy(source.at[rows], into, sems.at[len(copies)]))
    for copy in copies:
        copy.start()
    for copy in copies:
        copy.wait()


def permuted(block, pairs):
    return lax.ppermute(block, "dom", pairs)


def inverse_index(offset, slots, empty):
    order = jnp.arange(offset.shape[1], dtype=jnp.int32)[None, :, None]
    hit = offset[:, :, None] == jnp.arange(slots, dtype=jnp.int32)[None, None, :]
    return empty + jnp.sum(jnp.where(hit, order - empty, 0), axis=1)


def body(a_blocks, p_blocks, cols_a, cols_p):
    devices = lax.axis_size("dom")
    device = lax.axis_index("dom")
    count_agg = NC * devices
    count_rows = NB * devices
    first_agg = device * NC
    first_row = device * NB
    core = jnp.stack([device % 2, device // 2 % 2]).astype(jnp.int32)

    def shifted(distance):
        return [(i, (i + distance) % devices) for i in range(devices)]

    parity = device % 2
    smem = pl.BlockSpec(memory_space=pltpu.SMEM)
    vmem = pl.BlockSpec(memory_space=pltpu.VMEM)
    hbm = pl.BlockSpec(memory_space=pltpu.HBM)
    bf16 = jnp.bfloat16

    def params(mebibytes):
        return pltpu.CompilerParams(vmem_limit_bytes=mebibytes * 1024 * 1024)

    def cost(flops, size):
        return pl.CostEstimate(flops=flops, bytes_accessed=size, transcendentals=0)

    edge = jax.ShapeDtypeStruct((AGG,) + p_blocks.shape[1:], bf16)
    outer, inner = pl.pallas_call(
        pick_kernel,
        out_shape=[edge, edge],
        in_specs=[smem, hbm],
        out_specs=[vmem, vmem],
        scratch_shapes=[pltpu.SemaphoreType.DMA((8,))],
        compiler_params=params(60),
        name="pick",
    )(core, p_blocks)
    outward = [(i, (i + (1 if i % 2 else -1)) % devices) for i in range(devices)]
    inward = [(i, i ^ 1) for i in range(devices)]
    p_slow = permuted(outer, outward)
    p_fast = permuted(inner, inward)
    edge_cols = jnp.stack([cols_p[:AGG], cols_p[NB - AGG :]])
    cols_slow = permuted(edge_cols[parity], outward)
    cols_fast = permuted(edge_cols[1 - parity], inward)

    def slots(cols, agg):
        return (cols - agg + H) % count_agg

    own_agg = jnp.arange(NB, dtype=jnp.int32)[:, None] // AGG
    inv_own = inverse_index(slots(cols_p, first_agg + own_agg) + own_agg + 1, COLS, KP)
    fast_place = NC * (1 - parity) - parity
    inv_fast = inverse_index(slots(cols_fast, first_agg + fast_place) + fast_place + 1, COLS, KP)
    slow_place = NC * parity - (1 - parity)
    inv_slow = inverse_index(slots(cols_slow, first_agg + slow_place) + 2 * parity, WSLOT, KP)
    inv_fast, inv_slow = lax.optimization_barrier((inv_fast, inv_slow))
    inv_a = inverse_index((cols_a - first_row - (own_agg - 1) * AGG) % count_rows, 3 * AGG, KA)

    def block(rows, width, kind=bf16):
        return jax.ShapeDtypeStruct((rows, BS, width), kind)

    span = WINDOW * BS
    outs = [
        block(NC, span),
        block(NC, span),
        block(NC, span),
        block(FIRST, span),
        block(REST, span),
        block(REST, 2 * AW),
        block(FIRST + NC, AW),
        block(REST, AW),
        block(FIRST, AW),
        block(REST, AW),
        block(WCOLS, 2 * AW),
        block(WSLOT, AW, jnp.float32),
        block(AGG, AW),
    ]
    (
        send_low,
        send_high,
        far,
        inner,
        send_rest,
        fast_rest,
        slow_first,
        slow_rest,
        other_first,
        other_rest,
        wt_fast,
        rest,
        at_halo,
    ) = pl.pallas_call(
        fast_kernel,
        out_shape=outs,
        in_specs=[smem] * 4 + [hbm, hbm, vmem],
        out_specs=[hbm] * len(outs),
        scratch_shapes=[
            pltpu.VMEM((NB + AGG, BS, KP * BS), bf16),
            pltpu.VMEM((COLS, BS, EXT * BS), bf16),
            pltpu.VMEM((NC, 3 * AGG, BS, AW), bf16),
            pltpu.VMEM((LANES, LANES), bf16),
            pltpu.VMEM((KP + 1, BS, LANES), bf16),
            pltpu.VMEM((KA + 1, BS, LANES), bf16),
            pltpu.VMEM((ROWS + REST, BS, 2 * AW), bf16),
            pltpu.VMEM((ROWS + REST, BS, span), bf16),
            pltpu.VMEM((REST, BS, 2 * AW), bf16),
            pltpu.VMEM((ROWS + NC, BS, AW), bf16),
            pltpu.VMEM((ROWS, BS, AW), bf16),
            pltpu.VMEM((WCOLS, BS, 2 * AW), bf16),
            pltpu.VMEM((WSLOT, BS, AW), jnp.float32),
            pltpu.SemaphoreType.DMA(((NB + AGG) // QUAD,)),
            pltpu.SemaphoreType.DMA((len(outs) + 10,)),
        ],
        compiler_params=params(56),
        cost_estimate=cost(20 * 10**9, 30 * 10**6),
        name="fast",
    )(core, inv_own, inv_fast, inv_a, p_blocks, p_fast, a_blocks)

    low = permuted(send_low, inward)
    high = permuted(send_high, inward)
    other_first = permuted(other_first, inward)
    at_halo, rest = pl.pallas_call(
        stage_kernel,
        out_shape=[block(AGG, AW), block(WSLOT, AW, jnp.float32)],
        in_specs=[hbm] * 2,
        out_specs=[vmem] * 2,
        scratch_shapes=[pltpu.SemaphoreType.DMA((2,))],
        compiler_params=params(8),
        cost_estimate=cost(10**6, 10**6),
        name="stage",
    )(at_halo, rest)
    p_slow, low, high, other_first = lax.optimization_barrier((p_slow, low, high, other_first))

    wt_slow = pl.pallas_call(
        slow_kernel,
        out_shape=block(WCOLS, AW),
        in_specs=[smem] * 2 + [vmem] * 3,
        out_specs=vmem,
        scratch_shapes=[
            pltpu.VMEM((LANES, LANES), bf16),
            pltpu.VMEM((KP + 1, BS, LANES), bf16),
            pltpu.VMEM((WSLOT, BS, AW), bf16),
        ],
        compiler_params=params(24),
        cost_estimate=cost(20 * 10**9, 200 * 10**6),
        name="slow",
    )(core, inv_slow, p_slow, at_halo, rest)
    wt_other = permuted(wt_slow, inward)

    wt_slow, low, high = lax.optimization_barrier((wt_slow, low, high))
    wt_slow, send_rest, other_rest = lax.optimization_barrier((wt_slow, send_rest, other_rest))
    mine, far = pl.pallas_call(
        mine_kernel,
        out_shape=[block(FIRST, span, jnp.float32), block(NC, span)],
        in_specs=[vmem] * 6,
        out_specs=[vmem] * 2,
        compiler_params=params(24),
        cost_estimate=cost(10**10, 100 * 10**6),
        name="mine",
    )(slow_first, wt_slow, inner, low, high, far)
    mine, wt_other, send_rest, other_rest = lax.optimization_barrier(
        (mine, wt_other, send_rest, other_rest)
    )
    arrived_rest = permuted(send_rest, inward)
    other_rest = permuted(other_rest, inward)
    relay, direct = pl.pallas_call(
        join_first_kernel,
        out_shape=[block(NC, span)] * 2,
        in_specs=[vmem] * 3,
        out_specs=[vmem] * 2,
        compiler_params=params(16),
        cost_estimate=cost(3 * 10**9, 10**7),
        name="join_first",
    )(other_first, wt_other, mine)
    along_x = [(i, i ^ 2) for i in range(devices)]
    x_sign = [1 if i // 2 % 2 else -1 for i in range(devices)]
    relay = permuted(relay, along_x)
    direct = permuted(direct, [(i, (i + 4 * x_sign[i]) % devices) for i in range(devices)])
    merge, pair, own = pl.pallas_call(
        join_rest_kernel,
        out_shape=[block(NC, span, jnp.float32), block(NC, span), block(NC, span, jnp.float32)],
        in_specs=[vmem] * 7,
        out_specs=[vmem] * 3,
        compiler_params=params(30),
        cost_estimate=cost(40 * 10**9, 200 * 10**6),
        name="join_rest",
    )(fast_rest, slow_rest, other_rest, wt_fast, wt_slow, wt_other, arrived_rest)
    relay, direct = lax.optimization_barrier((relay, direct))
    pair, far = lax.optimization_barrier((pair, far))
    merged = pl.pallas_call(
        merge_kernel,
        out_shape=block(NC, MERGED * BS),
        in_specs=[smem, vmem, vmem],
        out_specs=vmem,
        scratch_shapes=[pltpu.VMEM((BS, MERGED * BS), jnp.float32)],
        compiler_params=params(16),
        cost_estimate=cost(10**7, 10**7),
        name="merge",
    )(core, merge, relay)
    merged = permuted(merged, [(i, (i - 4 * x_sign[i]) % devices) for i in range(devices)])
    pair = permuted(pair, along_x)
    far = permuted(far, [(i, (i + (5 if i % 2 else -5)) % devices) for i in range(devices)])

    total = block(NC, BAND * BS, jnp.float32)
    frame = pltpu.VMEM((BS, FRAME * BS), jnp.float32)
    early = pl.pallas_call(
        early_kernel,
        out_shape=total,
        in_specs=[smem] + [vmem] * 4,
        out_specs=vmem,
        scratch_shapes=[frame],
        compiler_params=params(16),
        cost_estimate=cost(10**10, 100 * 10**6),
        name="early",
    )(core, own, direct, pair, far)
    return pl.pallas_call(
        total_kernel,
        out_shape=total,
        in_specs=[smem] + [vmem] * 2,
        out_specs=hbm,
        scratch_shapes=[
            frame,
            pltpu.VMEM(total.shape, jnp.float32),
            pltpu.SemaphoreType.DMA((NC,)),
        ],
        compiler_params=params(20),
        cost_estimate=cost(10**7, 10**7),
        name="total",
    )(core, early, merged)


def solution(mesh):
    in_specs = (P("dom", None, None), P("dom", None, None), P("dom", None), P("dom", None))
    out_specs = P("dom", None, None)
    return jax.shard_map(body, mesh=mesh, in_specs=in_specs, out_specs=out_specs, check_vma=False)
```

```python
import functools

import jax
import jax.numpy as jnp
from jax import lax
from jax.experimental import pallas as pl
from jax.experimental.pallas import tpu as pltpu
from jax.sharding import PartitionSpec as P

BS = 64
KA = 7
KP = 27
AGG = 8
H = 15
NC = 3
NB = 24
WIN = 31
WSLOT = 33
BAND = 63

QUAD = 4
LANES = QUAD * BS
EXT = NB + 2 * AGG
COLS = NC + 2 * H + 2
WCOLS = 40
WINDOW = 38
TILES = 10
GROUPS = 5
K = NB * BS
AW = AGG * BS
FRAME = 76
NT = (((1,), (1,)), ((), ()))
ROWS = NC * GROUPS
FIRST = 2 * NC
REST = ROWS - FIRST
MERGED = WINDOW + 6


def eye(n):
    rows = lax.broadcasted_iota(jnp.int32, (n, n), 0)
    lanes = lax.broadcasted_iota(jnp.int32, (n, n), 1)
    return jnp.where(rows == lanes, 1.0, 0.0).astype(jnp.bfloat16)


def low_half():
    return lax.broadcasted_iota(jnp.int32, (BS, 2 * BS), 1) < BS


def places(device):
    return device[0] % 2, device[0] // 2 % 2


def transpose_quad(unit, block, turned, width):
    for start in range(0, width, LANES):
        size = min(LANES, width - start)
        part = lax.dot_general(
            unit[:size, :size],
            block[:, start : start + size],
            NT,
            preferred_element_type=jnp.float32,
        )
        turned[start // BS : (start + size) // BS] = part.astype(jnp.bfloat16).reshape(
            size // BS, BS, LANES
        )


def spread_quad(turned, index, first, store, count, unroll):
    half = low_half()

    def place(slot, carry):
        for pair in range(2):
            lanes = slice(pair * 2 * BS, (pair + 1) * 2 * BS)
            left = turned[index[first + 2 * pair, slot], :, lanes]
            right = turned[index[first + 2 * pair + 1, slot], :, lanes]
            store(slot, pair, jnp.where(half, left, right))
        return carry

    lax.fori_loop(0, count, place, 0, unroll=unroll)


def fast_kernel(
    core,
    inv_own,
    inv_fast,
    inv_a,
    p_own,
    p_fast,
    a_own,
    send_low,
    send_high,
    far,
    inner,
    send_rest,
    fast_rest,
    slow_first,
    slow_rest,
    other_first,
    other_rest,
    wt,
    rest,
    at_halo,
    p_buf,
    ext,
    at,
    unit,
    turned_p,
    turned_a,
    lhs,
    rows_buf,
    fast_buf,
    slow_buf,
    other_buf,
    wt_buf,
    rest_buf,
    in_sems,
    out_sems,
):
    s, x = places(core)
    own_quads = NB // QUAD
    halo_quads = AGG // QUAD

    def load(quad):
        if quad < own_quads:
            source = p_own.at[quad * QUAD : (quad + 1) * QUAD]
        else:
            source = p_fast.at[(quad - own_quads) * QUAD : (quad - own_quads + 1) * QUAD]
        target = p_buf.at[quad * QUAD : (quad + 1) * QUAD]
        return pltpu.make_async_copy(source, target, in_sems.at[quad])

    for quad in range(own_quads + halo_quads):
        load(quad).start()

    unit[...] = eye(LANES)
    turned_p[KP] = jnp.zeros((BS, LANES), jnp.bfloat16)
    turned_a[KA] = jnp.zeros((BS, LANES), jnp.bfloat16)

    @pl.loop(0, own_quads)
    def _(quad):
        block = a_own[pl.ds(quad * QUAD, QUAD)].reshape(LANES, KA * BS)
        transpose_quad(unit, block, turned_a, KA * BS)
        agg = quad // halo_quads

        def store(slot, pair, value):
            lane = pl.multiple_of((quad % halo_quads) * LANES + pair * 2 * BS, 2 * BS)
            at[agg, slot, :, pl.ds(lane, 2 * BS)] = value

        spread_quad(turned_a, inv_a, quad * QUAD, store, 3 * AGG, 8)

    slow_agg = 2 * s
    halo_copy = pltpu.make_async_copy(at.at[slow_agg, pl.ds(16 * s, AGG)], at_halo, out_sems.at[0])
    halo_copy.start()

    def band_quad(source_row, index, index_row, first_lane):
        block = p_buf[pl.ds(source_row, QUAD)].reshape(LANES, KP * BS)
        transpose_quad(unit, block, turned_p, KP * BS)

        def store(slot, pair, value):
            lane = pl.multiple_of(first_lane + pair * 2 * BS, 2 * BS)
            ext[slot, :, pl.ds(lane, 2 * BS)] = value

        spread_quad(turned_p, index, index_row, store, COLS, 7)

    for quad in range(own_quads + halo_quads):
        load(quad).wait()

    @pl.loop(0, own_quads)
    def _(quad):
        band_quad(quad * QUAD, inv_own, quad * QUAD, AW + quad * LANES)

    @pl.loop(0, halo_quads)
    def _(quad):
        first_lane = (AW + K) * (1 - s) + quad * LANES
        band_quad((own_quads + quad) * QUAD, inv_fast, quad * QUAD, first_lane)

    fast_lanes = pl.ds(pl.multiple_of(AW + (1 - s) * AW, AW), 2 * AW)
    slow_lanes = pl.ds(pl.multiple_of(AW + 2 * s * AW, AW), AW)
    for place, i in enumerate((1 + 2 * x, 4 * x, 4 - 4 * x, 3 - 2 * x, 2)):
        for j in range(NC):
            row = NC * place + j
            mine, other = 6 * i + 3 + j + 1, 6 * i + 6 * (1 - s) + j + 1
            if place < 2:
                lhs[row] = ext[other, :, fast_lanes]
                lhs[FIRST + NC + row] = ext[mine, :, fast_lanes]
            else:
                lhs[ROWS + row - FIRST] = ext[other, :, fast_lanes]
                fast_buf[row - FIRST] = ext[mine, :, fast_lanes]
            slow_buf[row if place < 2 else row + NC] = ext[mine, :, slow_lanes]
            other_buf[row] = ext[other, :, slow_lanes]
    for j in range(NC):
        lhs[FIRST + j] = ext[30 * s + j + 1, :, fast_lanes]
        slow_buf[FIRST + j] = ext[30 * s + j + 1, :, slow_lanes]
    copies = [halo_copy]

    def write(source, target):
        copy = pltpu.make_async_copy(source, target, out_sems.at[len(copies)])
        copy.start()
        copies.append(copy)

    write(other_buf.at[:FIRST], other_first)
    write(other_buf.at[FIRST:], other_rest)
    write(fast_buf, fast_rest)
    write(slow_buf.at[: FIRST + NC], slow_first)
    write(slow_buf.at[FIRST + NC :], slow_rest)

    wt_buf[0:7] = jnp.zeros((7, BS, 2 * AW), jnp.bfloat16)
    wt_buf[33:] = jnp.zeros((WCOLS - 33, BS, 2 * AW), jnp.bfloat16)
    chunk = WSLOT // 3

    @pl.loop(0, 2)
    def _(place):
        agg = place + 1 - s
        lane = pl.multiple_of(agg * AW, AW)
        target = pl.multiple_of(place * AW, AW)

        @pl.loop(0, 3)
        def _(part):
            first = agg + part * chunk
            left = ext[pl.ds(first, chunk), :, pl.ds(lane, 3 * AW)].reshape(chunk * BS, 3 * AW)
            value = jnp.dot(
                left, at[agg].reshape(3 * AW, AW), preferred_element_type=jnp.float32
            )
            wt_buf[pl.ds(3 * s + first, chunk), :, pl.ds(target, AW)] = value.astype(
                jnp.bfloat16
            ).reshape(chunk, BS, AW)

    write(wt_buf, wt)

    @pl.loop(0, 3)
    def _(part):
        lane = pl.multiple_of(AW + s * AW, AW)
        left = ext[pl.ds(slow_agg + part * chunk, chunk), :, pl.ds(lane, 2 * AW)]
        right = at[slow_agg, pl.ds(AGG - AGG * s, 2 * AGG)].reshape(2 * AW, AW)
        value = jnp.dot(
            left.reshape(chunk * BS, 2 * AW), right, preferred_element_type=jnp.float32
        )
        rest_buf[pl.ds(part * chunk, chunk)] = value.reshape(chunk, BS, AW)

    write(rest_buf, rest)

    def emit(tile, width):
        right = wt_buf[pl.ds(QUAD * tile, width // BS)].reshape(width, 2 * AW)
        left = lhs[...].reshape((ROWS + REST) * BS, 2 * AW)
        value = lax.dot_general(left, right, NT, preferred_element_type=jnp.float32)
        rows_buf[:, :, tile_lanes(tile, width)] = value.astype(jnp.bfloat16).reshape(
            ROWS + REST, BS, width
        )

    parts = (
        (send_low, 0),
        (send_high, NC),
        (far, FIRST),
        (inner, FIRST + NC),
        (send_rest, ROWS),
    )
    bounds = (0, 4, 8, TILES)
    for first, last in zip(bounds[:-1], bounds[1:]):

        @pl.loop(first, min(last, TILES - 1))
        def _(tile):
            emit(tile, LANES)

        if last == TILES:
            emit(TILES - 1, LANES // 2)
        lanes = slice(first * LANES, min(last * LANES, WINDOW * BS))
        for target, row in parts:
            rows = slice(row, row + target.shape[0])
            write(rows_buf.at[rows, :, lanes], target.at[:, :, lanes])
    for copy in copies:
        copy.wait()


def each_tile(step):
    @pl.loop(0, TILES - 1)
    def _(tile):
        step(tile, LANES)

    step(TILES - 1, LANES // 2)


def tile_dot(rows, cols, tile, width):
    left = rows[...].reshape(rows.shape[0] * BS, rows.shape[2])
    right = cols[pl.ds(QUAD * tile, width // BS)].reshape(width, cols.shape[2])
    value = lax.dot_general(left, right, NT, preferred_element_type=jnp.float32)
    return value.reshape(rows.shape[0], BS, width)


def tile_lanes(tile, width):
    return pl.ds(pl.multiple_of(tile * LANES, LANES), width)


def mine_kernel(slow, wt_slow, inner, low, high, far_fast, out, far):
    def step(tile, width):
        lanes = tile_lanes(tile, width)
        outer = tile_dot(slow, wt_slow, tile, width)
        near = outer[:FIRST] + inner[:, :, lanes].astype(jnp.float32)
        out[:NC, :, lanes] = near[:NC] + low[:, :, lanes].astype(jnp.float32)
        out[NC:, :, lanes] = near[NC:] + high[:, :, lanes].astype(jnp.float32)
        tail = outer[FIRST:] + far_fast[:, :, lanes].astype(jnp.float32)
        far[:, :, lanes] = tail.astype(jnp.bfloat16)

    each_tile(step)


def slow_kernel(core, inv_slow, p_slow, at_halo, rest, wt, unit, turned_p, ext):
    s, x = places(core)
    unit[...] = eye(LANES)
    turned_p[KP] = jnp.zeros((BS, LANES), jnp.bfloat16)

    @pl.loop(0, AGG // QUAD)
    def _(quad):
        block = p_slow[pl.ds(quad * QUAD, QUAD)].reshape(LANES, KP * BS)
        transpose_quad(unit, block, turned_p, KP * BS)

        def store(slot, pair, value):
            lane = pl.multiple_of(quad * LANES + pair * 2 * BS, 2 * BS)
            ext[slot, :, pl.ds(lane, 2 * BS)] = value

        spread_quad(turned_p, inv_slow, quad * QUAD, store, WSLOT, 11)

    wt[0:5] = jnp.zeros((5, BS, AW), jnp.bfloat16)
    wt[WSLOT:] = jnp.zeros((WCOLS - WSLOT, BS, AW), jnp.bfloat16)
    chunk = WSLOT // 3

    @pl.loop(0, 3)
    def _(part):
        rows = pl.ds(part * chunk, chunk)
        value = jnp.dot(
            ext[rows].reshape(chunk * BS, AW),
            at_halo[...].reshape(AW, AW),
            preferred_element_type=jnp.float32,
        )
        value = value.reshape(chunk, BS, AW) + rest[rows]
        wt[pl.ds(5 * s + part * chunk, chunk)] = value.astype(jnp.bfloat16)


def join_first_kernel(other, wt_other, mine, relay, direct):
    def step(tile, width):
        lanes = tile_lanes(tile, width)
        value = tile_dot(other, wt_other, tile, width) + mine[:, :, lanes]
        relay[:, :, lanes] = value[:NC].astype(jnp.bfloat16)
        direct[:, :, lanes] = value[NC:].astype(jnp.bfloat16)

    each_tile(step)


def join_rest_kernel(fast, slow, other, wt_fast, wt_slow, wt_other, arrived, merge, pair, own):
    def step(tile, width):
        lanes = tile_lanes(tile, width)
        value = tile_dot(fast, wt_fast, tile, width) + tile_dot(slow, wt_slow, tile, width)
        value = value + tile_dot(other, wt_other, tile, width)
        value = value + arrived[:, :, lanes].astype(jnp.float32)
        merge[:, :, lanes] = value[:NC]
        pair[:, :, lanes] = value[NC : 2 * NC].astype(jnp.bfloat16)
        own[:, :, lanes] = value[2 * NC :]

    each_tile(step)


def stage_kernel(at_halo, rest, at_out, rest_out, sems):
    copies = [
        pltpu.make_async_copy(at_halo, at_out, sems.at[0]),
        pltpu.make_async_copy(rest, rest_out, sems.at[1]),
    ]
    for copy in copies:
        copy.start()
    for copy in copies:
        copy.wait()


def merge_kernel(core, rows, relay, out, frame):
    s, x = places(core)
    step = 6 * BS
    for j in range(NC):
        frame[...] = jnp.zeros_like(frame)
        frame[:, pl.ds(pl.multiple_of(step * x, step), WINDOW * BS)] = rows[j]
        lanes = pl.ds(pl.multiple_of(step * (1 - x), step), WINDOW * BS)
        frame[:, lanes] += relay[j].astype(jnp.float32)
        out[j] = frame[...].astype(jnp.bfloat16)


def in_frame(s, j, frame, messages, store):
    odd = (j + 1 - s) % 2
    frame[...] = jnp.zeros_like(frame)
    for message, start in messages:
        lane = pl.multiple_of((start - odd + 6) * BS, 2 * BS)
        frame[:, pl.ds(lane, message.shape[2])] += message[j].astype(jnp.float32)
    first, last = 6 * BS, (6 + BAND) * BS

    @pl.when(odd == 0)
    def _():
        store(frame[:, first:last])

    @pl.when(odd == 1)
    def _():
        store(frame[:, first - BS : last - BS])


def early_kernel(core, own, direct, pair, far, out, frame):
    s, x = places(core)
    for j in range(NC):
        top = 27 - 3 * s - j
        far_start = jnp.where(s == 1, 30 - j, -3 - j)
        messages = [(own, top - 12), (direct, top - 24 * x), (pair, top - 6 - 12 * x)]
        messages.append((far, far_start))

        def store(value, j=j):
            out[j] = value

        in_frame(s, j, frame, messages, store)


def total_kernel(core, early, merged, out, frame, buf, sems):
    s, x = places(core)
    copies = []
    for j in range(NC):

        def store(value, j=j):
            buf[j] = value + early[j]

        in_frame(s, j, frame, [(merged, 3 - 3 * s - j + 18 * x)], store)
        copy = pltpu.make_async_copy(buf.at[j], out.at[j], sems.at[j])
        copy.start()
        copies.append(copy)
    for copy in copies:
        copy.wait()


def pick_kernel(core, source, outer, inner, buf, in_sems, out_sems):
    s, x = places(core)
    step = AGG // 4
    reads, writes = [], []
    for side, (target, which) in enumerate(((outer, s), (inner, 1 - s))):
        for k in range(4):
            n = len(reads)
            rows = pl.ds((NB - AGG) * which + k * step, step)
            part = buf.at[side, k * step : (k + 1) * step]
            into = target.at[k * step : (k + 1) * step]
            reads.append(pltpu.make_async_copy(source.at[rows], part, in_sems.at[n]))
            writes.append(pltpu.make_async_copy(part, into, out_sems.at[n]))
    for copy in reads:
        copy.start()
    for read, write in zip(reads, writes):
        read.wait()
        write.start()
    for copy in writes:
        copy.wait()


def permuted(block, pairs):
    return lax.ppermute(block, "dom", pairs)


def inverse_index(offset, slots, empty):
    order = jnp.arange(offset.shape[1], dtype=jnp.int32)[None, :, None]
    hit = offset[:, :, None] == jnp.arange(slots, dtype=jnp.int32)[None, None, :]
    return empty + jnp.sum(jnp.where(hit, order - empty, 0), axis=1)


def body(a_blocks, p_blocks, cols_a, cols_p):
    devices = lax.axis_size("dom")
    device = lax.axis_index("dom")
    count_agg = NC * devices
    count_rows = NB * devices
    first_agg = device * NC
    first_row = device * NB
    core = device.astype(jnp.int32).reshape(1)

    def shifted(distance):
        return [(i, (i + distance) % devices) for i in range(devices)]

    parity = device % 2
    smem = pl.BlockSpec(memory_space=pltpu.SMEM)
    vmem = pl.BlockSpec(memory_space=pltpu.VMEM)
    hbm = pl.BlockSpec(memory_space=pltpu.HBM)
    bf16 = jnp.bfloat16

    def params(mebibytes):
        return pltpu.CompilerParams(vmem_limit_bytes=mebibytes * 1024 * 1024)

    def cost(flops, size):
        return pl.CostEstimate(flops=flops, bytes_accessed=size, transcendentals=0)

    edge = jax.ShapeDtypeStruct((AGG,) + p_blocks.shape[1:], bf16)
    outer, inner = pl.pallas_call(
        pick_kernel,
        out_shape=[edge, edge],
        in_specs=[smem, hbm],
        out_specs=[hbm, hbm],
        scratch_shapes=[
            pltpu.VMEM((2,) + edge.shape, bf16),
            pltpu.SemaphoreType.DMA((8,)),
            pltpu.SemaphoreType.DMA((8,)),
        ],
        compiler_params=params(60),
        name="pick",
    )(core, p_blocks)
    outward = [(i, (i + (1 if i % 2 else -1)) % devices) for i in range(devices)]
    inward = [(i, i ^ 1) for i in range(devices)]
    outer, inner, edge_cols = lax.optimization_barrier((outer, inner, cols_p))
    p_slow = permuted(outer, outward)
    p_fast = permuted(inner, inward)
    edge_cols = jnp.stack([edge_cols[:AGG], edge_cols[NB - AGG :]])
    cols_slow = permuted(edge_cols[parity], outward)
    cols_fast = permuted(edge_cols[1 - parity], inward)

    def slots(cols, agg):
        return (cols - agg + H) % count_agg

    own_agg = jnp.arange(NB, dtype=jnp.int32)[:, None] // AGG
    inv_own = inverse_index(slots(cols_p, first_agg + own_agg) + own_agg + 1, COLS, KP)
    fast_place = NC * (1 - parity) - parity
    inv_fast = inverse_index(slots(cols_fast, first_agg + fast_place) + fast_place + 1, COLS, KP)
    slow_place = NC * parity - (1 - parity)
    inv_slow = inverse_index(slots(cols_slow, first_agg + slow_place) + 2 * parity, WSLOT, KP)
    inv_fast, inv_slow = lax.optimization_barrier((inv_fast, inv_slow))
    inv_a = inverse_index((cols_a - first_row - (own_agg - 1) * AGG) % count_rows, 3 * AGG, KA)

    def block(rows, width, kind=bf16):
        return jax.ShapeDtypeStruct((rows, BS, width), kind)

    span = WINDOW * BS
    outs = [
        block(NC, span),
        block(NC, span),
        block(NC, span),
        block(FIRST, span),
        block(REST, span),
        block(REST, 2 * AW),
        block(FIRST + NC, AW),
        block(REST, AW),
        block(FIRST, AW),
        block(REST, AW),
        block(WCOLS, 2 * AW),
        block(WSLOT, AW, jnp.float32),
        block(AGG, AW),
    ]
    (
        send_low,
        send_high,
        far,
        inner,
        send_rest,
        fast_rest,
        slow_first,
        slow_rest,
        other_first,
        other_rest,
        wt_fast,
        rest,
        at_halo,
    ) = pl.pallas_call(
        fast_kernel,
        out_shape=outs,
        in_specs=[smem] * 4 + [hbm, hbm, vmem],
        out_specs=[hbm] * len(outs),
        scratch_shapes=[
            pltpu.VMEM((NB + AGG, BS, KP * BS), bf16),
            pltpu.VMEM((COLS, BS, EXT * BS), bf16),
            pltpu.VMEM((NC, 3 * AGG, BS, AW), bf16),
            pltpu.VMEM((LANES, LANES), bf16),
            pltpu.VMEM((KP + 1, BS, LANES), bf16),
            pltpu.VMEM((KA + 1, BS, LANES), bf16),
            pltpu.VMEM((ROWS + REST, BS, 2 * AW), bf16),
            pltpu.VMEM((ROWS + REST, BS, span), bf16),
            pltpu.VMEM((REST, BS, 2 * AW), bf16),
            pltpu.VMEM((ROWS + NC, BS, AW), bf16),
            pltpu.VMEM((ROWS, BS, AW), bf16),
            pltpu.VMEM((WCOLS, BS, 2 * AW), bf16),
            pltpu.VMEM((WSLOT, BS, AW), jnp.float32),
            pltpu.SemaphoreType.DMA(((NB + AGG) // QUAD,)),
            pltpu.SemaphoreType.DMA((len(outs) + 10,)),
        ],
        compiler_params=params(56),
        cost_estimate=cost(20 * 10**9, 30 * 10**6),
        name="fast",
    )(core, inv_own, inv_fast, inv_a, p_blocks, p_fast, a_blocks)

    low = permuted(send_low, inward)
    high = permuted(send_high, inward)
    other_first = permuted(other_first, inward)
    at_halo, rest = pl.pallas_call(
        stage_kernel,
        out_shape=[block(AGG, AW), block(WSLOT, AW, jnp.float32)],
        in_specs=[hbm] * 2,
        out_specs=[vmem] * 2,
        scratch_shapes=[pltpu.SemaphoreType.DMA((2,))],
        compiler_params=params(8),
        cost_estimate=cost(10**6, 10**6),
        name="stage",
    )(at_halo, rest)
    p_slow, low, high, other_first = lax.optimization_barrier((p_slow, low, high, other_first))

    wt_slow = pl.pallas_call(
        slow_kernel,
        out_shape=block(WCOLS, AW),
        in_specs=[smem] * 2 + [vmem] * 3,
        out_specs=vmem,
        scratch_shapes=[
            pltpu.VMEM((LANES, LANES), bf16),
            pltpu.VMEM((KP + 1, BS, LANES), bf16),
            pltpu.VMEM((WSLOT, BS, AW), bf16),
        ],
        compiler_params=params(24),
        cost_estimate=cost(20 * 10**9, 200 * 10**6),
        name="slow",
    )(core, inv_slow, p_slow, at_halo, rest)
    wt_other = permuted(wt_slow, inward)

    wt_slow, low, high = lax.optimization_barrier((wt_slow, low, high))
    wt_slow, send_rest, other_rest = lax.optimization_barrier((wt_slow, send_rest, other_rest))
    mine, far = pl.pallas_call(
        mine_kernel,
        out_shape=[block(FIRST, span, jnp.float32), block(NC, span)],
        in_specs=[vmem] * 6,
        out_specs=[vmem] * 2,
        compiler_params=params(24),
        cost_estimate=cost(10**10, 100 * 10**6),
        name="mine",
    )(slow_first, wt_slow, inner, low, high, far)
    mine, wt_other, send_rest, other_rest = lax.optimization_barrier(
        (mine, wt_other, send_rest, other_rest)
    )
    arrived_rest = permuted(send_rest, inward)
    other_rest = permuted(other_rest, inward)
    relay, direct = pl.pallas_call(
        join_first_kernel,
        out_shape=[block(NC, span)] * 2,
        in_specs=[vmem] * 3,
        out_specs=[vmem] * 2,
        compiler_params=params(16),
        cost_estimate=cost(3 * 10**9, 10**7),
        name="join_first",
    )(other_first, wt_other, mine)
    along_x = [(i, i ^ 2) for i in range(devices)]
    x_sign = [1 if i // 2 % 2 else -1 for i in range(devices)]
    relay = permuted(relay, along_x)
    direct = permuted(direct, [(i, (i + 4 * x_sign[i]) % devices) for i in range(devices)])
    merge, pair, own = pl.pallas_call(
        join_rest_kernel,
        out_shape=[block(NC, span, jnp.float32), block(NC, span), block(NC, span, jnp.float32)],
        in_specs=[vmem] * 7,
        out_specs=[vmem] * 3,
        compiler_params=params(30),
        cost_estimate=cost(40 * 10**9, 200 * 10**6),
        name="join_rest",
    )(fast_rest, slow_rest, other_rest, wt_fast, wt_slow, wt_other, arrived_rest)
    relay, pair, far = lax.optimization_barrier((relay, pair, far))
    relay_in, direct = lax.optimization_barrier((relay, direct))
    merged = pl.pallas_call(
        merge_kernel,
        out_shape=block(NC, MERGED * BS),
        in_specs=[smem, vmem, vmem],
        out_specs=vmem,
        scratch_shapes=[pltpu.VMEM((BS, MERGED * BS), jnp.float32)],
        compiler_params=params(16),
        cost_estimate=cost(10**7, 10**7),
        name="merge",
    )(core, merge, relay_in)
    merged = permuted(merged, [(i, (i - 4 * x_sign[i]) % devices) for i in range(devices)])
    pair = permuted(pair, along_x)
    far = permuted(far, [(i, (i + (5 if i % 2 else -5)) % devices) for i in range(devices)])

    total = block(NC, BAND * BS, jnp.float32)
    frame = pltpu.VMEM((BS, FRAME * BS), jnp.float32)
    early = pl.pallas_call(
        early_kernel,
        out_shape=total,
        in_specs=[smem] + [vmem] * 4,
        out_specs=vmem,
        scratch_shapes=[frame],
        compiler_params=params(16),
        cost_estimate=cost(10**10, 100 * 10**6),
        name="early",
    )(core, own, direct, pair, far)
    return pl.pallas_call(
        total_kernel,
        out_shape=total,
        in_specs=[smem] + [vmem] * 2,
        out_specs=hbm,
        scratch_shapes=[
            frame,
            pltpu.VMEM(total.shape, jnp.float32),
            pltpu.SemaphoreType.DMA((NC,)),
        ],
        compiler_params=params(20),
        cost_estimate=cost(10**7, 10**7),
        name="total",
    )(core, early, merged)


def solution(mesh):
    in_specs = (P("dom", None, None), P("dom", None, None), P("dom", None), P("dom", None))
    out_specs = P("dom", None, None)
    return jax.shard_map(body, mesh=mesh, in_specs=in_specs, out_specs=out_specs, check_vma=False)
```

```python
import functools

import jax
import jax.numpy as jnp
from jax import lax
from jax.experimental import pallas as pl
from jax.experimental.pallas import tpu as pltpu
from jax.sharding import PartitionSpec as P

BS = 64
KA = 7
KP = 27
AGG = 8
H = 15
NC = 3
NB = 24
WIN = 31
WSLOT = 33
BAND = 63

QUAD = 4
LANES = QUAD * BS
EXT = NB + 2 * AGG
COLS = NC + 2 * H + 2
WCOLS = 40
WINDOW = 38
TILES = 10
GROUPS = 5
K = NB * BS
AW = AGG * BS
FRAME = 80
NT = (((1,), (1,)), ((), ()))
ROWS = NC * GROUPS
FIRST = 2 * NC
REST = ROWS - FIRST
MERGED = WINDOW + 6


def eye(n):
    rows = lax.broadcasted_iota(jnp.int32, (n, n), 0)
    lanes = lax.broadcasted_iota(jnp.int32, (n, n), 1)
    return jnp.where(rows == lanes, 1.0, 0.0).astype(jnp.bfloat16)


def low_half():
    return lax.broadcasted_iota(jnp.int32, (BS, 2 * BS), 1) < BS


def places(device):
    return device[0] % 2, device[0] // 2 % 2


def transpose_quad(unit, block, turned, width):
    for start in range(0, width, LANES):
        size = min(LANES, width - start)
        part = lax.dot_general(
            unit[:size, :size],
            block[:, start : start + size],
            NT,
            preferred_element_type=jnp.float32,
        )
        turned[start // BS : (start + size) // BS] = part.astype(jnp.bfloat16).reshape(
            size // BS, BS, LANES
        )


def spread_quad(turned, index, first, store, count, unroll):
    half = low_half()

    def place(slot, carry):
        for pair in range(2):
            lanes = slice(pair * 2 * BS, (pair + 1) * 2 * BS)
            left = turned[index[first + 2 * pair, slot], :, lanes]
            right = turned[index[first + 2 * pair + 1, slot], :, lanes]
            store(slot, pair, jnp.where(half, left, right))
        return carry

    lax.fori_loop(0, count, place, 0, unroll=unroll)


def fast_kernel(
    core,
    inv_own,
    inv_fast,
    inv_a,
    p_own,
    p_fast,
    a_own,
    send_low,
    send_high,
    far,
    inner,
    send_rest,
    fast_rest,
    slow_first,
    slow_rest,
    slow_far,
    other_first,
    other_rest,
    wt,
    rest,
    at_halo,
    p_buf,
    ext,
    at,
    unit,
    turned_p,
    turned_a,
    lhs,
    rows_buf,
    fast_buf,
    slow_buf,
    other_buf,
    wt_buf,
    rest_buf,
    in_sems,
    out_sems,
):
    s, x = places(core)
    own_quads = NB // QUAD
    halo_quads = AGG // QUAD

    def load(quad):
        if quad < own_quads:
            source = p_own.at[quad * QUAD : (quad + 1) * QUAD]
        else:
            source = p_fast.at[(quad - own_quads) * QUAD : (quad - own_quads + 1) * QUAD]
        target = p_buf.at[quad * QUAD : (quad + 1) * QUAD]
        return pltpu.make_async_copy(source, target, in_sems.at[quad])

    for quad in range(own_quads + halo_quads):
        load(quad).start()

    unit[...] = eye(LANES)
    turned_p[KP] = jnp.zeros((BS, LANES), jnp.bfloat16)
    turned_a[KA] = jnp.zeros((BS, LANES), jnp.bfloat16)

    @pl.loop(0, own_quads)
    def _(quad):
        block = a_own[pl.ds(quad * QUAD, QUAD)].reshape(LANES, KA * BS)
        transpose_quad(unit, block, turned_a, KA * BS)
        agg = quad // halo_quads

        def store(slot, pair, value):
            lane = pl.multiple_of((quad % halo_quads) * LANES + pair * 2 * BS, 2 * BS)
            at[agg, slot, :, pl.ds(lane, 2 * BS)] = value

        spread_quad(turned_a, inv_a, quad * QUAD, store, 3 * AGG, 8)

    slow_agg = 2 * s
    halo_copy = pltpu.make_async_copy(at.at[slow_agg, pl.ds(16 * s, AGG)], at_halo, out_sems.at[0])
    halo_copy.start()

    def band_quad(source_row, index, index_row, first_lane):
        block = p_buf[pl.ds(source_row, QUAD)].reshape(LANES, KP * BS)
        transpose_quad(unit, block, turned_p, KP * BS)

        def store(slot, pair, value):
            lane = pl.multiple_of(first_lane + pair * 2 * BS, 2 * BS)
            ext[slot, :, pl.ds(lane, 2 * BS)] = value

        spread_quad(turned_p, index, index_row, store, COLS, 7)

    for quad in range(own_quads + halo_quads):
        load(quad).wait()

    @pl.loop(0, own_quads)
    def _(quad):
        band_quad(quad * QUAD, inv_own, quad * QUAD, AW + quad * LANES)

    @pl.loop(0, halo_quads)
    def _(quad):
        first_lane = (AW + K) * (1 - s) + quad * LANES
        band_quad((own_quads + quad) * QUAD, inv_fast, quad * QUAD, first_lane)

    fast_lanes = pl.ds(pl.multiple_of(AW + (1 - s) * AW, AW), 2 * AW)
    slow_lanes = pl.ds(pl.multiple_of(AW + 2 * s * AW, AW), AW)
    for place, i in enumerate((1 + 2 * x, 4 * x, 4 - 4 * x, 3 - 2 * x, 2)):
        for j in range(NC):
            row = NC * place + j
            mine, other = 6 * i + 3 + j + 1, 6 * i + 6 * (1 - s) + j + 1
            if place < 2:
                lhs[row] = ext[other, :, fast_lanes]
                lhs[FIRST + NC + row] = ext[mine, :, fast_lanes]
            else:
                lhs[ROWS + row - FIRST] = ext[other, :, fast_lanes]
                fast_buf[row - FIRST] = ext[mine, :, fast_lanes]
            slow_buf[row] = ext[mine, :, slow_lanes]
            other_buf[row] = ext[other, :, slow_lanes]
    for j in range(NC):
        lhs[FIRST + j] = ext[30 * s + j + 1, :, fast_lanes]
        slow_buf[ROWS + j] = ext[30 * s + j + 1, :, slow_lanes]
    copies = [halo_copy]

    def write(source, target):
        copy = pltpu.make_async_copy(source, target, out_sems.at[len(copies)])
        copy.start()
        copies.append(copy)

    write(other_buf.at[:FIRST], other_first)
    write(other_buf.at[FIRST:], other_rest)
    write(fast_buf, fast_rest)
    write(slow_buf.at[:FIRST], slow_first)
    write(slow_buf.at[FIRST:ROWS], slow_rest)
    write(slow_buf.at[ROWS:], slow_far)

    wt_buf[0:7] = jnp.zeros((7, BS, 2 * AW), jnp.bfloat16)
    wt_buf[33:] = jnp.zeros((WCOLS - 33, BS, 2 * AW), jnp.bfloat16)
    chunk = WSLOT // 3

    @pl.loop(0, 2)
    def _(place):
        agg = place + 1 - s
        lane = pl.multiple_of(agg * AW, AW)
        target = pl.multiple_of(place * AW, AW)

        @pl.loop(0, 3)
        def _(part):
            first = agg + part * chunk
            left = ext[pl.ds(first, chunk), :, pl.ds(lane, 3 * AW)].reshape(chunk * BS, 3 * AW)
            value = jnp.dot(
                left, at[agg].reshape(3 * AW, AW), preferred_element_type=jnp.float32
            )
            wt_buf[pl.ds(3 * s + first, chunk), :, pl.ds(target, AW)] = value.astype(
                jnp.bfloat16
            ).reshape(chunk, BS, AW)

    write(wt_buf, wt)

    @pl.loop(0, 3)
    def _(part):
        lane = pl.multiple_of(AW + s * AW, AW)
        left = ext[pl.ds(slow_agg + part * chunk, chunk), :, pl.ds(lane, 2 * AW)]
        right = at[slow_agg, pl.ds(AGG - AGG * s, 2 * AGG)].reshape(2 * AW, AW)
        value = jnp.dot(
            left.reshape(chunk * BS, 2 * AW), right, preferred_element_type=jnp.float32
        )
        rest_buf[pl.ds(part * chunk, chunk)] = value.reshape(chunk, BS, AW)

    write(rest_buf, rest)

    def emit(tile, width):
        right = wt_buf[pl.ds(QUAD * tile, width // BS)].reshape(width, 2 * AW)
        left = lhs[...].reshape((ROWS + REST) * BS, 2 * AW)
        value = lax.dot_general(left, right, NT, preferred_element_type=jnp.float32)
        rows_buf[:, :, tile_lanes(tile, width)] = value.astype(jnp.bfloat16).reshape(
            ROWS + REST, BS, width
        )

    parts = (
        (send_low, 0),
        (send_high, NC),
        (far, FIRST),
        (inner, FIRST + NC),
        (send_rest, ROWS),
    )
    bounds = (0, 4, 8, TILES)
    for first, last in zip(bounds[:-1], bounds[1:]):

        @pl.loop(first, min(last, TILES - 1))
        def _(tile):
            emit(tile, LANES)

        if last == TILES:
            emit(TILES - 1, LANES // 2)
        lanes = slice(first * LANES, min(last * LANES, WINDOW * BS))
        for target, row in parts:
            rows = slice(row, row + target.shape[0])
            write(rows_buf.at[rows, :, lanes], target.at[:, :, lanes])
    for copy in copies:
        copy.wait()


def each_tile(step):
    @pl.loop(0, TILES - 1)
    def _(tile):
        step(tile, LANES)

    step(TILES - 1, LANES // 2)


def tile_dot(rows, cols, tile, width):
    left = rows[...].reshape(rows.shape[0] * BS, rows.shape[2])
    right = cols[pl.ds(QUAD * tile, width // BS)].reshape(width, cols.shape[2])
    value = lax.dot_general(left, right, NT, preferred_element_type=jnp.float32)
    return value.reshape(rows.shape[0], BS, width)


def tile_lanes(tile, width):
    return pl.ds(pl.multiple_of(tile * LANES, LANES), width)


def far_kernel(slow, wt_slow, far_fast, far):
    def step(tile, width):
        lanes = tile_lanes(tile, width)
        value = tile_dot(slow, wt_slow, tile, width) + far_fast[:, :, lanes].astype(jnp.float32)
        far[:, :, lanes] = value.astype(jnp.bfloat16)

    each_tile(step)


def mine_kernel(slow, wt_slow, inner, low, high, out):
    def step(tile, width):
        lanes = tile_lanes(tile, width)
        near = tile_dot(slow, wt_slow, tile, width) + inner[:, :, lanes].astype(jnp.float32)
        out[:NC, :, lanes] = near[:NC] + low[:, :, lanes].astype(jnp.float32)
        out[NC:, :, lanes] = near[NC:] + high[:, :, lanes].astype(jnp.float32)

    each_tile(step)


def slow_kernel(core, inv_slow, p_slow, at_halo, rest, wt, unit, turned_p, ext):
    s, x = places(core)
    unit[...] = eye(LANES)
    turned_p[KP] = jnp.zeros((BS, LANES), jnp.bfloat16)

    @pl.loop(0, AGG // QUAD)
    def _(quad):
        block = p_slow[pl.ds(quad * QUAD, QUAD)].reshape(LANES, KP * BS)
        transpose_quad(unit, block, turned_p, KP * BS)

        def store(slot, pair, value):
            lane = pl.multiple_of(quad * LANES + pair * 2 * BS, 2 * BS)
            ext[slot, :, pl.ds(lane, 2 * BS)] = value

        spread_quad(turned_p, inv_slow, quad * QUAD, store, WSLOT, 11)

    wt[0:5] = jnp.zeros((5, BS, AW), jnp.bfloat16)
    wt[WSLOT:] = jnp.zeros((WCOLS - WSLOT, BS, AW), jnp.bfloat16)
    chunk = WSLOT // 3

    @pl.loop(0, 3)
    def _(part):
        rows = pl.ds(part * chunk, chunk)
        value = jnp.dot(
            ext[rows].reshape(chunk * BS, AW),
            at_halo[...].reshape(AW, AW),
            preferred_element_type=jnp.float32,
        )
        value = value.reshape(chunk, BS, AW) + rest[rows]
        wt[pl.ds(5 * s + part * chunk, chunk)] = value.astype(jnp.bfloat16)


def join_first_kernel(other, wt_other, mine, relay, direct):
    def step(tile, width):
        lanes = tile_lanes(tile, width)
        value = tile_dot(other, wt_other, tile, width) + mine[:, :, lanes]
        relay[:, :, lanes] = value[:NC].astype(jnp.bfloat16)
        direct[:, :, lanes] = value[NC:]

    each_tile(step)


def join_rest_kernel(fast, slow, other, wt_fast, wt_slow, wt_other, arrived, merge, pair, own):
    def step(tile, width):
        lanes = tile_lanes(tile, width)
        value = tile_dot(fast, wt_fast, tile, width) + tile_dot(slow, wt_slow, tile, width)
        value = value + tile_dot(other, wt_other, tile, width)
        value = value + arrived[:, :, lanes].astype(jnp.float32)
        merge[:, :, lanes] = value[:NC]
        pair[:, :, lanes] = value[NC : 2 * NC].astype(jnp.bfloat16)
        own[:, :, lanes] = value[2 * NC :]

    each_tile(step)


def stage_kernel(at_halo, rest, at_out, rest_out, sems):
    copies = [
        pltpu.make_async_copy(at_halo, at_out, sems.at[0]),
        pltpu.make_async_copy(rest, rest_out, sems.at[1]),
    ]
    for copy in copies:
        copy.start()
    for copy in copies:
        copy.wait()


def merge_kernel(core, rows, other, out, frame):
    s, x = places(core)
    step = 6 * BS
    for j in range(NC):
        frame[...] = jnp.zeros_like(frame)
        frame[:, pl.ds(pl.multiple_of(step * x, step), WINDOW * BS)] = rows[j]
        lanes = pl.ds(pl.multiple_of(step * (1 - x), step), WINDOW * BS)
        frame[:, lanes] += other[j].astype(jnp.float32)
        out[j] = frame[...].astype(jnp.bfloat16)


def in_frame(s, j, frame, messages, store):
    odd = (j + 1 - s) % 2
    frame[...] = jnp.zeros_like(frame)
    for message, start in messages:
        lane = pl.multiple_of((start - odd + 8) * BS, 2 * BS)
        frame[:, pl.ds(lane, message.shape[2])] += message[j].astype(jnp.float32)
    first, last = 8 * BS, (8 + BAND) * BS

    @pl.when(odd == 0)
    def _():
        store(frame[:, first:last])

    @pl.when(odd == 1)
    def _():
        store(frame[:, first - BS : last - BS])


def early_kernel(core, own, direct, pair, far, out, frame):
    s, x = places(core)
    for j in range(NC):
        top = 27 - 3 * s - j
        far_start = jnp.where(s == 1, 30 - j, -3 - j)
        messages = [(own, top - 12), (direct, top - 30 * x), (pair, top - 6 - 12 * x)]
        messages.append((far, far_start))

        def store(value, j=j):
            out[j] = value

        in_frame(s, j, frame, messages, store)


def total_kernel(core, early, merged, out, frame, buf, sems):
    s, x = places(core)
    copies = []
    for j in range(NC):

        def store(value, j=j):
            buf[j] = value + early[j]

        in_frame(s, j, frame, [(merged, 3 - 3 * s - j + 18 * x)], store)
        copy = pltpu.make_async_copy(buf.at[j], out.at[j], sems.at[j])
        copy.start()
        copies.append(copy)
    for copy in copies:
        copy.wait()


def pick_kernel(core, source, outer, inner, buf, in_sems, out_sems):
    s, x = places(core)
    step = AGG // 4
    reads, writes = [], []
    for side, (target, which) in enumerate(((outer, s), (inner, 1 - s))):
        for k in range(4):
            n = len(reads)
            rows = pl.ds((NB - AGG) * which + k * step, step)
            part = buf.at[side, k * step : (k + 1) * step]
            into = target.at[k * step : (k + 1) * step]
            reads.append(pltpu.make_async_copy(source.at[rows], part, in_sems.at[n]))
            writes.append(pltpu.make_async_copy(part, into, out_sems.at[n]))
    for copy in reads:
        copy.start()
    for read, write in zip(reads, writes):
        read.wait()
        write.start()
    for copy in writes:
        copy.wait()


def permuted(block, pairs):
    return lax.ppermute(block, "dom", pairs)


def inverse_index(offset, slots, empty):
    order = jnp.arange(offset.shape[1], dtype=jnp.int32)[None, :, None]
    hit = offset[:, :, None] == jnp.arange(slots, dtype=jnp.int32)[None, None, :]
    return empty + jnp.sum(jnp.where(hit, order - empty, 0), axis=1)


def body(a_blocks, p_blocks, cols_a, cols_p):
    devices = lax.axis_size("dom")
    device = lax.axis_index("dom")
    count_agg = NC * devices
    count_rows = NB * devices
    first_agg = device * NC
    first_row = device * NB
    core = device.astype(jnp.int32).reshape(1)

    def shifted(distance):
        return [(i, (i + distance) % devices) for i in range(devices)]

    parity = device % 2
    smem = pl.BlockSpec(memory_space=pltpu.SMEM)
    vmem = pl.BlockSpec(memory_space=pltpu.VMEM)
    hbm = pl.BlockSpec(memory_space=pltpu.HBM)
    bf16 = jnp.bfloat16

    def params(mebibytes):
        return pltpu.CompilerParams(vmem_limit_bytes=mebibytes * 1024 * 1024)

    def cost(flops, size):
        return pl.CostEstimate(flops=flops, bytes_accessed=size, transcendentals=0)

    edge = jax.ShapeDtypeStruct((AGG,) + p_blocks.shape[1:], bf16)
    outer, inner = pl.pallas_call(
        pick_kernel,
        out_shape=[edge, edge],
        in_specs=[smem, hbm],
        out_specs=[hbm, hbm],
        scratch_shapes=[
            pltpu.VMEM((2,) + edge.shape, bf16),
            pltpu.SemaphoreType.DMA((8,)),
            pltpu.SemaphoreType.DMA((8,)),
        ],
        compiler_params=params(60),
        name="pick",
    )(core, p_blocks)
    outward = [(i, (i + (1 if i % 2 else -1)) % devices) for i in range(devices)]
    inward = [(i, i ^ 1) for i in range(devices)]
    outer, inner, edge_cols = lax.optimization_barrier((outer, inner, cols_p))
    p_slow = permuted(outer, outward)
    p_fast = permuted(inner, inward)
    edge_cols = jnp.stack([edge_cols[:AGG], edge_cols[NB - AGG :]])
    cols_slow = permuted(edge_cols[parity], outward)
    cols_fast = permuted(edge_cols[1 - parity], inward)

    def slots(cols, agg):
        return (cols - agg + H) % count_agg

    own_agg = jnp.arange(NB, dtype=jnp.int32)[:, None] // AGG
    inv_own = inverse_index(slots(cols_p, first_agg + own_agg) + own_agg + 1, COLS, KP)
    fast_place = NC * (1 - parity) - parity
    inv_fast = inverse_index(slots(cols_fast, first_agg + fast_place) + fast_place + 1, COLS, KP)
    slow_place = NC * parity - (1 - parity)
    inv_slow = inverse_index(slots(cols_slow, first_agg + slow_place) + 2 * parity, WSLOT, KP)
    inv_fast, inv_slow = lax.optimization_barrier((inv_fast, inv_slow))
    inv_a = inverse_index((cols_a - first_row - (own_agg - 1) * AGG) % count_rows, 3 * AGG, KA)

    def block(rows, width, kind=bf16):
        return jax.ShapeDtypeStruct((rows, BS, width), kind)

    span = WINDOW * BS
    outs = [
        block(NC, span),
        block(NC, span),
        block(NC, span),
        block(FIRST, span),
        block(REST, span),
        block(REST, 2 * AW),
        block(FIRST, AW),
        block(REST, AW),
        block(NC, AW),
        block(FIRST, AW),
        block(REST, AW),
        block(WCOLS, 2 * AW),
        block(WSLOT, AW, jnp.float32),
        block(AGG, AW),
    ]
    (
        send_low,
        send_high,
        far,
        inner,
        send_rest,
        fast_rest,
        slow_first,
        slow_rest,
        slow_far,
        other_first,
        other_rest,
        wt_fast,
        rest,
        at_halo,
    ) = pl.pallas_call(
        fast_kernel,
        out_shape=outs,
        in_specs=[smem] * 4 + [hbm, hbm, vmem],
        out_specs=[hbm] * len(outs),
        scratch_shapes=[
            pltpu.VMEM((NB + AGG, BS, KP * BS), bf16),
            pltpu.VMEM((COLS, BS, EXT * BS), bf16),
            pltpu.VMEM((NC, 3 * AGG, BS, AW), bf16),
            pltpu.VMEM((LANES, LANES), bf16),
            pltpu.VMEM((KP + 1, BS, LANES), bf16),
            pltpu.VMEM((KA + 1, BS, LANES), bf16),
            pltpu.VMEM((ROWS + REST, BS, 2 * AW), bf16),
            pltpu.VMEM((ROWS + REST, BS, span), bf16),
            pltpu.VMEM((REST, BS, 2 * AW), bf16),
            pltpu.VMEM((ROWS + NC, BS, AW), bf16),
            pltpu.VMEM((ROWS, BS, AW), bf16),
            pltpu.VMEM((WCOLS, BS, 2 * AW), bf16),
            pltpu.VMEM((WSLOT, BS, AW), jnp.float32),
            pltpu.SemaphoreType.DMA(((NB + AGG) // QUAD,)),
            pltpu.SemaphoreType.DMA((len(outs) + 10,)),
        ],
        compiler_params=params(56),
        cost_estimate=cost(20 * 10**9, 30 * 10**6),
        name="fast",
    )(core, inv_own, inv_fast, inv_a, p_blocks, p_fast, a_blocks)

    low = permuted(send_low, inward)
    high = permuted(send_high, inward)
    other_first = permuted(other_first, inward)
    at_halo, rest = pl.pallas_call(
        stage_kernel,
        out_shape=[block(AGG, AW), block(WSLOT, AW, jnp.float32)],
        in_specs=[hbm] * 2,
        out_specs=[vmem] * 2,
        scratch_shapes=[pltpu.SemaphoreType.DMA((2,))],
        compiler_params=params(8),
        cost_estimate=cost(10**6, 10**6),
        name="stage",
    )(at_halo, rest)
    p_slow, low, high, other_first = lax.optimization_barrier((p_slow, low, high, other_first))

    wt_slow = pl.pallas_call(
        slow_kernel,
        out_shape=block(WCOLS, AW),
        in_specs=[smem] * 2 + [vmem] * 3,
        out_specs=vmem,
        scratch_shapes=[
            pltpu.VMEM((LANES, LANES), bf16),
            pltpu.VMEM((KP + 1, BS, LANES), bf16),
            pltpu.VMEM((WSLOT, BS, AW), bf16),
        ],
        compiler_params=params(24),
        cost_estimate=cost(20 * 10**9, 200 * 10**6),
        name="slow",
    )(core, inv_slow, p_slow, at_halo, rest)
    wt_other = permuted(wt_slow, inward)

    wt_slow, low, high = lax.optimization_barrier((wt_slow, low, high))
    far = pl.pallas_call(
        far_kernel,
        out_shape=block(NC, span),
        in_specs=[vmem] * 3,
        out_specs=vmem,
        compiler_params=params(16),
        cost_estimate=cost(10**9, 10**7),
        name="far",
    )(slow_far, wt_slow, far)
    far, wt_slow = lax.optimization_barrier((far, wt_slow))
    mine = pl.pallas_call(
        mine_kernel,
        out_shape=block(FIRST, span, jnp.float32),
        in_specs=[vmem] * 5,
        out_specs=vmem,
        compiler_params=params(24),
        cost_estimate=cost(10**10, 100 * 10**6),
        name="mine",
    )(slow_first, wt_slow, inner, low, high)
    crossing = [i for i in range(devices) if i % 4 in (1, 2)]
    far_near = permuted(far, [(i, i ^ 3) for i in crossing])
    relay, direct = pl.pallas_call(
        join_first_kernel,
        out_shape=[block(NC, span), block(NC, span, jnp.float32)],
        in_specs=[vmem] * 3,
        out_specs=[vmem] * 2,
        compiler_params=params(16),
        cost_estimate=cost(10**6, 10**5),
        name="join_first",
    )(other_first, wt_other, mine)
    relay, direct, send_rest, other_rest = lax.optimization_barrier(
        (relay, direct, send_rest, other_rest)
    )
    arrived_rest = permuted(send_rest, inward)
    other_rest = permuted(other_rest, inward)
    along_x = [(i, i ^ 2) for i in range(devices)]
    x_sign = [1 if i // 2 % 2 else -1 for i in range(devices)]
    relay = permuted(relay, along_x)

    def merge_rows(rows, other, name):
        return pl.pallas_call(
            merge_kernel,
            out_shape=block(NC, MERGED * BS),
            in_specs=[smem, vmem, vmem],
            out_specs=vmem,
            scratch_shapes=[pltpu.VMEM((BS, MERGED * BS), jnp.float32)],
            compiler_params=params(16),
            cost_estimate=cost(10**7, 10**7),
            name=name,
        )(core, rows, other)

    direct = merge_rows(direct, far_near, "merge_far")
    direct = permuted(direct, [(i, (i + 4 * x_sign[i]) % devices) for i in range(devices)])
    merge, pair, own = pl.pallas_call(
        join_rest_kernel,
        out_shape=[block(NC, span, jnp.float32), block(NC, span), block(NC, span, jnp.float32)],
        in_specs=[vmem] * 7,
        out_specs=[vmem] * 3,
        compiler_params=params(30),
        cost_estimate=cost(40 * 10**9, 200 * 10**6),
        name="join_rest",
    )(fast_rest, slow_rest, other_rest, wt_fast, wt_slow, wt_other, arrived_rest)
    relay, pair, far = lax.optimization_barrier((relay, pair, far))
    relay_in, direct = lax.optimization_barrier((relay, direct))
    merged = merge_rows(merge, relay_in, "merge")
    merged = permuted(merged, [(i, (i - 4 * x_sign[i]) % devices) for i in range(devices)])
    pair = permuted(pair, along_x)
    straight = [i for i in range(devices) if i % 4 in (0, 3)]
    far = permuted(far, [(i, (i + (5 if i % 2 else -5)) % devices) for i in straight])

    total = block(NC, BAND * BS, jnp.float32)
    frame = pltpu.VMEM((BS, FRAME * BS), jnp.float32)
    early = pl.pallas_call(
        early_kernel,
        out_shape=total,
        in_specs=[smem] + [vmem] * 4,
        out_specs=vmem,
        scratch_shapes=[frame],
        compiler_params=params(16),
        cost_estimate=cost(10**10, 100 * 10**6),
        name="early",
    )(core, own, direct, pair, far)
    return pl.pallas_call(
        total_kernel,
        out_shape=total,
        in_specs=[smem] + [vmem] * 2,
        out_specs=hbm,
        scratch_shapes=[
            frame,
            pltpu.VMEM(total.shape, jnp.float32),
            pltpu.SemaphoreType.DMA((NC,)),
        ],
        compiler_params=params(20),
        cost_estimate=cost(10**7, 10**7),
        name="total",
    )(core, early, merged)


def solution(mesh):
    in_specs = (P("dom", None, None), P("dom", None, None), P("dom", None), P("dom", None))
    out_specs = P("dom", None, None)
    return jax.shard_map(body, mesh=mesh, in_specs=in_specs, out_specs=out_specs, check_vma=False)
```

```python
import functools

import jax
import jax.numpy as jnp
from jax import lax
from jax.experimental import pallas as pl
from jax.experimental.pallas import tpu as pltpu
from jax.sharding import PartitionSpec as P

BS = 64
KA = 7
KP = 27
AGG = 8
H = 15
NC = 3
NB = 24
WIN = 31
WSLOT = 33
BAND = 63

QUAD = 4
LANES = QUAD * BS
EXT = NB + 2 * AGG
COLS = NC + 2 * H + 2
WCOLS = 40
WINDOW = 38
TILES = 10
GROUPS = 5
K = NB * BS
AW = AGG * BS
FRAME = 80
NT = (((1,), (1,)), ((), ()))
ROWS = NC * GROUPS
FIRST = 2 * NC
REST = ROWS - FIRST
MERGED = WINDOW + 6


def eye(n):
    rows = lax.broadcasted_iota(jnp.int32, (n, n), 0)
    lanes = lax.broadcasted_iota(jnp.int32, (n, n), 1)
    return jnp.where(rows == lanes, 1.0, 0.0).astype(jnp.bfloat16)


def low_half():
    return lax.broadcasted_iota(jnp.int32, (BS, 2 * BS), 1) < BS


def places(device):
    return device[0] % 2, device[0] // 2 % 2


def transpose_quad(unit, block, turned, width):
    for start in range(0, width, LANES):
        size = min(LANES, width - start)
        part = lax.dot_general(
            unit[:size, :size],
            block[:, start : start + size],
            NT,
            preferred_element_type=jnp.float32,
        )
        turned[start // BS : (start + size) // BS] = part.astype(jnp.bfloat16).reshape(
            size // BS, BS, LANES
        )


def spread_quad(turned, index, first, store, count, unroll):
    half = low_half()

    def place(slot, carry):
        for pair in range(2):
            lanes = slice(pair * 2 * BS, (pair + 1) * 2 * BS)
            left = turned[index[first + 2 * pair, slot], :, lanes]
            right = turned[index[first + 2 * pair + 1, slot], :, lanes]
            store(slot, pair, jnp.where(half, left, right))
        return carry

    lax.fori_loop(0, count, place, 0, unroll=unroll)


def fast_kernel(
    core,
    inv_own,
    inv_fast,
    inv_a,
    p_own,
    p_fast,
    a_own,
    send_low,
    send_high,
    far,
    inner,
    send_rest,
    fast_rest,
    slow_first,
    slow_rest,
    slow_far,
    other_first,
    other_rest,
    wt,
    rest,
    at_halo,
    p_buf,
    ext,
    at,
    unit,
    turned_p,
    turned_a,
    lhs,
    rows_buf,
    fast_buf,
    slow_buf,
    other_buf,
    wt_buf,
    rest_buf,
    in_sems,
    out_sems,
):
    s, x = places(core)
    own_quads = NB // QUAD
    halo_quads = AGG // QUAD

    def load(quad):
        if quad < own_quads:
            source = p_own.at[quad * QUAD : (quad + 1) * QUAD]
        else:
            source = p_fast.at[(quad - own_quads) * QUAD : (quad - own_quads + 1) * QUAD]
        target = p_buf.at[quad * QUAD : (quad + 1) * QUAD]
        return pltpu.make_async_copy(source, target, in_sems.at[quad])

    for quad in range(own_quads + halo_quads):
        load(quad).start()

    unit[...] = eye(LANES)
    turned_p[KP] = jnp.zeros((BS, LANES), jnp.bfloat16)
    turned_a[KA] = jnp.zeros((BS, LANES), jnp.bfloat16)

    @pl.loop(0, own_quads)
    def _(quad):
        block = a_own[pl.ds(quad * QUAD, QUAD)].reshape(LANES, KA * BS)
        transpose_quad(unit, block, turned_a, KA * BS)
        agg = quad // halo_quads

        def store(slot, pair, value):
            lane = pl.multiple_of((quad % halo_quads) * LANES + pair * 2 * BS, 2 * BS)
            at[agg, slot, :, pl.ds(lane, 2 * BS)] = value

        spread_quad(turned_a, inv_a, quad * QUAD, store, 3 * AGG, 8)

    slow_agg = 2 * s
    halo_copy = pltpu.make_async_copy(at.at[slow_agg, pl.ds(16 * s, AGG)], at_halo, out_sems.at[0])
    halo_copy.start()

    def band_quad(source_row, index, index_row, first_lane):
        block = p_buf[pl.ds(source_row, QUAD)].reshape(LANES, KP * BS)
        transpose_quad(unit, block, turned_p, KP * BS)

        def store(slot, pair, value):
            lane = pl.multiple_of(first_lane + pair * 2 * BS, 2 * BS)
            ext[slot, :, pl.ds(lane, 2 * BS)] = value

        spread_quad(turned_p, index, index_row, store, COLS, 7)

    for quad in range(own_quads + halo_quads):
        load(quad).wait()

    @pl.loop(0, own_quads)
    def _(quad):
        band_quad(quad * QUAD, inv_own, quad * QUAD, AW + quad * LANES)

    @pl.loop(0, halo_quads)
    def _(quad):
        first_lane = (AW + K) * (1 - s) + quad * LANES
        band_quad((own_quads + quad) * QUAD, inv_fast, quad * QUAD, first_lane)

    fast_lanes = pl.ds(pl.multiple_of(AW + (1 - s) * AW, AW), 2 * AW)
    slow_lanes = pl.ds(pl.multiple_of(AW + 2 * s * AW, AW), AW)
    for place, i in enumerate((1 + 2 * x, 4 * x, 4 - 4 * x, 3 - 2 * x, 2)):
        for j in range(NC):
            row = NC * place + j
            mine, other = 6 * i + 3 + j + 1, 6 * i + 6 * (1 - s) + j + 1
            if place < 2:
                lhs[row] = ext[other, :, fast_lanes]
                lhs[FIRST + NC + row] = ext[mine, :, fast_lanes]
            else:
                lhs[ROWS + row - FIRST] = ext[other, :, fast_lanes]
                fast_buf[row - FIRST] = ext[mine, :, fast_lanes]
            slow_buf[row] = ext[mine, :, slow_lanes]
            other_buf[row] = ext[other, :, slow_lanes]
    for j in range(NC):
        lhs[FIRST + j] = ext[30 * s + j + 1, :, fast_lanes]
        slow_buf[ROWS + j] = ext[30 * s + j + 1, :, slow_lanes]
    copies = [halo_copy]

    def write(source, target):
        copy = pltpu.make_async_copy(source, target, out_sems.at[len(copies)])
        copy.start()
        copies.append(copy)

    write(other_buf.at[:FIRST], other_first)
    write(other_buf.at[FIRST:], other_rest)
    write(fast_buf, fast_rest)
    write(slow_buf.at[:FIRST], slow_first)
    write(slow_buf.at[FIRST:ROWS], slow_rest)
    write(slow_buf.at[ROWS:], slow_far)

    wt_buf[0:7] = jnp.zeros((7, BS, 2 * AW), jnp.bfloat16)
    wt_buf[33:] = jnp.zeros((WCOLS - 33, BS, 2 * AW), jnp.bfloat16)
    chunk = WSLOT // 3

    @pl.loop(0, 2)
    def _(place):
        agg = place + 1 - s
        lane = pl.multiple_of(agg * AW, AW)
        target = pl.multiple_of(place * AW, AW)

        @pl.loop(0, 3)
        def _(part):
            first = agg + part * chunk
            left = ext[pl.ds(first, chunk), :, pl.ds(lane, 3 * AW)].reshape(chunk * BS, 3 * AW)
            value = jnp.dot(
                left, at[agg].reshape(3 * AW, AW), preferred_element_type=jnp.float32
            )
            wt_buf[pl.ds(3 * s + first, chunk), :, pl.ds(target, AW)] = value.astype(
                jnp.bfloat16
            ).reshape(chunk, BS, AW)

    write(wt_buf, wt)

    @pl.loop(0, 3)
    def _(part):
        lane = pl.multiple_of(AW + s * AW, AW)
        left = ext[pl.ds(slow_agg + part * chunk, chunk), :, pl.ds(lane, 2 * AW)]
        right = at[slow_agg, pl.ds(AGG - AGG * s, 2 * AGG)].reshape(2 * AW, AW)
        value = jnp.dot(
            left.reshape(chunk * BS, 2 * AW), right, preferred_element_type=jnp.float32
        )
        rest_buf[pl.ds(part * chunk, chunk)] = value.reshape(chunk, BS, AW)

    write(rest_buf, rest)

    def emit(tile, width):
        right = wt_buf[pl.ds(QUAD * tile, width // BS)].reshape(width, 2 * AW)
        left = lhs[...].reshape((ROWS + REST) * BS, 2 * AW)
        value = lax.dot_general(left, right, NT, preferred_element_type=jnp.float32)
        rows_buf[:, :, tile_lanes(tile, width)] = value.astype(jnp.bfloat16).reshape(
            ROWS + REST, BS, width
        )

    parts = (
        (send_low, 0),
        (send_high, NC),
        (far, FIRST),
        (inner, FIRST + NC),
        (send_rest, ROWS),
    )
    bounds = (0, 4, 8, TILES)
    for first, last in zip(bounds[:-1], bounds[1:]):

        @pl.loop(first, min(last, TILES - 1))
        def _(tile):
            emit(tile, LANES)

        if last == TILES:
            emit(TILES - 1, LANES // 2)
        lanes = slice(first * LANES, min(last * LANES, WINDOW * BS))
        for target, row in parts:
            rows = slice(row, row + target.shape[0])
            write(rows_buf.at[rows, :, lanes], target.at[:, :, lanes])
    for copy in copies:
        copy.wait()


def each_tile(step):
    @pl.loop(0, TILES - 1)
    def _(tile):
        step(tile, LANES)

    step(TILES - 1, LANES // 2)


def tile_dot(rows, cols, tile, width):
    left = rows[...].reshape(rows.shape[0] * BS, rows.shape[2])
    right = cols[pl.ds(QUAD * tile, width // BS)].reshape(width, cols.shape[2])
    value = lax.dot_general(left, right, NT, preferred_element_type=jnp.float32)
    return value.reshape(rows.shape[0], BS, width)


def tile_lanes(tile, width):
    return pl.ds(pl.multiple_of(tile * LANES, LANES), width)


def far_kernel(slow, wt_slow, far_fast, far):
    def step(tile, width):
        lanes = tile_lanes(tile, width)
        value = tile_dot(slow, wt_slow, tile, width) + far_fast[:, :, lanes].astype(jnp.float32)
        far[:, :, lanes] = value.astype(jnp.bfloat16)

    each_tile(step)


def mine_kernel(slow, wt_slow, inner, low, high, out):
    def step(tile, width):
        lanes = tile_lanes(tile, width)
        near = tile_dot(slow, wt_slow, tile, width) + inner[:, :, lanes].astype(jnp.float32)
        out[:NC, :, lanes] = near[:NC] + low[:, :, lanes].astype(jnp.float32)
        out[NC:, :, lanes] = near[NC:] + high[:, :, lanes].astype(jnp.float32)

    each_tile(step)


def slow_kernel(core, inv_slow, p_slow, at_halo, rest, wt, unit, turned_p, ext):
    s, x = places(core)
    unit[...] = eye(LANES)
    turned_p[KP] = jnp.zeros((BS, LANES), jnp.bfloat16)

    @pl.loop(0, AGG // QUAD)
    def _(quad):
        block = p_slow[pl.ds(quad * QUAD, QUAD)].reshape(LANES, KP * BS)
        transpose_quad(unit, block, turned_p, KP * BS)

        def store(slot, pair, value):
            lane = pl.multiple_of(quad * LANES + pair * 2 * BS, 2 * BS)
            ext[slot, :, pl.ds(lane, 2 * BS)] = value

        spread_quad(turned_p, inv_slow, quad * QUAD, store, WSLOT, 11)

    wt[0:5] = jnp.zeros((5, BS, AW), jnp.bfloat16)
    wt[WSLOT:] = jnp.zeros((WCOLS - WSLOT, BS, AW), jnp.bfloat16)
    chunk = WSLOT // 3

    @pl.loop(0, 3)
    def _(part):
        rows = pl.ds(part * chunk, chunk)
        value = jnp.dot(
            ext[rows].reshape(chunk * BS, AW),
            at_halo[...].reshape(AW, AW),
            preferred_element_type=jnp.float32,
        )
        value = value.reshape(chunk, BS, AW) + rest[rows]
        wt[pl.ds(5 * s + part * chunk, chunk)] = value.astype(jnp.bfloat16)


def join_first_kernel(other, wt_other, mine, relay, direct):
    def step(tile, width):
        lanes = tile_lanes(tile, width)
        value = tile_dot(other, wt_other, tile, width) + mine[:, :, lanes]
        relay[:, :, lanes] = value[:NC].astype(jnp.bfloat16)
        direct[:, :, lanes] = value[NC:]

    each_tile(step)


def join_rest_kernel(fast, slow, other, wt_fast, wt_slow, wt_other, arrived, merge, pair, own):
    def step(tile, width):
        lanes = tile_lanes(tile, width)
        value = tile_dot(fast, wt_fast, tile, width) + tile_dot(slow, wt_slow, tile, width)
        value = value + tile_dot(other, wt_other, tile, width)
        value = value + arrived[:, :, lanes].astype(jnp.float32)
        merge[:, :, lanes] = value[:NC]
        pair[:, :, lanes] = value[NC : 2 * NC].astype(jnp.bfloat16)
        own[:, :, lanes] = value[2 * NC :]

    each_tile(step)


def stage_kernel(at_halo, rest, at_out, rest_out, sems):
    copies = [
        pltpu.make_async_copy(at_halo, at_out, sems.at[0]),
        pltpu.make_async_copy(rest, rest_out, sems.at[1]),
    ]
    for copy in copies:
        copy.start()
    for copy in copies:
        copy.wait()


def merge_kernel(core, rows, other, out, frame):
    s, x = places(core)
    step = 6 * BS
    for j in range(NC):
        frame[...] = jnp.zeros_like(frame)
        frame[:, pl.ds(pl.multiple_of(step * x, step), WINDOW * BS)] = rows[j]
        lanes = pl.ds(pl.multiple_of(step * (1 - x), step), WINDOW * BS)
        frame[:, lanes] += other[j].astype(jnp.float32)
        out[j] = frame[...].astype(jnp.bfloat16)


def in_frame(s, j, frame, messages, store):
    odd = (j + 1 - s) % 2
    frame[...] = jnp.zeros_like(frame)
    for message, start in messages:
        lane = pl.multiple_of((start - odd + 8) * BS, 2 * BS)
        frame[:, pl.ds(lane, message.shape[2])] += message[j].astype(jnp.float32)
    first, last = 8 * BS, (8 + BAND) * BS

    @pl.when(odd == 0)
    def _():
        store(frame[:, first:last])

    @pl.when(odd == 1)
    def _():
        store(frame[:, first - BS : last - BS])


def early_kernel(core, own, direct, pair, far, out, frame):
    s, x = places(core)
    for j in range(NC):
        top = 27 - 3 * s - j
        far_start = jnp.where(s == 1, 30 - j, -3 - j)
        messages = [(own, top - 12), (direct, top - 30 * x), (pair, top - 6 - 12 * x)]
        messages.append((far, far_start))

        def store(value, j=j):
            out[j] = value

        in_frame(s, j, frame, messages, store)


def total_kernel(core, early, merged, out, frame, buf, sems):
    s, x = places(core)
    copies = []
    for j in range(NC):

        def store(value, j=j):
            buf[j] = value + early[j]

        in_frame(s, j, frame, [(merged, 3 - 3 * s - j + 18 * x)], store)
        copy = pltpu.make_async_copy(buf.at[j], out.at[j], sems.at[j])
        copy.start()
        copies.append(copy)
    for copy in copies:
        copy.wait()


def pick_kernel(core, source, outer, inner, buf, in_sems, out_sems):
    s, x = places(core)
    step = AGG // 4
    reads, writes = [], []
    for side, (target, which) in enumerate(((outer, s), (inner, 1 - s))):
        for k in range(4):
            n = len(reads)
            rows = pl.ds((NB - AGG) * which + k * step, step)
            part = buf.at[side, k * step : (k + 1) * step]
            into = target.at[k * step : (k + 1) * step]
            reads.append(pltpu.make_async_copy(source.at[rows], part, in_sems.at[n]))
            writes.append(pltpu.make_async_copy(part, into, out_sems.at[n]))
    for copy in reads:
        copy.start()
    for read, write in zip(reads, writes):
        read.wait()
        write.start()
    for copy in writes:
        copy.wait()


def permuted(block, pairs):
    return lax.ppermute(block, "dom", pairs)


def inverse_index(offset, slots, empty):
    order = jnp.arange(offset.shape[1], dtype=jnp.int32)[None, :, None]
    hit = offset[:, :, None] == jnp.arange(slots, dtype=jnp.int32)[None, None, :]
    return empty + jnp.sum(jnp.where(hit, order - empty, 0), axis=1)


def body(a_blocks, p_blocks, cols_a, cols_p):
    devices = lax.axis_size("dom")
    device = lax.axis_index("dom")
    count_agg = NC * devices
    count_rows = NB * devices
    first_agg = device * NC
    first_row = device * NB
    core = device.astype(jnp.int32).reshape(1)

    def shifted(distance):
        return [(i, (i + distance) % devices) for i in range(devices)]

    parity = device % 2
    smem = pl.BlockSpec(memory_space=pltpu.SMEM)
    vmem = pl.BlockSpec(memory_space=pltpu.VMEM)
    hbm = pl.BlockSpec(memory_space=pltpu.HBM)
    bf16 = jnp.bfloat16

    def params(mebibytes):
        return pltpu.CompilerParams(vmem_limit_bytes=mebibytes * 1024 * 1024)

    def cost(flops, size):
        return pl.CostEstimate(flops=flops, bytes_accessed=size, transcendentals=0)

    edge = jax.ShapeDtypeStruct((AGG,) + p_blocks.shape[1:], bf16)
    outer, inner = pl.pallas_call(
        pick_kernel,
        out_shape=[edge, edge],
        in_specs=[smem, hbm],
        out_specs=[hbm, hbm],
        scratch_shapes=[
            pltpu.VMEM((2,) + edge.shape, bf16),
            pltpu.SemaphoreType.DMA((8,)),
            pltpu.SemaphoreType.DMA((8,)),
        ],
        compiler_params=params(60),
        name="pick",
    )(core, p_blocks)
    outward = [(i, (i + (1 if i % 2 else -1)) % devices) for i in range(devices)]
    inward = [(i, i ^ 1) for i in range(devices)]
    outer, inner, edge_cols = lax.optimization_barrier((outer, inner, cols_p))
    p_slow = permuted(outer, outward)
    p_fast = permuted(inner, inward)
    edge_cols = jnp.stack([edge_cols[:AGG], edge_cols[NB - AGG :]])
    cols_slow = permuted(edge_cols[parity], outward)
    cols_fast = permuted(edge_cols[1 - parity], inward)

    def slots(cols, agg):
        return (cols - agg + H) % count_agg

    own_agg = jnp.arange(NB, dtype=jnp.int32)[:, None] // AGG
    inv_own = inverse_index(slots(cols_p, first_agg + own_agg) + own_agg + 1, COLS, KP)
    fast_place = NC * (1 - parity) - parity
    inv_fast = inverse_index(slots(cols_fast, first_agg + fast_place) + fast_place + 1, COLS, KP)
    slow_place = NC * parity - (1 - parity)
    inv_slow = inverse_index(slots(cols_slow, first_agg + slow_place) + 2 * parity, WSLOT, KP)
    inv_fast, inv_slow = lax.optimization_barrier((inv_fast, inv_slow))
    inv_a = inverse_index((cols_a - first_row - (own_agg - 1) * AGG) % count_rows, 3 * AGG, KA)

    def block(rows, width, kind=bf16):
        return jax.ShapeDtypeStruct((rows, BS, width), kind)

    span = WINDOW * BS
    outs = [
        block(NC, span),
        block(NC, span),
        block(NC, span),
        block(FIRST, span),
        block(REST, span),
        block(REST, 2 * AW),
        block(FIRST, AW),
        block(REST, AW),
        block(NC, AW),
        block(FIRST, AW),
        block(REST, AW),
        block(WCOLS, 2 * AW),
        block(WSLOT, AW, jnp.float32),
        block(AGG, AW),
    ]
    (
        send_low,
        send_high,
        far,
        inner,
        send_rest,
        fast_rest,
        slow_first,
        slow_rest,
        slow_far,
        other_first,
        other_rest,
        wt_fast,
        rest,
        at_halo,
    ) = pl.pallas_call(
        fast_kernel,
        out_shape=outs,
        in_specs=[smem] * 4 + [hbm, hbm, vmem],
        out_specs=[hbm] * len(outs),
        scratch_shapes=[
            pltpu.VMEM((NB + AGG, BS, KP * BS), bf16),
            pltpu.VMEM((COLS, BS, EXT * BS), bf16),
            pltpu.VMEM((NC, 3 * AGG, BS, AW), bf16),
            pltpu.VMEM((LANES, LANES), bf16),
            pltpu.VMEM((KP + 1, BS, LANES), bf16),
            pltpu.VMEM((KA + 1, BS, LANES), bf16),
            pltpu.VMEM((ROWS + REST, BS, 2 * AW), bf16),
            pltpu.VMEM((ROWS + REST, BS, span), bf16),
            pltpu.VMEM((REST, BS, 2 * AW), bf16),
            pltpu.VMEM((ROWS + NC, BS, AW), bf16),
            pltpu.VMEM((ROWS, BS, AW), bf16),
            pltpu.VMEM((WCOLS, BS, 2 * AW), bf16),
            pltpu.VMEM((WSLOT, BS, AW), jnp.float32),
            pltpu.SemaphoreType.DMA(((NB + AGG) // QUAD,)),
            pltpu.SemaphoreType.DMA((len(outs) + 10,)),
        ],
        compiler_params=params(56),
        cost_estimate=cost(20 * 10**9, 30 * 10**6),
        name="fast",
    )(core, inv_own, inv_fast, inv_a, p_blocks, p_fast, a_blocks)

    low = permuted(send_low, inward)
    high = permuted(send_high, inward)
    other_first = permuted(other_first, inward)
    at_halo, rest = pl.pallas_call(
        stage_kernel,
        out_shape=[block(AGG, AW), block(WSLOT, AW, jnp.float32)],
        in_specs=[hbm] * 2,
        out_specs=[vmem] * 2,
        scratch_shapes=[pltpu.SemaphoreType.DMA((2,))],
        compiler_params=params(8),
        cost_estimate=cost(10**6, 10**6),
        name="stage",
    )(at_halo, rest)
    p_slow, low, high, other_first = lax.optimization_barrier((p_slow, low, high, other_first))

    wt_slow = pl.pallas_call(
        slow_kernel,
        out_shape=block(WCOLS, AW),
        in_specs=[smem] * 2 + [vmem] * 3,
        out_specs=vmem,
        scratch_shapes=[
            pltpu.VMEM((LANES, LANES), bf16),
            pltpu.VMEM((KP + 1, BS, LANES), bf16),
            pltpu.VMEM((WSLOT, BS, AW), bf16),
        ],
        compiler_params=params(24),
        cost_estimate=cost(20 * 10**9, 200 * 10**6),
        name="slow",
    )(core, inv_slow, p_slow, at_halo, rest)
    wt_other = permuted(wt_slow, inward)

    wt_slow, low, high = lax.optimization_barrier((wt_slow, low, high))
    far = pl.pallas_call(
        far_kernel,
        out_shape=block(NC, span),
        in_specs=[vmem] * 3,
        out_specs=vmem,
        compiler_params=params(16),
        cost_estimate=cost(10**9, 10**7),
        name="far",
    )(slow_far, wt_slow, far)
    far, wt_slow = lax.optimization_barrier((far, wt_slow))
    mine = pl.pallas_call(
        mine_kernel,
        out_shape=block(FIRST, span, jnp.float32),
        in_specs=[vmem] * 5,
        out_specs=vmem,
        compiler_params=params(24),
        cost_estimate=cost(10**10, 100 * 10**6),
        name="mine",
    )(slow_first, wt_slow, inner, low, high)
    crossing = [i for i in range(devices) if i % 4 in (1, 2)]
    far_near = permuted(far, [(i, i ^ 3) for i in crossing])
    relay, direct = pl.pallas_call(
        join_first_kernel,
        out_shape=[block(NC, span), block(NC, span, jnp.float32)],
        in_specs=[vmem] * 3,
        out_specs=[vmem] * 2,
        compiler_params=params(16),
        cost_estimate=cost(10**6, 10**5),
        name="join_first",
    )(other_first, wt_other, mine)
    relay, direct, far_near, send_rest, other_rest = lax.optimization_barrier(
        (relay, direct, far_near, send_rest, other_rest)
    )
    arrived_rest = permuted(send_rest, inward)
    other_rest = permuted(other_rest, inward)
    along_x = [(i, i ^ 2) for i in range(devices)]
    x_sign = [1 if i // 2 % 2 else -1 for i in range(devices)]
    relay = permuted(relay, along_x)

    def merge_rows(rows, other, name):
        return pl.pallas_call(
            merge_kernel,
            out_shape=block(NC, MERGED * BS),
            in_specs=[smem, vmem, vmem],
            out_specs=vmem,
            scratch_shapes=[pltpu.VMEM((BS, MERGED * BS), jnp.float32)],
            compiler_params=params(16),
            cost_estimate=cost(10**7, 10**7),
            name=name,
        )(core, rows, other)

    direct = merge_rows(direct, far_near, "merge_far")
    direct = permuted(direct, [(i, (i + 4 * x_sign[i]) % devices) for i in range(devices)])
    merge, pair, own = pl.pallas_call(
        join_rest_kernel,
        out_shape=[block(NC, span, jnp.float32), block(NC, span), block(NC, span, jnp.float32)],
        in_specs=[vmem] * 7,
        out_specs=[vmem] * 3,
        compiler_params=params(30),
        cost_estimate=cost(40 * 10**9, 200 * 10**6),
        name="join_rest",
    )(fast_rest, slow_rest, other_rest, wt_fast, wt_slow, wt_other, arrived_rest)
    relay, pair, far = lax.optimization_barrier((relay, pair, far))
    relay_in, direct = lax.optimization_barrier((relay, direct))
    merged = merge_rows(merge, relay_in, "merge")
    merged = permuted(merged, [(i, (i - 4 * x_sign[i]) % devices) for i in range(devices)])
    pair = permuted(pair, along_x)
    straight = [i for i in range(devices) if i % 4 in (0, 3)]
    far = permuted(far, [(i, (i + (5 if i % 2 else -5)) % devices) for i in straight])

    total = block(NC, BAND * BS, jnp.float32)
    frame = pltpu.VMEM((BS, FRAME * BS), jnp.float32)
    early = pl.pallas_call(
        early_kernel,
        out_shape=total,
        in_specs=[smem] + [vmem] * 4,
        out_specs=vmem,
        scratch_shapes=[frame],
        compiler_params=params(16),
        cost_estimate=cost(10**10, 100 * 10**6),
        name="early",
    )(core, own, direct, pair, far)
    return pl.pallas_call(
        total_kernel,
        out_shape=total,
        in_specs=[smem] + [vmem] * 2,
        out_specs=hbm,
        scratch_shapes=[
            frame,
            pltpu.VMEM(total.shape, jnp.float32),
            pltpu.SemaphoreType.DMA((NC,)),
        ],
        compiler_params=params(20),
        cost_estimate=cost(10**7, 10**7),
        name="total",
    )(core, early, merged)


def solution(mesh):
    in_specs = (P("dom", None, None), P("dom", None, None), P("dom", None), P("dom", None))
    out_specs = P("dom", None, None)
    return jax.shard_map(body, mesh=mesh, in_specs=in_specs, out_specs=out_specs, check_vma=False)
```

```python
import functools

import jax
import jax.numpy as jnp
from jax import lax
from jax.experimental import pallas as pl
from jax.experimental.pallas import tpu as pltpu
from jax.sharding import PartitionSpec as P

BS = 64
KA = 7
KP = 27
AGG = 8
H = 15
NC = 3
NB = 24
WIN = 31
WSLOT = 33
BAND = 63

QUAD = 4
LANES = QUAD * BS
EXT = NB + 2 * AGG
COLS = NC + 2 * H + 2
WCOLS = 40
WINDOW = 38
TILES = 10
GROUPS = 5
K = NB * BS
AW = AGG * BS
FRAME = 80
NT = (((1,), (1,)), ((), ()))
ROWS = NC * GROUPS
FIRST = 2 * NC
REST = ROWS - FIRST
MERGED = WINDOW + 6


def eye(n):
    rows = lax.broadcasted_iota(jnp.int32, (n, n), 0)
    lanes = lax.broadcasted_iota(jnp.int32, (n, n), 1)
    return jnp.where(rows == lanes, 1.0, 0.0).astype(jnp.bfloat16)


def low_half():
    return lax.broadcasted_iota(jnp.int32, (BS, 2 * BS), 1) < BS


def places(device):
    return device[0] % 2, device[0] // 2 % 2


def transpose_quad(unit, block, turned, width):
    for start in range(0, width, LANES):
        size = min(LANES, width - start)
        part = lax.dot_general(
            unit[:size, :size],
            block[:, start : start + size],
            NT,
            preferred_element_type=jnp.float32,
        )
        turned[start // BS : (start + size) // BS] = part.astype(jnp.bfloat16).reshape(
            size // BS, BS, LANES
        )


def spread_quad(turned, index, first, store, count, unroll):
    half = low_half()

    def place(slot, carry):
        for pair in range(2):
            lanes = slice(pair * 2 * BS, (pair + 1) * 2 * BS)
            left = turned[index[first + 2 * pair, slot], :, lanes]
            right = turned[index[first + 2 * pair + 1, slot], :, lanes]
            store(slot, pair, jnp.where(half, left, right))
        return carry

    lax.fori_loop(0, count, place, 0, unroll=unroll)


def fast_kernel(
    core,
    inv_own,
    inv_fast,
    inv_a,
    p_own,
    p_fast,
    a_own,
    send_low,
    send_high,
    far,
    inner,
    send_rest,
    fast_rest,
    slow_first,
    slow_rest,
    slow_far,
    other_first,
    other_rest,
    wt,
    rest_0,
    rest_1,
    rest_2,
    at_halo,
    ext,
    at,
    unit,
    turned_p,
    turned_a,
    lhs,
    fast_buf,
    slow_buf,
    other_buf,
    wt_buf,
    in_sems,
    out_sems,
):
    s, x = places(core)
    own_quads = NB // QUAD
    halo_quads = AGG // QUAD

    def band_phase(p_buf):
        def load(quad):
            if quad < own_quads:
                source = p_own.at[quad * QUAD : (quad + 1) * QUAD]
            else:
                source = p_fast.at[(quad - own_quads) * QUAD : (quad - own_quads + 1) * QUAD]
            target = p_buf.at[quad * QUAD : (quad + 1) * QUAD]
            return pltpu.make_async_copy(source, target, in_sems.at[quad])

        for quad in range(own_quads + halo_quads):
            load(quad).start()

        unit[...] = eye(LANES)
        turned_p[KP] = jnp.zeros((BS, LANES), jnp.bfloat16)
        turned_a[KA] = jnp.zeros((BS, LANES), jnp.bfloat16)

        @pl.loop(0, own_quads)
        def _(quad):
            block = a_own[pl.ds(quad * QUAD, QUAD)].reshape(LANES, KA * BS)
            transpose_quad(unit, block, turned_a, KA * BS)
            agg = quad // halo_quads

            def store(slot, pair, value):
                lane = pl.multiple_of((quad % halo_quads) * LANES + pair * 2 * BS, 2 * BS)
                at[agg, slot, :, pl.ds(lane, 2 * BS)] = value

            spread_quad(turned_a, inv_a, quad * QUAD, store, 3 * AGG, 8)

        def band_quad(source_row, index, index_row, first_lane):
            block = p_buf[pl.ds(source_row, QUAD)].reshape(LANES, KP * BS)
            transpose_quad(unit, block, turned_p, KP * BS)

            def store(slot, pair, value):
                lane = pl.multiple_of(first_lane + pair * 2 * BS, 2 * BS)
                ext[slot, :, pl.ds(lane, 2 * BS)] = value

            spread_quad(turned_p, index, index_row, store, COLS, 7)

        for quad in range(own_quads + halo_quads):
            load(quad).wait()

        @pl.loop(0, own_quads)
        def _(quad):
            band_quad(quad * QUAD, inv_own, quad * QUAD, AW + quad * LANES)

        @pl.loop(0, halo_quads)
        def _(quad):
            first_lane = (AW + K) * (1 - s) + quad * LANES
            band_quad((own_quads + quad) * QUAD, inv_fast, quad * QUAD, first_lane)

    pl.run_scoped(band_phase, pltpu.VMEM((NB + AGG, BS, KP * BS), jnp.bfloat16))
    slow_agg = 2 * s
    at_halo[...] = at[slow_agg, pl.ds(16 * s, AGG)]
    fast_lanes = pl.ds(pl.multiple_of(AW + (1 - s) * AW, AW), 2 * AW)
    slow_lanes = pl.ds(pl.multiple_of(AW + 2 * s * AW, AW), AW)
    for place, i in enumerate((1 + 2 * x, 4 * x, 4 - 4 * x, 3 - 2 * x, 2)):
        for j in range(NC):
            row = NC * place + j
            mine, other = 6 * i + 3 + j + 1, 6 * i + 6 * (1 - s) + j + 1
            if place < 2:
                lhs[row] = ext[other, :, fast_lanes]
                lhs[FIRST + NC + row] = ext[mine, :, fast_lanes]
            else:
                lhs[ROWS + row - FIRST] = ext[other, :, fast_lanes]
                fast_buf[row - FIRST] = ext[mine, :, fast_lanes]
            slow_buf[row] = ext[mine, :, slow_lanes]
            other_buf[row] = ext[other, :, slow_lanes]
    for j in range(NC):
        lhs[FIRST + j] = ext[30 * s + j + 1, :, fast_lanes]
        slow_buf[ROWS + j] = ext[30 * s + j + 1, :, slow_lanes]
    copies = []

    def write(source, target):
        copy = pltpu.make_async_copy(source, target, out_sems.at[len(copies)])
        copy.start()
        copies.append(copy)

    write(other_buf.at[:FIRST], other_first)
    write(other_buf.at[FIRST:], other_rest)
    write(fast_buf, fast_rest)
    write(slow_buf.at[:FIRST], slow_first)
    write(slow_buf.at[FIRST:ROWS], slow_rest)
    write(slow_buf.at[ROWS:], slow_far)

    wt_buf[0:7] = jnp.zeros((7, BS, 2 * AW), jnp.bfloat16)
    wt_buf[33:] = jnp.zeros((WCOLS - 33, BS, 2 * AW), jnp.bfloat16)
    chunk = WSLOT // 3

    @pl.loop(0, 2)
    def _(place):
        agg = place + 1 - s
        lane = pl.multiple_of(agg * AW, AW)
        target = pl.multiple_of(place * AW, AW)

        @pl.loop(0, 3)
        def _(part):
            first = agg + part * chunk
            left = ext[pl.ds(first, chunk), :, pl.ds(lane, 3 * AW)].reshape(chunk * BS, 3 * AW)
            value = jnp.dot(
                left, at[agg].reshape(3 * AW, AW), preferred_element_type=jnp.float32
            )
            wt_buf[pl.ds(3 * s + first, chunk), :, pl.ds(target, AW)] = value.astype(
                jnp.bfloat16
            ).reshape(chunk, BS, AW)

    write(wt_buf, wt)

    for part, rest in enumerate((rest_0, rest_1, rest_2)):
        lane = pl.multiple_of(AW + s * AW, AW)
        left = ext[pl.ds(slow_agg + part * chunk, chunk), :, pl.ds(lane, 2 * AW)]
        right = at[slow_agg, pl.ds(AGG - AGG * s, 2 * AGG)].reshape(2 * AW, AW)
        value = jnp.dot(
            left.reshape(chunk * BS, 2 * AW), right, preferred_element_type=jnp.float32
        )
        rest[...] = value.reshape(chunk, BS, AW)

    def send_phase(rows_buf):
        def emit(tile, width):
            right = wt_buf[pl.ds(QUAD * tile, width // BS)].reshape(width, 2 * AW)
            left = lhs[...].reshape((ROWS + REST) * BS, 2 * AW)
            value = lax.dot_general(left, right, NT, preferred_element_type=jnp.float32)
            rows_buf[:, :, tile_lanes(tile, width)] = value.astype(jnp.bfloat16).reshape(
                ROWS + REST, BS, width
            )

        parts = (
            (send_low, 0),
            (send_high, NC),
            (far, FIRST),
            (inner, FIRST + NC),
            (send_rest, ROWS),
        )
        bounds = (0, 4, 8, TILES)
        for first, last in zip(bounds[:-1], bounds[1:]):

            @pl.loop(first, min(last, TILES - 1))
            def _(tile):
                emit(tile, LANES)

            if last == TILES:
                emit(TILES - 1, LANES // 2)
            lanes = slice(first * LANES, min(last * LANES, WINDOW * BS))
            for target, row in parts:
                rows = slice(row, row + target.shape[0])
                write(rows_buf.at[rows, :, lanes], target.at[:, :, lanes])
        for copy in copies:
            copy.wait()

    pl.run_scoped(send_phase, pltpu.VMEM((ROWS + REST, BS, WINDOW * BS), jnp.bfloat16))


def each_tile(step):
    @pl.loop(0, TILES - 1)
    def _(tile):
        step(tile, LANES)

    step(TILES - 1, LANES // 2)


def tile_dot(rows, cols, tile, width):
    left = rows[...].reshape(rows.shape[0] * BS, rows.shape[2])
    right = cols[pl.ds(QUAD * tile, width // BS)].reshape(width, cols.shape[2])
    value = lax.dot_general(left, right, NT, preferred_element_type=jnp.float32)
    return value.reshape(rows.shape[0], BS, width)


def tile_lanes(tile, width):
    return pl.ds(pl.multiple_of(tile * LANES, LANES), width)


def far_kernel(slow, wt_slow, far_fast, far):
    def step(tile, width):
        lanes = tile_lanes(tile, width)
        value = tile_dot(slow, wt_slow, tile, width) + far_fast[:, :, lanes].astype(jnp.float32)
        far[:, :, lanes] = value.astype(jnp.bfloat16)

    each_tile(step)


def mine_kernel(slow, wt_slow, inner, low, high, out):
    def step(tile, width):
        lanes = tile_lanes(tile, width)
        near = tile_dot(slow, wt_slow, tile, width) + inner[:, :, lanes].astype(jnp.float32)
        out[:NC, :, lanes] = near[:NC] + low[:, :, lanes].astype(jnp.float32)
        out[NC:, :, lanes] = near[NC:] + high[:, :, lanes].astype(jnp.float32)

    each_tile(step)


def slow_kernel(core, inv_slow, p_slow, at_halo, rest_0, rest_1, rest_2, wt, unit, turned_p, ext):
    s, x = places(core)
    unit[...] = eye(LANES)
    turned_p[KP] = jnp.zeros((BS, LANES), jnp.bfloat16)

    @pl.loop(0, AGG // QUAD)
    def _(quad):
        block = p_slow[pl.ds(quad * QUAD, QUAD)].reshape(LANES, KP * BS)
        transpose_quad(unit, block, turned_p, KP * BS)

        def store(slot, pair, value):
            lane = pl.multiple_of(quad * LANES + pair * 2 * BS, 2 * BS)
            ext[slot, :, pl.ds(lane, 2 * BS)] = value

        spread_quad(turned_p, inv_slow, quad * QUAD, store, WSLOT, 11)

    wt[0:5] = jnp.zeros((5, BS, AW), jnp.bfloat16)
    wt[WSLOT:] = jnp.zeros((WCOLS - WSLOT, BS, AW), jnp.bfloat16)
    chunk = WSLOT // 3

    for part, rest in enumerate((rest_0, rest_1, rest_2)):
        value = jnp.dot(
            ext[part * chunk : (part + 1) * chunk].reshape(chunk * BS, AW),
            at_halo[...].reshape(AW, AW),
            preferred_element_type=jnp.float32,
        )
        value = value.reshape(chunk, BS, AW) + rest[...]
        wt[pl.ds(5 * s + part * chunk, chunk)] = value.astype(jnp.bfloat16)


def join_first_kernel(other, wt_other, mine, relay, direct):
    def step(tile, width):
        lanes = tile_lanes(tile, width)
        value = tile_dot(other, wt_other, tile, width) + mine[:, :, lanes]
        relay[:, :, lanes] = value[:NC].astype(jnp.bfloat16)
        direct[:, :, lanes] = value[NC:]

    each_tile(step)


def join_rest_kernel(fast, slow, other, wt_fast, wt_slow, wt_other, arrived, merge, pair, own):
    def step(tile, width):
        lanes = tile_lanes(tile, width)
        value = tile_dot(fast, wt_fast, tile, width) + tile_dot(slow, wt_slow, tile, width)
        value = value + tile_dot(other, wt_other, tile, width)
        value = value + arrived[:, :, lanes].astype(jnp.float32)
        merge[:, :, lanes] = value[:NC]
        pair[:, :, lanes] = value[NC : 2 * NC].astype(jnp.bfloat16)
        own[:, :, lanes] = value[2 * NC :]

    each_tile(step)


def merge_kernel(core, rows, other, out, frame):
    s, x = places(core)
    step = 6 * BS
    for j in range(NC):
        frame[...] = jnp.zeros_like(frame)
        frame[:, pl.ds(pl.multiple_of(step * x, step), WINDOW * BS)] = rows[j]
        lanes = pl.ds(pl.multiple_of(step * (1 - x), step), WINDOW * BS)
        frame[:, lanes] += other[j].astype(jnp.float32)
        out[j] = frame[...].astype(jnp.bfloat16)


def in_frame(s, j, frame, messages, store):
    odd = (j + 1 - s) % 2
    frame[...] = jnp.zeros_like(frame)
    for message, start in messages:
        lane = pl.multiple_of((start - odd + 8) * BS, 2 * BS)
        frame[:, pl.ds(lane, message.shape[2])] += message[j].astype(jnp.float32)
    first, last = 8 * BS, (8 + BAND) * BS

    @pl.when(odd == 0)
    def _():
        store(frame[:, first:last])

    @pl.when(odd == 1)
    def _():
        store(frame[:, first - BS : last - BS])


def early_kernel(core, own, direct, pair, far, out, frame):
    s, x = places(core)
    for j in range(NC):
        top = 27 - 3 * s - j
        far_start = jnp.where(s == 1, 30 - j, -3 - j)
        messages = [(own, top - 12), (direct, top - 30 * x), (pair, top - 6 - 12 * x)]
        messages.append((far, far_start))

        def store(value, j=j):
            out[j] = value

        in_frame(s, j, frame, messages, store)


def total_kernel(core, early, merged, out, frame, buf, sems):
    s, x = places(core)
    copies = []
    for j in range(NC):

        def store(value, j=j):
            buf[j] = value + early[j]

        in_frame(s, j, frame, [(merged, 3 - 3 * s - j + 18 * x)], store)
        copy = pltpu.make_async_copy(buf.at[j], out.at[j], sems.at[j])
        copy.start()
        copies.append(copy)
    for copy in copies:
        copy.wait()


def pick_kernel(core, source, outer, inner, buf, in_sems, out_sems):
    s, x = places(core)
    step = AGG // 4
    reads, writes = [], []
    for side, (target, which) in enumerate(((outer, s), (inner, 1 - s))):
        for k in range(4):
            n = len(reads)
            rows = pl.ds((NB - AGG) * which + k * step, step)
            part = buf.at[side, k * step : (k + 1) * step]
            into = target.at[k * step : (k + 1) * step]
            reads.append(pltpu.make_async_copy(source.at[rows], part, in_sems.at[n]))
            writes.append(pltpu.make_async_copy(part, into, out_sems.at[n]))
    for copy in reads:
        copy.start()
    for read, write in zip(reads, writes):
        read.wait()
        write.start()
    for copy in writes:
        copy.wait()


def permuted(block, pairs):
    return lax.ppermute(block, "dom", pairs)


def inverse_index(offset, slots, empty):
    order = jnp.arange(offset.shape[1], dtype=jnp.int32)[None, :, None]
    hit = offset[:, :, None] == jnp.arange(slots, dtype=jnp.int32)[None, None, :]
    return empty + jnp.sum(jnp.where(hit, order - empty, 0), axis=1)


def body(a_blocks, p_blocks, cols_a, cols_p):
    devices = lax.axis_size("dom")
    device = lax.axis_index("dom")
    count_agg = NC * devices
    count_rows = NB * devices
    first_agg = device * NC
    first_row = device * NB
    core = device.astype(jnp.int32).reshape(1)

    def shifted(distance):
        return [(i, (i + distance) % devices) for i in range(devices)]

    parity = device % 2
    smem = pl.BlockSpec(memory_space=pltpu.SMEM)
    vmem = pl.BlockSpec(memory_space=pltpu.VMEM)
    hbm = pl.BlockSpec(memory_space=pltpu.HBM)
    bf16 = jnp.bfloat16

    def params(mebibytes):
        return pltpu.CompilerParams(vmem_limit_bytes=mebibytes * 1024 * 1024)

    def cost(flops, size):
        return pl.CostEstimate(flops=flops, bytes_accessed=size, transcendentals=0)

    edge = jax.ShapeDtypeStruct((AGG,) + p_blocks.shape[1:], bf16)
    outer, inner = pl.pallas_call(
        pick_kernel,
        out_shape=[edge, edge],
        in_specs=[smem, hbm],
        out_specs=[hbm, hbm],
        scratch_shapes=[
            pltpu.VMEM((2,) + edge.shape, bf16),
            pltpu.SemaphoreType.DMA((8,)),
            pltpu.SemaphoreType.DMA((8,)),
        ],
        compiler_params=params(60),
        name="pick",
    )(core, p_blocks)
    outward = [(i, (i + (1 if i % 2 else -1)) % devices) for i in range(devices)]
    inward = [(i, i ^ 1) for i in range(devices)]
    outer, inner, edge_cols = lax.optimization_barrier((outer, inner, cols_p))
    p_slow = permuted(outer, outward)
    p_fast = permuted(inner, inward)
    edge_cols = jnp.stack([edge_cols[:AGG], edge_cols[NB - AGG :]])
    cols_slow = permuted(edge_cols[parity], outward)
    cols_fast = permuted(edge_cols[1 - parity], inward)

    def slots(cols, agg):
        return (cols - agg + H) % count_agg

    own_agg = jnp.arange(NB, dtype=jnp.int32)[:, None] // AGG
    inv_own = inverse_index(slots(cols_p, first_agg + own_agg) + own_agg + 1, COLS, KP)
    fast_place = NC * (1 - parity) - parity
    inv_fast = inverse_index(slots(cols_fast, first_agg + fast_place) + fast_place + 1, COLS, KP)
    slow_place = NC * parity - (1 - parity)
    inv_slow = inverse_index(slots(cols_slow, first_agg + slow_place) + 2 * parity, WSLOT, KP)
    inv_fast, inv_slow = lax.optimization_barrier((inv_fast, inv_slow))
    inv_a = inverse_index((cols_a - first_row - (own_agg - 1) * AGG) % count_rows, 3 * AGG, KA)

    def block(rows, width, kind=bf16):
        return jax.ShapeDtypeStruct((rows, BS, width), kind)

    span = WINDOW * BS
    outs = [
        block(NC, span),
        block(NC, span),
        block(NC, span),
        block(FIRST, span),
        block(REST, span),
        block(REST, 2 * AW),
        block(FIRST, AW),
        block(REST, AW),
        block(NC, AW),
        block(FIRST, AW),
        block(REST, AW),
        block(WCOLS, 2 * AW),
    ]
    outs += [block(WSLOT // 3, AW, jnp.float32)] * 3 + [block(AGG, AW)]
    (
        send_low,
        send_high,
        far,
        inner,
        send_rest,
        fast_rest,
        slow_first,
        slow_rest,
        slow_far,
        other_first,
        other_rest,
        wt_fast,
        *rest,
        at_halo,
    ) = pl.pallas_call(
        fast_kernel,
        out_shape=outs,
        in_specs=[smem] * 4 + [hbm, hbm, vmem],
        out_specs=[hbm] * (len(outs) - 4) + [vmem] * 4,
        scratch_shapes=[
            pltpu.VMEM((COLS, BS, EXT * BS), bf16),
            pltpu.VMEM((NC, 3 * AGG, BS, AW), bf16),
            pltpu.VMEM((LANES, LANES), bf16),
            pltpu.VMEM((KP + 1, BS, LANES), bf16),
            pltpu.VMEM((KA + 1, BS, LANES), bf16),
            pltpu.VMEM((ROWS + REST, BS, 2 * AW), bf16),
            pltpu.VMEM((REST, BS, 2 * AW), bf16),
            pltpu.VMEM((ROWS + NC, BS, AW), bf16),
            pltpu.VMEM((ROWS, BS, AW), bf16),
            pltpu.VMEM((WCOLS, BS, 2 * AW), bf16),
            pltpu.SemaphoreType.DMA(((NB + AGG) // QUAD,)),
            pltpu.SemaphoreType.DMA((len(outs) + 10,)),
        ],
        compiler_params=params(44),
        cost_estimate=cost(20 * 10**9, 30 * 10**6),
        name="fast",
    )(core, inv_own, inv_fast, inv_a, p_blocks, p_fast, a_blocks)

    low = permuted(send_low, inward)
    high = permuted(send_high, inward)
    other_first = permuted(other_first, inward)
    p_slow, low, high, other_first = lax.optimization_barrier((p_slow, low, high, other_first))

    wt_slow = pl.pallas_call(
        slow_kernel,
        out_shape=block(WCOLS, AW),
        in_specs=[smem] * 2 + [vmem] * 5,
        out_specs=vmem,
        scratch_shapes=[
            pltpu.VMEM((LANES, LANES), bf16),
            pltpu.VMEM((KP + 1, BS, LANES), bf16),
            pltpu.VMEM((WSLOT, BS, AW), bf16),
        ],
        compiler_params=params(24),
        cost_estimate=cost(20 * 10**9, 200 * 10**6),
        name="slow",
    )(core, inv_slow, p_slow, at_halo, *rest)
    wt_other = permuted(wt_slow, inward)

    wt_slow, low, high = lax.optimization_barrier((wt_slow, low, high))
    far = pl.pallas_call(
        far_kernel,
        out_shape=block(NC, span),
        in_specs=[vmem] * 3,
        out_specs=vmem,
        compiler_params=params(16),
        cost_estimate=cost(10**9, 10**7),
        name="far",
    )(slow_far, wt_slow, far)
    far, wt_slow = lax.optimization_barrier((far, wt_slow))
    mine = pl.pallas_call(
        mine_kernel,
        out_shape=block(FIRST, span, jnp.float32),
        in_specs=[vmem] * 5,
        out_specs=vmem,
        compiler_params=params(24),
        cost_estimate=cost(10**10, 100 * 10**6),
        name="mine",
    )(slow_first, wt_slow, inner, low, high)
    crossing = [i for i in range(devices) if i % 4 in (1, 2)]
    far_near = permuted(far, [(i, i ^ 3) for i in crossing])
    relay, direct = pl.pallas_call(
        join_first_kernel,
        out_shape=[block(NC, span), block(NC, span, jnp.float32)],
        in_specs=[vmem] * 3,
        out_specs=[vmem] * 2,
        compiler_params=params(16),
        cost_estimate=cost(10**6, 10**5),
        name="join_first",
    )(other_first, wt_other, mine)
    relay, direct, far_near, send_rest, other_rest = lax.optimization_barrier(
        (relay, direct, far_near, send_rest, other_rest)
    )
    arrived_rest = permuted(send_rest, inward)
    other_rest = permuted(other_rest, inward)
    along_x = [(i, i ^ 2) for i in range(devices)]
    x_sign = [1 if i // 2 % 2 else -1 for i in range(devices)]
    relay = permuted(relay, along_x)

    def merge_rows(rows, other, name):
        return pl.pallas_call(
            merge_kernel,
            out_shape=block(NC, MERGED * BS),
            in_specs=[smem, vmem, vmem],
            out_specs=vmem,
            scratch_shapes=[pltpu.VMEM((BS, MERGED * BS), jnp.float32)],
            compiler_params=params(16),
            cost_estimate=cost(10**7, 10**7),
            name=name,
        )(core, rows, other)

    direct = merge_rows(direct, far_near, "merge_far")
    direct = permuted(direct, [(i, (i + 4 * x_sign[i]) % devices) for i in range(devices)])
    merge, pair, own = pl.pallas_call(
        join_rest_kernel,
        out_shape=[block(NC, span, jnp.float32), block(NC, span), block(NC, span, jnp.float32)],
        in_specs=[vmem] * 7,
        out_specs=[vmem] * 3,
        compiler_params=params(30),
        cost_estimate=cost(40 * 10**9, 200 * 10**6),
        name="join_rest",
    )(fast_rest, slow_rest, other_rest, wt_fast, wt_slow, wt_other, arrived_rest)
    relay, pair, far = lax.optimization_barrier((relay, pair, far))
    merged = merge_rows(merge, relay, "merge")
    merged = permuted(merged, [(i, (i - 4 * x_sign[i]) % devices) for i in range(devices)])
    pair = permuted(pair, along_x)
    straight = [i for i in range(devices) if i % 4 in (0, 3)]
    far = permuted(far, [(i, (i + (5 if i % 2 else -5)) % devices) for i in straight])

    total = block(NC, BAND * BS, jnp.float32)
    frame = pltpu.VMEM((BS, FRAME * BS), jnp.float32)
    early = pl.pallas_call(
        early_kernel,
        out_shape=total,
        in_specs=[smem] + [vmem] * 4,
        out_specs=vmem,
        scratch_shapes=[frame],
        compiler_params=params(16),
        cost_estimate=cost(10**10, 100 * 10**6),
        name="early",
    )(core, own, direct, pair, far)
    return pl.pallas_call(
        total_kernel,
        out_shape=total,
        in_specs=[smem] + [vmem] * 2,
        out_specs=hbm,
        scratch_shapes=[
            frame,
            pltpu.VMEM(total.shape, jnp.float32),
            pltpu.SemaphoreType.DMA((NC,)),
        ],
        compiler_params=params(20),
        cost_estimate=cost(10**7, 10**7),
        name="total",
    )(core, early, merged)


def solution(mesh):
    in_specs = (P("dom", None, None), P("dom", None, None), P("dom", None), P("dom", None))
    out_specs = P("dom", None, None)
    return jax.shard_map(body, mesh=mesh, in_specs=in_specs, out_specs=out_specs, check_vma=False)
```

```python
import functools

import jax
import jax.numpy as jnp
from jax import lax
from jax.experimental import pallas as pl
from jax.experimental.pallas import tpu as pltpu
from jax.sharding import PartitionSpec as P

BS = 64
KA = 7
KP = 27
AGG = 8
H = 15
NC = 3
NB = 24
WIN = 31
WSLOT = 33
BAND = 63

QUAD = 4
LANES = QUAD * BS
EXT = NB + 2 * AGG
COLS = NC + 2 * H + 2
WCOLS = 40
WINDOW = 38
TILES = 10
GROUPS = 5
K = NB * BS
AW = AGG * BS
FRAME = 80
NT = (((1,), (1,)), ((), ()))
ROWS = NC * GROUPS
FIRST = 2 * NC
REST = ROWS - FIRST
MERGED = WINDOW + 6


def eye(n):
    rows = lax.broadcasted_iota(jnp.int32, (n, n), 0)
    lanes = lax.broadcasted_iota(jnp.int32, (n, n), 1)
    return jnp.where(rows == lanes, 1.0, 0.0).astype(jnp.bfloat16)


def low_half():
    return lax.broadcasted_iota(jnp.int32, (BS, 2 * BS), 1) < BS


def places(device):
    return device[0] % 2, device[0] // 2 % 2


def transpose_quad(unit, block, turned, width):
    for start in range(0, width, LANES):
        size = min(LANES, width - start)
        part = lax.dot_general(
            unit[:size, :size],
            block[:, start : start + size],
            NT,
            preferred_element_type=jnp.float32,
        )
        turned[start // BS : (start + size) // BS] = part.astype(jnp.bfloat16).reshape(
            size // BS, BS, LANES
        )


def spread_quad(turned, index, first, store, count):
    half = low_half()
    for slot in range(count):
        for pair in range(2):
            lanes = slice(pair * 2 * BS, (pair + 1) * 2 * BS)
            left = turned[index[first + 2 * pair, slot], :, lanes]
            right = turned[index[first + 2 * pair + 1, slot], :, lanes]
            store(slot, pair, jnp.where(half, left, right))


def turn_and_spread(count, turn, spread, buffers):
    even, odd = buffers
    turn(0, even)

    def two(step):
        turn(2 * step + 1, odd)
        spread(2 * step, even)
        turn(2 * step + 2, even)
        spread(2 * step + 1, odd)

    if count > 2:
        pl.loop(0, count // 2 - 1)(two)

    turn(count - 1, odd)
    spread(count - 2, even)
    spread(count - 1, odd)


def fast_kernel(
    core,
    inv_p,
    inv_a,
    p_own,
    p_fast,
    a_own,
    send_low,
    send_high,
    far,
    inner,
    send_rest,
    fast_rest,
    slow_first,
    slow_rest,
    slow_far,
    other_first,
    other_rest,
    wt,
    rest,
    at_halo,
    p_buf,
    ext,
    at,
    unit,
    turned_p,
    turned_p2,
    turned_a,
    turned_a2,
    lhs,
    rows_buf,
    fast_buf,
    slow_buf,
    other_buf,
    wt_buf,
    rest_buf,
    in_sems,
    out_sems,
):
    s, x = places(core)
    own_quads = NB // QUAD
    halo_quads = AGG // QUAD

    def load(quad):
        if quad < own_quads:
            source = p_own.at[quad * QUAD : (quad + 1) * QUAD]
        else:
            source = p_fast.at[(quad - own_quads) * QUAD : (quad - own_quads + 1) * QUAD]
        target = p_buf.at[quad * QUAD : (quad + 1) * QUAD]
        return pltpu.make_async_copy(source, target, in_sems.at[quad])

    for quad in range(own_quads + halo_quads):
        load(quad).start()

    unit[...] = eye(LANES)
    for buffers, empty in (((turned_p, turned_p2), KP), ((turned_a, turned_a2), KA)):
        for buffer in buffers:
            buffer[empty] = jnp.zeros((BS, LANES), jnp.bfloat16)

    def turn_a(quad, turned):
        block = a_own[pl.ds(quad * QUAD, QUAD)].reshape(LANES, KA * BS)
        transpose_quad(unit, block, turned, KA * BS)

    def spread_a(quad, turned):
        agg = quad // halo_quads
        first_lane = (quad % halo_quads) * LANES

        def store(slot, pair, value):
            lane = pl.multiple_of(first_lane + pair * 2 * BS, 2 * BS)
            at[agg, slot, :, pl.ds(lane, 2 * BS)] = value

        spread_quad(turned, inv_a, quad * QUAD, store, 3 * AGG)

    turn_and_spread(own_quads, turn_a, spread_a, (turned_a, turned_a2))

    slow_agg = 2 * s
    halo_copy = pltpu.make_async_copy(at.at[slow_agg, pl.ds(16 * s, AGG)], at_halo, out_sems.at[0])
    halo_copy.start()

    def turn_p(quad, turned):
        block = p_buf[pl.ds(quad * QUAD, QUAD)].reshape(LANES, KP * BS)
        transpose_quad(unit, block, turned, KP * BS)

    def spread_p(quad, turned):
        own_lane = AW + quad * LANES
        halo_lane = (AW + K) * (1 - s) + (quad - own_quads) * LANES
        first_lane = jnp.where(quad < own_quads, own_lane, halo_lane)

        def store(slot, pair, value):
            lane = pl.multiple_of(first_lane + pair * 2 * BS, 2 * BS)
            ext[slot, :, pl.ds(lane, 2 * BS)] = value

        spread_quad(turned, inv_p, quad * QUAD, store, COLS)

    for quad in range(own_quads + halo_quads):
        load(quad).wait()
    turn_and_spread(own_quads + halo_quads, turn_p, spread_p, (turned_p, turned_p2))

    fast_lanes = pl.ds(pl.multiple_of(AW + (1 - s) * AW, AW), 2 * AW)
    slow_lanes = pl.ds(pl.multiple_of(AW + 2 * s * AW, AW), AW)
    for place, i in enumerate((1 + 2 * x, 4 * x, 4 - 4 * x, 3 - 2 * x, 2)):
        for j in range(NC):
            row = NC * place + j
            mine, other = 6 * i + 3 + j + 1, 6 * i + 6 * (1 - s) + j + 1
            if place < 2:
                lhs[row] = ext[other, :, fast_lanes]
                lhs[FIRST + NC + row] = ext[mine, :, fast_lanes]
            else:
                lhs[ROWS + row - FIRST] = ext[other, :, fast_lanes]
                fast_buf[row - FIRST] = ext[mine, :, fast_lanes]
            slow_buf[row] = ext[mine, :, slow_lanes]
            other_buf[row] = ext[other, :, slow_lanes]
    for j in range(NC):
        lhs[FIRST + j] = ext[30 * s + j + 1, :, fast_lanes]
        slow_buf[ROWS + j] = ext[30 * s + j + 1, :, slow_lanes]
    copies = [halo_copy]

    def write(source, target):
        copy = pltpu.make_async_copy(source, target, out_sems.at[len(copies)])
        copy.start()
        copies.append(copy)

    write(other_buf.at[:FIRST], other_first)
    write(other_buf.at[FIRST:], other_rest)
    write(fast_buf, fast_rest)
    write(slow_buf.at[:FIRST], slow_first)
    write(slow_buf.at[FIRST:ROWS], slow_rest)
    write(slow_buf.at[ROWS:], slow_far)

    wt_buf[0:7] = jnp.zeros((7, BS, 2 * AW), jnp.bfloat16)
    wt_buf[33:] = jnp.zeros((WCOLS - 33, BS, 2 * AW), jnp.bfloat16)
    chunk = WSLOT // 3

    @pl.loop(0, 2)
    def _(place):
        agg = place + 1 - s
        lane = pl.multiple_of(agg * AW, AW)
        target = pl.multiple_of(place * AW, AW)

        @pl.loop(0, 3)
        def _(part):
            first = agg + part * chunk
            left = ext[pl.ds(first, chunk), :, pl.ds(lane, 3 * AW)].reshape(chunk * BS, 3 * AW)
            value = jnp.dot(
                left, at[agg].reshape(3 * AW, AW), preferred_element_type=jnp.float32
            )
            wt_buf[pl.ds(3 * s + first, chunk), :, pl.ds(target, AW)] = value.astype(
                jnp.bfloat16
            ).reshape(chunk, BS, AW)

    write(wt_buf, wt)

    @pl.loop(0, 3)
    def _(part):
        lane = pl.multiple_of(AW + s * AW, AW)
        left = ext[pl.ds(slow_agg + part * chunk, chunk), :, pl.ds(lane, 2 * AW)]
        right = at[slow_agg, pl.ds(AGG - AGG * s, 2 * AGG)].reshape(2 * AW, AW)
        value = jnp.dot(
            left.reshape(chunk * BS, 2 * AW), right, preferred_element_type=jnp.float32
        )
        rest_buf[pl.ds(part * chunk, chunk)] = value.reshape(chunk, BS, AW)

    write(rest_buf, rest)

    def emit(tile, width):
        right = wt_buf[pl.ds(QUAD * tile, width // BS)].reshape(width, 2 * AW)
        left = lhs[...].reshape((ROWS + REST) * BS, 2 * AW)
        value = lax.dot_general(left, right, NT, preferred_element_type=jnp.float32)
        rows_buf[:, :, tile_lanes(tile, width)] = value.astype(jnp.bfloat16).reshape(
            ROWS + REST, BS, width
        )

    parts = (
        (send_low, 0),
        (send_high, NC),
        (far, FIRST),
        (inner, FIRST + NC),
        (send_rest, ROWS),
    )
    bounds = (0, 4, 8, TILES)
    for first, last in zip(bounds[:-1], bounds[1:]):

        @pl.loop(first, min(last, TILES - 1))
        def _(tile):
            emit(tile, LANES)

        if last == TILES:
            emit(TILES - 1, LANES // 2)
        lanes = slice(first * LANES, min(last * LANES, WINDOW * BS))
        for target, row in parts:
            rows = slice(row, row + target.shape[0])
            write(rows_buf.at[rows, :, lanes], target.at[:, :, lanes])
    for copy in copies:
        copy.wait()


def each_tile(step):
    @pl.loop(0, TILES - 1)
    def _(tile):
        step(tile, LANES)

    step(TILES - 1, LANES // 2)


def tile_dot(rows, cols, tile, width):
    left = rows[...].reshape(rows.shape[0] * BS, rows.shape[2])
    right = cols[pl.ds(QUAD * tile, width // BS)].reshape(width, cols.shape[2])
    value = lax.dot_general(left, right, NT, preferred_element_type=jnp.float32)
    return value.reshape(rows.shape[0], BS, width)


def tile_lanes(tile, width):
    return pl.ds(pl.multiple_of(tile * LANES, LANES), width)


def far_kernel(slow, wt_slow, far_fast, far):
    def step(tile, width):
        lanes = tile_lanes(tile, width)
        value = tile_dot(slow, wt_slow, tile, width) + far_fast[:, :, lanes].astype(jnp.float32)
        far[:, :, lanes] = value.astype(jnp.bfloat16)

    each_tile(step)


def mine_kernel(slow, wt_slow, inner, low, high, out):
    def step(tile, width):
        lanes = tile_lanes(tile, width)
        near = tile_dot(slow, wt_slow, tile, width) + inner[:, :, lanes].astype(jnp.float32)
        out[:NC, :, lanes] = near[:NC] + low[:, :, lanes].astype(jnp.float32)
        out[NC:, :, lanes] = near[NC:] + high[:, :, lanes].astype(jnp.float32)

    each_tile(step)


def slow_kernel(core, inv_slow, p_slow, at_halo, rest, wt, unit, turned_p, turned_p2, ext):
    s, x = places(core)
    unit[...] = eye(LANES)
    for buffer in (turned_p, turned_p2):
        buffer[KP] = jnp.zeros((BS, LANES), jnp.bfloat16)

    def turn(quad, turned):
        block = p_slow[quad * QUAD : (quad + 1) * QUAD].reshape(LANES, KP * BS)
        transpose_quad(unit, block, turned, KP * BS)

    def spread(quad, turned):
        def store(slot, pair, value):
            lane = quad * LANES + pair * 2 * BS
            ext[slot, :, lane : lane + 2 * BS] = value

        spread_quad(turned, inv_slow, quad * QUAD, store, WSLOT)

    turn_and_spread(AGG // QUAD, turn, spread, (turned_p, turned_p2))
    wt[0:5] = jnp.zeros((5, BS, AW), jnp.bfloat16)
    wt[WSLOT:] = jnp.zeros((WCOLS - WSLOT, BS, AW), jnp.bfloat16)
    chunk = WSLOT // 3

    @pl.loop(0, 3)
    def _(part):
        rows = pl.ds(part * chunk, chunk)
        value = jnp.dot(
            ext[rows].reshape(chunk * BS, AW),
            at_halo[...].reshape(AW, AW),
            preferred_element_type=jnp.float32,
        )
        value = value.reshape(chunk, BS, AW) + rest[rows]
        wt[pl.ds(5 * s + part * chunk, chunk)] = value.astype(jnp.bfloat16)


def join_first_kernel(other, wt_other, mine, relay, direct):
    def step(tile, width):
        lanes = tile_lanes(tile, width)
        value = tile_dot(other, wt_other, tile, width) + mine[:, :, lanes]
        relay[:, :, lanes] = value[:NC].astype(jnp.bfloat16)
        direct[:, :, lanes] = value[NC:]

    each_tile(step)


def join_rest_kernel(fast, slow, other, wt_fast, wt_slow, wt_other, arrived, merge, pair, own):
    def step(tile, width):
        lanes = tile_lanes(tile, width)
        value = tile_dot(fast, wt_fast, tile, width) + tile_dot(slow, wt_slow, tile, width)
        value = value + tile_dot(other, wt_other, tile, width)
        value = value + arrived[:, :, lanes].astype(jnp.float32)
        merge[:, :, lanes] = value[:NC]
        pair[:, :, lanes] = value[NC : 2 * NC].astype(jnp.bfloat16)
        own[:, :, lanes] = value[2 * NC :]

    each_tile(step)


def stage_kernel(at_halo, rest, at_out, rest_out, sems):
    copies = [
        pltpu.make_async_copy(at_halo, at_out, sems.at[0]),
        pltpu.make_async_copy(rest, rest_out, sems.at[1]),
    ]
    for copy in copies:
        copy.start()
    for copy in copies:
        copy.wait()


def merge_kernel(core, rows, other, out, frame):
    s, x = places(core)
    step = 6 * BS
    for j in range(NC):
        frame[...] = jnp.zeros_like(frame)
        frame[:, pl.ds(pl.multiple_of(step * x, step), WINDOW * BS)] = rows[j]
        lanes = pl.ds(pl.multiple_of(step * (1 - x), step), WINDOW * BS)
        frame[:, lanes] += other[j].astype(jnp.float32)
        out[j] = frame[...].astype(jnp.bfloat16)


def in_frame(s, j, frame, messages, store):
    odd = (j + 1 - s) % 2
    frame[...] = jnp.zeros_like(frame)
    for message, start in messages:
        lane = pl.multiple_of((start - odd + 8) * BS, 2 * BS)
        frame[:, pl.ds(lane, message.shape[2])] += message[j].astype(jnp.float32)
    first, last = 8 * BS, (8 + BAND) * BS

    @pl.when(odd == 0)
    def _():
        store(frame[:, first:last])

    @pl.when(odd == 1)
    def _():
        store(frame[:, first - BS : last - BS])


def early_kernel(core, own, direct, pair, far, out, frame):
    s, x = places(core)
    for j in range(NC):
        top = 27 - 3 * s - j
        far_start = jnp.where(s == 1, 30 - j, -3 - j)
        messages = [(own, top - 12), (direct, top - 30 * x), (pair, top - 6 - 12 * x)]
        messages.append((far, far_start))

        def store(value, j=j):
            out[j] = value

        in_frame(s, j, frame, messages, store)


def total_kernel(core, early, merged, out, frame, buf, sems):
    s, x = places(core)
    copies = []
    for j in range(NC):

        def store(value, j=j):
            buf[j] = value + early[j]

        in_frame(s, j, frame, [(merged, 3 - 3 * s - j + 18 * x)], store)
        copy = pltpu.make_async_copy(buf.at[j], out.at[j], sems.at[j])
        copy.start()
        copies.append(copy)
    for copy in copies:
        copy.wait()


def pick_kernel(core, source, outer, inner, buf, in_sems, out_sems):
    s, x = places(core)
    step = AGG // 4
    reads, writes = [], []
    for side, (target, which) in enumerate(((outer, s), (inner, 1 - s))):
        for k in range(4):
            n = len(reads)
            rows = pl.ds((NB - AGG) * which + k * step, step)
            part = buf.at[side, k * step : (k + 1) * step]
            into = target.at[k * step : (k + 1) * step]
            reads.append(pltpu.make_async_copy(source.at[rows], part, in_sems.at[n]))
            writes.append(pltpu.make_async_copy(part, into, out_sems.at[n]))
    for copy in reads:
        copy.start()
    for read, write in zip(reads, writes):
        read.wait()
        write.start()
    for copy in writes:
        copy.wait()


def permuted(block, pairs):
    return lax.ppermute(block, "dom", pairs)


def inverse_index(offset, slots, empty):
    order = jnp.arange(offset.shape[1], dtype=jnp.int32)[None, :, None]
    hit = offset[:, :, None] == jnp.arange(slots, dtype=jnp.int32)[None, None, :]
    return empty + jnp.sum(jnp.where(hit, order - empty, 0), axis=1)


def body(a_blocks, p_blocks, cols_a, cols_p):
    devices = lax.axis_size("dom")
    device = lax.axis_index("dom")
    count_agg = NC * devices
    count_rows = NB * devices
    first_agg = device * NC
    first_row = device * NB
    core = device.astype(jnp.int32).reshape(1)

    def shifted(distance):
        return [(i, (i + distance) % devices) for i in range(devices)]

    parity = device % 2
    smem = pl.BlockSpec(memory_space=pltpu.SMEM)
    vmem = pl.BlockSpec(memory_space=pltpu.VMEM)
    hbm = pl.BlockSpec(memory_space=pltpu.HBM)
    bf16 = jnp.bfloat16

    def params(mebibytes):
        return pltpu.CompilerParams(vmem_limit_bytes=mebibytes * 1024 * 1024)

    def cost(flops, size):
        return pl.CostEstimate(flops=flops, bytes_accessed=size, transcendentals=0)

    edge = jax.ShapeDtypeStruct((AGG,) + p_blocks.shape[1:], bf16)
    outer, inner = pl.pallas_call(
        pick_kernel,
        out_shape=[edge, edge],
        in_specs=[smem, hbm],
        out_specs=[hbm, hbm],
        scratch_shapes=[
            pltpu.VMEM((2,) + edge.shape, bf16),
            pltpu.SemaphoreType.DMA((8,)),
            pltpu.SemaphoreType.DMA((8,)),
        ],
        compiler_params=params(60),
        name="pick",
    )(core, p_blocks)
    outward = [(i, (i + (1 if i % 2 else -1)) % devices) for i in range(devices)]
    inward = [(i, i ^ 1) for i in range(devices)]
    outer, inner, edge_cols = lax.optimization_barrier((outer, inner, cols_p))
    p_slow = permuted(outer, outward)
    p_fast = permuted(inner, inward)
    edge_cols = jnp.stack([edge_cols[:AGG], edge_cols[NB - AGG :]])
    cols_slow = permuted(edge_cols[parity], outward)
    cols_fast = permuted(edge_cols[1 - parity], inward)

    def slots(cols, agg):
        return (cols - agg + H) % count_agg

    own_agg = jnp.arange(NB, dtype=jnp.int32)[:, None] // AGG
    inv_own = inverse_index(slots(cols_p, first_agg + own_agg) + own_agg + 1, COLS, KP)
    fast_place = NC * (1 - parity) - parity
    inv_fast = inverse_index(slots(cols_fast, first_agg + fast_place) + fast_place + 1, COLS, KP)
    slow_place = NC * parity - (1 - parity)
    inv_slow = inverse_index(slots(cols_slow, first_agg + slow_place) + 2 * parity, WSLOT, KP)
    inv_fast, inv_slow = lax.optimization_barrier((inv_fast, inv_slow))
    inv_a = inverse_index((cols_a - first_row - (own_agg - 1) * AGG) % count_rows, 3 * AGG, KA)

    def block(rows, width, kind=bf16):
        return jax.ShapeDtypeStruct((rows, BS, width), kind)

    span = WINDOW * BS
    outs = [
        block(NC, span),
        block(NC, span),
        block(NC, span),
        block(FIRST, span),
        block(REST, span),
        block(REST, 2 * AW),
        block(FIRST, AW),
        block(REST, AW),
        block(NC, AW),
        block(FIRST, AW),
        block(REST, AW),
        block(WCOLS, 2 * AW),
        block(WSLOT, AW, jnp.float32),
        block(AGG, AW),
    ]
    (
        send_low,
        send_high,
        far,
        inner,
        send_rest,
        fast_rest,
        slow_first,
        slow_rest,
        slow_far,
        other_first,
        other_rest,
        wt_fast,
        rest,
        at_halo,
    ) = pl.pallas_call(
        fast_kernel,
        out_shape=outs,
        in_specs=[smem] * 3 + [hbm, hbm, vmem],
        out_specs=[hbm] * len(outs),
        scratch_shapes=[
            pltpu.VMEM((NB + AGG, BS, KP * BS), bf16),
            pltpu.VMEM((COLS, BS, EXT * BS), bf16),
            pltpu.VMEM((NC, 3 * AGG, BS, AW), bf16),
            pltpu.VMEM((LANES, LANES), bf16),
            pltpu.VMEM((KP + 1, BS, LANES), bf16),
            pltpu.VMEM((KP + 1, BS, LANES), bf16),
            pltpu.VMEM((KA + 1, BS, LANES), bf16),
            pltpu.VMEM((KA + 1, BS, LANES), bf16),
            pltpu.VMEM((ROWS + REST, BS, 2 * AW), bf16),
            pltpu.VMEM((ROWS + REST, BS, span), bf16),
            pltpu.VMEM((REST, BS, 2 * AW), bf16),
            pltpu.VMEM((ROWS + NC, BS, AW), bf16),
            pltpu.VMEM((ROWS, BS, AW), bf16),
            pltpu.VMEM((WCOLS, BS, 2 * AW), bf16),
            pltpu.VMEM((WSLOT, BS, AW), jnp.float32),
            pltpu.SemaphoreType.DMA(((NB + AGG) // QUAD,)),
            pltpu.SemaphoreType.DMA((len(outs) + 10,)),
        ],
        compiler_params=params(56),
        cost_estimate=cost(20 * 10**9, 30 * 10**6),
        name="fast",
    )(core, jnp.concatenate([inv_own, inv_fast]), inv_a, p_blocks, p_fast, a_blocks)

    low = permuted(send_low, inward)
    high = permuted(send_high, inward)
    other_first = permuted(other_first, inward)
    at_halo, rest = pl.pallas_call(
        stage_kernel,
        out_shape=[block(AGG, AW), block(WSLOT, AW, jnp.float32)],
        in_specs=[hbm] * 2,
        out_specs=[vmem] * 2,
        scratch_shapes=[pltpu.SemaphoreType.DMA((2,))],
        compiler_params=params(8),
        cost_estimate=cost(10**6, 10**6),
        name="stage",
    )(at_halo, rest)
    p_slow, low, high, other_first = lax.optimization_barrier((p_slow, low, high, other_first))

    wt_slow = pl.pallas_call(
        slow_kernel,
        out_shape=block(WCOLS, AW),
        in_specs=[smem] * 2 + [vmem] * 3,
        out_specs=vmem,
        scratch_shapes=[
            pltpu.VMEM((LANES, LANES), bf16),
            pltpu.VMEM((KP + 1, BS, LANES), bf16),
            pltpu.VMEM((KP + 1, BS, LANES), bf16),
            pltpu.VMEM((WSLOT, BS, AW), bf16),
        ],
        compiler_params=params(24),
        cost_estimate=cost(20 * 10**9, 200 * 10**6),
        name="slow",
    )(core, inv_slow, p_slow, at_halo, rest)
    wt_other = permuted(wt_slow, inward)

    wt_slow, low, high = lax.optimization_barrier((wt_slow, low, high))
    far = pl.pallas_call(
        far_kernel,
        out_shape=block(NC, span),
        in_specs=[vmem] * 3,
        out_specs=vmem,
        compiler_params=params(16),
        cost_estimate=cost(10**9, 10**7),
        name="far",
    )(slow_far, wt_slow, far)
    far, wt_slow = lax.optimization_barrier((far, wt_slow))
    mine = pl.pallas_call(
        mine_kernel,
        out_shape=block(FIRST, span, jnp.float32),
        in_specs=[vmem] * 5,
        out_specs=vmem,
        compiler_params=params(24),
        cost_estimate=cost(10**10, 100 * 10**6),
        name="mine",
    )(slow_first, wt_slow, inner, low, high)
    crossing = [i for i in range(devices) if i % 4 in (1, 2)]
    far_near = permuted(far, [(i, i ^ 3) for i in crossing])
    relay, direct = pl.pallas_call(
        join_first_kernel,
        out_shape=[block(NC, span), block(NC, span, jnp.float32)],
        in_specs=[vmem] * 3,
        out_specs=[vmem] * 2,
        compiler_params=params(16),
        cost_estimate=cost(10**6, 10**5),
        name="join_first",
    )(other_first, wt_other, mine)
    straight = [i for i in range(devices) if i % 4 in (0, 3)]
    far = permuted(far, [(i, (i + (5 if i % 2 else -5)) % devices) for i in straight])
    relay, direct, far_near, far, send_rest, other_rest = lax.optimization_barrier(
        (relay, direct, far_near, far, send_rest, other_rest)
    )
    arrived_rest = permuted(send_rest, inward)
    other_rest = permuted(other_rest, inward)
    along_x = [(i, i ^ 2) for i in range(devices)]
    x_sign = [1 if i // 2 % 2 else -1 for i in range(devices)]
    relay = permuted(relay, along_x)

    def merge_rows(rows, other, name):
        return pl.pallas_call(
            merge_kernel,
            out_shape=block(NC, MERGED * BS),
            in_specs=[smem, vmem, vmem],
            out_specs=vmem,
            scratch_shapes=[pltpu.VMEM((BS, MERGED * BS), jnp.float32)],
            compiler_params=params(16),
            cost_estimate=cost(10**7, 10**7),
            name=name,
        )(core, rows, other)

    direct = merge_rows(direct, far_near, "merge_far")
    direct = permuted(direct, [(i, (i + 4 * x_sign[i]) % devices) for i in range(devices)])
    merge, pair, own = pl.pallas_call(
        join_rest_kernel,
        out_shape=[block(NC, span, jnp.float32), block(NC, span), block(NC, span, jnp.float32)],
        in_specs=[vmem] * 7,
        out_specs=[vmem] * 3,
        compiler_params=params(30),
        cost_estimate=cost(40 * 10**9, 200 * 10**6),
        name="join_rest",
    )(fast_rest, slow_rest, other_rest, wt_fast, wt_slow, wt_other, arrived_rest)
    relay, pair = lax.optimization_barrier((relay, pair))
    merged = merge_rows(merge, relay, "merge")
    merged = permuted(merged, [(i, (i - 4 * x_sign[i]) % devices) for i in range(devices)])
    pair = permuted(pair, along_x)

    total = block(NC, BAND * BS, jnp.float32)
    frame = pltpu.VMEM((BS, FRAME * BS), jnp.float32)
    early = pl.pallas_call(
        early_kernel,
        out_shape=total,
        in_specs=[smem] + [vmem] * 4,
        out_specs=vmem,
        scratch_shapes=[frame],
        compiler_params=params(16),
        cost_estimate=cost(10**10, 100 * 10**6),
        name="early",
    )(core, own, direct, pair, far)
    return pl.pallas_call(
        total_kernel,
        out_shape=total,
        in_specs=[smem] + [vmem] * 2,
        out_specs=hbm,
        scratch_shapes=[
            frame,
            pltpu.VMEM(total.shape, jnp.float32),
            pltpu.SemaphoreType.DMA((NC,)),
        ],
        compiler_params=params(20),
        cost_estimate=cost(10**7, 10**7),
        name="total",
    )(core, early, merged)


def solution(mesh):
    in_specs = (P("dom", None, None), P("dom", None, None), P("dom", None), P("dom", None))
    out_specs = P("dom", None, None)
    return jax.shard_map(body, mesh=mesh, in_specs=in_specs, out_specs=out_specs, check_vma=False)
```

```python
import functools

import jax
import jax.numpy as jnp
from jax import lax
from jax.experimental import pallas as pl
from jax.experimental.pallas import tpu as pltpu
from jax.sharding import PartitionSpec as P

BS = 64
KA = 7
KP = 27
AGG = 8
H = 15
NC = 3
NB = 24
WIN = 31
WSLOT = 33
BAND = 63

QUAD = 4
LANES = QUAD * BS
EXT = NB + 2 * AGG
COLS = NC + 2 * H + 2
WCOLS = 40
WINDOW = 38
TILES = 10
GROUPS = 5
K = NB * BS
AW = AGG * BS
FRAME = 80
NT = (((1,), (1,)), ((), ()))
ROWS = NC * GROUPS
FIRST = 2 * NC
REST = ROWS - FIRST
MERGED = WINDOW + 6


def eye(n):
    rows = lax.broadcasted_iota(jnp.int32, (n, n), 0)
    lanes = lax.broadcasted_iota(jnp.int32, (n, n), 1)
    return jnp.where(rows == lanes, 1.0, 0.0).astype(jnp.bfloat16)


def low_half():
    return lax.broadcasted_iota(jnp.int32, (BS, 2 * BS), 1) < BS


def places(device):
    return device[0] % 2, device[0] // 2 % 2


def transpose_quad(unit, block, turned, width):
    for start in range(0, width, LANES):
        size = min(LANES, width - start)
        part = lax.dot_general(
            unit[:size, :size],
            block[:, start : start + size],
            NT,
            preferred_element_type=jnp.float32,
        )
        turned[start // BS : (start + size) // BS] = part.astype(jnp.bfloat16).reshape(
            size // BS, BS, LANES
        )


def spread_quad(turned, index, first, store, count):
    half = low_half()
    for slot in range(count):
        for pair in range(2):
            lanes = slice(pair * 2 * BS, (pair + 1) * 2 * BS)
            left = turned[index[first + 2 * pair, slot], :, lanes]
            right = turned[index[first + 2 * pair + 1, slot], :, lanes]
            store(slot, pair, jnp.where(half, left, right))


def turn_and_spread(count, turn, spread, buffers):
    even, odd = buffers
    turn(0, even)

    def two(step):
        turn(2 * step + 1, odd)
        spread(2 * step, even)
        turn(2 * step + 2, even)
        spread(2 * step + 1, odd)

    if count > 2:
        pl.loop(0, count // 2 - 1)(two)

    turn(count - 1, odd)
    spread(count - 2, even)
    spread(count - 1, odd)


def fast_kernel(
    core,
    inv_p,
    inv_a,
    p_own,
    p_fast,
    a_own,
    send_low,
    send_high,
    far,
    inner,
    send_rest,
    fast_rest,
    slow_first,
    slow_rest,
    slow_far,
    other_first,
    other_rest,
    wt,
    rest,
    at_halo,
    p_buf,
    ext,
    at,
    unit,
    turned_p,
    turned_p2,
    turned_a,
    turned_a2,
    lhs,
    rows_buf,
    fast_buf,
    slow_buf,
    other_buf,
    wt_buf,
    rest_buf,
    in_sems,
    out_sems,
):
    s, x = places(core)
    own_quads = NB // QUAD
    halo_quads = AGG // QUAD

    def load(quad):
        if quad < own_quads:
            source = p_own.at[quad * QUAD : (quad + 1) * QUAD]
        else:
            source = p_fast.at[(quad - own_quads) * QUAD : (quad - own_quads + 1) * QUAD]
        target = p_buf.at[quad * QUAD : (quad + 1) * QUAD]
        return pltpu.make_async_copy(source, target, in_sems.at[quad])

    for quad in range(own_quads + halo_quads):
        load(quad).start()

    unit[...] = eye(LANES)
    for buffers, empty in (((turned_p, turned_p2), KP), ((turned_a, turned_a2), KA)):
        for buffer in buffers:
            buffer[empty] = jnp.zeros((BS, LANES), jnp.bfloat16)

    def turn_a(quad, turned):
        block = a_own[pl.ds(quad * QUAD, QUAD)].reshape(LANES, KA * BS)
        transpose_quad(unit, block, turned, KA * BS)

    def spread_a(quad, turned):
        agg = quad // halo_quads
        first_lane = (quad % halo_quads) * LANES

        def store(slot, pair, value):
            lane = pl.multiple_of(first_lane + pair * 2 * BS, 2 * BS)
            at[agg, slot, :, pl.ds(lane, 2 * BS)] = value

        spread_quad(turned, inv_a, quad * QUAD, store, 3 * AGG)

    turn_and_spread(own_quads, turn_a, spread_a, (turned_a, turned_a2))

    slow_agg = 2 * s
    halo_copy = pltpu.make_async_copy(at.at[slow_agg, pl.ds(16 * s, AGG)], at_halo, out_sems.at[0])
    halo_copy.start()

    def turn_p(quad, turned):
        block = p_buf[pl.ds(quad * QUAD, QUAD)].reshape(LANES, KP * BS)
        transpose_quad(unit, block, turned, KP * BS)

    def spread_p(quad, turned):
        own_lane = AW + quad * LANES
        halo_lane = (AW + K) * (1 - s) + (quad - own_quads) * LANES
        first_lane = jnp.where(quad < own_quads, own_lane, halo_lane)

        def store(slot, pair, value):
            lane = pl.multiple_of(first_lane + pair * 2 * BS, 2 * BS)
            ext[slot, :, pl.ds(lane, 2 * BS)] = value

        spread_quad(turned, inv_p, quad * QUAD, store, COLS)

    for quad in range(own_quads + halo_quads):
        load(quad).wait()
    turn_and_spread(own_quads + halo_quads, turn_p, spread_p, (turned_p, turned_p2))

    fast_lanes = pl.ds(pl.multiple_of(AW + (1 - s) * AW, AW), 2 * AW)
    slow_lanes = pl.ds(pl.multiple_of(AW + 2 * s * AW, AW), AW)
    for place, i in enumerate((1 + 2 * x, 4 * x, 4 - 4 * x, 3 - 2 * x, 2)):
        for j in range(NC):
            row = NC * place + j
            mine, other = 6 * i + 3 + j + 1, 6 * i + 6 * (1 - s) + j + 1
            if place < 2:
                lhs[row] = ext[other, :, fast_lanes]
                lhs[FIRST + NC + row] = ext[mine, :, fast_lanes]
            else:
                lhs[ROWS + row - FIRST] = ext[other, :, fast_lanes]
                fast_buf[row - FIRST] = ext[mine, :, fast_lanes]
            slow_buf[row] = ext[mine, :, slow_lanes]
            other_buf[row] = ext[other, :, slow_lanes]
    for j in range(NC):
        lhs[FIRST + j] = ext[30 * s + j + 1, :, fast_lanes]
        slow_buf[ROWS + j] = ext[30 * s + j + 1, :, slow_lanes]
    copies = [halo_copy]

    def write(source, target):
        copy = pltpu.make_async_copy(source, target, out_sems.at[len(copies)])
        copy.start()
        copies.append(copy)

    write(other_buf.at[:FIRST], other_first)
    write(other_buf.at[FIRST:], other_rest)
    write(fast_buf, fast_rest)
    write(slow_buf.at[:FIRST], slow_first)
    write(slow_buf.at[FIRST:ROWS], slow_rest)
    write(slow_buf.at[ROWS:], slow_far)

    wt_buf[0:7] = jnp.zeros((7, BS, 2 * AW), jnp.bfloat16)
    wt_buf[33:] = jnp.zeros((WCOLS - 33, BS, 2 * AW), jnp.bfloat16)
    chunk = WSLOT // 3

    @pl.loop(0, 2)
    def _(place):
        agg = place + 1 - s
        lane = pl.multiple_of(agg * AW, AW)
        target = pl.multiple_of(place * AW, AW)

        @pl.loop(0, 3)
        def _(part):
            first = agg + part * chunk
            left = ext[pl.ds(first, chunk), :, pl.ds(lane, 3 * AW)].reshape(chunk * BS, 3 * AW)
            value = jnp.dot(
                left, at[agg].reshape(3 * AW, AW), preferred_element_type=jnp.float32
            )
            wt_buf[pl.ds(3 * s + first, chunk), :, pl.ds(target, AW)] = value.astype(
                jnp.bfloat16
            ).reshape(chunk, BS, AW)

    write(wt_buf, wt)

    @pl.loop(0, 3)
    def _(part):
        lane = pl.multiple_of(AW + s * AW, AW)
        left = ext[pl.ds(slow_agg + part * chunk, chunk), :, pl.ds(lane, 2 * AW)]
        right = at[slow_agg, pl.ds(AGG - AGG * s, 2 * AGG)].reshape(2 * AW, AW)
        value = jnp.dot(
            left.reshape(chunk * BS, 2 * AW), right, preferred_element_type=jnp.float32
        )
        rest_buf[pl.ds(part * chunk, chunk)] = value.reshape(chunk, BS, AW)

    write(rest_buf, rest)

    def emit(tile, width):
        right = wt_buf[pl.ds(QUAD * tile, width // BS)].reshape(width, 2 * AW)
        left = lhs[...].reshape((ROWS + REST) * BS, 2 * AW)
        value = lax.dot_general(left, right, NT, preferred_element_type=jnp.float32)
        rows_buf[:, :, tile_lanes(tile, width)] = value.astype(jnp.bfloat16).reshape(
            ROWS + REST, BS, width
        )

    parts = (
        (send_low, 0),
        (send_high, NC),
        (far, FIRST),
        (inner, FIRST + NC),
        (send_rest, ROWS),
    )
    bounds = (0, 4, 8, TILES)
    for first, last in zip(bounds[:-1], bounds[1:]):

        @pl.loop(first, min(last, TILES - 1))
        def _(tile):
            emit(tile, LANES)

        if last == TILES:
            emit(TILES - 1, LANES // 2)
        lanes = slice(first * LANES, min(last * LANES, WINDOW * BS))
        for target, row in parts:
            rows = slice(row, row + target.shape[0])
            write(rows_buf.at[rows, :, lanes], target.at[:, :, lanes])
    for copy in copies:
        copy.wait()


def each_tile(step):
    @pl.loop(0, TILES - 1)
    def _(tile):
        step(tile, LANES)

    step(TILES - 1, LANES // 2)


def tile_dot(rows, cols, tile, width):
    left = rows[...].reshape(rows.shape[0] * BS, rows.shape[2])
    right = cols[pl.ds(QUAD * tile, width // BS)].reshape(width, cols.shape[2])
    value = lax.dot_general(left, right, NT, preferred_element_type=jnp.float32)
    return value.reshape(rows.shape[0], BS, width)


def tile_lanes(tile, width):
    return pl.ds(pl.multiple_of(tile * LANES, LANES), width)


def far_kernel(slow, wt_slow, far_fast, far):
    def step(tile, width):
        lanes = tile_lanes(tile, width)
        value = tile_dot(slow, wt_slow, tile, width) + far_fast[:, :, lanes].astype(jnp.float32)
        far[:, :, lanes] = value.astype(jnp.bfloat16)

    each_tile(step)


def mine_kernel(slow, wt_slow, inner, low, high, out):
    def step(tile, width):
        lanes = tile_lanes(tile, width)
        near = tile_dot(slow, wt_slow, tile, width) + inner[:, :, lanes].astype(jnp.float32)
        out[:NC, :, lanes] = near[:NC] + low[:, :, lanes].astype(jnp.float32)
        out[NC:, :, lanes] = near[NC:] + high[:, :, lanes].astype(jnp.float32)

    each_tile(step)


def slow_kernel(core, inv_slow, p_slow, at_halo, rest, wt, unit, turned_p, turned_p2, ext):
    s, x = places(core)
    unit[...] = eye(LANES)
    for buffer in (turned_p, turned_p2):
        buffer[KP] = jnp.zeros((BS, LANES), jnp.bfloat16)

    def turn(quad, turned):
        block = p_slow[quad * QUAD : (quad + 1) * QUAD].reshape(LANES, KP * BS)
        transpose_quad(unit, block, turned, KP * BS)

    def spread(quad, turned):
        def store(slot, pair, value):
            lane = quad * LANES + pair * 2 * BS
            ext[slot, :, lane : lane + 2 * BS] = value

        spread_quad(turned, inv_slow, quad * QUAD, store, WSLOT)

    turn_and_spread(AGG // QUAD, turn, spread, (turned_p, turned_p2))
    wt[0:5] = jnp.zeros((5, BS, AW), jnp.bfloat16)
    wt[WSLOT:] = jnp.zeros((WCOLS - WSLOT, BS, AW), jnp.bfloat16)
    chunk = WSLOT // 3

    @pl.loop(0, 3)
    def _(part):
        rows = pl.ds(part * chunk, chunk)
        value = jnp.dot(
            ext[rows].reshape(chunk * BS, AW),
            at_halo[...].reshape(AW, AW),
            preferred_element_type=jnp.float32,
        )
        value = value.reshape(chunk, BS, AW) + rest[rows]
        wt[pl.ds(5 * s + part * chunk, chunk)] = value.astype(jnp.bfloat16)


def join_first_kernel(other, wt_other, mine, relay, direct):
    def step(tile, width):
        lanes = tile_lanes(tile, width)
        value = tile_dot(other, wt_other, tile, width) + mine[:, :, lanes]
        relay[:, :, lanes] = value[:NC].astype(jnp.bfloat16)
        direct[:, :, lanes] = value[NC:]

    each_tile(step)


def join_rest_kernel(fast, slow, other, wt_fast, wt_slow, wt_other, arrived, merge, pair, own):
    def step(tile, width):
        lanes = tile_lanes(tile, width)
        value = tile_dot(fast, wt_fast, tile, width) + tile_dot(slow, wt_slow, tile, width)
        value = value + tile_dot(other, wt_other, tile, width)
        value = value + arrived[:, :, lanes].astype(jnp.float32)
        merge[:, :, lanes] = value[:NC]
        pair[:, :, lanes] = value[NC : 2 * NC].astype(jnp.bfloat16)
        own[:, :, lanes] = value[2 * NC :]

    each_tile(step)


def stage_kernel(at_halo, rest, at_out, rest_out, sems):
    copies = [
        pltpu.make_async_copy(at_halo, at_out, sems.at[0]),
        pltpu.make_async_copy(rest, rest_out, sems.at[1]),
    ]
    for copy in copies:
        copy.start()
    for copy in copies:
        copy.wait()


def merge_kernel(core, rows, other, out, frame):
    s, x = places(core)
    step = 6 * BS
    for j in range(NC):
        frame[...] = jnp.zeros_like(frame)
        frame[:, pl.ds(pl.multiple_of(step * x, step), WINDOW * BS)] = rows[j]
        lanes = pl.ds(pl.multiple_of(step * (1 - x), step), WINDOW * BS)
        frame[:, lanes] += other[j].astype(jnp.float32)
        out[j] = frame[...].astype(jnp.bfloat16)


def in_frame(s, j, frame, messages, store):
    odd = (j + 1 - s) % 2
    frame[...] = jnp.zeros_like(frame)
    for message, start in messages:
        lane = pl.multiple_of((start - odd + 8) * BS, 2 * BS)
        frame[:, pl.ds(lane, message.shape[2])] += message[j].astype(jnp.float32)
    first, last = 8 * BS, (8 + BAND) * BS

    @pl.when(odd == 0)
    def _():
        store(frame[:, first:last])

    @pl.when(odd == 1)
    def _():
        store(frame[:, first - BS : last - BS])


def early_kernel(core, own, direct, pair, far, out, frame):
    s, x = places(core)
    for j in range(NC):
        top = 27 - 3 * s - j
        far_start = jnp.where(s == 1, 30 - j, -3 - j)
        messages = [(own, top - 12), (direct, top - 30 * x), (pair, top - 6 - 12 * x)]
        messages.append((far, far_start))

        def store(value, j=j):
            out[j] = value

        in_frame(s, j, frame, messages, store)


def total_kernel(core, early, merged, out, frame, buf, sems):
    s, x = places(core)
    copies = []
    for j in range(NC):

        def store(value, j=j):
            buf[j] = value + early[j]

        in_frame(s, j, frame, [(merged, 3 - 3 * s - j + 18 * x)], store)
        copy = pltpu.make_async_copy(buf.at[j], out.at[j], sems.at[j])
        copy.start()
        copies.append(copy)
    for copy in copies:
        copy.wait()


def pick_kernel(core, source, outer, inner, buf, in_sems, out_sems):
    s, x = places(core)
    step = AGG // 4
    reads, writes = [], []
    for side, (target, which) in enumerate(((outer, s), (inner, 1 - s))):
        for k in range(4):
            n = len(reads)
            rows = pl.ds((NB - AGG) * which + k * step, step)
            part = buf.at[side, k * step : (k + 1) * step]
            into = target.at[k * step : (k + 1) * step]
            reads.append(pltpu.make_async_copy(source.at[rows], part, in_sems.at[n]))
            writes.append(pltpu.make_async_copy(part, into, out_sems.at[n]))
    for copy in reads:
        copy.start()
    for read, write in zip(reads, writes):
        read.wait()
        write.start()
    for copy in writes:
        copy.wait()


def permuted(block, pairs):
    return lax.ppermute(block, "dom", pairs)


def inverse_index(offset, slots, empty):
    order = jnp.arange(offset.shape[1], dtype=jnp.int32)[None, :, None]
    hit = offset[:, :, None] == jnp.arange(slots, dtype=jnp.int32)[None, None, :]
    return empty + jnp.sum(jnp.where(hit, order - empty, 0), axis=1)


def body(a_blocks, p_blocks, cols_a, cols_p):
    devices = lax.axis_size("dom")
    device = lax.axis_index("dom")
    count_agg = NC * devices
    count_rows = NB * devices
    first_agg = device * NC
    first_row = device * NB
    core = device.astype(jnp.int32).reshape(1)

    def shifted(distance):
        return [(i, (i + distance) % devices) for i in range(devices)]

    parity = device % 2
    smem = pl.BlockSpec(memory_space=pltpu.SMEM)
    vmem = pl.BlockSpec(memory_space=pltpu.VMEM)
    hbm = pl.BlockSpec(memory_space=pltpu.HBM)
    bf16 = jnp.bfloat16

    def params(mebibytes):
        return pltpu.CompilerParams(vmem_limit_bytes=mebibytes * 1024 * 1024)

    def cost(flops, size):
        return pl.CostEstimate(flops=flops, bytes_accessed=size, transcendentals=0)

    edge = jax.ShapeDtypeStruct((AGG,) + p_blocks.shape[1:], bf16)
    outer, inner = pl.pallas_call(
        pick_kernel,
        out_shape=[edge, edge],
        in_specs=[smem, hbm],
        out_specs=[hbm, hbm],
        scratch_shapes=[
            pltpu.VMEM((2,) + edge.shape, bf16),
            pltpu.SemaphoreType.DMA((8,)),
            pltpu.SemaphoreType.DMA((8,)),
        ],
        compiler_params=params(60),
        name="pick",
    )(core, p_blocks)
    outward = [(i, (i + (1 if i % 2 else -1)) % devices) for i in range(devices)]
    inward = [(i, i ^ 1) for i in range(devices)]
    outer, inner, edge_cols = lax.optimization_barrier((outer, inner, cols_p))
    p_slow = permuted(outer, outward)
    p_fast = permuted(inner, inward)
    edge_cols = jnp.stack([edge_cols[:AGG], edge_cols[NB - AGG :]])
    cols_slow = permuted(edge_cols[parity], outward)
    cols_fast = permuted(edge_cols[1 - parity], inward)

    def slots(cols, agg):
        return (cols - agg + H) % count_agg

    own_agg = jnp.arange(NB, dtype=jnp.int32)[:, None] // AGG
    inv_own = inverse_index(slots(cols_p, first_agg + own_agg) + own_agg + 1, COLS, KP)
    fast_place = NC * (1 - parity) - parity
    inv_fast = inverse_index(slots(cols_fast, first_agg + fast_place) + fast_place + 1, COLS, KP)
    slow_place = NC * parity - (1 - parity)
    inv_slow = inverse_index(slots(cols_slow, first_agg + slow_place) + 2 * parity, WSLOT, KP)
    inv_fast, inv_slow = lax.optimization_barrier((inv_fast, inv_slow))
    inv_a = inverse_index((cols_a - first_row - (own_agg - 1) * AGG) % count_rows, 3 * AGG, KA)

    def block(rows, width, kind=bf16):
        return jax.ShapeDtypeStruct((rows, BS, width), kind)

    span = WINDOW * BS
    outs = [
        block(NC, span),
        block(NC, span),
        block(NC, span),
        block(FIRST, span),
        block(REST, span),
        block(REST, 2 * AW),
        block(FIRST, AW),
        block(REST, AW),
        block(NC, AW),
        block(FIRST, AW),
        block(REST, AW),
        block(WCOLS, 2 * AW),
        block(WSLOT, AW, jnp.float32),
        block(AGG, AW),
    ]
    (
        send_low,
        send_high,
        far,
        inner,
        send_rest,
        fast_rest,
        slow_first,
        slow_rest,
        slow_far,
        other_first,
        other_rest,
        wt_fast,
        rest,
        at_halo,
    ) = pl.pallas_call(
        fast_kernel,
        out_shape=outs,
        in_specs=[smem] * 3 + [hbm, hbm, vmem],
        out_specs=[hbm] * len(outs),
        scratch_shapes=[
            pltpu.VMEM((NB + AGG, BS, KP * BS), bf16),
            pltpu.VMEM((COLS, BS, EXT * BS), bf16),
            pltpu.VMEM((NC, 3 * AGG, BS, AW), bf16),
            pltpu.VMEM((LANES, LANES), bf16),
            pltpu.VMEM((KP + 1, BS, LANES), bf16),
            pltpu.VMEM((KP + 1, BS, LANES), bf16),
            pltpu.VMEM((KA + 1, BS, LANES), bf16),
            pltpu.VMEM((KA + 1, BS, LANES), bf16),
            pltpu.VMEM((ROWS + REST, BS, 2 * AW), bf16),
            pltpu.VMEM((ROWS + REST, BS, span), bf16),
            pltpu.VMEM((REST, BS, 2 * AW), bf16),
            pltpu.VMEM((ROWS + NC, BS, AW), bf16),
            pltpu.VMEM((ROWS, BS, AW), bf16),
            pltpu.VMEM((WCOLS, BS, 2 * AW), bf16),
            pltpu.VMEM((WSLOT, BS, AW), jnp.float32),
            pltpu.SemaphoreType.DMA(((NB + AGG) // QUAD,)),
            pltpu.SemaphoreType.DMA((len(outs) + 10,)),
        ],
        compiler_params=params(56),
        cost_estimate=cost(20 * 10**9, 30 * 10**6),
        name="fast",
    )(core, jnp.concatenate([inv_own, inv_fast]), inv_a, p_blocks, p_fast, a_blocks)

    low = permuted(send_low, inward)
    high = permuted(send_high, inward)
    other_first = permuted(other_first, inward)
    at_halo, rest = pl.pallas_call(
        stage_kernel,
        out_shape=[block(AGG, AW), block(WSLOT, AW, jnp.float32)],
        in_specs=[hbm] * 2,
        out_specs=[vmem] * 2,
        scratch_shapes=[pltpu.SemaphoreType.DMA((2,))],
        compiler_params=params(8),
        cost_estimate=cost(10**6, 10**6),
        name="stage",
    )(at_halo, rest)
    p_slow, low, high, other_first = lax.optimization_barrier((p_slow, low, high, other_first))

    wt_slow = pl.pallas_call(
        slow_kernel,
        out_shape=block(WCOLS, AW),
        in_specs=[smem] * 2 + [vmem] * 3,
        out_specs=vmem,
        scratch_shapes=[
            pltpu.VMEM((LANES, LANES), bf16),
            pltpu.VMEM((KP + 1, BS, LANES), bf16),
            pltpu.VMEM((KP + 1, BS, LANES), bf16),
            pltpu.VMEM((WSLOT, BS, AW), bf16),
        ],
        compiler_params=params(24),
        cost_estimate=cost(20 * 10**9, 200 * 10**6),
        name="slow",
    )(core, inv_slow, p_slow, at_halo, rest)
    wt_other = permuted(wt_slow, inward)

    wt_slow, low, high = lax.optimization_barrier((wt_slow, low, high))
    far = pl.pallas_call(
        far_kernel,
        out_shape=block(NC, span),
        in_specs=[vmem] * 3,
        out_specs=vmem,
        compiler_params=params(16),
        cost_estimate=cost(10**9, 10**7),
        name="far",
    )(slow_far, wt_slow, far)
    far, wt_slow = lax.optimization_barrier((far, wt_slow))
    mine = pl.pallas_call(
        mine_kernel,
        out_shape=block(FIRST, span, jnp.float32),
        in_specs=[vmem] * 5,
        out_specs=vmem,
        compiler_params=params(24),
        cost_estimate=cost(10**10, 100 * 10**6),
        name="mine",
    )(slow_first, wt_slow, inner, low, high)
    crossing = [i for i in range(devices) if i % 4 in (1, 2)]
    far_near = permuted(far, [(i, i ^ 3) for i in crossing])
    relay, direct = pl.pallas_call(
        join_first_kernel,
        out_shape=[block(NC, span), block(NC, span, jnp.float32)],
        in_specs=[vmem] * 3,
        out_specs=[vmem] * 2,
        compiler_params=params(16),
        cost_estimate=cost(10**6, 10**5),
        name="join_first",
    )(other_first, wt_other, mine)
    relay, direct, far_near, far, send_rest, other_rest = lax.optimization_barrier(
        (relay, direct, far_near, far, send_rest, other_rest)
    )
    straight = [i for i in range(devices) if i % 4 in (0, 3)]
    far = permuted(far, [(i, (i + (5 if i % 2 else -5)) % devices) for i in straight])
    arrived_rest = permuted(send_rest, inward)
    other_rest = permuted(other_rest, inward)
    along_x = [(i, i ^ 2) for i in range(devices)]
    x_sign = [1 if i // 2 % 2 else -1 for i in range(devices)]
    relay = permuted(relay, along_x)

    def merge_rows(rows, other, name):
        return pl.pallas_call(
            merge_kernel,
            out_shape=block(NC, MERGED * BS),
            in_specs=[smem, vmem, vmem],
            out_specs=vmem,
            scratch_shapes=[pltpu.VMEM((BS, MERGED * BS), jnp.float32)],
            compiler_params=params(16),
            cost_estimate=cost(10**7, 10**7),
            name=name,
        )(core, rows, other)

    direct = merge_rows(direct, far_near, "merge_far")
    direct = permuted(direct, [(i, (i + 4 * x_sign[i]) % devices) for i in range(devices)])
    merge, pair, own = pl.pallas_call(
        join_rest_kernel,
        out_shape=[block(NC, span, jnp.float32), block(NC, span), block(NC, span, jnp.float32)],
        in_specs=[vmem] * 7,
        out_specs=[vmem] * 3,
        compiler_params=params(30),
        cost_estimate=cost(40 * 10**9, 200 * 10**6),
        name="join_rest",
    )(fast_rest, slow_rest, other_rest, wt_fast, wt_slow, wt_other, arrived_rest)
    relay, pair, far = lax.optimization_barrier((relay, pair, far))
    merged = merge_rows(merge, relay, "merge")
    merged = permuted(merged, [(i, (i - 4 * x_sign[i]) % devices) for i in range(devices)])
    pair = permuted(pair, along_x)

    total = block(NC, BAND * BS, jnp.float32)
    frame = pltpu.VMEM((BS, FRAME * BS), jnp.float32)
    early = pl.pallas_call(
        early_kernel,
        out_shape=total,
        in_specs=[smem] + [vmem] * 4,
        out_specs=vmem,
        scratch_shapes=[frame],
        compiler_params=params(16),
        cost_estimate=cost(10**10, 100 * 10**6),
        name="early",
    )(core, own, direct, pair, far)
    return pl.pallas_call(
        total_kernel,
        out_shape=total,
        in_specs=[smem] + [vmem] * 2,
        out_specs=hbm,
        scratch_shapes=[
            frame,
            pltpu.VMEM(total.shape, jnp.float32),
            pltpu.SemaphoreType.DMA((NC,)),
        ],
        compiler_params=params(20),
        cost_estimate=cost(10**7, 10**7),
        name="total",
    )(core, early, merged)


def solution(mesh):
    in_specs = (P("dom", None, None), P("dom", None, None), P("dom", None), P("dom", None))
    out_specs = P("dom", None, None)
    return jax.shard_map(body, mesh=mesh, in_specs=in_specs, out_specs=out_specs, check_vma=False)
```

```python
import functools

import jax
import jax.numpy as jnp
from jax import lax
from jax.experimental import pallas as pl
from jax.experimental.pallas import tpu as pltpu
from jax.sharding import PartitionSpec as P

BS = 64
KA = 7
KP = 27
AGG = 8
H = 15
NC = 3
NB = 24
WIN = 31
WSLOT = 33
BAND = 63

QUAD = 4
LANES = QUAD * BS
EXT = NB + 2 * AGG
COLS = NC + 2 * H + 2
WCOLS = 40
WINDOW = 38
TILES = 10
GROUPS = 5
K = NB * BS
AW = AGG * BS
FRAME = 80
NT = (((1,), (1,)), ((), ()))
ROWS = NC * GROUPS
FIRST = 2 * NC
REST = ROWS - FIRST
MERGED = WINDOW + 6
FAR = 36


def eye(n):
    rows = lax.broadcasted_iota(jnp.int32, (n, n), 0)
    lanes = lax.broadcasted_iota(jnp.int32, (n, n), 1)
    return jnp.where(rows == lanes, 1.0, 0.0).astype(jnp.bfloat16)


def low_half():
    return lax.broadcasted_iota(jnp.int32, (BS, 2 * BS), 1) < BS


def places(device):
    return device[0] % 2, device[0] // 2 % 2


def transpose_quad(unit, block, turned, width):
    for start in range(0, width, LANES):
        size = min(LANES, width - start)
        part = lax.dot_general(
            unit[:size, :size],
            block[:, start : start + size],
            NT,
            preferred_element_type=jnp.float32,
        )
        turned[start // BS : (start + size) // BS] = part.astype(jnp.bfloat16).reshape(
            size // BS, BS, LANES
        )


def spread_quad(turned, index, first, store, count):
    half = low_half()
    for slot in range(count):
        for pair in range(2):
            lanes = slice(pair * 2 * BS, (pair + 1) * 2 * BS)
            left = turned[index[first + 2 * pair, slot], :, lanes]
            right = turned[index[first + 2 * pair + 1, slot], :, lanes]
            store(slot, pair, jnp.where(half, left, right))


def turn_and_spread(count, turn, spread, buffers):
    even, odd = buffers
    turn(0, even)

    def two(step):
        turn(2 * step + 1, odd)
        spread(2 * step, even)
        turn(2 * step + 2, even)
        spread(2 * step + 1, odd)

    if count > 2:
        pl.loop(0, count // 2 - 1)(two)

    turn(count - 1, odd)
    spread(count - 2, even)
    spread(count - 1, odd)


def fast_kernel(
    core,
    inv_p,
    inv_a,
    p_own,
    p_fast,
    a_own,
    send_low,
    send_high,
    far,
    inner,
    send_rest,
    fast_rest,
    slow_first,
    slow_rest,
    slow_far,
    other_first,
    other_rest,
    wt,
    rest,
    at_halo,
    p_buf,
    ext,
    at,
    unit,
    turned_p,
    turned_p2,
    turned_a,
    turned_a2,
    lhs,
    rows_buf,
    fast_buf,
    slow_buf,
    other_buf,
    wt_buf,
    rest_buf,
    in_sems,
    out_sems,
):
    s, x = places(core)
    own_quads = NB // QUAD
    halo_quads = AGG // QUAD

    def load(quad):
        if quad < own_quads:
            source = p_own.at[quad * QUAD : (quad + 1) * QUAD]
        else:
            source = p_fast.at[(quad - own_quads) * QUAD : (quad - own_quads + 1) * QUAD]
        target = p_buf.at[quad * QUAD : (quad + 1) * QUAD]
        return pltpu.make_async_copy(source, target, in_sems.at[quad])

    for quad in range(own_quads + halo_quads):
        load(quad).start()

    unit[...] = eye(LANES)
    for buffers, empty in (((turned_p, turned_p2), KP), ((turned_a, turned_a2), KA)):
        for buffer in buffers:
            buffer[empty] = jnp.zeros((BS, LANES), jnp.bfloat16)

    def turn_a(quad, turned):
        block = a_own[pl.ds(quad * QUAD, QUAD)].reshape(LANES, KA * BS)
        transpose_quad(unit, block, turned, KA * BS)

    def spread_a(quad, turned):
        agg = quad // halo_quads
        first_lane = (quad % halo_quads) * LANES

        def store(slot, pair, value):
            lane = pl.multiple_of(first_lane + pair * 2 * BS, 2 * BS)
            at[agg, slot, :, pl.ds(lane, 2 * BS)] = value

        spread_quad(turned, inv_a, quad * QUAD, store, 3 * AGG)

    turn_and_spread(own_quads, turn_a, spread_a, (turned_a, turned_a2))

    slow_agg = 2 * s
    halo_copy = pltpu.make_async_copy(at.at[slow_agg, pl.ds(16 * s, AGG)], at_halo, out_sems.at[0])
    halo_copy.start()

    def turn_p(quad, turned):
        block = p_buf[pl.ds(quad * QUAD, QUAD)].reshape(LANES, KP * BS)
        transpose_quad(unit, block, turned, KP * BS)

    def spread_p(quad, turned):
        own_lane = AW + quad * LANES
        halo_lane = (AW + K) * (1 - s) + (quad - own_quads) * LANES
        first_lane = jnp.where(quad < own_quads, own_lane, halo_lane)

        def store(slot, pair, value):
            lane = pl.multiple_of(first_lane + pair * 2 * BS, 2 * BS)
            ext[slot, :, pl.ds(lane, 2 * BS)] = value

        spread_quad(turned, inv_p, quad * QUAD, store, COLS)

    for quad in range(own_quads + halo_quads):
        load(quad).wait()
    turn_and_spread(own_quads + halo_quads, turn_p, spread_p, (turned_p, turned_p2))

    fast_lanes = pl.ds(pl.multiple_of(AW + (1 - s) * AW, AW), 2 * AW)
    slow_lanes = pl.ds(pl.multiple_of(AW + 2 * s * AW, AW), AW)
    for place, i in enumerate((1 + 2 * x, 4 * x, 4 - 4 * x, 3 - 2 * x, 2)):
        for j in range(NC):
            row = NC * place + j
            mine, other = 6 * i + 3 + j + 1, 6 * i + 6 * (1 - s) + j + 1
            if place < 2:
                lhs[row] = ext[other, :, fast_lanes]
                lhs[FIRST + NC + row] = ext[mine, :, fast_lanes]
            else:
                lhs[ROWS + row - FIRST] = ext[other, :, fast_lanes]
                fast_buf[row - FIRST] = ext[mine, :, fast_lanes]
            slow_buf[row] = ext[mine, :, slow_lanes]
            other_buf[row] = ext[other, :, slow_lanes]
    for j in range(NC):
        lhs[FIRST + j] = ext[30 * s + j + 1, :, fast_lanes]
        slow_buf[ROWS + j] = ext[30 * s + j + 1, :, slow_lanes]
    copies = [halo_copy]

    def write(source, target):
        copy = pltpu.make_async_copy(source, target, out_sems.at[len(copies)])
        copy.start()
        copies.append(copy)

    write(other_buf.at[:FIRST], other_first)
    write(other_buf.at[FIRST:], other_rest)
    write(fast_buf, fast_rest)
    write(slow_buf.at[:FIRST], slow_first)
    write(slow_buf.at[FIRST:ROWS], slow_rest)
    write(slow_buf.at[ROWS:], slow_far)

    wt_buf[0:7] = jnp.zeros((7, BS, 2 * AW), jnp.bfloat16)
    wt_buf[33:] = jnp.zeros((WCOLS - 33, BS, 2 * AW), jnp.bfloat16)
    chunk = WSLOT // 3

    @pl.loop(0, 2)
    def _(place):
        agg = place + 1 - s
        lane = pl.multiple_of(agg * AW, AW)
        target = pl.multiple_of(place * AW, AW)

        @pl.loop(0, 3)
        def _(part):
            first = agg + part * chunk
            left = ext[pl.ds(first, chunk), :, pl.ds(lane, 3 * AW)].reshape(chunk * BS, 3 * AW)
            value = jnp.dot(
                left, at[agg].reshape(3 * AW, AW), preferred_element_type=jnp.float32
            )
            wt_buf[pl.ds(3 * s + first, chunk), :, pl.ds(target, AW)] = value.astype(
                jnp.bfloat16
            ).reshape(chunk, BS, AW)

    write(wt_buf, wt)

    @pl.loop(0, 3)
    def _(part):
        lane = pl.multiple_of(AW + s * AW, AW)
        left = ext[pl.ds(slow_agg + part * chunk, chunk), :, pl.ds(lane, 2 * AW)]
        right = at[slow_agg, pl.ds(AGG - AGG * s, 2 * AGG)].reshape(2 * AW, AW)
        value = jnp.dot(
            left.reshape(chunk * BS, 2 * AW), right, preferred_element_type=jnp.float32
        )
        rest_buf[pl.ds(part * chunk, chunk)] = value.reshape(chunk, BS, AW)

    write(rest_buf, rest)

    def emit(tile, width):
        right = wt_buf[pl.ds(QUAD * tile, width // BS)].reshape(width, 2 * AW)
        left = lhs[...].reshape((ROWS + REST) * BS, 2 * AW)
        value = lax.dot_general(left, right, NT, preferred_element_type=jnp.float32)
        rows_buf[:, :, tile_lanes(tile, width)] = value.astype(jnp.bfloat16).reshape(
            ROWS + REST, BS, width
        )

    parts = (
        (send_low, 0),
        (send_high, NC),
        (far, FIRST),
        (inner, FIRST + NC),
        (send_rest, ROWS),
    )
    bounds = (0, 4, 8, TILES)
    for first, last in zip(bounds[:-1], bounds[1:]):

        @pl.loop(first, min(last, TILES - 1))
        def _(tile):
            emit(tile, LANES)

        if last == TILES:
            emit(TILES - 1, LANES // 2)
        lanes = slice(first * LANES, min(last * LANES, WINDOW * BS))
        for target, row in parts:
            rows = slice(row, row + target.shape[0])
            write(rows_buf.at[rows, :, lanes], target.at[:, :, lanes])
    for copy in copies:
        copy.wait()


def each_tile(step):
    @pl.loop(0, TILES - 1)
    def _(tile):
        step(tile, LANES)

    step(TILES - 1, LANES // 2)


def tile_dot(rows, cols, tile, width):
    left = rows[...].reshape(rows.shape[0] * BS, rows.shape[2])
    right = cols[pl.ds(QUAD * tile, width // BS)].reshape(width, cols.shape[2])
    value = lax.dot_general(left, right, NT, preferred_element_type=jnp.float32)
    return value.reshape(rows.shape[0], BS, width)


def tile_lanes(tile, width):
    return pl.ds(pl.multiple_of(tile * LANES, LANES), width)


def far_kernel(core, slow, wt_slow, far_fast, far):
    s, x = places(core)

    @pl.loop(0, FAR // QUAD)
    def _(tile):
        left = slow[...].reshape(NC * BS, AW)
        right = wt_slow[pl.ds(QUAD * tile + 2 * s, QUAD)].reshape(LANES, AW)
        value = lax.dot_general(left, right, NT, preferred_element_type=jnp.float32)
        lanes = pl.ds(pl.multiple_of(tile * LANES + 2 * BS * s, 2 * BS), LANES)
        value = value.reshape(NC, BS, LANES) + far_fast[:, :, lanes].astype(jnp.float32)
        far[:, :, tile_lanes(tile, LANES)] = value.astype(jnp.bfloat16)


def mine_kernel(slow, wt_slow, inner, low, high, out):
    def step(tile, width):
        lanes = tile_lanes(tile, width)
        near = tile_dot(slow, wt_slow, tile, width) + inner[:, :, lanes].astype(jnp.float32)
        out[:NC, :, lanes] = near[:NC] + low[:, :, lanes].astype(jnp.float32)
        out[NC:, :, lanes] = near[NC:] + high[:, :, lanes].astype(jnp.float32)

    each_tile(step)


def slow_kernel(core, inv_slow, p_slow, at_halo, rest, wt, unit, turned_p, turned_p2, ext):
    s, x = places(core)
    unit[...] = eye(LANES)
    for buffer in (turned_p, turned_p2):
        buffer[KP] = jnp.zeros((BS, LANES), jnp.bfloat16)

    def turn(quad, turned):
        block = p_slow[quad * QUAD : (quad + 1) * QUAD].reshape(LANES, KP * BS)
        transpose_quad(unit, block, turned, KP * BS)

    def spread(quad, turned):
        def store(slot, pair, value):
            lane = quad * LANES + pair * 2 * BS
            ext[slot, :, lane : lane + 2 * BS] = value

        spread_quad(turned, inv_slow, quad * QUAD, store, WSLOT)

    turn_and_spread(AGG // QUAD, turn, spread, (turned_p, turned_p2))
    wt[0:5] = jnp.zeros((5, BS, AW), jnp.bfloat16)
    wt[WSLOT:] = jnp.zeros((WCOLS - WSLOT, BS, AW), jnp.bfloat16)
    chunk = WSLOT // 3

    @pl.loop(0, 3)
    def _(part):
        rows = pl.ds(part * chunk, chunk)
        value = jnp.dot(
            ext[rows].reshape(chunk * BS, AW),
            at_halo[...].reshape(AW, AW),
            preferred_element_type=jnp.float32,
        )
        value = value.reshape(chunk, BS, AW) + rest[rows]
        wt[pl.ds(5 * s + part * chunk, chunk)] = value.astype(jnp.bfloat16)


def join_first_kernel(other, wt_other, mine, relay, direct):
    def step(tile, width):
        lanes = tile_lanes(tile, width)
        value = tile_dot(other, wt_other, tile, width) + mine[:, :, lanes]
        relay[:, :, lanes] = value[:NC].astype(jnp.bfloat16)
        direct[:, :, lanes] = value[NC:]

    each_tile(step)


def join_rest_kernel(fast, slow, other, wt_fast, wt_slow, wt_other, arrived, merge, pair, own):
    def step(tile, width):
        lanes = tile_lanes(tile, width)
        value = tile_dot(fast, wt_fast, tile, width) + tile_dot(slow, wt_slow, tile, width)
        value = value + tile_dot(other, wt_other, tile, width)
        value = value + arrived[:, :, lanes].astype(jnp.float32)
        merge[:, :, lanes] = value[:NC]
        pair[:, :, lanes] = value[NC : 2 * NC].astype(jnp.bfloat16)
        own[:, :, lanes] = value[2 * NC :]

    each_tile(step)


def stage_kernel(at_halo, rest, at_out, rest_out, sems):
    copies = [
        pltpu.make_async_copy(at_halo, at_out, sems.at[0]),
        pltpu.make_async_copy(rest, rest_out, sems.at[1]),
    ]
    for copy in copies:
        copy.start()
    for copy in copies:
        copy.wait()


def merge_kernel(core, rows, other, out, frame, *, shift):
    s, x = places(core)
    step = 6 * BS
    for j in range(NC):
        frame[...] = jnp.zeros_like(frame)
        frame[:, pl.ds(pl.multiple_of(step * x, step), WINDOW * BS)] = rows[j]
        lane = pl.multiple_of(step * (1 - x) + shift * BS * x, 2 * BS)
        lanes = pl.ds(lane, other.shape[2])
        frame[:, lanes] += other[j].astype(jnp.float32)
        out[j] = frame[...].astype(jnp.bfloat16)


def in_frame(s, j, frame, messages, store):
    odd = (j + 1 - s) % 2
    frame[...] = jnp.zeros_like(frame)
    for message, start in messages:
        lane = pl.multiple_of((start - odd + 8) * BS, 2 * BS)
        frame[:, pl.ds(lane, message.shape[2])] += message[j].astype(jnp.float32)
    first, last = 8 * BS, (8 + BAND) * BS

    @pl.when(odd == 0)
    def _():
        store(frame[:, first:last])

    @pl.when(odd == 1)
    def _():
        store(frame[:, first - BS : last - BS])


def early_kernel(core, own, direct, pair, out, frame):
    s, x = places(core)
    for j in range(NC):
        top = 27 - 3 * s - j
        messages = [(own, top - 12), (direct, top - 30 * x), (pair, top - 6 - 12 * x)]

        def store(value, j=j):
            out[j] = value

        in_frame(s, j, frame, messages, store)


def total_kernel(core, early, merged, far, out, frame, buf, sems):
    s, x = places(core)
    copies = []
    for j in range(NC):
        far_start = jnp.where(s == 1, 30 - j, -1 - j)

        def store(value, j=j):
            buf[j] = value + early[j]

        in_frame(s, j, frame, [(merged, 3 - 3 * s - j + 18 * x), (far, far_start)], store)
        copy = pltpu.make_async_copy(buf.at[j], out.at[j], sems.at[j])
        copy.start()
        copies.append(copy)
    for copy in copies:
        copy.wait()


def pick_kernel(core, source, outer, inner, buf, in_sems, out_sems):
    s, x = places(core)
    step = AGG // 4
    reads, writes = [], []
    for side, (target, which) in enumerate(((outer, s), (inner, 1 - s))):
        for k in range(4):
            n = len(reads)
            rows = pl.ds((NB - AGG) * which + k * step, step)
            part = buf.at[side, k * step : (k + 1) * step]
            into = target.at[k * step : (k + 1) * step]
            reads.append(pltpu.make_async_copy(source.at[rows], part, in_sems.at[n]))
            writes.append(pltpu.make_async_copy(part, into, out_sems.at[n]))
    for copy in reads:
        copy.start()
    for read, write in zip(reads, writes):
        read.wait()
        write.start()
    for copy in writes:
        copy.wait()


def permuted(block, pairs):
    return lax.ppermute(block, "dom", pairs)


def inverse_index(offset, slots, empty):
    order = jnp.arange(offset.shape[1], dtype=jnp.int32)[None, :, None]
    hit = offset[:, :, None] == jnp.arange(slots, dtype=jnp.int32)[None, None, :]
    return empty + jnp.sum(jnp.where(hit, order - empty, 0), axis=1)


def body(a_blocks, p_blocks, cols_a, cols_p):
    devices = lax.axis_size("dom")
    device = lax.axis_index("dom")
    count_agg = NC * devices
    count_rows = NB * devices
    first_agg = device * NC
    first_row = device * NB
    core = device.astype(jnp.int32).reshape(1)

    def shifted(distance):
        return [(i, (i + distance) % devices) for i in range(devices)]

    parity = device % 2
    smem = pl.BlockSpec(memory_space=pltpu.SMEM)
    vmem = pl.BlockSpec(memory_space=pltpu.VMEM)
    hbm = pl.BlockSpec(memory_space=pltpu.HBM)
    bf16 = jnp.bfloat16

    def params(mebibytes):
        return pltpu.CompilerParams(vmem_limit_bytes=mebibytes * 1024 * 1024)

    def cost(flops, size):
        return pl.CostEstimate(flops=flops, bytes_accessed=size, transcendentals=0)

    edge = jax.ShapeDtypeStruct((AGG,) + p_blocks.shape[1:], bf16)
    outer, inner = pl.pallas_call(
        pick_kernel,
        out_shape=[edge, edge],
        in_specs=[smem, hbm],
        out_specs=[hbm, hbm],
        scratch_shapes=[
            pltpu.VMEM((2,) + edge.shape, bf16),
            pltpu.SemaphoreType.DMA((8,)),
            pltpu.SemaphoreType.DMA((8,)),
        ],
        compiler_params=params(60),
        name="pick",
    )(core, p_blocks)
    outward = [(i, (i + (1 if i % 2 else -1)) % devices) for i in range(devices)]
    inward = [(i, i ^ 1) for i in range(devices)]
    outer, inner, edge_cols = lax.optimization_barrier((outer, inner, cols_p))
    p_slow = permuted(outer, outward)
    p_fast = permuted(inner, inward)
    edge_cols = jnp.stack([edge_cols[:AGG], edge_cols[NB - AGG :]])
    cols_slow = permuted(edge_cols[parity], outward)
    cols_fast = permuted(edge_cols[1 - parity], inward)

    def slots(cols, agg):
        return (cols - agg + H) % count_agg

    own_agg = jnp.arange(NB, dtype=jnp.int32)[:, None] // AGG
    inv_own = inverse_index(slots(cols_p, first_agg + own_agg) + own_agg + 1, COLS, KP)
    fast_place = NC * (1 - parity) - parity
    inv_fast = inverse_index(slots(cols_fast, first_agg + fast_place) + fast_place + 1, COLS, KP)
    slow_place = NC * parity - (1 - parity)
    inv_slow = inverse_index(slots(cols_slow, first_agg + slow_place) + 2 * parity, WSLOT, KP)
    inv_fast, inv_slow = lax.optimization_barrier((inv_fast, inv_slow))
    inv_a = inverse_index((cols_a - first_row - (own_agg - 1) * AGG) % count_rows, 3 * AGG, KA)

    def block(rows, width, kind=bf16):
        return jax.ShapeDtypeStruct((rows, BS, width), kind)

    span = WINDOW * BS
    outs = [
        block(NC, span),
        block(NC, span),
        block(NC, span),
        block(FIRST, span),
        block(REST, span),
        block(REST, 2 * AW),
        block(FIRST, AW),
        block(REST, AW),
        block(NC, AW),
        block(FIRST, AW),
        block(REST, AW),
        block(WCOLS, 2 * AW),
        block(WSLOT, AW, jnp.float32),
        block(AGG, AW),
    ]
    (
        send_low,
        send_high,
        far,
        inner,
        send_rest,
        fast_rest,
        slow_first,
        slow_rest,
        slow_far,
        other_first,
        other_rest,
        wt_fast,
        rest,
        at_halo,
    ) = pl.pallas_call(
        fast_kernel,
        out_shape=outs,
        in_specs=[smem] * 3 + [hbm, hbm, vmem],
        out_specs=[hbm] * len(outs),
        scratch_shapes=[
            pltpu.VMEM((NB + AGG, BS, KP * BS), bf16),
            pltpu.VMEM((COLS, BS, EXT * BS), bf16),
            pltpu.VMEM((NC, 3 * AGG, BS, AW), bf16),
            pltpu.VMEM((LANES, LANES), bf16),
            pltpu.VMEM((KP + 1, BS, LANES), bf16),
            pltpu.VMEM((KP + 1, BS, LANES), bf16),
            pltpu.VMEM((KA + 1, BS, LANES), bf16),
            pltpu.VMEM((KA + 1, BS, LANES), bf16),
            pltpu.VMEM((ROWS + REST, BS, 2 * AW), bf16),
            pltpu.VMEM((ROWS + REST, BS, span), bf16),
            pltpu.VMEM((REST, BS, 2 * AW), bf16),
            pltpu.VMEM((ROWS + NC, BS, AW), bf16),
            pltpu.VMEM((ROWS, BS, AW), bf16),
            pltpu.VMEM((WCOLS, BS, 2 * AW), bf16),
            pltpu.VMEM((WSLOT, BS, AW), jnp.float32),
            pltpu.SemaphoreType.DMA(((NB + AGG) // QUAD,)),
            pltpu.SemaphoreType.DMA((len(outs) + 10,)),
        ],
        compiler_params=params(56),
        cost_estimate=cost(20 * 10**9, 30 * 10**6),
        name="fast",
    )(core, jnp.concatenate([inv_own, inv_fast]), inv_a, p_blocks, p_fast, a_blocks)

    low = permuted(send_low, inward)
    high = permuted(send_high, inward)
    other_first = permuted(other_first, inward)
    at_halo, rest = pl.pallas_call(
        stage_kernel,
        out_shape=[block(AGG, AW), block(WSLOT, AW, jnp.float32)],
        in_specs=[hbm] * 2,
        out_specs=[vmem] * 2,
        scratch_shapes=[pltpu.SemaphoreType.DMA((2,))],
        compiler_params=params(8),
        cost_estimate=cost(10**6, 10**6),
        name="stage",
    )(at_halo, rest)
    p_slow, low, high, other_first = lax.optimization_barrier((p_slow, low, high, other_first))

    wt_slow = pl.pallas_call(
        slow_kernel,
        out_shape=block(WCOLS, AW),
        in_specs=[smem] * 2 + [vmem] * 3,
        out_specs=vmem,
        scratch_shapes=[
            pltpu.VMEM((LANES, LANES), bf16),
            pltpu.VMEM((KP + 1, BS, LANES), bf16),
            pltpu.VMEM((KP + 1, BS, LANES), bf16),
            pltpu.VMEM((WSLOT, BS, AW), bf16),
        ],
        compiler_params=params(24),
        cost_estimate=cost(20 * 10**9, 200 * 10**6),
        name="slow",
    )(core, inv_slow, p_slow, at_halo, rest)
    wt_other = permuted(wt_slow, inward)

    wt_slow, low, high = lax.optimization_barrier((wt_slow, low, high))
    far = pl.pallas_call(
        far_kernel,
        out_shape=block(NC, FAR * BS),
        in_specs=[smem] + [vmem] * 3,
        out_specs=vmem,
        compiler_params=params(16),
        cost_estimate=cost(10**9, 10**7),
        name="far",
    )(core, slow_far, wt_slow, far)
    far, wt_slow = lax.optimization_barrier((far, wt_slow))
    mine = pl.pallas_call(
        mine_kernel,
        out_shape=block(FIRST, span, jnp.float32),
        in_specs=[vmem] * 5,
        out_specs=vmem,
        compiler_params=params(24),
        cost_estimate=cost(10**10, 100 * 10**6),
        name="mine",
    )(slow_first, wt_slow, inner, low, high)
    crossing = [i for i in range(devices) if i % 4 in (1, 2)]
    far_near = permuted(far, [(i, i ^ 3) for i in crossing])
    relay, direct = pl.pallas_call(
        join_first_kernel,
        out_shape=[block(NC, span), block(NC, span, jnp.float32)],
        in_specs=[vmem] * 3,
        out_specs=[vmem] * 2,
        compiler_params=params(16),
        cost_estimate=cost(10**6, 10**5),
        name="join_first",
    )(other_first, wt_other, mine)
    relay, direct, far_near, send_rest, other_rest = lax.optimization_barrier(
        (relay, direct, far_near, send_rest, other_rest)
    )
    arrived_rest = permuted(send_rest, inward)
    other_rest = permuted(other_rest, inward)
    along_x = [(i, i ^ 2) for i in range(devices)]
    x_sign = [1 if i // 2 % 2 else -1 for i in range(devices)]
    relay = permuted(relay, along_x)

    def merge_rows(rows, other, shift, name):
        return pl.pallas_call(
            functools.partial(merge_kernel, shift=shift),
            out_shape=block(NC, MERGED * BS),
            in_specs=[smem, vmem, vmem],
            out_specs=vmem,
            scratch_shapes=[pltpu.VMEM((BS, MERGED * BS), jnp.float32)],
            compiler_params=params(16),
            cost_estimate=cost(10**7, 10**7),
            name=name,
        )(core, rows, other)

    direct = merge_rows(direct, far_near, 2, "merge_far")
    direct = permuted(direct, [(i, (i + 4 * x_sign[i]) % devices) for i in range(devices)])
    merge, pair, own = pl.pallas_call(
        join_rest_kernel,
        out_shape=[block(NC, span, jnp.float32), block(NC, span), block(NC, span, jnp.float32)],
        in_specs=[vmem] * 7,
        out_specs=[vmem] * 3,
        compiler_params=params(30),
        cost_estimate=cost(40 * 10**9, 200 * 10**6),
        name="join_rest",
    )(fast_rest, slow_rest, other_rest, wt_fast, wt_slow, wt_other, arrived_rest)
    relay, pair = lax.optimization_barrier((relay, pair))
    merged = merge_rows(merge, relay, 0, "merge")
    merged = permuted(merged, [(i, (i - 4 * x_sign[i]) % devices) for i in range(devices)])
    pair = permuted(pair, along_x)
    pair, far = lax.optimization_barrier((pair, far))
    straight = [i for i in range(devices) if i % 4 in (0, 3)]
    far = permuted(far, [(i, (i + (5 if i % 2 else -5)) % devices) for i in straight])

    total = block(NC, BAND * BS, jnp.float32)
    frame = pltpu.VMEM((BS, FRAME * BS), jnp.float32)
    early = pl.pallas_call(
        early_kernel,
        out_shape=total,
        in_specs=[smem] + [vmem] * 3,
        out_specs=vmem,
        scratch_shapes=[frame],
        compiler_params=params(16),
        cost_estimate=cost(10**10, 100 * 10**6),
        name="early",
    )(core, own, direct, pair)
    return pl.pallas_call(
        total_kernel,
        out_shape=total,
        in_specs=[smem] + [vmem] * 3,
        out_specs=hbm,
        scratch_shapes=[
            frame,
            pltpu.VMEM(total.shape, jnp.float32),
            pltpu.SemaphoreType.DMA((NC,)),
        ],
        compiler_params=params(20),
        cost_estimate=cost(10**7, 10**7),
        name="total",
    )(core, early, merged, far)


def solution(mesh):
    in_specs = (P("dom", None, None), P("dom", None, None), P("dom", None), P("dom", None))
    out_specs = P("dom", None, None)
    return jax.shard_map(body, mesh=mesh, in_specs=in_specs, out_specs=out_specs, check_vma=False)
```

```python
import functools

import jax
import jax.numpy as jnp
from jax import lax
from jax.experimental import pallas as pl
from jax.experimental.pallas import tpu as pltpu
from jax.sharding import PartitionSpec as P

BS = 64
KA = 7
KP = 27
AGG = 8
H = 15
NC = 3
NB = 24
WIN = 31
WSLOT = 33
BAND = 63

QUAD = 4
LANES = QUAD * BS
EXT = NB + 2 * AGG
COLS = NC + 2 * H + 2
WCOLS = 40
WINDOW = 38
TILES = 10
GROUPS = 5
K = NB * BS
AW = AGG * BS
FRAME = 80
NT = (((1,), (1,)), ((), ()))
ROWS = NC * GROUPS
FIRST = 2 * NC
REST = ROWS - FIRST
MERGED = WINDOW + 6
FAR = 36


def eye(n):
    rows = lax.broadcasted_iota(jnp.int32, (n, n), 0)
    lanes = lax.broadcasted_iota(jnp.int32, (n, n), 1)
    return jnp.where(rows == lanes, 1.0, 0.0).astype(jnp.bfloat16)


def low_half():
    return lax.broadcasted_iota(jnp.int32, (BS, 2 * BS), 1) < BS


def places(device):
    return device[0] % 2, device[0] // 2 % 2


def transpose_quad(unit, block, turned, width):
    for start in range(0, width, LANES):
        size = min(LANES, width - start)
        part = lax.dot_general(
            unit[:size, :size],
            block[:, start : start + size],
            NT,
            preferred_element_type=jnp.float32,
        )
        turned[start // BS : (start + size) // BS] = part.astype(jnp.bfloat16).reshape(
            size // BS, BS, LANES
        )


def spread_quad(turned, index, first, store, count):
    half = low_half()
    for slot in range(count):
        for pair in range(2):
            lanes = slice(pair * 2 * BS, (pair + 1) * 2 * BS)
            left = turned[index[first + 2 * pair, slot], :, lanes]
            right = turned[index[first + 2 * pair + 1, slot], :, lanes]
            store(slot, pair, jnp.where(half, left, right))


def turn_and_spread(count, turn, spread, buffers):
    even, odd = buffers
    turn(0, even)

    def two(step):
        turn(2 * step + 1, odd)
        spread(2 * step, even)
        turn(2 * step + 2, even)
        spread(2 * step + 1, odd)

    if count > 2:
        pl.loop(0, count // 2 - 1)(two)

    turn(count - 1, odd)
    spread(count - 2, even)
    spread(count - 1, odd)


def fast_kernel(
    core,
    inv_p,
    inv_a,
    p_own,
    p_fast,
    a_own,
    send_low,
    send_high,
    far,
    inner,
    send_rest,
    fast_rest,
    slow_first,
    slow_rest,
    slow_far,
    other_first,
    other_rest,
    wt,
    rest,
    at_halo,
    p_buf,
    ext,
    at,
    unit,
    turned_p,
    turned_p2,
    turned_a,
    turned_a2,
    lhs,
    rows_buf,
    fast_buf,
    slow_buf,
    other_buf,
    wt_buf,
    rest_buf,
    in_sems,
    out_sems,
):
    s, x = places(core)
    own_quads = NB // QUAD
    halo_quads = AGG // QUAD

    def load(quad):
        if quad < own_quads:
            source = p_own.at[quad * QUAD : (quad + 1) * QUAD]
        else:
            source = p_fast.at[(quad - own_quads) * QUAD : (quad - own_quads + 1) * QUAD]
        target = p_buf.at[quad * QUAD : (quad + 1) * QUAD]
        return pltpu.make_async_copy(source, target, in_sems.at[quad])

    for quad in range(own_quads + halo_quads):
        load(quad).start()

    unit[...] = eye(LANES)
    for buffers, empty in (((turned_p, turned_p2), KP), ((turned_a, turned_a2), KA)):
        for buffer in buffers:
            buffer[empty] = jnp.zeros((BS, LANES), jnp.bfloat16)

    def turn_a(quad, turned):
        block = a_own[pl.ds(quad * QUAD, QUAD)].reshape(LANES, KA * BS)
        transpose_quad(unit, block, turned, KA * BS)

    def spread_a(quad, turned):
        agg = quad // halo_quads
        first_lane = (quad % halo_quads) * LANES

        def store(slot, pair, value):
            lane = pl.multiple_of(first_lane + pair * 2 * BS, 2 * BS)
            at[agg, slot, :, pl.ds(lane, 2 * BS)] = value

        spread_quad(turned, inv_a, quad * QUAD, store, 3 * AGG)

    turn_and_spread(own_quads, turn_a, spread_a, (turned_a, turned_a2))

    slow_agg = 2 * s
    halo_copy = pltpu.make_async_copy(at.at[slow_agg, pl.ds(16 * s, AGG)], at_halo, out_sems.at[0])
    halo_copy.start()

    def turn_p(quad, turned):
        block = p_buf[pl.ds(quad * QUAD, QUAD)].reshape(LANES, KP * BS)
        transpose_quad(unit, block, turned, KP * BS)

    def spread_p(quad, turned):
        own_lane = AW + quad * LANES
        halo_lane = (AW + K) * (1 - s) + (quad - own_quads) * LANES
        first_lane = jnp.where(quad < own_quads, own_lane, halo_lane)

        def store(slot, pair, value):
            lane = pl.multiple_of(first_lane + pair * 2 * BS, 2 * BS)
            ext[slot, :, pl.ds(lane, 2 * BS)] = value

        spread_quad(turned, inv_p, quad * QUAD, store, COLS)

    for quad in range(own_quads + halo_quads):
        load(quad).wait()
    turn_and_spread(own_quads + halo_quads, turn_p, spread_p, (turned_p, turned_p2))

    fast_lanes = pl.ds(pl.multiple_of(AW + (1 - s) * AW, AW), 2 * AW)
    slow_lanes = pl.ds(pl.multiple_of(AW + 2 * s * AW, AW), AW)
    for place, i in enumerate((1 + 2 * x, 4 * x, 4 - 4 * x, 3 - 2 * x, 2)):
        for j in range(NC):
            row = NC * place + j
            mine, other = 6 * i + 3 + j + 1, 6 * i + 6 * (1 - s) + j + 1
            if place < 2:
                lhs[row] = ext[other, :, fast_lanes]
                lhs[FIRST + NC + row] = ext[mine, :, fast_lanes]
            else:
                lhs[ROWS + row - FIRST] = ext[other, :, fast_lanes]
                fast_buf[row - FIRST] = ext[mine, :, fast_lanes]
            slow_buf[row] = ext[mine, :, slow_lanes]
            other_buf[row] = ext[other, :, slow_lanes]
    for j in range(NC):
        lhs[FIRST + j] = ext[30 * s + j + 1, :, fast_lanes]
        slow_buf[ROWS + j] = ext[30 * s + j + 1, :, slow_lanes]
    copies = [halo_copy]

    def write(source, target):
        copy = pltpu.make_async_copy(source, target, out_sems.at[len(copies)])
        copy.start()
        copies.append(copy)

    write(other_buf.at[:FIRST], other_first)
    write(other_buf.at[FIRST:], other_rest)
    write(fast_buf, fast_rest)
    write(slow_buf.at[:FIRST], slow_first)
    write(slow_buf.at[FIRST:ROWS], slow_rest)
    write(slow_buf.at[ROWS:], slow_far)

    wt_buf[0:7] = jnp.zeros((7, BS, 2 * AW), jnp.bfloat16)
    wt_buf[33:] = jnp.zeros((WCOLS - 33, BS, 2 * AW), jnp.bfloat16)
    chunk = WSLOT // 3

    @pl.loop(0, 2)
    def _(place):
        agg = place + 1 - s
        lane = pl.multiple_of(agg * AW, AW)
        target = pl.multiple_of(place * AW, AW)

        @pl.loop(0, 3)
        def _(part):
            first = agg + part * chunk
            left = ext[pl.ds(first, chunk), :, pl.ds(lane, 3 * AW)].reshape(chunk * BS, 3 * AW)
            value = jnp.dot(
                left, at[agg].reshape(3 * AW, AW), preferred_element_type=jnp.float32
            )
            wt_buf[pl.ds(3 * s + first, chunk), :, pl.ds(target, AW)] = value.astype(
                jnp.bfloat16
            ).reshape(chunk, BS, AW)

    write(wt_buf, wt)

    @pl.loop(0, 3)
    def _(part):
        lane = pl.multiple_of(AW + s * AW, AW)
        left = ext[pl.ds(slow_agg + part * chunk, chunk), :, pl.ds(lane, 2 * AW)]
        right = at[slow_agg, pl.ds(AGG - AGG * s, 2 * AGG)].reshape(2 * AW, AW)
        value = jnp.dot(
            left.reshape(chunk * BS, 2 * AW), right, preferred_element_type=jnp.float32
        )
        rest_buf[pl.ds(part * chunk, chunk)] = value.reshape(chunk, BS, AW)

    write(rest_buf, rest)

    def emit(tile, width):
        right = wt_buf[pl.ds(QUAD * tile, width // BS)].reshape(width, 2 * AW)
        left = lhs[...].reshape((ROWS + REST) * BS, 2 * AW)
        value = lax.dot_general(left, right, NT, preferred_element_type=jnp.float32)
        rows_buf[:, :, tile_lanes(tile, width)] = value.astype(jnp.bfloat16).reshape(
            ROWS + REST, BS, width
        )

    parts = (
        (send_low, 0),
        (send_high, NC),
        (far, FIRST),
        (inner, FIRST + NC),
        (send_rest, ROWS),
    )
    bounds = (0, 4, 8, TILES)
    for first, last in zip(bounds[:-1], bounds[1:]):

        @pl.loop(first, min(last, TILES - 1))
        def _(tile):
            emit(tile, LANES)

        if last == TILES:
            emit(TILES - 1, LANES // 2)
        lanes = slice(first * LANES, min(last * LANES, WINDOW * BS))
        for target, row in parts:
            rows = slice(row, row + target.shape[0])
            write(rows_buf.at[rows, :, lanes], target.at[:, :, lanes])
    for copy in copies:
        copy.wait()


def each_tile(step):
    @pl.loop(0, TILES - 1)
    def _(tile):
        step(tile, LANES)

    step(TILES - 1, LANES // 2)


def tile_dot(rows, cols, tile, width):
    left = rows[...].reshape(rows.shape[0] * BS, rows.shape[2])
    right = cols[pl.ds(QUAD * tile, width // BS)].reshape(width, cols.shape[2])
    value = lax.dot_general(left, right, NT, preferred_element_type=jnp.float32)
    return value.reshape(rows.shape[0], BS, width)


def tile_lanes(tile, width):
    return pl.ds(pl.multiple_of(tile * LANES, LANES), width)


def far_kernel(core, slow, wt_slow, far_fast, far):
    s, x = places(core)

    @pl.loop(0, FAR // QUAD)
    def _(tile):
        left = slow[...].reshape(NC * BS, AW)
        right = wt_slow[pl.ds(QUAD * tile + 2 * s, QUAD)].reshape(LANES, AW)
        value = lax.dot_general(left, right, NT, preferred_element_type=jnp.float32)
        lanes = pl.ds(pl.multiple_of(tile * LANES + 2 * BS * s, 2 * BS), LANES)
        value = value.reshape(NC, BS, LANES) + far_fast[:, :, lanes].astype(jnp.float32)
        far[:, :, tile_lanes(tile, LANES)] = value.astype(jnp.bfloat16)


def mine_kernel(slow, wt_slow, inner, low, high, out):
    def step(tile, width):
        lanes = tile_lanes(tile, width)
        near = tile_dot(slow, wt_slow, tile, width) + inner[:, :, lanes].astype(jnp.float32)
        out[:NC, :, lanes] = near[:NC] + low[:, :, lanes].astype(jnp.float32)
        out[NC:, :, lanes] = near[NC:] + high[:, :, lanes].astype(jnp.float32)

    each_tile(step)


def slow_kernel(core, inv_slow, p_slow, at_halo, rest, wt, unit, turned_p, turned_p2, ext):
    s, x = places(core)
    unit[...] = eye(LANES)
    for buffer in (turned_p, turned_p2):
        buffer[KP] = jnp.zeros((BS, LANES), jnp.bfloat16)

    def turn(quad, turned):
        block = p_slow[quad * QUAD : (quad + 1) * QUAD].reshape(LANES, KP * BS)
        transpose_quad(unit, block, turned, KP * BS)

    def spread(quad, turned):
        def store(slot, pair, value):
            lane = quad * LANES + pair * 2 * BS
            ext[slot, :, lane : lane + 2 * BS] = value

        spread_quad(turned, inv_slow, quad * QUAD, store, WSLOT)

    turn_and_spread(AGG // QUAD, turn, spread, (turned_p, turned_p2))
    wt[0:5] = jnp.zeros((5, BS, AW), jnp.bfloat16)
    wt[WSLOT:] = jnp.zeros((WCOLS - WSLOT, BS, AW), jnp.bfloat16)
    chunk = WSLOT // 3

    @pl.loop(0, 3)
    def _(part):
        rows = pl.ds(part * chunk, chunk)
        value = jnp.dot(
            ext[rows].reshape(chunk * BS, AW),
            at_halo[...].reshape(AW, AW),
            preferred_element_type=jnp.float32,
        )
        value = value.reshape(chunk, BS, AW) + rest[rows]
        wt[pl.ds(5 * s + part * chunk, chunk)] = value.astype(jnp.bfloat16)


def join_first_kernel(other, wt_other, mine, relay, direct):
    def step(tile, width):
        lanes = tile_lanes(tile, width)
        value = tile_dot(other, wt_other, tile, width) + mine[:, :, lanes]
        relay[:, :, lanes] = value[:NC].astype(jnp.bfloat16)
        direct[:, :, lanes] = value[NC:]

    each_tile(step)


def join_rest_kernel(fast, slow, other, wt_fast, wt_slow, wt_other, arrived, merge, pair, own):
    def step(tile, width):
        lanes = tile_lanes(tile, width)
        value = tile_dot(fast, wt_fast, tile, width) + tile_dot(slow, wt_slow, tile, width)
        value = value + tile_dot(other, wt_other, tile, width)
        value = value + arrived[:, :, lanes].astype(jnp.float32)
        merge[:, :, lanes] = value[:NC]
        pair[:, :, lanes] = value[NC : 2 * NC].astype(jnp.bfloat16)
        own[:, :, lanes] = value[2 * NC :]

    each_tile(step)


def stage_kernel(at_halo, rest, at_out, rest_out, sems):
    copies = [
        pltpu.make_async_copy(at_halo, at_out, sems.at[0]),
        pltpu.make_async_copy(rest, rest_out, sems.at[1]),
    ]
    for copy in copies:
        copy.start()
    for copy in copies:
        copy.wait()


def merge_kernel(core, rows, other, out, frame, *, shift):
    s, x = places(core)
    step = 6 * BS
    for j in range(NC):
        frame[...] = jnp.zeros_like(frame)
        frame[:, pl.ds(pl.multiple_of(step * x, step), WINDOW * BS)] = rows[j]
        lane = pl.multiple_of(step * (1 - x) + shift * BS * x, 2 * BS)
        lanes = pl.ds(lane, other.shape[2])
        frame[:, lanes] += other[j].astype(jnp.float32)
        out[j] = frame[...].astype(jnp.bfloat16)


def in_frame(s, j, frame, messages, store):
    odd = (j + 1 - s) % 2
    frame[...] = jnp.zeros_like(frame)
    for message, start in messages:
        lane = pl.multiple_of((start - odd + 8) * BS, 2 * BS)
        frame[:, pl.ds(lane, message.shape[2])] += message[j].astype(jnp.float32)
    first, last = 8 * BS, (8 + BAND) * BS

    @pl.when(odd == 0)
    def _():
        store(frame[:, first:last])

    @pl.when(odd == 1)
    def _():
        store(frame[:, first - BS : last - BS])


def early_kernel(core, own, direct, pair, far, out, frame):
    s, x = places(core)
    for j in range(NC):
        top = 27 - 3 * s - j
        messages = [(own, top - 12), (direct, top - 30 * x), (pair, top - 6 - 12 * x)]
        messages.append((far, jnp.where(s == 1, 30 - j, -1 - j)))

        def store(value, j=j):
            out[j] = value

        in_frame(s, j, frame, messages, store)


def total_kernel(core, early, merged, out, frame, buf, sems):
    s, x = places(core)
    copies = []
    for j in range(NC):

        def store(value, j=j):
            buf[j] = value + early[j]

        in_frame(s, j, frame, [(merged, 3 - 3 * s - j + 18 * x)], store)
        copy = pltpu.make_async_copy(buf.at[j], out.at[j], sems.at[j])
        copy.start()
        copies.append(copy)
    for copy in copies:
        copy.wait()


def pick_kernel(core, source, outer, inner, buf, in_sems, out_sems):
    s, x = places(core)
    step = AGG // 4
    reads, writes = [], []
    for side, (target, which) in enumerate(((outer, s), (inner, 1 - s))):
        for k in range(4):
            n = len(reads)
            rows = pl.ds((NB - AGG) * which + k * step, step)
            part = buf.at[side, k * step : (k + 1) * step]
            into = target.at[k * step : (k + 1) * step]
            reads.append(pltpu.make_async_copy(source.at[rows], part, in_sems.at[n]))
            writes.append(pltpu.make_async_copy(part, into, out_sems.at[n]))
    for copy in reads:
        copy.start()
    for read, write in zip(reads, writes):
        read.wait()
        write.start()
    for copy in writes:
        copy.wait()


def permuted(block, pairs):
    return lax.ppermute(block, "dom", pairs)


def inverse_index(offset, slots, empty):
    order = jnp.arange(offset.shape[1], dtype=jnp.int32)[None, :, None]
    hit = offset[:, :, None] == jnp.arange(slots, dtype=jnp.int32)[None, None, :]
    return empty + jnp.sum(jnp.where(hit, order - empty, 0), axis=1)


def body(a_blocks, p_blocks, cols_a, cols_p):
    devices = lax.axis_size("dom")
    device = lax.axis_index("dom")
    count_agg = NC * devices
    count_rows = NB * devices
    first_agg = device * NC
    first_row = device * NB
    core = device.astype(jnp.int32).reshape(1)

    def shifted(distance):
        return [(i, (i + distance) % devices) for i in range(devices)]

    parity = device % 2
    smem = pl.BlockSpec(memory_space=pltpu.SMEM)
    vmem = pl.BlockSpec(memory_space=pltpu.VMEM)
    hbm = pl.BlockSpec(memory_space=pltpu.HBM)
    bf16 = jnp.bfloat16

    def params(mebibytes):
        return pltpu.CompilerParams(vmem_limit_bytes=mebibytes * 1024 * 1024)

    def cost(flops, size):
        return pl.CostEstimate(flops=flops, bytes_accessed=size, transcendentals=0)

    edge = jax.ShapeDtypeStruct((AGG,) + p_blocks.shape[1:], bf16)
    outer, inner = pl.pallas_call(
        pick_kernel,
        out_shape=[edge, edge],
        in_specs=[smem, hbm],
        out_specs=[hbm, hbm],
        scratch_shapes=[
            pltpu.VMEM((2,) + edge.shape, bf16),
            pltpu.SemaphoreType.DMA((8,)),
            pltpu.SemaphoreType.DMA((8,)),
        ],
        compiler_params=params(60),
        name="pick",
    )(core, p_blocks)
    outward = [(i, (i + (1 if i % 2 else -1)) % devices) for i in range(devices)]
    inward = [(i, i ^ 1) for i in range(devices)]
    outer, inner, edge_cols = lax.optimization_barrier((outer, inner, cols_p))
    p_slow = permuted(outer, outward)
    p_fast = permuted(inner, inward)
    edge_cols = jnp.stack([edge_cols[:AGG], edge_cols[NB - AGG :]])
    cols_slow = permuted(edge_cols[parity], outward)
    cols_fast = permuted(edge_cols[1 - parity], inward)

    def slots(cols, agg):
        return (cols - agg + H) % count_agg

    own_agg = jnp.arange(NB, dtype=jnp.int32)[:, None] // AGG
    inv_own = inverse_index(slots(cols_p, first_agg + own_agg) + own_agg + 1, COLS, KP)
    fast_place = NC * (1 - parity) - parity
    inv_fast = inverse_index(slots(cols_fast, first_agg + fast_place) + fast_place + 1, COLS, KP)
    slow_place = NC * parity - (1 - parity)
    inv_slow = inverse_index(slots(cols_slow, first_agg + slow_place) + 2 * parity, WSLOT, KP)
    inv_fast, inv_slow = lax.optimization_barrier((inv_fast, inv_slow))
    inv_a = inverse_index((cols_a - first_row - (own_agg - 1) * AGG) % count_rows, 3 * AGG, KA)

    def block(rows, width, kind=bf16):
        return jax.ShapeDtypeStruct((rows, BS, width), kind)

    span = WINDOW * BS
    outs = [
        block(NC, span),
        block(NC, span),
        block(NC, span),
        block(FIRST, span),
        block(REST, span),
        block(REST, 2 * AW),
        block(FIRST, AW),
        block(REST, AW),
        block(NC, AW),
        block(FIRST, AW),
        block(REST, AW),
        block(WCOLS, 2 * AW),
        block(WSLOT, AW, jnp.float32),
        block(AGG, AW),
    ]
    (
        send_low,
        send_high,
        far,
        inner,
        send_rest,
        fast_rest,
        slow_first,
        slow_rest,
        slow_far,
        other_first,
        other_rest,
        wt_fast,
        rest,
        at_halo,
    ) = pl.pallas_call(
        fast_kernel,
        out_shape=outs,
        in_specs=[smem] * 3 + [hbm, hbm, vmem],
        out_specs=[hbm] * len(outs),
        scratch_shapes=[
            pltpu.VMEM((NB + AGG, BS, KP * BS), bf16),
            pltpu.VMEM((COLS, BS, EXT * BS), bf16),
            pltpu.VMEM((NC, 3 * AGG, BS, AW), bf16),
            pltpu.VMEM((LANES, LANES), bf16),
            pltpu.VMEM((KP + 1, BS, LANES), bf16),
            pltpu.VMEM((KP + 1, BS, LANES), bf16),
            pltpu.VMEM((KA + 1, BS, LANES), bf16),
            pltpu.VMEM((KA + 1, BS, LANES), bf16),
            pltpu.VMEM((ROWS + REST, BS, 2 * AW), bf16),
            pltpu.VMEM((ROWS + REST, BS, span), bf16),
            pltpu.VMEM((REST, BS, 2 * AW), bf16),
            pltpu.VMEM((ROWS + NC, BS, AW), bf16),
            pltpu.VMEM((ROWS, BS, AW), bf16),
            pltpu.VMEM((WCOLS, BS, 2 * AW), bf16),
            pltpu.VMEM((WSLOT, BS, AW), jnp.float32),
            pltpu.SemaphoreType.DMA(((NB + AGG) // QUAD,)),
            pltpu.SemaphoreType.DMA((len(outs) + 10,)),
        ],
        compiler_params=params(56),
        cost_estimate=cost(20 * 10**9, 30 * 10**6),
        name="fast",
    )(core, jnp.concatenate([inv_own, inv_fast]), inv_a, p_blocks, p_fast, a_blocks)

    low = permuted(send_low, inward)
    high = permuted(send_high, inward)
    other_first = permuted(other_first, inward)
    at_halo, rest = pl.pallas_call(
        stage_kernel,
        out_shape=[block(AGG, AW), block(WSLOT, AW, jnp.float32)],
        in_specs=[hbm] * 2,
        out_specs=[vmem] * 2,
        scratch_shapes=[pltpu.SemaphoreType.DMA((2,))],
        compiler_params=params(8),
        cost_estimate=cost(10**6, 10**6),
        name="stage",
    )(at_halo, rest)
    p_slow, low, high, other_first = lax.optimization_barrier((p_slow, low, high, other_first))

    wt_slow = pl.pallas_call(
        slow_kernel,
        out_shape=block(WCOLS, AW),
        in_specs=[smem] * 2 + [vmem] * 3,
        out_specs=vmem,
        scratch_shapes=[
            pltpu.VMEM((LANES, LANES), bf16),
            pltpu.VMEM((KP + 1, BS, LANES), bf16),
            pltpu.VMEM((KP + 1, BS, LANES), bf16),
            pltpu.VMEM((WSLOT, BS, AW), bf16),
        ],
        compiler_params=params(24),
        cost_estimate=cost(20 * 10**9, 200 * 10**6),
        name="slow",
    )(core, inv_slow, p_slow, at_halo, rest)
    wt_other = permuted(wt_slow, inward)

    wt_slow, low, high = lax.optimization_barrier((wt_slow, low, high))
    far = pl.pallas_call(
        far_kernel,
        out_shape=block(NC, FAR * BS),
        in_specs=[smem] + [vmem] * 3,
        out_specs=vmem,
        compiler_params=params(16),
        cost_estimate=cost(10**9, 10**7),
        name="far",
    )(core, slow_far, wt_slow, far)
    far, wt_slow = lax.optimization_barrier((far, wt_slow))
    mine = pl.pallas_call(
        mine_kernel,
        out_shape=block(FIRST, span, jnp.float32),
        in_specs=[vmem] * 5,
        out_specs=vmem,
        compiler_params=params(24),
        cost_estimate=cost(10**10, 100 * 10**6),
        name="mine",
    )(slow_first, wt_slow, inner, low, high)
    crossing = [i for i in range(devices) if i % 4 in (1, 2)]
    far_near = permuted(far, [(i, i ^ 3) for i in crossing])
    relay, direct = pl.pallas_call(
        join_first_kernel,
        out_shape=[block(NC, span), block(NC, span, jnp.float32)],
        in_specs=[vmem] * 3,
        out_specs=[vmem] * 2,
        compiler_params=params(16),
        cost_estimate=cost(10**6, 10**5),
        name="join_first",
    )(other_first, wt_other, mine)
    relay, direct, far_near, send_rest, other_rest = lax.optimization_barrier(
        (relay, direct, far_near, send_rest, other_rest)
    )
    arrived_rest = permuted(send_rest, inward)
    other_rest = permuted(other_rest, inward)
    along_x = [(i, i ^ 2) for i in range(devices)]
    x_sign = [1 if i // 2 % 2 else -1 for i in range(devices)]
    relay = permuted(relay, along_x)

    def merge_rows(rows, other, shift, name):
        return pl.pallas_call(
            functools.partial(merge_kernel, shift=shift),
            out_shape=block(NC, MERGED * BS),
            in_specs=[smem, vmem, vmem],
            out_specs=vmem,
            scratch_shapes=[pltpu.VMEM((BS, MERGED * BS), jnp.float32)],
            compiler_params=params(16),
            cost_estimate=cost(10**7, 10**7),
            name=name,
        )(core, rows, other)

    direct = merge_rows(direct, far_near, 2, "merge_far")
    direct = permuted(direct, [(i, (i + 4 * x_sign[i]) % devices) for i in range(devices)])
    merge, pair, own = pl.pallas_call(
        join_rest_kernel,
        out_shape=[block(NC, span, jnp.float32), block(NC, span), block(NC, span, jnp.float32)],
        in_specs=[vmem] * 7,
        out_specs=[vmem] * 3,
        compiler_params=params(30),
        cost_estimate=cost(40 * 10**9, 200 * 10**6),
        name="join_rest",
    )(fast_rest, slow_rest, other_rest, wt_fast, wt_slow, wt_other, arrived_rest)
    relay, pair = lax.optimization_barrier((relay, pair))
    merged = merge_rows(merge, relay, 0, "merge")
    merged = permuted(merged, [(i, (i - 4 * x_sign[i]) % devices) for i in range(devices)])
    pair = permuted(pair, along_x)
    direct, far = lax.optimization_barrier((direct, far))
    straight = [i for i in range(devices) if i % 4 in (0, 3)]
    far = permuted(far, [(i, (i + (5 if i % 2 else -5)) % devices) for i in straight])

    total = block(NC, BAND * BS, jnp.float32)
    frame = pltpu.VMEM((BS, FRAME * BS), jnp.float32)
    early = pl.pallas_call(
        early_kernel,
        out_shape=total,
        in_specs=[smem] + [vmem] * 4,
        out_specs=vmem,
        scratch_shapes=[frame],
        compiler_params=params(16),
        cost_estimate=cost(10**10, 100 * 10**6),
        name="early",
    )(core, own, direct, pair, far)
    return pl.pallas_call(
        total_kernel,
        out_shape=total,
        in_specs=[smem] + [vmem] * 2,
        out_specs=hbm,
        scratch_shapes=[
            frame,
            pltpu.VMEM(total.shape, jnp.float32),
            pltpu.SemaphoreType.DMA((NC,)),
        ],
        compiler_params=params(20),
        cost_estimate=cost(10**7, 10**7),
        name="total",
    )(core, early, merged)


def solution(mesh):
    in_specs = (P("dom", None, None), P("dom", None, None), P("dom", None), P("dom", None))
    out_specs = P("dom", None, None)
    return jax.shard_map(body, mesh=mesh, in_specs=in_specs, out_specs=out_specs, check_vma=False)
```

```python
import functools

import jax
import jax.numpy as jnp
from jax import lax
from jax.experimental import pallas as pl
from jax.experimental.pallas import tpu as pltpu
from jax.sharding import PartitionSpec as P

BS = 64
KA = 7
KP = 27
AGG = 8
H = 15
NC = 3
NB = 24
WIN = 31
WSLOT = 33
BAND = 63

QUAD = 4
LANES = QUAD * BS
EXT = NB + 2 * AGG
COLS = NC + 2 * H + 2
WCOLS = 40
WINDOW = 38
TILES = 10
GROUPS = 5
K = NB * BS
AW = AGG * BS
FRAME = 80
NT = (((1,), (1,)), ((), ()))
ROWS = NC * GROUPS
FIRST = 2 * NC
REST = ROWS - FIRST
MERGED = WINDOW + 6
FAR = 36


def eye(n):
    rows = lax.broadcasted_iota(jnp.int32, (n, n), 0)
    lanes = lax.broadcasted_iota(jnp.int32, (n, n), 1)
    return jnp.where(rows == lanes, 1.0, 0.0).astype(jnp.bfloat16)


def low_half():
    return lax.broadcasted_iota(jnp.int32, (BS, 2 * BS), 1) < BS


def places(device):
    return device[0] % 2, device[0] // 2 % 2


def transpose_quad(unit, block, turned, width):
    for start in range(0, width, LANES):
        size = min(LANES, width - start)
        part = lax.dot_general(
            unit[:size, :size],
            block[:, start : start + size],
            NT,
            preferred_element_type=jnp.float32,
        )
        turned[start // BS : (start + size) // BS] = part.astype(jnp.bfloat16).reshape(
            size // BS, BS, LANES
        )


def spread_quad(turned, index, first, store, count):
    half = low_half()
    for slot in range(count):
        for pair in range(2):
            lanes = slice(pair * 2 * BS, (pair + 1) * 2 * BS)
            left = turned[index[first + 2 * pair, slot], :, lanes]
            right = turned[index[first + 2 * pair + 1, slot], :, lanes]
            store(slot, pair, jnp.where(half, left, right))


def turn_and_spread(count, turn, spread, buffers):
    even, odd = buffers
    turn(0, even)

    def two(step):
        turn(2 * step + 1, odd)
        spread(2 * step, even)
        turn(2 * step + 2, even)
        spread(2 * step + 1, odd)

    if count > 2:
        pl.loop(0, count // 2 - 1)(two)

    turn(count - 1, odd)
    spread(count - 2, even)
    spread(count - 1, odd)


def fast_kernel(
    core,
    inv_p,
    inv_a,
    p_own,
    p_fast,
    a_own,
    send_low,
    send_high,
    far,
    inner,
    send_rest,
    fast_rest,
    slow_first,
    slow_rest,
    slow_far,
    other_first,
    other_rest,
    wt,
    rest,
    at_halo,
    p_buf,
    ext,
    at,
    unit,
    turned_p,
    turned_p2,
    turned_a,
    turned_a2,
    lhs,
    rows_buf,
    fast_buf,
    slow_buf,
    other_buf,
    wt_buf,
    rest_buf,
    in_sems,
    out_sems,
):
    s, x = places(core)
    own_quads = NB // QUAD
    halo_quads = AGG // QUAD

    def load(quad):
        if quad < own_quads:
            source = p_own.at[quad * QUAD : (quad + 1) * QUAD]
        else:
            source = p_fast.at[(quad - own_quads) * QUAD : (quad - own_quads + 1) * QUAD]
        target = p_buf.at[quad * QUAD : (quad + 1) * QUAD]
        return pltpu.make_async_copy(source, target, in_sems.at[quad])

    for quad in range(own_quads + halo_quads):
        load(quad).start()

    unit[...] = eye(LANES)
    for buffers, empty in (((turned_p, turned_p2), KP), ((turned_a, turned_a2), KA)):
        for buffer in buffers:
            buffer[empty] = jnp.zeros((BS, LANES), jnp.bfloat16)

    def turn_a(quad, turned):
        block = a_own[pl.ds(quad * QUAD, QUAD)].reshape(LANES, KA * BS)
        transpose_quad(unit, block, turned, KA * BS)

    def spread_a(quad, turned):
        agg = quad // halo_quads
        first_lane = (quad % halo_quads) * LANES

        def store(slot, pair, value):
            lane = pl.multiple_of(first_lane + pair * 2 * BS, 2 * BS)
            at[agg, slot, :, pl.ds(lane, 2 * BS)] = value

        spread_quad(turned, inv_a, quad * QUAD, store, 3 * AGG)

    turn_and_spread(own_quads, turn_a, spread_a, (turned_a, turned_a2))

    slow_agg = 2 * s
    halo_copy = pltpu.make_async_copy(at.at[slow_agg, pl.ds(16 * s, AGG)], at_halo, out_sems.at[0])
    halo_copy.start()

    def turn_p(quad, turned):
        block = p_buf[pl.ds(quad * QUAD, QUAD)].reshape(LANES, KP * BS)
        transpose_quad(unit, block, turned, KP * BS)

    def spread_p(quad, turned):
        own_lane = AW + quad * LANES
        halo_lane = (AW + K) * (1 - s) + (quad - own_quads) * LANES
        first_lane = jnp.where(quad < own_quads, own_lane, halo_lane)

        def store(slot, pair, value):
            lane = pl.multiple_of(first_lane + pair * 2 * BS, 2 * BS)
            ext[slot, :, pl.ds(lane, 2 * BS)] = value

        spread_quad(turned, inv_p, quad * QUAD, store, COLS)

    for quad in range(own_quads + halo_quads):
        load(quad).wait()
    turn_and_spread(own_quads + halo_quads, turn_p, spread_p, (turned_p, turned_p2))

    fast_lanes = pl.ds(pl.multiple_of(AW + (1 - s) * AW, AW), 2 * AW)
    slow_lanes = pl.ds(pl.multiple_of(AW + 2 * s * AW, AW), AW)
    for place, i in enumerate((1 + 2 * x, 4 * x, 4 - 4 * x, 3 - 2 * x, 2)):
        for j in range(NC):
            row = NC * place + j
            mine, other = 6 * i + 3 + j + 1, 6 * i + 6 * (1 - s) + j + 1
            if place < 2:
                lhs[row] = ext[other, :, fast_lanes]
                lhs[FIRST + NC + row] = ext[mine, :, fast_lanes]
            else:
                lhs[ROWS + row - FIRST] = ext[other, :, fast_lanes]
                fast_buf[row - FIRST] = ext[mine, :, fast_lanes]
            slow_buf[row] = ext[mine, :, slow_lanes]
            other_buf[row] = ext[other, :, slow_lanes]
    for j in range(NC):
        lhs[FIRST + j] = ext[30 * s + j + 1, :, fast_lanes]
        slow_buf[ROWS + j] = ext[30 * s + j + 1, :, slow_lanes]
    copies = [halo_copy]

    def write(source, target):
        copy = pltpu.make_async_copy(source, target, out_sems.at[len(copies)])
        copy.start()
        copies.append(copy)

    write(other_buf.at[:FIRST], other_first)
    write(other_buf.at[FIRST:], other_rest)
    write(fast_buf, fast_rest)
    write(slow_buf.at[:FIRST], slow_first)
    write(slow_buf.at[FIRST:ROWS], slow_rest)
    write(slow_buf.at[ROWS:], slow_far)

    wt_buf[0:7] = jnp.zeros((7, BS, 2 * AW), jnp.bfloat16)
    wt_buf[33:] = jnp.zeros((WCOLS - 33, BS, 2 * AW), jnp.bfloat16)
    chunk = WSLOT // 3

    @pl.loop(0, 2)
    def _(place):
        agg = place + 1 - s
        lane = pl.multiple_of(agg * AW, AW)
        target = pl.multiple_of(place * AW, AW)

        @pl.loop(0, 3)
        def _(part):
            first = agg + part * chunk
            left = ext[pl.ds(first, chunk), :, pl.ds(lane, 3 * AW)].reshape(chunk * BS, 3 * AW)
            value = jnp.dot(
                left, at[agg].reshape(3 * AW, AW), preferred_element_type=jnp.float32
            )
            wt_buf[pl.ds(3 * s + first, chunk), :, pl.ds(target, AW)] = value.astype(
                jnp.bfloat16
            ).reshape(chunk, BS, AW)

    write(wt_buf, wt)

    @pl.loop(0, 3)
    def _(part):
        lane = pl.multiple_of(AW + s * AW, AW)
        left = ext[pl.ds(slow_agg + part * chunk, chunk), :, pl.ds(lane, 2 * AW)]
        right = at[slow_agg, pl.ds(AGG - AGG * s, 2 * AGG)].reshape(2 * AW, AW)
        value = jnp.dot(
            left.reshape(chunk * BS, 2 * AW), right, preferred_element_type=jnp.float32
        )
        rest_buf[pl.ds(part * chunk, chunk)] = value.reshape(chunk, BS, AW)

    write(rest_buf, rest)

    def emit(tile, width):
        right = wt_buf[pl.ds(QUAD * tile, width // BS)].reshape(width, 2 * AW)
        left = lhs[...].reshape((ROWS + REST) * BS, 2 * AW)
        value = lax.dot_general(left, right, NT, preferred_element_type=jnp.float32)
        rows_buf[:, :, tile_lanes(tile, width)] = value.astype(jnp.bfloat16).reshape(
            ROWS + REST, BS, width
        )

    parts = (
        (send_low, 0),
        (send_high, NC),
        (far, FIRST),
        (inner, FIRST + NC),
        (send_rest, ROWS),
    )
    bounds = (0, 4, 8, TILES)
    for first, last in zip(bounds[:-1], bounds[1:]):

        @pl.loop(first, min(last, TILES - 1))
        def _(tile):
            emit(tile, LANES)

        if last == TILES:
            emit(TILES - 1, LANES // 2)
        lanes = slice(first * LANES, min(last * LANES, WINDOW * BS))
        for target, row in parts:
            rows = slice(row, row + target.shape[0])
            write(rows_buf.at[rows, :, lanes], target.at[:, :, lanes])
    for copy in copies:
        copy.wait()


def each_tile(step):
    @pl.loop(0, TILES - 1)
    def _(tile):
        step(tile, LANES)

    step(TILES - 1, LANES // 2)


def tile_dot(rows, cols, tile, width):
    left = rows[...].reshape(rows.shape[0] * BS, rows.shape[2])
    right = cols[pl.ds(QUAD * tile, width // BS)].reshape(width, cols.shape[2])
    value = lax.dot_general(left, right, NT, preferred_element_type=jnp.float32)
    return value.reshape(rows.shape[0], BS, width)


def tile_lanes(tile, width):
    return pl.ds(pl.multiple_of(tile * LANES, LANES), width)


def far_kernel(core, slow, wt_slow, far_fast, far):
    s, x = places(core)

    @pl.loop(0, FAR // QUAD)
    def _(tile):
        left = slow[...].reshape(NC * BS, AW)
        right = wt_slow[pl.ds(QUAD * tile + 2 * s, QUAD)].reshape(LANES, AW)
        value = lax.dot_general(left, right, NT, preferred_element_type=jnp.float32)
        lanes = pl.ds(pl.multiple_of(tile * LANES + 2 * BS * s, 2 * BS), LANES)
        value = value.reshape(NC, BS, LANES) + far_fast[:, :, lanes].astype(jnp.float32)
        far[:, :, tile_lanes(tile, LANES)] = value.astype(jnp.bfloat16)


def mine_kernel(slow, wt_slow, inner, low, high, out):
    def step(tile, width):
        lanes = tile_lanes(tile, width)
        near = tile_dot(slow, wt_slow, tile, width) + inner[:, :, lanes].astype(jnp.float32)
        out[:NC, :, lanes] = near[:NC] + low[:, :, lanes].astype(jnp.float32)
        out[NC:, :, lanes] = near[NC:] + high[:, :, lanes].astype(jnp.float32)

    each_tile(step)


def slow_kernel(core, inv_slow, p_slow, at_halo, rest, wt, unit, turned_p, turned_p2, ext):
    s, x = places(core)
    unit[...] = eye(LANES)
    for buffer in (turned_p, turned_p2):
        buffer[KP] = jnp.zeros((BS, LANES), jnp.bfloat16)

    def turn(quad, turned):
        block = p_slow[quad * QUAD : (quad + 1) * QUAD].reshape(LANES, KP * BS)
        transpose_quad(unit, block, turned, KP * BS)

    def spread(quad, turned):
        def store(slot, pair, value):
            lane = quad * LANES + pair * 2 * BS
            ext[slot, :, lane : lane + 2 * BS] = value

        spread_quad(turned, inv_slow, quad * QUAD, store, WSLOT)

    turn_and_spread(AGG // QUAD, turn, spread, (turned_p, turned_p2))
    wt[0:5] = jnp.zeros((5, BS, AW), jnp.bfloat16)
    wt[WSLOT:] = jnp.zeros((WCOLS - WSLOT, BS, AW), jnp.bfloat16)
    chunk = WSLOT // 3

    @pl.loop(0, 3)
    def _(part):
        rows = pl.ds(part * chunk, chunk)
        value = jnp.dot(
            ext[rows].reshape(chunk * BS, AW),
            at_halo[...].reshape(AW, AW),
            preferred_element_type=jnp.float32,
        )
        value = value.reshape(chunk, BS, AW) + rest[rows]
        wt[pl.ds(5 * s + part * chunk, chunk)] = value.astype(jnp.bfloat16)


def join_first_kernel(other, wt_other, mine, relay, direct):
    def step(tile, width):
        lanes = tile_lanes(tile, width)
        value = tile_dot(other, wt_other, tile, width) + mine[:, :, lanes]
        relay[:, :, lanes] = value[:NC].astype(jnp.bfloat16)
        direct[:, :, lanes] = value[NC:]

    each_tile(step)


def join_rest_kernel(fast, slow, other, wt_fast, wt_slow, wt_other, arrived, merge, pair, own):
    def step(tile, width):
        lanes = tile_lanes(tile, width)
        value = tile_dot(fast, wt_fast, tile, width) + tile_dot(slow, wt_slow, tile, width)
        value = value + tile_dot(other, wt_other, tile, width)
        value = value + arrived[:, :, lanes].astype(jnp.float32)
        merge[:, :, lanes] = value[:NC]
        pair[:, :, lanes] = value[NC : 2 * NC].astype(jnp.bfloat16)
        own[:, :, lanes] = value[2 * NC :]

    each_tile(step)


def stage_kernel(at_halo, rest, at_out, rest_out, sems):
    copies = [
        pltpu.make_async_copy(at_halo, at_out, sems.at[0]),
        pltpu.make_async_copy(rest, rest_out, sems.at[1]),
    ]
    for copy in copies:
        copy.start()
    for copy in copies:
        copy.wait()


def merge_kernel(core, rows, other, out, frame, *, shift):
    s, x = places(core)
    step = 6 * BS
    for j in range(NC):
        frame[...] = jnp.zeros_like(frame)
        frame[:, pl.ds(pl.multiple_of(step * x, step), WINDOW * BS)] = rows[j]
        lane = pl.multiple_of(step * (1 - x) + shift * BS * x, 2 * BS)
        lanes = pl.ds(lane, other.shape[2])
        frame[:, lanes] += other[j].astype(jnp.float32)
        out[j] = frame[...].astype(jnp.bfloat16)


def in_frame(s, j, frame, messages, store):
    odd = (j + 1 - s) % 2
    frame[...] = jnp.zeros_like(frame)
    for message, start in messages:
        lane = pl.multiple_of((start - odd + 8) * BS, 2 * BS)
        frame[:, pl.ds(lane, message.shape[2])] += message[j].astype(jnp.float32)
    first, last = 8 * BS, (8 + BAND) * BS

    @pl.when(odd == 0)
    def _():
        store(frame[:, first:last])

    @pl.when(odd == 1)
    def _():
        store(frame[:, first - BS : last - BS])


def early_kernel(core, own, direct, pair, merged, out, frame):
    s, x = places(core)
    for j in range(NC):
        top = 27 - 3 * s - j
        messages = [(own, top - 12), (direct, top - 30 * x), (pair, top - 6 - 12 * x)]
        messages.append((merged, top - 24 + 18 * x))

        def store(value, j=j):
            out[j] = value

        in_frame(s, j, frame, messages, store)


def total_kernel(core, early, far, out, frame, buf, sems):
    s, x = places(core)
    copies = []
    for j in range(NC):
        far_start = jnp.where(s == 1, 30 - j, -1 - j)

        def store(value, j=j):
            buf[j] = value + early[j]

        in_frame(s, j, frame, [(far, far_start)], store)
        copy = pltpu.make_async_copy(buf.at[j], out.at[j], sems.at[j])
        copy.start()
        copies.append(copy)
    for copy in copies:
        copy.wait()


def pick_kernel(core, source, outer, inner, buf, in_sems, out_sems):
    s, x = places(core)
    step = AGG // 4
    reads, writes = [], []
    for side, (target, which) in enumerate(((outer, s), (inner, 1 - s))):
        for k in range(4):
            n = len(reads)
            rows = pl.ds((NB - AGG) * which + k * step, step)
            part = buf.at[side, k * step : (k + 1) * step]
            into = target.at[k * step : (k + 1) * step]
            reads.append(pltpu.make_async_copy(source.at[rows], part, in_sems.at[n]))
            writes.append(pltpu.make_async_copy(part, into, out_sems.at[n]))
    for copy in reads:
        copy.start()
    for read, write in zip(reads, writes):
        read.wait()
        write.start()
    for copy in writes:
        copy.wait()


def permuted(block, pairs):
    return lax.ppermute(block, "dom", pairs)


def inverse_index(offset, slots, empty):
    order = jnp.arange(offset.shape[1], dtype=jnp.int32)[None, :, None]
    hit = offset[:, :, None] == jnp.arange(slots, dtype=jnp.int32)[None, None, :]
    return empty + jnp.sum(jnp.where(hit, order - empty, 0), axis=1)


def body(a_blocks, p_blocks, cols_a, cols_p):
    devices = lax.axis_size("dom")
    device = lax.axis_index("dom")
    count_agg = NC * devices
    count_rows = NB * devices
    first_agg = device * NC
    first_row = device * NB
    core = device.astype(jnp.int32).reshape(1)

    def shifted(distance):
        return [(i, (i + distance) % devices) for i in range(devices)]

    parity = device % 2
    smem = pl.BlockSpec(memory_space=pltpu.SMEM)
    vmem = pl.BlockSpec(memory_space=pltpu.VMEM)
    hbm = pl.BlockSpec(memory_space=pltpu.HBM)
    bf16 = jnp.bfloat16

    def params(mebibytes):
        return pltpu.CompilerParams(vmem_limit_bytes=mebibytes * 1024 * 1024)

    def cost(flops, size):
        return pl.CostEstimate(flops=flops, bytes_accessed=size, transcendentals=0)

    edge = jax.ShapeDtypeStruct((AGG,) + p_blocks.shape[1:], bf16)
    outer, inner = pl.pallas_call(
        pick_kernel,
        out_shape=[edge, edge],
        in_specs=[smem, hbm],
        out_specs=[hbm, hbm],
        scratch_shapes=[
            pltpu.VMEM((2,) + edge.shape, bf16),
            pltpu.SemaphoreType.DMA((8,)),
            pltpu.SemaphoreType.DMA((8,)),
        ],
        compiler_params=params(60),
        name="pick",
    )(core, p_blocks)
    outward = [(i, (i + (1 if i % 2 else -1)) % devices) for i in range(devices)]
    inward = [(i, i ^ 1) for i in range(devices)]
    outer, inner, edge_cols = lax.optimization_barrier((outer, inner, cols_p))
    p_slow = permuted(outer, outward)
    p_fast = permuted(inner, inward)
    edge_cols = jnp.stack([edge_cols[:AGG], edge_cols[NB - AGG :]])
    cols_slow = permuted(edge_cols[parity], outward)
    cols_fast = permuted(edge_cols[1 - parity], inward)

    def slots(cols, agg):
        return (cols - agg + H) % count_agg

    own_agg = jnp.arange(NB, dtype=jnp.int32)[:, None] // AGG
    inv_own = inverse_index(slots(cols_p, first_agg + own_agg) + own_agg + 1, COLS, KP)
    fast_place = NC * (1 - parity) - parity
    inv_fast = inverse_index(slots(cols_fast, first_agg + fast_place) + fast_place + 1, COLS, KP)
    slow_place = NC * parity - (1 - parity)
    inv_slow = inverse_index(slots(cols_slow, first_agg + slow_place) + 2 * parity, WSLOT, KP)
    inv_fast, inv_slow = lax.optimization_barrier((inv_fast, inv_slow))
    inv_a = inverse_index((cols_a - first_row - (own_agg - 1) * AGG) % count_rows, 3 * AGG, KA)

    def block(rows, width, kind=bf16):
        return jax.ShapeDtypeStruct((rows, BS, width), kind)

    span = WINDOW * BS
    outs = [
        block(NC, span),
        block(NC, span),
        block(NC, span),
        block(FIRST, span),
        block(REST, span),
        block(REST, 2 * AW),
        block(FIRST, AW),
        block(REST, AW),
        block(NC, AW),
        block(FIRST, AW),
        block(REST, AW),
        block(WCOLS, 2 * AW),
        block(WSLOT, AW, jnp.float32),
        block(AGG, AW),
    ]
    (
        send_low,
        send_high,
        far,
        inner,
        send_rest,
        fast_rest,
        slow_first,
        slow_rest,
        slow_far,
        other_first,
        other_rest,
        wt_fast,
        rest,
        at_halo,
    ) = pl.pallas_call(
        fast_kernel,
        out_shape=outs,
        in_specs=[smem] * 3 + [hbm, hbm, vmem],
        out_specs=[hbm] * len(outs),
        scratch_shapes=[
            pltpu.VMEM((NB + AGG, BS, KP * BS), bf16),
            pltpu.VMEM((COLS, BS, EXT * BS), bf16),
            pltpu.VMEM((NC, 3 * AGG, BS, AW), bf16),
            pltpu.VMEM((LANES, LANES), bf16),
            pltpu.VMEM((KP + 1, BS, LANES), bf16),
            pltpu.VMEM((KP + 1, BS, LANES), bf16),
            pltpu.VMEM((KA + 1, BS, LANES), bf16),
            pltpu.VMEM((KA + 1, BS, LANES), bf16),
            pltpu.VMEM((ROWS + REST, BS, 2 * AW), bf16),
            pltpu.VMEM((ROWS + REST, BS, span), bf16),
            pltpu.VMEM((REST, BS, 2 * AW), bf16),
            pltpu.VMEM((ROWS + NC, BS, AW), bf16),
            pltpu.VMEM((ROWS, BS, AW), bf16),
            pltpu.VMEM((WCOLS, BS, 2 * AW), bf16),
            pltpu.VMEM((WSLOT, BS, AW), jnp.float32),
            pltpu.SemaphoreType.DMA(((NB + AGG) // QUAD,)),
            pltpu.SemaphoreType.DMA((len(outs) + 10,)),
        ],
        compiler_params=params(56),
        cost_estimate=cost(20 * 10**9, 30 * 10**6),
        name="fast",
    )(core, jnp.concatenate([inv_own, inv_fast]), inv_a, p_blocks, p_fast, a_blocks)

    low = permuted(send_low, inward)
    high = permuted(send_high, inward)
    other_first = permuted(other_first, inward)
    at_halo, rest = pl.pallas_call(
        stage_kernel,
        out_shape=[block(AGG, AW), block(WSLOT, AW, jnp.float32)],
        in_specs=[hbm] * 2,
        out_specs=[vmem] * 2,
        scratch_shapes=[pltpu.SemaphoreType.DMA((2,))],
        compiler_params=params(8),
        cost_estimate=cost(10**6, 10**6),
        name="stage",
    )(at_halo, rest)
    p_slow, low, high, other_first = lax.optimization_barrier((p_slow, low, high, other_first))

    wt_slow = pl.pallas_call(
        slow_kernel,
        out_shape=block(WCOLS, AW),
        in_specs=[smem] * 2 + [vmem] * 3,
        out_specs=vmem,
        scratch_shapes=[
            pltpu.VMEM((LANES, LANES), bf16),
            pltpu.VMEM((KP + 1, BS, LANES), bf16),
            pltpu.VMEM((KP + 1, BS, LANES), bf16),
            pltpu.VMEM((WSLOT, BS, AW), bf16),
        ],
        compiler_params=params(24),
        cost_estimate=cost(20 * 10**9, 200 * 10**6),
        name="slow",
    )(core, inv_slow, p_slow, at_halo, rest)
    wt_other = permuted(wt_slow, inward)

    wt_slow, low, high = lax.optimization_barrier((wt_slow, low, high))
    far = pl.pallas_call(
        far_kernel,
        out_shape=block(NC, FAR * BS),
        in_specs=[smem] + [vmem] * 3,
        out_specs=vmem,
        compiler_params=params(16),
        cost_estimate=cost(10**9, 10**7),
        name="far",
    )(core, slow_far, wt_slow, far)
    far, wt_slow = lax.optimization_barrier((far, wt_slow))
    mine = pl.pallas_call(
        mine_kernel,
        out_shape=block(FIRST, span, jnp.float32),
        in_specs=[vmem] * 5,
        out_specs=vmem,
        compiler_params=params(24),
        cost_estimate=cost(10**10, 100 * 10**6),
        name="mine",
    )(slow_first, wt_slow, inner, low, high)
    crossing = [i for i in range(devices) if i % 4 in (1, 2)]
    far_near = permuted(far, [(i, i ^ 3) for i in crossing])
    relay, direct = pl.pallas_call(
        join_first_kernel,
        out_shape=[block(NC, span), block(NC, span, jnp.float32)],
        in_specs=[vmem] * 3,
        out_specs=[vmem] * 2,
        compiler_params=params(16),
        cost_estimate=cost(10**6, 10**5),
        name="join_first",
    )(other_first, wt_other, mine)
    relay, direct, far_near, send_rest, other_rest = lax.optimization_barrier(
        (relay, direct, far_near, send_rest, other_rest)
    )
    arrived_rest = permuted(send_rest, inward)
    other_rest = permuted(other_rest, inward)
    along_x = [(i, i ^ 2) for i in range(devices)]
    x_sign = [1 if i // 2 % 2 else -1 for i in range(devices)]
    relay = permuted(relay, along_x)

    def merge_rows(rows, other, shift, name):
        return pl.pallas_call(
            functools.partial(merge_kernel, shift=shift),
            out_shape=block(NC, MERGED * BS),
            in_specs=[smem, vmem, vmem],
            out_specs=vmem,
            scratch_shapes=[pltpu.VMEM((BS, MERGED * BS), jnp.float32)],
            compiler_params=params(16),
            cost_estimate=cost(10**7, 10**7),
            name=name,
        )(core, rows, other)

    direct = merge_rows(direct, far_near, 2, "merge_far")
    direct = permuted(direct, [(i, (i + 4 * x_sign[i]) % devices) for i in range(devices)])
    merge, pair, own = pl.pallas_call(
        join_rest_kernel,
        out_shape=[block(NC, span, jnp.float32), block(NC, span), block(NC, span, jnp.float32)],
        in_specs=[vmem] * 7,
        out_specs=[vmem] * 3,
        compiler_params=params(30),
        cost_estimate=cost(40 * 10**9, 200 * 10**6),
        name="join_rest",
    )(fast_rest, slow_rest, other_rest, wt_fast, wt_slow, wt_other, arrived_rest)
    relay, pair = lax.optimization_barrier((relay, pair))
    merged = merge_rows(merge, relay, 0, "merge")
    merged, far = lax.optimization_barrier((merged, far))
    merged = permuted(merged, [(i, (i - 4 * x_sign[i]) % devices) for i in range(devices)])
    pair = permuted(pair, along_x)
    straight = [i for i in range(devices) if i % 4 in (0, 3)]
    far = permuted(far, [(i, (i + (5 if i % 2 else -5)) % devices) for i in straight])

    total = block(NC, BAND * BS, jnp.float32)
    frame = pltpu.VMEM((BS, FRAME * BS), jnp.float32)
    early = pl.pallas_call(
        early_kernel,
        out_shape=total,
        in_specs=[smem] + [vmem] * 4,
        out_specs=vmem,
        scratch_shapes=[frame],
        compiler_params=params(16),
        cost_estimate=cost(10**10, 100 * 10**6),
        name="early",
    )(core, own, direct, pair, merged)
    return pl.pallas_call(
        total_kernel,
        out_shape=total,
        in_specs=[smem] + [vmem] * 2,
        out_specs=hbm,
        scratch_shapes=[
            frame,
            pltpu.VMEM(total.shape, jnp.float32),
            pltpu.SemaphoreType.DMA((NC,)),
        ],
        compiler_params=params(20),
        cost_estimate=cost(10**7, 10**7),
        name="total",
    )(core, early, far)


def solution(mesh):
    in_specs = (P("dom", None, None), P("dom", None, None), P("dom", None), P("dom", None))
    out_specs = P("dom", None, None)
    return jax.shard_map(body, mesh=mesh, in_specs=in_specs, out_specs=out_specs, check_vma=False)
```

```python
import functools

import jax
import jax.numpy as jnp
from jax import lax
from jax.experimental import pallas as pl
from jax.experimental.pallas import tpu as pltpu
from jax.sharding import PartitionSpec as P

BS = 64
KA = 7
KP = 27
AGG = 8
H = 15
NC = 3
NB = 24
WIN = 31
WSLOT = 33
BAND = 63

QUAD = 4
LANES = QUAD * BS
EXT = NB + 2 * AGG
COLS = NC + 2 * H + 2
WCOLS = 40
WINDOW = 38
TILES = 10
GROUPS = 5
K = NB * BS
AW = AGG * BS
FRAME = 80
NT = (((1,), (1,)), ((), ()))
ROWS = NC * GROUPS
FIRST = 2 * NC
REST = ROWS - FIRST
MERGED = WINDOW + 6
FAR = 36


def eye(n):
    rows = lax.broadcasted_iota(jnp.int32, (n, n), 0)
    lanes = lax.broadcasted_iota(jnp.int32, (n, n), 1)
    return jnp.where(rows == lanes, 1.0, 0.0).astype(jnp.bfloat16)


def low_half():
    return lax.broadcasted_iota(jnp.int32, (BS, 2 * BS), 1) < BS


def places(device):
    return device[0] % 2, device[0] // 2 % 2


def transpose_quad(unit, block, turned, width):
    for start in range(0, width, LANES):
        size = min(LANES, width - start)
        part = lax.dot_general(
            unit[:size, :size],
            block[:, start : start + size],
            NT,
            preferred_element_type=jnp.float32,
        )
        turned[start // BS : (start + size) // BS] = part.astype(jnp.bfloat16).reshape(
            size // BS, BS, LANES
        )


def spread_quad(turned, index, first, store, count):
    half = low_half()
    for slot in range(count):
        for pair in range(2):
            lanes = slice(pair * 2 * BS, (pair + 1) * 2 * BS)
            left = turned[index[first + 2 * pair, slot], :, lanes]
            right = turned[index[first + 2 * pair + 1, slot], :, lanes]
            store(slot, pair, jnp.where(half, left, right))


def turn_and_spread(count, turn, spread, buffers):
    even, odd = buffers
    turn(0, even)

    def two(step):
        turn(2 * step + 1, odd)
        spread(2 * step, even)
        turn(2 * step + 2, even)
        spread(2 * step + 1, odd)

    if count > 2:
        pl.loop(0, count // 2 - 1)(two)

    turn(count - 1, odd)
    spread(count - 2, even)
    spread(count - 1, odd)


def fast_kernel(
    core,
    inv_p,
    inv_a,
    p_own,
    p_fast,
    a_own,
    send_low,
    send_high,
    far,
    inner,
    send_rest,
    fast_rest,
    slow_first,
    slow_rest,
    slow_far,
    other_first,
    other_rest,
    wt,
    rest,
    at_halo,
    p_buf,
    ext,
    at,
    unit,
    turned_p,
    turned_p2,
    turned_a,
    turned_a2,
    lhs,
    rows_buf,
    fast_buf,
    slow_buf,
    other_buf,
    wt_buf,
    rest_buf,
    in_sems,
    out_sems,
):
    s, x = places(core)
    own_quads = NB // QUAD
    halo_quads = AGG // QUAD

    def load(quad):
        if quad < own_quads:
            source = p_own.at[quad * QUAD : (quad + 1) * QUAD]
        else:
            source = p_fast.at[(quad - own_quads) * QUAD : (quad - own_quads + 1) * QUAD]
        target = p_buf.at[quad * QUAD : (quad + 1) * QUAD]
        return pltpu.make_async_copy(source, target, in_sems.at[quad])

    for quad in range(own_quads + halo_quads):
        load(quad).start()

    unit[...] = eye(LANES)
    for buffers, empty in (((turned_p, turned_p2), KP), ((turned_a, turned_a2), KA)):
        for buffer in buffers:
            buffer[empty] = jnp.zeros((BS, LANES), jnp.bfloat16)

    def turn_a(quad, turned):
        block = a_own[pl.ds(quad * QUAD, QUAD)].reshape(LANES, KA * BS)
        transpose_quad(unit, block, turned, KA * BS)

    def spread_a(quad, turned):
        agg = quad // halo_quads
        first_lane = (quad % halo_quads) * LANES

        def store(slot, pair, value):
            lane = pl.multiple_of(first_lane + pair * 2 * BS, 2 * BS)
            at[agg, slot, :, pl.ds(lane, 2 * BS)] = value

        spread_quad(turned, inv_a, quad * QUAD, store, 3 * AGG)

    turn_and_spread(own_quads, turn_a, spread_a, (turned_a, turned_a2))

    slow_agg = 2 * s
    halo_copy = pltpu.make_async_copy(at.at[slow_agg, pl.ds(16 * s, AGG)], at_halo, out_sems.at[0])
    halo_copy.start()

    def turn_p(quad, turned):
        block = p_buf[pl.ds(quad * QUAD, QUAD)].reshape(LANES, KP * BS)
        transpose_quad(unit, block, turned, KP * BS)

    def spread_p(quad, turned):
        own_lane = AW + quad * LANES
        halo_lane = (AW + K) * (1 - s) + (quad - own_quads) * LANES
        first_lane = jnp.where(quad < own_quads, own_lane, halo_lane)

        def store(slot, pair, value):
            lane = pl.multiple_of(first_lane + pair * 2 * BS, 2 * BS)
            ext[slot, :, pl.ds(lane, 2 * BS)] = value

        spread_quad(turned, inv_p, quad * QUAD, store, COLS)

    for quad in range(own_quads + halo_quads):
        load(quad).wait()
    turn_and_spread(own_quads + halo_quads, turn_p, spread_p, (turned_p, turned_p2))

    fast_lanes = pl.ds(pl.multiple_of(AW + (1 - s) * AW, AW), 2 * AW)
    slow_lanes = pl.ds(pl.multiple_of(AW + 2 * s * AW, AW), AW)
    for place, i in enumerate((1 + 2 * x, 4 * x, 4 - 4 * x, 3 - 2 * x, 2)):
        for j in range(NC):
            row = NC * place + j
            mine, other = 6 * i + 3 + j + 1, 6 * i + 6 * (1 - s) + j + 1
            if place < 2:
                lhs[row] = ext[other, :, fast_lanes]
                lhs[FIRST + NC + row] = ext[mine, :, fast_lanes]
            else:
                lhs[ROWS + row - FIRST] = ext[other, :, fast_lanes]
                fast_buf[row - FIRST] = ext[mine, :, fast_lanes]
            slow_buf[row] = ext[mine, :, slow_lanes]
            other_buf[row] = ext[other, :, slow_lanes]
    for j in range(NC):
        lhs[FIRST + j] = ext[30 * s + j + 1, :, fast_lanes]
        slow_buf[ROWS + j] = ext[30 * s + j + 1, :, slow_lanes]
    copies = [halo_copy]

    def write(source, target):
        copy = pltpu.make_async_copy(source, target, out_sems.at[len(copies)])
        copy.start()
        copies.append(copy)

    write(other_buf.at[:FIRST], other_first)
    write(other_buf.at[FIRST:], other_rest)
    write(fast_buf, fast_rest)
    write(slow_buf.at[:FIRST], slow_first)
    write(slow_buf.at[FIRST:ROWS], slow_rest)
    write(slow_buf.at[ROWS:], slow_far)

    wt_buf[0:7] = jnp.zeros((7, BS, 2 * AW), jnp.bfloat16)
    wt_buf[33:] = jnp.zeros((WCOLS - 33, BS, 2 * AW), jnp.bfloat16)
    chunk = WSLOT // 3

    @pl.loop(0, 2)
    def _(place):
        agg = place + 1 - s
        lane = pl.multiple_of(agg * AW, AW)
        target = pl.multiple_of(place * AW, AW)

        @pl.loop(0, 3)
        def _(part):
            first = agg + part * chunk
            left = ext[pl.ds(first, chunk), :, pl.ds(lane, 3 * AW)].reshape(chunk * BS, 3 * AW)
            value = jnp.dot(
                left, at[agg].reshape(3 * AW, AW), preferred_element_type=jnp.float32
            )
            wt_buf[pl.ds(3 * s + first, chunk), :, pl.ds(target, AW)] = value.astype(
                jnp.bfloat16
            ).reshape(chunk, BS, AW)

    write(wt_buf, wt)

    @pl.loop(0, 3)
    def _(part):
        lane = pl.multiple_of(AW + s * AW, AW)
        left = ext[pl.ds(slow_agg + part * chunk, chunk), :, pl.ds(lane, 2 * AW)]
        right = at[slow_agg, pl.ds(AGG - AGG * s, 2 * AGG)].reshape(2 * AW, AW)
        value = jnp.dot(
            left.reshape(chunk * BS, 2 * AW), right, preferred_element_type=jnp.float32
        )
        rest_buf[pl.ds(part * chunk, chunk)] = value.reshape(chunk, BS, AW)

    write(rest_buf, rest)

    def emit(tile, width):
        right = wt_buf[pl.ds(QUAD * tile, width // BS)].reshape(width, 2 * AW)
        left = lhs[...].reshape((ROWS + REST) * BS, 2 * AW)
        value = lax.dot_general(left, right, NT, preferred_element_type=jnp.float32)
        rows_buf[:, :, tile_lanes(tile, width)] = value.astype(jnp.bfloat16).reshape(
            ROWS + REST, BS, width
        )

    parts = (
        (send_low, 0),
        (send_high, NC),
        (far, FIRST),
        (inner, FIRST + NC),
        (send_rest, ROWS),
    )
    bounds = (0, 4, 8, TILES)
    for first, last in zip(bounds[:-1], bounds[1:]):

        @pl.loop(first, min(last, TILES - 1))
        def _(tile):
            emit(tile, LANES)

        if last == TILES:
            emit(TILES - 1, LANES // 2)
        lanes = slice(first * LANES, min(last * LANES, WINDOW * BS))
        for target, row in parts:
            rows = slice(row, row + target.shape[0])
            write(rows_buf.at[rows, :, lanes], target.at[:, :, lanes])
    for copy in copies:
        copy.wait()


def each_tile(step):
    @pl.loop(0, TILES - 1)
    def _(tile):
        step(tile, LANES)

    step(TILES - 1, LANES // 2)


def tile_dot(rows, cols, tile, width):
    left = rows[...].reshape(rows.shape[0] * BS, rows.shape[2])
    right = cols[pl.ds(QUAD * tile, width // BS)].reshape(width, cols.shape[2])
    value = lax.dot_general(left, right, NT, preferred_element_type=jnp.float32)
    return value.reshape(rows.shape[0], BS, width)


def tile_lanes(tile, width):
    return pl.ds(pl.multiple_of(tile * LANES, LANES), width)


def far_kernel(core, slow, wt_slow, far_fast, far):
    s, x = places(core)

    @pl.loop(0, FAR // QUAD)
    def _(tile):
        left = slow[...].reshape(NC * BS, AW)
        right = wt_slow[pl.ds(QUAD * tile + 2 * s, QUAD)].reshape(LANES, AW)
        value = lax.dot_general(left, right, NT, preferred_element_type=jnp.float32)
        lanes = pl.ds(pl.multiple_of(tile * LANES + 2 * BS * s, 2 * BS), LANES)
        value = value.reshape(NC, BS, LANES) + far_fast[:, :, lanes].astype(jnp.float32)
        far[:, :, tile_lanes(tile, LANES)] = value.astype(jnp.bfloat16)


def mine_kernel(slow, wt_slow, inner, low, high, out):
    def step(tile, width):
        lanes = tile_lanes(tile, width)
        near = tile_dot(slow, wt_slow, tile, width) + inner[:, :, lanes].astype(jnp.float32)
        out[:NC, :, lanes] = near[:NC] + low[:, :, lanes].astype(jnp.float32)
        out[NC:, :, lanes] = near[NC:] + high[:, :, lanes].astype(jnp.float32)

    each_tile(step)


def slow_kernel(core, inv_slow, p_slow, at_halo, rest, wt, unit, turned_p, turned_p2, ext):
    s, x = places(core)
    unit[...] = eye(LANES)
    for buffer in (turned_p, turned_p2):
        buffer[KP] = jnp.zeros((BS, LANES), jnp.bfloat16)

    def turn(quad, turned):
        block = p_slow[quad * QUAD : (quad + 1) * QUAD].reshape(LANES, KP * BS)
        transpose_quad(unit, block, turned, KP * BS)

    def spread(quad, turned):
        def store(slot, pair, value):
            lane = quad * LANES + pair * 2 * BS
            ext[slot, :, lane : lane + 2 * BS] = value

        spread_quad(turned, inv_slow, quad * QUAD, store, WSLOT)

    turn_and_spread(AGG // QUAD, turn, spread, (turned_p, turned_p2))
    wt[0:5] = jnp.zeros((5, BS, AW), jnp.bfloat16)
    wt[WSLOT:] = jnp.zeros((WCOLS - WSLOT, BS, AW), jnp.bfloat16)
    chunk = WSLOT // 3

    @pl.loop(0, 3)
    def _(part):
        rows = pl.ds(part * chunk, chunk)
        value = jnp.dot(
            ext[rows].reshape(chunk * BS, AW),
            at_halo[...].reshape(AW, AW),
            preferred_element_type=jnp.float32,
        )
        value = value.reshape(chunk, BS, AW) + rest[rows]
        wt[pl.ds(5 * s + part * chunk, chunk)] = value.astype(jnp.bfloat16)


def join_first_kernel(other, wt_other, mine, relay, direct):
    def step(tile, width):
        lanes = tile_lanes(tile, width)
        value = tile_dot(other, wt_other, tile, width) + mine[:, :, lanes]
        relay[:, :, lanes] = value[:NC].astype(jnp.bfloat16)
        direct[:, :, lanes] = value[NC:]

    each_tile(step)


def join_rest_kernel(fast, slow, other, wt_fast, wt_slow, wt_other, arrived, merge, pair, own):
    def step(tile, width):
        lanes = tile_lanes(tile, width)
        value = tile_dot(fast, wt_fast, tile, width) + tile_dot(slow, wt_slow, tile, width)
        value = value + tile_dot(other, wt_other, tile, width)
        value = value + arrived[:, :, lanes].astype(jnp.float32)
        merge[:, :, lanes] = value[:NC]
        pair[:, :, lanes] = value[NC : 2 * NC].astype(jnp.bfloat16)
        own[:, :, lanes] = value[2 * NC :]

    each_tile(step)


def stage_kernel(at_halo, rest, at_out, rest_out, sems):
    copies = [
        pltpu.make_async_copy(at_halo, at_out, sems.at[0]),
        pltpu.make_async_copy(rest, rest_out, sems.at[1]),
    ]
    for copy in copies:
        copy.start()
    for copy in copies:
        copy.wait()


def merge_kernel(core, rows, other, out, frame, *, shift):
    s, x = places(core)
    step = 6 * BS
    for j in range(NC):
        frame[...] = jnp.zeros_like(frame)
        frame[:, pl.ds(pl.multiple_of(step * x, step), WINDOW * BS)] = rows[j]
        lane = pl.multiple_of(step * (1 - x) + shift * BS * x, 2 * BS)
        lanes = pl.ds(lane, other.shape[2])
        frame[:, lanes] += other[j].astype(jnp.float32)
        out[j] = frame[...].astype(jnp.bfloat16)


def in_frame(s, j, frame, messages, store):
    odd = (j + 1 - s) % 2
    frame[...] = jnp.zeros_like(frame)
    for message, start in messages:
        lane = pl.multiple_of((start - odd + 8) * BS, 2 * BS)
        frame[:, pl.ds(lane, message.shape[2])] += message[j].astype(jnp.float32)
    first, last = 8 * BS, (8 + BAND) * BS

    @pl.when(odd == 0)
    def _():
        store(frame[:, first:last])

    @pl.when(odd == 1)
    def _():
        store(frame[:, first - BS : last - BS])


def early_kernel(core, own, direct, far, out, frame):
    s, x = places(core)
    for j in range(NC):
        top = 27 - 3 * s - j
        messages = [(own, top - 12), (direct, top - 30 * x)]
        messages.append((far, jnp.where(s == 1, 30 - j, -1 - j)))

        def store(value, j=j):
            out[j] = value

        in_frame(s, j, frame, messages, store)


def total_kernel(core, early, pair, merged, out, frame, buf, sems):
    s, x = places(core)
    copies = []
    for j in range(NC):
        top = 27 - 3 * s - j

        def store(value, j=j):
            buf[j] = value + early[j]

        messages = [(pair, top - 6 - 12 * x), (merged, top - 24 + 18 * x)]
        in_frame(s, j, frame, messages, store)
        copy = pltpu.make_async_copy(buf.at[j], out.at[j], sems.at[j])
        copy.start()
        copies.append(copy)
    for copy in copies:
        copy.wait()


def pick_kernel(core, source, outer, inner, buf, in_sems, out_sems):
    s, x = places(core)
    step = AGG // 4
    reads, writes = [], []
    for side, (target, which) in enumerate(((outer, s), (inner, 1 - s))):
        for k in range(4):
            n = len(reads)
            rows = pl.ds((NB - AGG) * which + k * step, step)
            part = buf.at[side, k * step : (k + 1) * step]
            into = target.at[k * step : (k + 1) * step]
            reads.append(pltpu.make_async_copy(source.at[rows], part, in_sems.at[n]))
            writes.append(pltpu.make_async_copy(part, into, out_sems.at[n]))
    for copy in reads:
        copy.start()
    for read, write in zip(reads, writes):
        read.wait()
        write.start()
    for copy in writes:
        copy.wait()


def permuted(block, pairs):
    return lax.ppermute(block, "dom", pairs)


def inverse_index(offset, slots, empty):
    order = jnp.arange(offset.shape[1], dtype=jnp.int32)[None, :, None]
    hit = offset[:, :, None] == jnp.arange(slots, dtype=jnp.int32)[None, None, :]
    return empty + jnp.sum(jnp.where(hit, order - empty, 0), axis=1)


def body(a_blocks, p_blocks, cols_a, cols_p):
    devices = lax.axis_size("dom")
    device = lax.axis_index("dom")
    count_agg = NC * devices
    count_rows = NB * devices
    first_agg = device * NC
    first_row = device * NB
    core = device.astype(jnp.int32).reshape(1)

    def shifted(distance):
        return [(i, (i + distance) % devices) for i in range(devices)]

    parity = device % 2
    smem = pl.BlockSpec(memory_space=pltpu.SMEM)
    vmem = pl.BlockSpec(memory_space=pltpu.VMEM)
    hbm = pl.BlockSpec(memory_space=pltpu.HBM)
    bf16 = jnp.bfloat16

    def params(mebibytes):
        return pltpu.CompilerParams(vmem_limit_bytes=mebibytes * 1024 * 1024)

    def cost(flops, size):
        return pl.CostEstimate(flops=flops, bytes_accessed=size, transcendentals=0)

    edge = jax.ShapeDtypeStruct((AGG,) + p_blocks.shape[1:], bf16)
    outer, inner = pl.pallas_call(
        pick_kernel,
        out_shape=[edge, edge],
        in_specs=[smem, hbm],
        out_specs=[hbm, hbm],
        scratch_shapes=[
            pltpu.VMEM((2,) + edge.shape, bf16),
            pltpu.SemaphoreType.DMA((8,)),
            pltpu.SemaphoreType.DMA((8,)),
        ],
        compiler_params=params(60),
        name="pick",
    )(core, p_blocks)
    outward = [(i, (i + (1 if i % 2 else -1)) % devices) for i in range(devices)]
    inward = [(i, i ^ 1) for i in range(devices)]
    outer, inner, edge_cols = lax.optimization_barrier((outer, inner, cols_p))
    p_slow = permuted(outer, outward)
    p_fast = permuted(inner, inward)
    edge_cols = jnp.stack([edge_cols[:AGG], edge_cols[NB - AGG :]])
    cols_slow = permuted(edge_cols[parity], outward)
    cols_fast = permuted(edge_cols[1 - parity], inward)

    def slots(cols, agg):
        return (cols - agg + H) % count_agg

    own_agg = jnp.arange(NB, dtype=jnp.int32)[:, None] // AGG
    inv_own = inverse_index(slots(cols_p, first_agg + own_agg) + own_agg + 1, COLS, KP)
    fast_place = NC * (1 - parity) - parity
    inv_fast = inverse_index(slots(cols_fast, first_agg + fast_place) + fast_place + 1, COLS, KP)
    slow_place = NC * parity - (1 - parity)
    inv_slow = inverse_index(slots(cols_slow, first_agg + slow_place) + 2 * parity, WSLOT, KP)
    inv_fast, inv_slow = lax.optimization_barrier((inv_fast, inv_slow))
    inv_a = inverse_index((cols_a - first_row - (own_agg - 1) * AGG) % count_rows, 3 * AGG, KA)

    def block(rows, width, kind=bf16):
        return jax.ShapeDtypeStruct((rows, BS, width), kind)

    span = WINDOW * BS
    outs = [
        block(NC, span),
        block(NC, span),
        block(NC, span),
        block(FIRST, span),
        block(REST, span),
        block(REST, 2 * AW),
        block(FIRST, AW),
        block(REST, AW),
        block(NC, AW),
        block(FIRST, AW),
        block(REST, AW),
        block(WCOLS, 2 * AW),
        block(WSLOT, AW, jnp.float32),
        block(AGG, AW),
    ]
    (
        send_low,
        send_high,
        far,
        inner,
        send_rest,
        fast_rest,
        slow_first,
        slow_rest,
        slow_far,
        other_first,
        other_rest,
        wt_fast,
        rest,
        at_halo,
    ) = pl.pallas_call(
        fast_kernel,
        out_shape=outs,
        in_specs=[smem] * 3 + [hbm, hbm, vmem],
        out_specs=[hbm] * len(outs),
        scratch_shapes=[
            pltpu.VMEM((NB + AGG, BS, KP * BS), bf16),
            pltpu.VMEM((COLS, BS, EXT * BS), bf16),
            pltpu.VMEM((NC, 3 * AGG, BS, AW), bf16),
            pltpu.VMEM((LANES, LANES), bf16),
            pltpu.VMEM((KP + 1, BS, LANES), bf16),
            pltpu.VMEM((KP + 1, BS, LANES), bf16),
            pltpu.VMEM((KA + 1, BS, LANES), bf16),
            pltpu.VMEM((KA + 1, BS, LANES), bf16),
            pltpu.VMEM((ROWS + REST, BS, 2 * AW), bf16),
            pltpu.VMEM((ROWS + REST, BS, span), bf16),
            pltpu.VMEM((REST, BS, 2 * AW), bf16),
            pltpu.VMEM((ROWS + NC, BS, AW), bf16),
            pltpu.VMEM((ROWS, BS, AW), bf16),
            pltpu.VMEM((WCOLS, BS, 2 * AW), bf16),
            pltpu.VMEM((WSLOT, BS, AW), jnp.float32),
            pltpu.SemaphoreType.DMA(((NB + AGG) // QUAD,)),
            pltpu.SemaphoreType.DMA((len(outs) + 10,)),
        ],
        compiler_params=params(56),
        cost_estimate=cost(20 * 10**9, 30 * 10**6),
        name="fast",
    )(core, jnp.concatenate([inv_own, inv_fast]), inv_a, p_blocks, p_fast, a_blocks)

    low = permuted(send_low, inward)
    high = permuted(send_high, inward)
    other_first = permuted(other_first, inward)
    at_halo, rest = pl.pallas_call(
        stage_kernel,
        out_shape=[block(AGG, AW), block(WSLOT, AW, jnp.float32)],
        in_specs=[hbm] * 2,
        out_specs=[vmem] * 2,
        scratch_shapes=[pltpu.SemaphoreType.DMA((2,))],
        compiler_params=params(8),
        cost_estimate=cost(10**6, 10**6),
        name="stage",
    )(at_halo, rest)
    p_slow, low, high, other_first = lax.optimization_barrier((p_slow, low, high, other_first))

    wt_slow = pl.pallas_call(
        slow_kernel,
        out_shape=block(WCOLS, AW),
        in_specs=[smem] * 2 + [vmem] * 3,
        out_specs=vmem,
        scratch_shapes=[
            pltpu.VMEM((LANES, LANES), bf16),
            pltpu.VMEM((KP + 1, BS, LANES), bf16),
            pltpu.VMEM((KP + 1, BS, LANES), bf16),
            pltpu.VMEM((WSLOT, BS, AW), bf16),
        ],
        compiler_params=params(24),
        cost_estimate=cost(20 * 10**9, 200 * 10**6),
        name="slow",
    )(core, inv_slow, p_slow, at_halo, rest)
    wt_other = permuted(wt_slow, inward)

    wt_slow, low, high = lax.optimization_barrier((wt_slow, low, high))
    far = pl.pallas_call(
        far_kernel,
        out_shape=block(NC, FAR * BS),
        in_specs=[smem] + [vmem] * 3,
        out_specs=vmem,
        compiler_params=params(16),
        cost_estimate=cost(10**9, 10**7),
        name="far",
    )(core, slow_far, wt_slow, far)
    far, wt_slow = lax.optimization_barrier((far, wt_slow))
    mine = pl.pallas_call(
        mine_kernel,
        out_shape=block(FIRST, span, jnp.float32),
        in_specs=[vmem] * 5,
        out_specs=vmem,
        compiler_params=params(24),
        cost_estimate=cost(10**10, 100 * 10**6),
        name="mine",
    )(slow_first, wt_slow, inner, low, high)
    crossing = [i for i in range(devices) if i % 4 in (1, 2)]
    far_near = permuted(far, [(i, i ^ 3) for i in crossing])
    relay, direct = pl.pallas_call(
        join_first_kernel,
        out_shape=[block(NC, span), block(NC, span, jnp.float32)],
        in_specs=[vmem] * 3,
        out_specs=[vmem] * 2,
        compiler_params=params(16),
        cost_estimate=cost(10**6, 10**5),
        name="join_first",
    )(other_first, wt_other, mine)
    relay, direct, far_near, send_rest, other_rest = lax.optimization_barrier(
        (relay, direct, far_near, send_rest, other_rest)
    )
    arrived_rest = permuted(send_rest, inward)
    other_rest = permuted(other_rest, inward)
    along_x = [(i, i ^ 2) for i in range(devices)]
    x_sign = [1 if i // 2 % 2 else -1 for i in range(devices)]
    relay = permuted(relay, along_x)

    def merge_rows(rows, other, shift, name):
        return pl.pallas_call(
            functools.partial(merge_kernel, shift=shift),
            out_shape=block(NC, MERGED * BS),
            in_specs=[smem, vmem, vmem],
            out_specs=vmem,
            scratch_shapes=[pltpu.VMEM((BS, MERGED * BS), jnp.float32)],
            compiler_params=params(16),
            cost_estimate=cost(10**7, 10**7),
            name=name,
        )(core, rows, other)

    direct = merge_rows(direct, far_near, 2, "merge_far")
    direct = permuted(direct, [(i, (i + 4 * x_sign[i]) % devices) for i in range(devices)])
    merge, pair, own = pl.pallas_call(
        join_rest_kernel,
        out_shape=[block(NC, span, jnp.float32), block(NC, span), block(NC, span, jnp.float32)],
        in_specs=[vmem] * 7,
        out_specs=[vmem] * 3,
        compiler_params=params(30),
        cost_estimate=cost(40 * 10**9, 200 * 10**6),
        name="join_rest",
    )(fast_rest, slow_rest, other_rest, wt_fast, wt_slow, wt_other, arrived_rest)
    pair, far = lax.optimization_barrier((pair, far))
    relay, pair = lax.optimization_barrier((relay, pair))
    merged = merge_rows(merge, relay, 0, "merge")
    merged = permuted(merged, [(i, (i - 4 * x_sign[i]) % devices) for i in range(devices)])
    pair = permuted(pair, along_x)
    straight = [i for i in range(devices) if i % 4 in (0, 3)]
    far = permuted(far, [(i, (i + (5 if i % 2 else -5)) % devices) for i in straight])

    total = block(NC, BAND * BS, jnp.float32)
    frame = pltpu.VMEM((BS, FRAME * BS), jnp.float32)
    early = pl.pallas_call(
        early_kernel,
        out_shape=total,
        in_specs=[smem] + [vmem] * 3,
        out_specs=vmem,
        scratch_shapes=[frame],
        compiler_params=params(16),
        cost_estimate=cost(10**10, 100 * 10**6),
        name="early",
    )(core, own, direct, far)
    return pl.pallas_call(
        total_kernel,
        out_shape=total,
        in_specs=[smem] + [vmem] * 3,
        out_specs=hbm,
        scratch_shapes=[
            frame,
            pltpu.VMEM(total.shape, jnp.float32),
            pltpu.SemaphoreType.DMA((NC,)),
        ],
        compiler_params=params(20),
        cost_estimate=cost(10**7, 10**7),
        name="total",
    )(core, early, pair, merged)


def solution(mesh):
    in_specs = (P("dom", None, None), P("dom", None, None), P("dom", None), P("dom", None))
    out_specs = P("dom", None, None)
    return jax.shard_map(body, mesh=mesh, in_specs=in_specs, out_specs=out_specs, check_vma=False)
```

```python
import functools

import jax
import jax.numpy as jnp
from jax import lax
from jax.experimental import pallas as pl
from jax.experimental.pallas import tpu as pltpu
from jax.sharding import PartitionSpec as P

BS = 64
KA = 7
KP = 27
AGG = 8
H = 15
NC = 3
NB = 24
WIN = 31
WSLOT = 33
BAND = 63

QUAD = 4
LANES = QUAD * BS
EXT = NB + 2 * AGG
COLS = NC + 2 * H + 2
WCOLS = 40
WINDOW = 38
TILES = 10
GROUPS = 5
K = NB * BS
AW = AGG * BS
FRAME = 80
NT = (((1,), (1,)), ((), ()))
ROWS = NC * GROUPS
FIRST = 2 * NC
REST = ROWS - FIRST
MERGED = WINDOW + 6
FAR = 36


def eye(n):
    rows = lax.broadcasted_iota(jnp.int32, (n, n), 0)
    lanes = lax.broadcasted_iota(jnp.int32, (n, n), 1)
    return jnp.where(rows == lanes, 1.0, 0.0).astype(jnp.bfloat16)


def low_half():
    return lax.broadcasted_iota(jnp.int32, (BS, 2 * BS), 1) < BS


def places(device):
    return device[0] % 2, device[0] // 2 % 2


def transpose_quad(unit, block, turned, width):
    for start in range(0, width, LANES):
        size = min(LANES, width - start)
        part = lax.dot_general(
            unit[:size, :size],
            block[:, start : start + size],
            NT,
            preferred_element_type=jnp.float32,
        )
        turned[start // BS : (start + size) // BS] = part.astype(jnp.bfloat16).reshape(
            size // BS, BS, LANES
        )


def spread_quad(turned, index, first, store, count):
    half = low_half()
    for slot in range(count):
        for pair in range(2):
            lanes = slice(pair * 2 * BS, (pair + 1) * 2 * BS)
            left = turned[index[first + 2 * pair, slot], :, lanes]
            right = turned[index[first + 2 * pair + 1, slot], :, lanes]
            store(slot, pair, jnp.where(half, left, right))


def turn_and_spread(count, turn, spread, buffers):
    even, odd = buffers
    turn(0, even)

    def two(step):
        turn(2 * step + 1, odd)
        spread(2 * step, even)
        turn(2 * step + 2, even)
        spread(2 * step + 1, odd)

    if count > 2:
        pl.loop(0, count // 2 - 1)(two)

    turn(count - 1, odd)
    spread(count - 2, even)
    spread(count - 1, odd)


def fast_kernel(
    core,
    inv_p,
    inv_a,
    p_own,
    p_fast,
    a_own,
    send_low,
    send_high,
    far,
    inner,
    send_rest,
    fast_rest,
    slow_first,
    slow_rest,
    slow_far,
    other_first,
    other_rest,
    wt,
    rest,
    at_halo,
    p_buf,
    ext,
    at,
    unit,
    turned_p,
    turned_p2,
    turned_a,
    turned_a2,
    lhs,
    rows_buf,
    fast_buf,
    slow_buf,
    other_buf,
    wt_buf,
    rest_buf,
    in_sems,
    out_sems,
):
    s, x = places(core)
    own_quads = NB // QUAD
    halo_quads = AGG // QUAD

    def load(quad):
        if quad < own_quads:
            source = p_own.at[quad * QUAD : (quad + 1) * QUAD]
        else:
            source = p_fast.at[(quad - own_quads) * QUAD : (quad - own_quads + 1) * QUAD]
        target = p_buf.at[quad * QUAD : (quad + 1) * QUAD]
        return pltpu.make_async_copy(source, target, in_sems.at[quad])

    for quad in range(own_quads + halo_quads):
        load(quad).start()

    unit[...] = eye(LANES)
    for buffers, empty in (((turned_p, turned_p2), KP), ((turned_a, turned_a2), KA)):
        for buffer in buffers:
            buffer[empty] = jnp.zeros((BS, LANES), jnp.bfloat16)

    def turn_a(quad, turned):
        block = a_own[pl.ds(quad * QUAD, QUAD)].reshape(LANES, KA * BS)
        transpose_quad(unit, block, turned, KA * BS)

    def spread_a(quad, turned):
        agg = quad // halo_quads
        first_lane = (quad % halo_quads) * LANES

        def store(slot, pair, value):
            lane = pl.multiple_of(first_lane + pair * 2 * BS, 2 * BS)
            at[agg, slot, :, pl.ds(lane, 2 * BS)] = value

        spread_quad(turned, inv_a, quad * QUAD, store, 3 * AGG)

    turn_and_spread(own_quads, turn_a, spread_a, (turned_a, turned_a2))

    slow_agg = 2 * s
    halo_copy = pltpu.make_async_copy(at.at[slow_agg, pl.ds(16 * s, AGG)], at_halo, out_sems.at[0])
    halo_copy.start()

    def turn_p(quad, turned):
        block = p_buf[pl.ds(quad * QUAD, QUAD)].reshape(LANES, KP * BS)
        transpose_quad(unit, block, turned, KP * BS)

    def spread_p(quad, turned):
        own_lane = AW + quad * LANES
        halo_lane = (AW + K) * (1 - s) + (quad - own_quads) * LANES
        first_lane = jnp.where(quad < own_quads, own_lane, halo_lane)

        def store(slot, pair, value):
            lane = pl.multiple_of(first_lane + pair * 2 * BS, 2 * BS)
            ext[slot, :, pl.ds(lane, 2 * BS)] = value

        spread_quad(turned, inv_p, quad * QUAD, store, COLS)

    for quad in range(own_quads + halo_quads):
        load(quad).wait()
    turn_and_spread(own_quads + halo_quads, turn_p, spread_p, (turned_p, turned_p2))

    fast_lanes = pl.ds(pl.multiple_of(AW + (1 - s) * AW, AW), 2 * AW)
    slow_lanes = pl.ds(pl.multiple_of(AW + 2 * s * AW, AW), AW)
    for place, i in enumerate((1 + 2 * x, 4 * x, 4 - 4 * x, 3 - 2 * x, 2)):
        for j in range(NC):
            row = NC * place + j
            mine, other = 6 * i + 3 + j + 1, 6 * i + 6 * (1 - s) + j + 1
            if place < 2:
                lhs[row] = ext[other, :, fast_lanes]
                lhs[FIRST + NC + row] = ext[mine, :, fast_lanes]
            else:
                lhs[ROWS + row - FIRST] = ext[other, :, fast_lanes]
                fast_buf[row - FIRST] = ext[mine, :, fast_lanes]
            slow_buf[row] = ext[mine, :, slow_lanes]
            other_buf[row] = ext[other, :, slow_lanes]
    for j in range(NC):
        lhs[FIRST + j] = ext[30 * s + j + 1, :, fast_lanes]
        slow_buf[ROWS + j] = ext[30 * s + j + 1, :, slow_lanes]
    copies = [halo_copy]

    def write(source, target):
        copy = pltpu.make_async_copy(source, target, out_sems.at[len(copies)])
        copy.start()
        copies.append(copy)

    write(other_buf.at[:FIRST], other_first)
    write(other_buf.at[FIRST:], other_rest)
    write(fast_buf, fast_rest)
    write(slow_buf.at[:FIRST], slow_first)
    write(slow_buf.at[FIRST:ROWS], slow_rest)
    write(slow_buf.at[ROWS:], slow_far)

    wt_buf[0:7] = jnp.zeros((7, BS, 2 * AW), jnp.bfloat16)
    wt_buf[33:] = jnp.zeros((WCOLS - 33, BS, 2 * AW), jnp.bfloat16)
    chunk = WSLOT // 3

    @pl.loop(0, 2)
    def _(place):
        agg = place + 1 - s
        lane = pl.multiple_of(agg * AW, AW)
        target = pl.multiple_of(place * AW, AW)

        @pl.loop(0, 3)
        def _(part):
            first = agg + part * chunk
            left = ext[pl.ds(first, chunk), :, pl.ds(lane, 3 * AW)].reshape(chunk * BS, 3 * AW)
            value = jnp.dot(
                left, at[agg].reshape(3 * AW, AW), preferred_element_type=jnp.float32
            )
            wt_buf[pl.ds(3 * s + first, chunk), :, pl.ds(target, AW)] = value.astype(
                jnp.bfloat16
            ).reshape(chunk, BS, AW)

    write(wt_buf, wt)

    @pl.loop(0, 3)
    def _(part):
        lane = pl.multiple_of(AW + s * AW, AW)
        left = ext[pl.ds(slow_agg + part * chunk, chunk), :, pl.ds(lane, 2 * AW)]
        right = at[slow_agg, pl.ds(AGG - AGG * s, 2 * AGG)].reshape(2 * AW, AW)
        value = jnp.dot(
            left.reshape(chunk * BS, 2 * AW), right, preferred_element_type=jnp.float32
        )
        rest_buf[pl.ds(part * chunk, chunk)] = value.reshape(chunk, BS, AW)

    write(rest_buf, rest)

    def emit(tile, width):
        right = wt_buf[pl.ds(QUAD * tile, width // BS)].reshape(width, 2 * AW)
        left = lhs[...].reshape((ROWS + REST) * BS, 2 * AW)
        value = lax.dot_general(left, right, NT, preferred_element_type=jnp.float32)
        rows_buf[:, :, tile_lanes(tile, width)] = value.astype(jnp.bfloat16).reshape(
            ROWS + REST, BS, width
        )

    parts = (
        (send_low, 0),
        (send_high, NC),
        (far, FIRST),
        (inner, FIRST + NC),
        (send_rest, ROWS),
    )
    bounds = (0, 4, 8, TILES)
    for first, last in zip(bounds[:-1], bounds[1:]):

        @pl.loop(first, min(last, TILES - 1))
        def _(tile):
            emit(tile, LANES)

        if last == TILES:
            emit(TILES - 1, LANES // 2)
        lanes = slice(first * LANES, min(last * LANES, WINDOW * BS))
        for target, row in parts:
            rows = slice(row, row + target.shape[0])
            write(rows_buf.at[rows, :, lanes], target.at[:, :, lanes])
    for copy in copies:
        copy.wait()


def each_tile(step):
    @pl.loop(0, TILES - 1)
    def _(tile):
        step(tile, LANES)

    step(TILES - 1, LANES // 2)


def tile_dot(rows, cols, tile, width):
    left = rows[...].reshape(rows.shape[0] * BS, rows.shape[2])
    right = cols[pl.ds(QUAD * tile, width // BS)].reshape(width, cols.shape[2])
    value = lax.dot_general(left, right, NT, preferred_element_type=jnp.float32)
    return value.reshape(rows.shape[0], BS, width)


def tile_lanes(tile, width):
    return pl.ds(pl.multiple_of(tile * LANES, LANES), width)


def far_kernel(core, slow, wt_slow, far_fast, far):
    s, x = places(core)

    @pl.loop(0, FAR // QUAD)
    def _(tile):
        left = slow[...].reshape(NC * BS, AW)
        right = wt_slow[pl.ds(QUAD * tile + 2 * s, QUAD)].reshape(LANES, AW)
        value = lax.dot_general(left, right, NT, preferred_element_type=jnp.float32)
        lanes = pl.ds(pl.multiple_of(tile * LANES + 2 * BS * s, 2 * BS), LANES)
        value = value.reshape(NC, BS, LANES) + far_fast[:, :, lanes].astype(jnp.float32)
        far[:, :, tile_lanes(tile, LANES)] = value.astype(jnp.bfloat16)


def mine_kernel(slow, wt_slow, inner, low, high, out):
    def step(tile, width):
        lanes = tile_lanes(tile, width)
        near = tile_dot(slow, wt_slow, tile, width) + inner[:, :, lanes].astype(jnp.float32)
        out[:NC, :, lanes] = near[:NC] + low[:, :, lanes].astype(jnp.float32)
        out[NC:, :, lanes] = near[NC:] + high[:, :, lanes].astype(jnp.float32)

    each_tile(step)


def slow_kernel(core, inv_slow, p_slow, at_halo, rest, wt, unit, turned_p, turned_p2, ext):
    s, x = places(core)
    unit[...] = eye(LANES)
    for buffer in (turned_p, turned_p2):
        buffer[KP] = jnp.zeros((BS, LANES), jnp.bfloat16)

    def turn(quad, turned):
        block = p_slow[quad * QUAD : (quad + 1) * QUAD].reshape(LANES, KP * BS)
        transpose_quad(unit, block, turned, KP * BS)

    def spread(quad, turned):
        def store(slot, pair, value):
            lane = quad * LANES + pair * 2 * BS
            ext[slot, :, lane : lane + 2 * BS] = value

        spread_quad(turned, inv_slow, quad * QUAD, store, WSLOT)

    turn_and_spread(AGG // QUAD, turn, spread, (turned_p, turned_p2))
    wt[0:5] = jnp.zeros((5, BS, AW), jnp.bfloat16)
    wt[WSLOT:] = jnp.zeros((WCOLS - WSLOT, BS, AW), jnp.bfloat16)
    chunk = WSLOT // 3

    @pl.loop(0, 3)
    def _(part):
        rows = pl.ds(part * chunk, chunk)
        value = jnp.dot(
            ext[rows].reshape(chunk * BS, AW),
            at_halo[...].reshape(AW, AW),
            preferred_element_type=jnp.float32,
        )
        value = value.reshape(chunk, BS, AW) + rest[rows]
        wt[pl.ds(5 * s + part * chunk, chunk)] = value.astype(jnp.bfloat16)


def join_first_kernel(other, wt_other, mine, relay, direct):
    def step(tile, width):
        lanes = tile_lanes(tile, width)
        value = tile_dot(other, wt_other, tile, width) + mine[:, :, lanes]
        relay[:, :, lanes] = value[:NC].astype(jnp.bfloat16)
        direct[:, :, lanes] = value[NC:]

    each_tile(step)


def join_rest_kernel(fast, slow, other, wt_fast, wt_slow, wt_other, arrived, merge, pair, own):
    def step(tile, width):
        lanes = tile_lanes(tile, width)
        value = tile_dot(fast, wt_fast, tile, width) + tile_dot(slow, wt_slow, tile, width)
        value = value + tile_dot(other, wt_other, tile, width)
        value = value + arrived[:, :, lanes].astype(jnp.float32)
        merge[:, :, lanes] = value[:NC]
        pair[:, :, lanes] = value[NC : 2 * NC].astype(jnp.bfloat16)
        own[:, :, lanes] = value[2 * NC :]

    each_tile(step)


def stage_kernel(at_halo, rest, at_out, rest_out, sems):
    copies = [
        pltpu.make_async_copy(at_halo, at_out, sems.at[0]),
        pltpu.make_async_copy(rest, rest_out, sems.at[1]),
    ]
    for copy in copies:
        copy.start()
    for copy in copies:
        copy.wait()


def merge_kernel(core, rows, other, out, frame, *, shift):
    s, x = places(core)
    step = 6 * BS
    for j in range(NC):
        frame[...] = jnp.zeros_like(frame)
        frame[:, pl.ds(pl.multiple_of(step * x, step), WINDOW * BS)] = rows[j]
        lane = pl.multiple_of(step * (1 - x) + shift * BS * x, 2 * BS)
        lanes = pl.ds(lane, other.shape[2])
        frame[:, lanes] += other[j].astype(jnp.float32)
        out[j] = frame[...].astype(jnp.bfloat16)


def in_frame(s, j, frame, messages, store):
    odd = (j + 1 - s) % 2
    frame[...] = jnp.zeros_like(frame)
    for message, start in messages:
        lane = pl.multiple_of((start - odd + 8) * BS, 2 * BS)
        frame[:, pl.ds(lane, message.shape[2])] += message[j].astype(jnp.float32)
    first, last = 8 * BS, (8 + BAND) * BS

    @pl.when(odd == 0)
    def _():
        store(frame[:, first:last])

    @pl.when(odd == 1)
    def _():
        store(frame[:, first - BS : last - BS])


def early_kernel(core, own, direct, pair, out, frame):
    s, x = places(core)
    for j in range(NC):
        top = 27 - 3 * s - j
        messages = [(own, top - 12), (direct, top - 30 * x), (pair, top - 6 - 12 * x)]

        def store(value, j=j):
            out[j] = value

        in_frame(s, j, frame, messages, store)


def total_kernel(core, early, merged, far, out, frame, buf, sems):
    s, x = places(core)
    copies = []
    for j in range(NC):
        far_start = jnp.where(s == 1, 30 - j, -1 - j)

        def store(value, j=j):
            buf[j] = value + early[j]

        in_frame(s, j, frame, [(merged, 3 - 3 * s - j + 18 * x), (far, far_start)], store)
        copy = pltpu.make_async_copy(buf.at[j], out.at[j], sems.at[j])
        copy.start()
        copies.append(copy)
    for copy in copies:
        copy.wait()


def pick_kernel(core, source, outer, inner, buf, in_sems, out_sems):
    s, x = places(core)
    step = AGG // 4
    reads, writes = [], []
    for side, (target, which) in enumerate(((outer, s), (inner, 1 - s))):
        for k in range(4):
            n = len(reads)
            rows = pl.ds((NB - AGG) * which + k * step, step)
            part = buf.at[side, k * step : (k + 1) * step]
            into = target.at[k * step : (k + 1) * step]
            reads.append(pltpu.make_async_copy(source.at[rows], part, in_sems.at[n]))
            writes.append(pltpu.make_async_copy(part, into, out_sems.at[n]))
    for copy in reads:
        copy.start()
    for read, write in zip(reads, writes):
        read.wait()
        write.start()
    for copy in writes:
        copy.wait()


def permuted(block, pairs):
    return lax.ppermute(block, "dom", pairs)


def inverse_index(offset, slots, empty):
    order = jnp.arange(offset.shape[1], dtype=jnp.int32)[None, :, None]
    hit = offset[:, :, None] == jnp.arange(slots, dtype=jnp.int32)[None, None, :]
    return empty + jnp.sum(jnp.where(hit, order - empty, 0), axis=1)


def body(a_blocks, p_blocks, cols_a, cols_p):
    devices = lax.axis_size("dom")
    device = lax.axis_index("dom")
    count_agg = NC * devices
    count_rows = NB * devices
    first_agg = device * NC
    first_row = device * NB
    core = device.astype(jnp.int32).reshape(1)

    def shifted(distance):
        return [(i, (i + distance) % devices) for i in range(devices)]

    parity = device % 2
    smem = pl.BlockSpec(memory_space=pltpu.SMEM)
    vmem = pl.BlockSpec(memory_space=pltpu.VMEM)
    hbm = pl.BlockSpec(memory_space=pltpu.HBM)
    bf16 = jnp.bfloat16

    def params(mebibytes):
        return pltpu.CompilerParams(vmem_limit_bytes=mebibytes * 1024 * 1024)

    def cost(flops, size):
        return pl.CostEstimate(flops=flops, bytes_accessed=size, transcendentals=0)

    edge = jax.ShapeDtypeStruct((AGG,) + p_blocks.shape[1:], bf16)
    outer, inner = pl.pallas_call(
        pick_kernel,
        out_shape=[edge, edge],
        in_specs=[smem, hbm],
        out_specs=[hbm, hbm],
        scratch_shapes=[
            pltpu.VMEM((2,) + edge.shape, bf16),
            pltpu.SemaphoreType.DMA((8,)),
            pltpu.SemaphoreType.DMA((8,)),
        ],
        compiler_params=params(60),
        name="pick",
    )(core, p_blocks)
    outward = [(i, (i + (1 if i % 2 else -1)) % devices) for i in range(devices)]
    inward = [(i, i ^ 1) for i in range(devices)]
    outer, inner, edge_cols = lax.optimization_barrier((outer, inner, cols_p))
    p_slow = permuted(outer, outward)
    p_fast = permuted(inner, inward)
    edge_cols = jnp.stack([edge_cols[:AGG], edge_cols[NB - AGG :]])
    cols_slow = permuted(edge_cols[parity], outward)
    cols_fast = permuted(edge_cols[1 - parity], inward)

    def slots(cols, agg):
        return (cols - agg + H) % count_agg

    own_agg = jnp.arange(NB, dtype=jnp.int32)[:, None] // AGG
    inv_own = inverse_index(slots(cols_p, first_agg + own_agg) + own_agg + 1, COLS, KP)
    fast_place = NC * (1 - parity) - parity
    inv_fast = inverse_index(slots(cols_fast, first_agg + fast_place) + fast_place + 1, COLS, KP)
    slow_place = NC * parity - (1 - parity)
    inv_slow = inverse_index(slots(cols_slow, first_agg + slow_place) + 2 * parity, WSLOT, KP)
    inv_fast, inv_slow = lax.optimization_barrier((inv_fast, inv_slow))
    inv_a = inverse_index((cols_a - first_row - (own_agg - 1) * AGG) % count_rows, 3 * AGG, KA)

    def block(rows, width, kind=bf16):
        return jax.ShapeDtypeStruct((rows, BS, width), kind)

    span = WINDOW * BS
    outs = [
        block(NC, span),
        block(NC, span),
        block(NC, span),
        block(FIRST, span),
        block(REST, span),
        block(REST, 2 * AW),
        block(FIRST, AW),
        block(REST, AW),
        block(NC, AW),
        block(FIRST, AW),
        block(REST, AW),
        block(WCOLS, 2 * AW),
        block(WSLOT, AW, jnp.float32),
        block(AGG, AW),
    ]
    (
        send_low,
        send_high,
        far,
        inner,
        send_rest,
        fast_rest,
        slow_first,
        slow_rest,
        slow_far,
        other_first,
        other_rest,
        wt_fast,
        rest,
        at_halo,
    ) = pl.pallas_call(
        fast_kernel,
        out_shape=outs,
        in_specs=[smem] * 3 + [hbm, hbm, vmem],
        out_specs=[hbm] * len(outs),
        scratch_shapes=[
            pltpu.VMEM((NB + AGG, BS, KP * BS), bf16),
            pltpu.VMEM((COLS, BS, EXT * BS), bf16),
            pltpu.VMEM((NC, 3 * AGG, BS, AW), bf16),
            pltpu.VMEM((LANES, LANES), bf16),
            pltpu.VMEM((KP + 1, BS, LANES), bf16),
            pltpu.VMEM((KP + 1, BS, LANES), bf16),
            pltpu.VMEM((KA + 1, BS, LANES), bf16),
            pltpu.VMEM((KA + 1, BS, LANES), bf16),
            pltpu.VMEM((ROWS + REST, BS, 2 * AW), bf16),
            pltpu.VMEM((ROWS + REST, BS, span), bf16),
            pltpu.VMEM((REST, BS, 2 * AW), bf16),
            pltpu.VMEM((ROWS + NC, BS, AW), bf16),
            pltpu.VMEM((ROWS, BS, AW), bf16),
            pltpu.VMEM((WCOLS, BS, 2 * AW), bf16),
            pltpu.VMEM((WSLOT, BS, AW), jnp.float32),
            pltpu.SemaphoreType.DMA(((NB + AGG) // QUAD,)),
            pltpu.SemaphoreType.DMA((len(outs) + 10,)),
        ],
        compiler_params=params(56),
        cost_estimate=cost(20 * 10**9, 30 * 10**6),
        name="fast",
    )(core, jnp.concatenate([inv_own, inv_fast]), inv_a, p_blocks, p_fast, a_blocks)

    low = permuted(send_low, inward)
    high = permuted(send_high, inward)
    other_first = permuted(other_first, inward)
    at_halo, rest = pl.pallas_call(
        stage_kernel,
        out_shape=[block(AGG, AW), block(WSLOT, AW, jnp.float32)],
        in_specs=[hbm] * 2,
        out_specs=[vmem] * 2,
        scratch_shapes=[pltpu.SemaphoreType.DMA((2,))],
        compiler_params=params(8),
        cost_estimate=cost(10**6, 10**6),
        name="stage",
    )(at_halo, rest)
    p_slow, low, high, other_first = lax.optimization_barrier((p_slow, low, high, other_first))

    wt_slow = pl.pallas_call(
        slow_kernel,
        out_shape=block(WCOLS, AW),
        in_specs=[smem] * 2 + [vmem] * 3,
        out_specs=vmem,
        scratch_shapes=[
            pltpu.VMEM((LANES, LANES), bf16),
            pltpu.VMEM((KP + 1, BS, LANES), bf16),
            pltpu.VMEM((KP + 1, BS, LANES), bf16),
            pltpu.VMEM((WSLOT, BS, AW), bf16),
        ],
        compiler_params=params(24),
        cost_estimate=cost(20 * 10**9, 200 * 10**6),
        name="slow",
    )(core, inv_slow, p_slow, at_halo, rest)
    wt_other = permuted(wt_slow, inward)

    wt_slow, low, high = lax.optimization_barrier((wt_slow, low, high))
    far = pl.pallas_call(
        far_kernel,
        out_shape=block(NC, FAR * BS),
        in_specs=[smem] + [vmem] * 3,
        out_specs=vmem,
        compiler_params=params(16),
        cost_estimate=cost(10**9, 10**7),
        name="far",
    )(core, slow_far, wt_slow, far)
    far, wt_slow = lax.optimization_barrier((far, wt_slow))
    mine = pl.pallas_call(
        mine_kernel,
        out_shape=block(FIRST, span, jnp.float32),
        in_specs=[vmem] * 5,
        out_specs=vmem,
        compiler_params=params(24),
        cost_estimate=cost(10**10, 100 * 10**6),
        name="mine",
    )(slow_first, wt_slow, inner, low, high)
    crossing = [i for i in range(devices) if i % 4 in (1, 2)]
    far_near = permuted(far, [(i, i ^ 3) for i in crossing])
    relay, direct = pl.pallas_call(
        join_first_kernel,
        out_shape=[block(NC, span), block(NC, span, jnp.float32)],
        in_specs=[vmem] * 3,
        out_specs=[vmem] * 2,
        compiler_params=params(16),
        cost_estimate=cost(10**6, 10**5),
        name="join_first",
    )(other_first, wt_other, mine)
    relay, direct, far_near, send_rest, other_rest = lax.optimization_barrier(
        (relay, direct, far_near, send_rest, other_rest)
    )
    arrived_rest = permuted(send_rest, inward)
    other_rest = permuted(other_rest, inward)
    along_x = [(i, i ^ 2) for i in range(devices)]
    x_sign = [1 if i // 2 % 2 else -1 for i in range(devices)]
    relay = permuted(relay, along_x)

    def merge_rows(rows, other, shift, name):
        return pl.pallas_call(
            functools.partial(merge_kernel, shift=shift),
            out_shape=block(NC, MERGED * BS),
            in_specs=[smem, vmem, vmem],
            out_specs=vmem,
            scratch_shapes=[pltpu.VMEM((BS, MERGED * BS), jnp.float32)],
            compiler_params=params(16),
            cost_estimate=cost(10**7, 10**7),
            name=name,
        )(core, rows, other)

    direct = merge_rows(direct, far_near, 2, "merge_far")
    direct = permuted(direct, [(i, (i + 4 * x_sign[i]) % devices) for i in range(devices)])
    merge, pair, own = pl.pallas_call(
        join_rest_kernel,
        out_shape=[block(NC, span, jnp.float32), block(NC, span), block(NC, span, jnp.float32)],
        in_specs=[vmem] * 7,
        out_specs=[vmem] * 3,
        compiler_params=params(30),
        cost_estimate=cost(40 * 10**9, 200 * 10**6),
        name="join_rest",
    )(fast_rest, slow_rest, other_rest, wt_fast, wt_slow, wt_other, arrived_rest)
    relay, pair = lax.optimization_barrier((relay, pair))
    merged = merge_rows(merge, relay, 0, "merge")
    merged, far = lax.optimization_barrier((merged, far))
    merged = permuted(merged, [(i, (i - 4 * x_sign[i]) % devices) for i in range(devices)])
    pair = permuted(pair, along_x)
    straight = [i for i in range(devices) if i % 4 in (0, 3)]
    far = permuted(far, [(i, (i + (5 if i % 2 else -5)) % devices) for i in straight])

    total = block(NC, BAND * BS, jnp.float32)
    frame = pltpu.VMEM((BS, FRAME * BS), jnp.float32)
    early = pl.pallas_call(
        early_kernel,
        out_shape=total,
        in_specs=[smem] + [vmem] * 3,
        out_specs=vmem,
        scratch_shapes=[frame],
        compiler_params=params(16),
        cost_estimate=cost(10**10, 100 * 10**6),
        name="early",
    )(core, own, direct, pair)
    return pl.pallas_call(
        total_kernel,
        out_shape=total,
        in_specs=[smem] + [vmem] * 3,
        out_specs=hbm,
        scratch_shapes=[
            frame,
            pltpu.VMEM(total.shape, jnp.float32),
            pltpu.SemaphoreType.DMA((NC,)),
        ],
        compiler_params=params(20),
        cost_estimate=cost(10**7, 10**7),
        name="total",
    )(core, early, merged, far)


def solution(mesh):
    in_specs = (P("dom", None, None), P("dom", None, None), P("dom", None), P("dom", None))
    out_specs = P("dom", None, None)
    return jax.shard_map(body, mesh=mesh, in_specs=in_specs, out_specs=out_specs, check_vma=False)
```

```python
import functools

import jax
import jax.numpy as jnp
from jax import lax
from jax.experimental import pallas as pl
from jax.experimental.pallas import tpu as pltpu
from jax.sharding import PartitionSpec as P

BS = 64
KA = 7
KP = 27
AGG = 8
H = 15
NC = 3
NB = 24
WIN = 31
WSLOT = 33
BAND = 63

QUAD = 4
LANES = QUAD * BS
EXT = NB + 2 * AGG
COLS = NC + 2 * H + 2
WCOLS = 40
WINDOW = 38
TILES = 10
GROUPS = 5
K = NB * BS
AW = AGG * BS
FRAME = 80
NT = (((1,), (1,)), ((), ()))
ROWS = NC * GROUPS
FIRST = 2 * NC
REST = ROWS - FIRST
MERGED = WINDOW + 6
FAR = 36


def eye(n):
    rows = lax.broadcasted_iota(jnp.int32, (n, n), 0)
    lanes = lax.broadcasted_iota(jnp.int32, (n, n), 1)
    return jnp.where(rows == lanes, 1.0, 0.0).astype(jnp.bfloat16)


def low_half():
    return lax.broadcasted_iota(jnp.int32, (BS, 2 * BS), 1) < BS


def places(device):
    return device[0] % 2, device[0] // 2 % 2


def transpose_quad(unit, block, turned, width):
    for start in range(0, width, LANES):
        size = min(LANES, width - start)
        part = lax.dot_general(
            unit[:size, :size],
            block[:, start : start + size],
            NT,
            preferred_element_type=jnp.float32,
        )
        turned[start // BS : (start + size) // BS] = part.astype(jnp.bfloat16).reshape(
            size // BS, BS, LANES
        )


def spread_quad(turned, index, first, store, count):
    half = low_half()
    for slot in range(count):
        for pair in range(2):
            lanes = slice(pair * 2 * BS, (pair + 1) * 2 * BS)
            left = turned[index[first + 2 * pair, slot], :, lanes]
            right = turned[index[first + 2 * pair + 1, slot], :, lanes]
            store(slot, pair, jnp.where(half, left, right))


def turn_and_spread(count, turn, spread, buffers):
    even, odd = buffers
    turn(0, even)

    def two(step):
        turn(2 * step + 1, odd)
        spread(2 * step, even)
        turn(2 * step + 2, even)
        spread(2 * step + 1, odd)

    if count > 2:
        pl.loop(0, count // 2 - 1)(two)

    turn(count - 1, odd)
    spread(count - 2, even)
    spread(count - 1, odd)


def fast_kernel(
    core,
    inv_p,
    inv_a,
    p_own,
    p_fast,
    a_own,
    send_low,
    send_high,
    far,
    inner,
    send_rest,
    fast_rest,
    slow_first,
    slow_rest,
    slow_far,
    other_first,
    other_rest,
    wt,
    rest,
    at_halo,
    p_buf,
    ext,
    at,
    unit,
    turned_p,
    turned_p2,
    turned_a,
    turned_a2,
    lhs,
    rows_buf,
    fast_buf,
    slow_buf,
    other_buf,
    wt_buf,
    rest_buf,
    in_sems,
    out_sems,
):
    s, x = places(core)
    own_quads = NB // QUAD
    halo_quads = AGG // QUAD

    def load(quad):
        if quad < own_quads:
            source = p_own.at[quad * QUAD : (quad + 1) * QUAD]
        else:
            source = p_fast.at[(quad - own_quads) * QUAD : (quad - own_quads + 1) * QUAD]
        target = p_buf.at[quad * QUAD : (quad + 1) * QUAD]
        return pltpu.make_async_copy(source, target, in_sems.at[quad])

    for quad in range(own_quads + halo_quads):
        load(quad).start()

    unit[...] = eye(LANES)
    for buffers, empty in (((turned_p, turned_p2), KP), ((turned_a, turned_a2), KA)):
        for buffer in buffers:
            buffer[empty] = jnp.zeros((BS, LANES), jnp.bfloat16)

    def turn_a(quad, turned):
        block = a_own[pl.ds(quad * QUAD, QUAD)].reshape(LANES, KA * BS)
        transpose_quad(unit, block, turned, KA * BS)

    def spread_a(quad, turned):
        agg = quad // halo_quads
        first_lane = (quad % halo_quads) * LANES

        def store(slot, pair, value):
            lane = pl.multiple_of(first_lane + pair * 2 * BS, 2 * BS)
            at[agg, slot, :, pl.ds(lane, 2 * BS)] = value

        spread_quad(turned, inv_a, quad * QUAD, store, 3 * AGG)

    turn_and_spread(own_quads, turn_a, spread_a, (turned_a, turned_a2))

    slow_agg = 2 * s
    halo_copy = pltpu.make_async_copy(at.at[slow_agg, pl.ds(16 * s, AGG)], at_halo, out_sems.at[0])
    halo_copy.start()

    def turn_p(quad, turned):
        block = p_buf[pl.ds(quad * QUAD, QUAD)].reshape(LANES, KP * BS)
        transpose_quad(unit, block, turned, KP * BS)

    def spread_p(quad, turned):
        own_lane = AW + quad * LANES
        halo_lane = (AW + K) * (1 - s) + (quad - own_quads) * LANES
        first_lane = jnp.where(quad < own_quads, own_lane, halo_lane)

        def store(slot, pair, value):
            lane = pl.multiple_of(first_lane + pair * 2 * BS, 2 * BS)
            ext[slot, :, pl.ds(lane, 2 * BS)] = value

        spread_quad(turned, inv_p, quad * QUAD, store, COLS)

    for quad in range(own_quads + halo_quads):
        load(quad).wait()
    turn_and_spread(own_quads + halo_quads, turn_p, spread_p, (turned_p, turned_p2))

    fast_lanes = pl.ds(pl.multiple_of(AW + (1 - s) * AW, AW), 2 * AW)
    slow_lanes = pl.ds(pl.multiple_of(AW + 2 * s * AW, AW), AW)
    for place, i in enumerate((1 + 2 * x, 4 * x, 4 - 4 * x, 3 - 2 * x, 2)):
        for j in range(NC):
            row = NC * place + j
            mine, other = 6 * i + 3 + j + 1, 6 * i + 6 * (1 - s) + j + 1
            if place < 2:
                lhs[row] = ext[other, :, fast_lanes]
                lhs[FIRST + NC + row] = ext[mine, :, fast_lanes]
            else:
                lhs[ROWS + row - FIRST] = ext[other, :, fast_lanes]
                fast_buf[row - FIRST] = ext[mine, :, fast_lanes]
            slow_buf[row] = ext[mine, :, slow_lanes]
            other_buf[row] = ext[other, :, slow_lanes]
    for j in range(NC):
        lhs[FIRST + j] = ext[30 * s + j + 1, :, fast_lanes]
        slow_buf[ROWS + j] = ext[30 * s + j + 1, :, slow_lanes]
    copies = [halo_copy]

    def write(source, target):
        copy = pltpu.make_async_copy(source, target, out_sems.at[len(copies)])
        copy.start()
        copies.append(copy)

    write(other_buf.at[:FIRST], other_first)
    write(other_buf.at[FIRST:], other_rest)
    write(fast_buf, fast_rest)
    write(slow_buf.at[:FIRST], slow_first)
    write(slow_buf.at[FIRST:ROWS], slow_rest)
    write(slow_buf.at[ROWS:], slow_far)

    wt_buf[0:7] = jnp.zeros((7, BS, 2 * AW), jnp.bfloat16)
    wt_buf[33:] = jnp.zeros((WCOLS - 33, BS, 2 * AW), jnp.bfloat16)
    chunk = WSLOT // 3

    @pl.loop(0, 2)
    def _(place):
        agg = place + 1 - s
        lane = pl.multiple_of(agg * AW, AW)
        target = pl.multiple_of(place * AW, AW)

        @pl.loop(0, 3)
        def _(part):
            first = agg + part * chunk
            left = ext[pl.ds(first, chunk), :, pl.ds(lane, 3 * AW)].reshape(chunk * BS, 3 * AW)
            value = jnp.dot(
                left, at[agg].reshape(3 * AW, AW), preferred_element_type=jnp.float32
            )
            wt_buf[pl.ds(3 * s + first, chunk), :, pl.ds(target, AW)] = value.astype(
                jnp.bfloat16
            ).reshape(chunk, BS, AW)

    write(wt_buf, wt)

    @pl.loop(0, 3)
    def _(part):
        lane = pl.multiple_of(AW + s * AW, AW)
        left = ext[pl.ds(slow_agg + part * chunk, chunk), :, pl.ds(lane, 2 * AW)]
        right = at[slow_agg, pl.ds(AGG - AGG * s, 2 * AGG)].reshape(2 * AW, AW)
        value = jnp.dot(
            left.reshape(chunk * BS, 2 * AW), right, preferred_element_type=jnp.float32
        )
        rest_buf[pl.ds(part * chunk, chunk)] = value.reshape(chunk, BS, AW)

    write(rest_buf, rest)

    def emit(tile, width):
        right = wt_buf[pl.ds(QUAD * tile, width // BS)].reshape(width, 2 * AW)
        left = lhs[...].reshape((ROWS + REST) * BS, 2 * AW)
        value = lax.dot_general(left, right, NT, preferred_element_type=jnp.float32)
        rows_buf[:, :, tile_lanes(tile, width)] = value.astype(jnp.bfloat16).reshape(
            ROWS + REST, BS, width
        )

    parts = (
        (send_low, 0),
        (send_high, NC),
        (far, FIRST),
        (inner, FIRST + NC),
        (send_rest, ROWS),
    )
    bounds = (0, 4, 8, TILES)
    for first, last in zip(bounds[:-1], bounds[1:]):

        @pl.loop(first, min(last, TILES - 1))
        def _(tile):
            emit(tile, LANES)

        if last == TILES:
            emit(TILES - 1, LANES // 2)
        lanes = slice(first * LANES, min(last * LANES, WINDOW * BS))
        for target, row in parts:
            rows = slice(row, row + target.shape[0])
            write(rows_buf.at[rows, :, lanes], target.at[:, :, lanes])
    for copy in copies:
        copy.wait()


def each_tile(step):
    @pl.loop(0, TILES - 1)
    def _(tile):
        step(tile, LANES)

    step(TILES - 1, LANES // 2)


def tile_dot(rows, cols, tile, width):
    left = rows[...].reshape(rows.shape[0] * BS, rows.shape[2])
    right = cols[pl.ds(QUAD * tile, width // BS)].reshape(width, cols.shape[2])
    value = lax.dot_general(left, right, NT, preferred_element_type=jnp.float32)
    return value.reshape(rows.shape[0], BS, width)


def tile_lanes(tile, width):
    return pl.ds(pl.multiple_of(tile * LANES, LANES), width)


def far_kernel(core, slow, wt_slow, far_fast, far):
    s, x = places(core)

    @pl.loop(0, FAR // QUAD)
    def _(tile):
        left = slow[...].reshape(NC * BS, AW)
        right = wt_slow[pl.ds(QUAD * tile + 2 * s, QUAD)].reshape(LANES, AW)
        value = lax.dot_general(left, right, NT, preferred_element_type=jnp.float32)
        lanes = pl.ds(pl.multiple_of(tile * LANES + 2 * BS * s, 2 * BS), LANES)
        value = value.reshape(NC, BS, LANES) + far_fast[:, :, lanes].astype(jnp.float32)
        far[:, :, tile_lanes(tile, LANES)] = value.astype(jnp.bfloat16)


def mine_kernel(slow, wt_slow, inner, low, high, out):
    def step(tile, width):
        lanes = tile_lanes(tile, width)
        near = tile_dot(slow, wt_slow, tile, width) + inner[:, :, lanes].astype(jnp.float32)
        out[:NC, :, lanes] = near[:NC] + low[:, :, lanes].astype(jnp.float32)
        out[NC:, :, lanes] = near[NC:] + high[:, :, lanes].astype(jnp.float32)

    each_tile(step)


def slow_kernel(core, inv_slow, p_slow, at_halo, rest, wt, unit, turned_p, turned_p2, ext):
    s, x = places(core)
    unit[...] = eye(LANES)
    for buffer in (turned_p, turned_p2):
        buffer[KP] = jnp.zeros((BS, LANES), jnp.bfloat16)

    def turn(quad, turned):
        block = p_slow[quad * QUAD : (quad + 1) * QUAD].reshape(LANES, KP * BS)
        transpose_quad(unit, block, turned, KP * BS)

    def spread(quad, turned):
        def store(slot, pair, value):
            lane = quad * LANES + pair * 2 * BS
            ext[slot, :, lane : lane + 2 * BS] = value

        spread_quad(turned, inv_slow, quad * QUAD, store, WSLOT)

    turn_and_spread(AGG // QUAD, turn, spread, (turned_p, turned_p2))
    wt[0:5] = jnp.zeros((5, BS, AW), jnp.bfloat16)
    wt[WSLOT:] = jnp.zeros((WCOLS - WSLOT, BS, AW), jnp.bfloat16)
    chunk = WSLOT // 3

    @pl.loop(0, 3)
    def _(part):
        rows = pl.ds(part * chunk, chunk)
        value = jnp.dot(
            ext[rows].reshape(chunk * BS, AW),
            at_halo[...].reshape(AW, AW),
            preferred_element_type=jnp.float32,
        )
        value = value.reshape(chunk, BS, AW) + rest[rows]
        wt[pl.ds(5 * s + part * chunk, chunk)] = value.astype(jnp.bfloat16)


def join_first_kernel(other, wt_other, mine, relay, direct):
    def step(tile, width):
        lanes = tile_lanes(tile, width)
        value = tile_dot(other, wt_other, tile, width) + mine[:, :, lanes]
        relay[:, :, lanes] = value[:NC].astype(jnp.bfloat16)
        direct[:, :, lanes] = value[NC:]

    each_tile(step)


def join_rest_kernel(fast, slow, other, wt_fast, wt_slow, wt_other, arrived, merge, pair, own):
    def step(tile, width):
        lanes = tile_lanes(tile, width)
        value = tile_dot(fast, wt_fast, tile, width) + tile_dot(slow, wt_slow, tile, width)
        value = value + tile_dot(other, wt_other, tile, width)
        value = value + arrived[:, :, lanes].astype(jnp.float32)
        merge[:, :, lanes] = value[:NC]
        pair[:, :, lanes] = value[NC : 2 * NC].astype(jnp.bfloat16)
        own[:, :, lanes] = value[2 * NC :]

    each_tile(step)


def stage_kernel(at_halo, rest, at_out, rest_out, sems):
    copies = [
        pltpu.make_async_copy(at_halo, at_out, sems.at[0]),
        pltpu.make_async_copy(rest, rest_out, sems.at[1]),
    ]
    for copy in copies:
        copy.start()
    for copy in copies:
        copy.wait()


def merge_kernel(core, rows, other, out, frame, *, shift):
    s, x = places(core)
    step = 6 * BS
    for j in range(NC):
        frame[...] = jnp.zeros_like(frame)
        frame[:, pl.ds(pl.multiple_of(step * x, step), WINDOW * BS)] = rows[j]
        lane = pl.multiple_of(step * (1 - x) + shift * BS * x, 2 * BS)
        lanes = pl.ds(lane, other.shape[2])
        frame[:, lanes] += other[j].astype(jnp.float32)
        out[j] = frame[...].astype(jnp.bfloat16)


def in_frame(s, j, frame, messages, store, row=None):
    odd = (j + 1 - s) % 2
    frame[...] = jnp.zeros_like(frame)
    for message, start in messages:
        lane = pl.multiple_of((start - odd + 8) * BS, 2 * BS)
        frame[:, pl.ds(lane, message.shape[2])] += message[j if row is None else row].astype(
            jnp.float32
        )
    first, last = 8 * BS, (8 + BAND) * BS

    @pl.when(odd == 0)
    def _():
        store(frame[:, first:last])

    @pl.when(odd == 1)
    def _():
        store(frame[:, first - BS : last - BS])


def far_place(s, j):
    return jnp.where(s == 1, 30 - j, -1 - j)


def first_kernel(core, own, direct, far, out, frame):
    s, x = places(core)
    for j in range(NC):
        top = 27 - 3 * s - j
        messages = [(own, top - 12), (direct, top - 30 * x)]
        if j == 0:
            messages.append((far, far_place(s, j)))

        def store(value, j=j):
            out[j] = value

        in_frame(s, j, frame, messages, store)


def early_kernel(core, first, pair, merged, out, frame):
    s, x = places(core)
    for j in range(NC):
        top = 27 - 3 * s - j

        def store(value, j=j):
            out[j] = value + first[j]

        messages = [(pair, top - 6 - 12 * x), (merged, top - 24 + 18 * x)]
        in_frame(s, j, frame, messages, store)


def total_kernel(core, early, far, out, frame, buf, sems):
    s, x = places(core)
    copies = []
    buf[0] = early[0]
    for j in range(NC):
        if j > 0:

            def store(value, j=j):
                buf[j] = value + early[j]

            in_frame(s, j, frame, [(far, far_place(s, j))], store, j - 1)
        copy = pltpu.make_async_copy(buf.at[j], out.at[j], sems.at[j])
        copy.start()
        copies.append(copy)
    for copy in copies:
        copy.wait()


def pick_kernel(core, source, outer, inner, buf, in_sems, out_sems):
    s, x = places(core)
    step = AGG // 4
    reads, writes = [], []
    for side, (target, which) in enumerate(((outer, s), (inner, 1 - s))):
        for k in range(4):
            n = len(reads)
            rows = pl.ds((NB - AGG) * which + k * step, step)
            part = buf.at[side, k * step : (k + 1) * step]
            into = target.at[k * step : (k + 1) * step]
            reads.append(pltpu.make_async_copy(source.at[rows], part, in_sems.at[n]))
            writes.append(pltpu.make_async_copy(part, into, out_sems.at[n]))
    for copy in reads:
        copy.start()
    for read, write in zip(reads, writes):
        read.wait()
        write.start()
    for copy in writes:
        copy.wait()


def permuted(block, pairs):
    return lax.ppermute(block, "dom", pairs)


def inverse_index(offset, slots, empty):
    order = jnp.arange(offset.shape[1], dtype=jnp.int32)[None, :, None]
    hit = offset[:, :, None] == jnp.arange(slots, dtype=jnp.int32)[None, None, :]
    return empty + jnp.sum(jnp.where(hit, order - empty, 0), axis=1)


def body(a_blocks, p_blocks, cols_a, cols_p):
    devices = lax.axis_size("dom")
    device = lax.axis_index("dom")
    count_agg = NC * devices
    count_rows = NB * devices
    first_agg = device * NC
    first_row = device * NB
    core = device.astype(jnp.int32).reshape(1)

    def shifted(distance):
        return [(i, (i + distance) % devices) for i in range(devices)]

    parity = device % 2
    smem = pl.BlockSpec(memory_space=pltpu.SMEM)
    vmem = pl.BlockSpec(memory_space=pltpu.VMEM)
    hbm = pl.BlockSpec(memory_space=pltpu.HBM)
    bf16 = jnp.bfloat16

    def params(mebibytes):
        return pltpu.CompilerParams(vmem_limit_bytes=mebibytes * 1024 * 1024)

    def cost(flops, size):
        return pl.CostEstimate(flops=flops, bytes_accessed=size, transcendentals=0)

    edge = jax.ShapeDtypeStruct((AGG,) + p_blocks.shape[1:], bf16)
    outer, inner = pl.pallas_call(
        pick_kernel,
        out_shape=[edge, edge],
        in_specs=[smem, hbm],
        out_specs=[hbm, hbm],
        scratch_shapes=[
            pltpu.VMEM((2,) + edge.shape, bf16),
            pltpu.SemaphoreType.DMA((8,)),
            pltpu.SemaphoreType.DMA((8,)),
        ],
        compiler_params=params(60),
        name="pick",
    )(core, p_blocks)
    outward = [(i, (i + (1 if i % 2 else -1)) % devices) for i in range(devices)]
    inward = [(i, i ^ 1) for i in range(devices)]
    outer, inner, edge_cols = lax.optimization_barrier((outer, inner, cols_p))
    p_slow = permuted(outer, outward)
    p_fast = permuted(inner, inward)
    edge_cols = jnp.stack([edge_cols[:AGG], edge_cols[NB - AGG :]])
    cols_slow = permuted(edge_cols[parity], outward)
    cols_fast = permuted(edge_cols[1 - parity], inward)

    def slots(cols, agg):
        return (cols - agg + H) % count_agg

    own_agg = jnp.arange(NB, dtype=jnp.int32)[:, None] // AGG
    inv_own = inverse_index(slots(cols_p, first_agg + own_agg) + own_agg + 1, COLS, KP)
    fast_place = NC * (1 - parity) - parity
    inv_fast = inverse_index(slots(cols_fast, first_agg + fast_place) + fast_place + 1, COLS, KP)
    slow_place = NC * parity - (1 - parity)
    inv_slow = inverse_index(slots(cols_slow, first_agg + slow_place) + 2 * parity, WSLOT, KP)
    inv_fast, inv_slow = lax.optimization_barrier((inv_fast, inv_slow))
    inv_a = inverse_index((cols_a - first_row - (own_agg - 1) * AGG) % count_rows, 3 * AGG, KA)

    def block(rows, width, kind=bf16):
        return jax.ShapeDtypeStruct((rows, BS, width), kind)

    span = WINDOW * BS
    outs = [
        block(NC, span),
        block(NC, span),
        block(NC, span),
        block(FIRST, span),
        block(REST, span),
        block(REST, 2 * AW),
        block(FIRST, AW),
        block(REST, AW),
        block(NC, AW),
        block(FIRST, AW),
        block(REST, AW),
        block(WCOLS, 2 * AW),
        block(WSLOT, AW, jnp.float32),
        block(AGG, AW),
    ]
    (
        send_low,
        send_high,
        far,
        inner,
        send_rest,
        fast_rest,
        slow_first,
        slow_rest,
        slow_far,
        other_first,
        other_rest,
        wt_fast,
        rest,
        at_halo,
    ) = pl.pallas_call(
        fast_kernel,
        out_shape=outs,
        in_specs=[smem] * 3 + [hbm, hbm, vmem],
        out_specs=[hbm] * len(outs),
        scratch_shapes=[
            pltpu.VMEM((NB + AGG, BS, KP * BS), bf16),
            pltpu.VMEM((COLS, BS, EXT * BS), bf16),
            pltpu.VMEM((NC, 3 * AGG, BS, AW), bf16),
            pltpu.VMEM((LANES, LANES), bf16),
            pltpu.VMEM((KP + 1, BS, LANES), bf16),
            pltpu.VMEM((KP + 1, BS, LANES), bf16),
            pltpu.VMEM((KA + 1, BS, LANES), bf16),
            pltpu.VMEM((KA + 1, BS, LANES), bf16),
            pltpu.VMEM((ROWS + REST, BS, 2 * AW), bf16),
            pltpu.VMEM((ROWS + REST, BS, span), bf16),
            pltpu.VMEM((REST, BS, 2 * AW), bf16),
            pltpu.VMEM((ROWS + NC, BS, AW), bf16),
            pltpu.VMEM((ROWS, BS, AW), bf16),
            pltpu.VMEM((WCOLS, BS, 2 * AW), bf16),
            pltpu.VMEM((WSLOT, BS, AW), jnp.float32),
            pltpu.SemaphoreType.DMA(((NB + AGG) // QUAD,)),
            pltpu.SemaphoreType.DMA((len(outs) + 10,)),
        ],
        compiler_params=params(56),
        cost_estimate=cost(20 * 10**9, 30 * 10**6),
        name="fast",
    )(core, jnp.concatenate([inv_own, inv_fast]), inv_a, p_blocks, p_fast, a_blocks)

    low = permuted(send_low, inward)
    high = permuted(send_high, inward)
    other_first = permuted(other_first, inward)
    at_halo, rest = pl.pallas_call(
        stage_kernel,
        out_shape=[block(AGG, AW), block(WSLOT, AW, jnp.float32)],
        in_specs=[hbm] * 2,
        out_specs=[vmem] * 2,
        scratch_shapes=[pltpu.SemaphoreType.DMA((2,))],
        compiler_params=params(8),
        cost_estimate=cost(10**6, 10**6),
        name="stage",
    )(at_halo, rest)
    p_slow, low, high, other_first = lax.optimization_barrier((p_slow, low, high, other_first))

    wt_slow = pl.pallas_call(
        slow_kernel,
        out_shape=block(WCOLS, AW),
        in_specs=[smem] * 2 + [vmem] * 3,
        out_specs=vmem,
        scratch_shapes=[
            pltpu.VMEM((LANES, LANES), bf16),
            pltpu.VMEM((KP + 1, BS, LANES), bf16),
            pltpu.VMEM((KP + 1, BS, LANES), bf16),
            pltpu.VMEM((WSLOT, BS, AW), bf16),
        ],
        compiler_params=params(24),
        cost_estimate=cost(20 * 10**9, 200 * 10**6),
        name="slow",
    )(core, inv_slow, p_slow, at_halo, rest)
    wt_other = permuted(wt_slow, inward)

    wt_slow, low, high = lax.optimization_barrier((wt_slow, low, high))
    far = pl.pallas_call(
        far_kernel,
        out_shape=block(NC, FAR * BS),
        in_specs=[smem] + [vmem] * 3,
        out_specs=vmem,
        compiler_params=params(16),
        cost_estimate=cost(10**9, 10**7),
        name="far",
    )(core, slow_far, wt_slow, far)
    far, wt_slow = lax.optimization_barrier((far, wt_slow))
    mine = pl.pallas_call(
        mine_kernel,
        out_shape=block(FIRST, span, jnp.float32),
        in_specs=[vmem] * 5,
        out_specs=vmem,
        compiler_params=params(24),
        cost_estimate=cost(10**10, 100 * 10**6),
        name="mine",
    )(slow_first, wt_slow, inner, low, high)
    crossing = [i for i in range(devices) if i % 4 in (1, 2)]
    far_near = permuted(far, [(i, i ^ 3) for i in crossing])
    relay, direct = pl.pallas_call(
        join_first_kernel,
        out_shape=[block(NC, span), block(NC, span, jnp.float32)],
        in_specs=[vmem] * 3,
        out_specs=[vmem] * 2,
        compiler_params=params(16),
        cost_estimate=cost(10**6, 10**5),
        name="join_first",
    )(other_first, wt_other, mine)
    relay, direct, far_near, send_rest, other_rest = lax.optimization_barrier(
        (relay, direct, far_near, send_rest, other_rest)
    )
    arrived_rest = permuted(send_rest, inward)
    other_rest = permuted(other_rest, inward)
    along_x = [(i, i ^ 2) for i in range(devices)]
    x_sign = [1 if i // 2 % 2 else -1 for i in range(devices)]
    relay = permuted(relay, along_x)

    def merge_rows(rows, other, shift, name):
        return pl.pallas_call(
            functools.partial(merge_kernel, shift=shift),
            out_shape=block(NC, MERGED * BS),
            in_specs=[smem, vmem, vmem],
            out_specs=vmem,
            scratch_shapes=[pltpu.VMEM((BS, MERGED * BS), jnp.float32)],
            compiler_params=params(16),
            cost_estimate=cost(10**7, 10**7),
            name=name,
        )(core, rows, other)

    direct = merge_rows(direct, far_near, 2, "merge_far")
    direct = permuted(direct, [(i, (i + 4 * x_sign[i]) % devices) for i in range(devices)])
    merge, pair, own = pl.pallas_call(
        join_rest_kernel,
        out_shape=[block(NC, span, jnp.float32), block(NC, span), block(NC, span, jnp.float32)],
        in_specs=[vmem] * 7,
        out_specs=[vmem] * 3,
        compiler_params=params(30),
        cost_estimate=cost(40 * 10**9, 200 * 10**6),
        name="join_rest",
    )(fast_rest, slow_rest, other_rest, wt_fast, wt_slow, wt_other, arrived_rest)
    pair, far_head = lax.optimization_barrier((pair, far[:1]))
    relay, pair = lax.optimization_barrier((relay, pair))
    merged = merge_rows(merge, relay, 0, "merge")
    merged, far_tail = lax.optimization_barrier((merged, far[1:]))
    merged = permuted(merged, [(i, (i - 4 * x_sign[i]) % devices) for i in range(devices)])
    pair = permuted(pair, along_x)
    straight = [i for i in range(devices) if i % 4 in (0, 3)]
    reach = [(i, (i + (5 if i % 2 else -5)) % devices) for i in straight]
    far_head = permuted(far_head, reach)
    far_tail = permuted(far_tail, reach)

    total = block(NC, BAND * BS, jnp.float32)
    frame = pltpu.VMEM((BS, FRAME * BS), jnp.float32)

    def partly(kernel, name, *terms):
        return pl.pallas_call(
            kernel,
            out_shape=total,
            in_specs=[smem] + [vmem] * len(terms),
            out_specs=vmem,
            scratch_shapes=[frame],
            compiler_params=params(16),
            cost_estimate=cost(10**10, 100 * 10**6),
            name=name,
        )(core, *terms)

    first = partly(first_kernel, "first", own, direct, far_head)
    early = partly(early_kernel, "early", first, pair, merged)
    return pl.pallas_call(
        total_kernel,
        out_shape=total,
        in_specs=[smem] + [vmem] * 2,
        out_specs=hbm,
        scratch_shapes=[
            frame,
            pltpu.VMEM(total.shape, jnp.float32),
            pltpu.SemaphoreType.DMA((NC,)),
        ],
        compiler_params=params(20),
        cost_estimate=cost(10**7, 10**7),
        name="total",
    )(core, early, far_tail)


def solution(mesh):
    in_specs = (P("dom", None, None), P("dom", None, None), P("dom", None), P("dom", None))
    out_specs = P("dom", None, None)
    return jax.shard_map(body, mesh=mesh, in_specs=in_specs, out_specs=out_specs, check_vma=False)
```
